128 devices in a mesh: lat: 8 (over z, x_lo), lon: 16 (over y, x_hi, core).
Axes of the slice: x: 4 (x_hi: 2, x_lo: 2; x = x_hi * 2 + x_lo), y: 4, z: 4, core: 2. Of those that a mesh axis runs over, the one named last changes fastest.
Arguments:
- tokens: bfloat16 [2, 96, 192, 512], P(None, 'lat', 'lon'), may hold values from -6 to 6
- window_ids: int32 [96, 192], P('lat', 'lon'), may hold values from 0 to 3, as said below
- cotangent: bfloat16 [2, 48, 96, 1024], P(None, 'lat', 'lon'), may hold values from -6 to 6
- w_qkv: bfloat16 [512, 1536], replicated, may hold values from -0.25 to 0.25
- w_out: bfloat16 [512, 512], replicated, may hold values from -0.25 to 0.25
- w_up: bfloat16 [512, 2048], replicated, may hold values from -0.25 to 0.25
- w_down: bfloat16 [2048, 512], replicated, may hold values from -0.125 to 0.125
- w_merge: bfloat16 [2048, 1024], replicated, may hold values from -0.125 to 0.125
Outputs:
- level_two: bfloat16 [2, 48, 96, 1024], P(None, 'lat', 'lon')
- grad_tokens: bfloat16 [2, 96, 192, 512], P(None, 'lat', 'lon')
- grad_qkv: float32 [512, 1536], P(('lat', 'lon'))
- grad_out: float32 [512, 512], P(('lat', 'lon'))
- grad_up: float32 [512, 2048], P(('lat', 'lon'))
- grad_down: float32 [2048, 512], P(('lat', 'lon'))
- grad_merge: float32 [2048, 1024], P(('lat', 'lon'))
The draws below stay inside these ranges and needn't reach their ends.
Inputs may be any that keep to these rules, and one draw needn't show every extreme that they name: window_ids gives the shift regions of the rolled grid: latitude rows below 84 have label 0; in each longitude column, rows 84 to 89 share one label of 1 to 3 and the last 6 rows, which wrapped from the other end, share another label of 1 to 3, different from the first; these two labels are drawn for each column.
All inputs are finite; a program needn't handle non-finite values.
Results may differ from the reference program's by a relative error of at most 0.018.
Values may be sent and summed in bfloat16 or wider, within the bound.
No kernel may reach another device: no remote copies, remote signals or barrier semaphores. Data moves between devices by JAX's collectives and lax.ppermute only.
A program may use at most 128 MiB of HBM per device.

```python
import jax
import jax.numpy as jnp
from jax import lax

D = 512
FF = 2048
D2 = 1024
HEAD = 32
WIN = 12
LEV = 2
NLAT = 96
NLON = 192
HALF_LAT = 48
HALF_LON = 96


def draw_window_ids(key, part):
    key = jax.random.fold_in(key, 5)
    key_seam, key_step = jax.random.split(key)
    columns = jnp.arange(NLON, dtype=jnp.int32)
    seam_label = jax.random.randint(key_seam, (NLON,), 1, 4).astype(jnp.int32)
    seam_label = jnp.where(columns == 0, 3, seam_label).astype(jnp.int32)
    step_size = jax.random.randint(key_step, (NLON,), 1, 3).astype(jnp.int32)
    wrap_label = (1 + (seam_label - 1 + step_size) % 3).astype(jnp.int32)
    rows = jnp.arange(NLAT, dtype=jnp.int32)[:, None]
    labels = jnp.where(rows >= NLAT - WIN // 2, wrap_label[None, :], jnp.where(rows >= NLAT - WIN, seam_label[None, :], 0))
    return labels.astype(jnp.int32)


def level_of(rng, dims, cuts, low, high):
    gain, own = 1.0, jax.random.fold_in(rng, 6)
    for dim, blocks in cuts:
        draws = jnp.exp(jax.random.uniform(jax.random.fold_in(own, dim), (blocks,), jnp.float32, low / len(cuts), high / len(cuts)))
        gain = gain * jnp.repeat(draws, dims[dim] // blocks).reshape([-1 if axis == dim else 1 for axis in range(len(dims))])
    return gain


def bell_draw(own_key, dims, spread, most, cuts=(), held_as=jnp.bfloat16):
    result = jax.random.normal(own_key, dims, jnp.float32) * spread
    if len(cuts) > 0:
        result = level_of(own_key, dims, cuts, -0.22, 0.18) * result
    return jnp.clip(result, min=-most, max=most).astype(held_as)


def setup_inputs(seed: int = 0) -> dict:
    key_list = jax.random.split(jax.random.key(seed), 9)
    tokens = bell_draw(key_list[0], (LEV, NLAT, NLON, D), 1.0, 6.0, ((1, 8), (2, 16)))
    window_ids = draw_window_ids(jax.random.fold_in(key_list[8], 71), 0)
    cotangent = bell_draw(key_list[2], (LEV, HALF_LAT, HALF_LON, D2), 1.0, 6.0, ((1, 8), (2, 16)))
    w_qkv = bell_draw(key_list[3], (D, 3 * D), D ** -0.5, 0.25)
    w_out = bell_draw(key_list[4], (D, D), D ** -0.5, 0.25)
    w_up = bell_draw(key_list[5], (D, FF), D ** -0.5, 0.25)
    w_down = bell_draw(key_list[6], (FF, D), FF ** -0.5, 0.125)
    w_merge = bell_draw(key_list[7], (4 * D, D2), (4 * D) ** -0.5, 0.125)
    return dict(tokens=tokens, window_ids=window_ids, cotangent=cotangent, w_qkv=w_qkv, w_out=w_out, w_up=w_up, w_down=w_down, w_merge=w_merge)


EPS = 1e-05

def normalize(values):
    wide = values.astype(jnp.float32)
    centered = wide - lax.optimization_barrier(jnp.mean(wide, axis=-1, keepdims=True))
    inverse_std = lax.rsqrt(lax.optimization_barrier(jnp.mean(centered * centered, axis=-1, keepdims=True)) + EPS)
    return (centered * inverse_std, inverse_std)

def norm_back(normed, inverse_std, upstream):
    mean_grad = lax.optimization_barrier(jnp.mean(upstream, axis=-1, keepdims=True))
    mean_cross = lax.optimization_barrier(jnp.mean(upstream * normed, axis=-1, keepdims=True))
    return inverse_std * (upstream - mean_grad - normed * mean_cross)

def gelu_slope(values):
    cumulative = 0.5 * (1.0 + jax.scipy.special.erf(values * 0.7071067811865476))
    return cumulative + values * jnp.exp(-0.5 * values * values) * 0.3989422804014327

def matmul(left, right):
    return jnp.dot(left, right, preferred_element_type=jnp.float32)

def matmul_t(left, right):
    return jnp.dot(left, right.T, preferred_element_type=jnp.float32)

def weight_grad(activations, upstream):
    fan_in = activations.shape[-1]
    flat_left = activations.reshape(-1, fan_in)
    flat_right = upstream.reshape(-1, upstream.shape[-1])
    return jnp.dot(flat_left.T, flat_right, preferred_element_type=jnp.float32)

def to_windows(packed, window):
    levels, lat_rows, lon_cols, channels = packed.shape
    shaped = packed.reshape(levels, lat_rows // window, window, lon_cols // window, window, channels)
    return shaped.transpose(1, 3, 0, 2, 4, 5).reshape(lat_rows // window, lon_cols // window, levels * window * window, channels)

def from_windows(windowed, levels, lat_rows, lon_cols, window):
    channels = windowed.shape[-1]
    shaped = windowed.reshape(lat_rows // window, lon_cols // window, levels, window, window, channels)
    return shaped.transpose(2, 0, 3, 1, 4, 5).reshape(levels, lat_rows, lon_cols, channels)

def window_labels(grid, levels, window):
    lat_rows, lon_cols = grid.shape
    tiles = grid.reshape(lat_rows // window, window, lon_cols // window, window).transpose(0, 2, 1, 3)
    tiles = tiles.reshape(lat_rows // window, lon_cols // window, 1, window * window)
    tiles = jnp.broadcast_to(tiles, (lat_rows // window, lon_cols // window, levels, window * window))
    return tiles.reshape(lat_rows // window, lon_cols // window, levels * window * window)

def split_heads(packed):
    num_windows, win_tokens, channels = packed.shape
    features = channels // 3
    heads = features // HEAD
    query = packed[:, :, :features].reshape(num_windows, win_tokens, heads, HEAD)
    keys = packed[:, :, features:2 * features].reshape(num_windows, win_tokens, heads, HEAD)
    values = packed[:, :, 2 * features:].reshape(num_windows, win_tokens, heads, HEAD)
    return (query, keys, values)

def attention_weights(query, keys, labels):
    scores = jnp.einsum('nqhd,nkhd->nhqk', query.astype(jnp.float32), keys.astype(jnp.float32)) * HEAD ** (-0.5)
    allowed = labels[:, None, :, None] == labels[:, None, None, :]
    scores = jnp.where(allowed, scores, -1e+30)
    return jax.nn.softmax(scores, axis=-1)

def window_forward(packed, labels):
    num_windows, win_tokens, channels = packed.shape
    query, keys, values = split_heads(packed)
    probs = attention_weights(query, keys, labels)
    weights = probs.astype(jnp.bfloat16)
    mixed = jnp.einsum('nhqk,nkhd->nqhd', weights.astype(jnp.float32), values.astype(jnp.float32))
    return mixed.astype(jnp.bfloat16).reshape(num_windows, win_tokens, channels // 3)

def window_backward(packed, labels, upstream):
    num_windows, win_tokens, channels = packed.shape
    query, keys, values = split_heads(packed)
    probs = attention_weights(query, keys, labels)
    weights = probs.astype(jnp.bfloat16)
    grad_heads = upstream.reshape(query.shape).astype(jnp.float32)
    grad_values = jnp.einsum('nhqk,nqhd->nkhd', weights.astype(jnp.float32), grad_heads)
    grad_weights = jnp.einsum('nqhd,nkhd->nhqk', grad_heads, values.astype(jnp.float32))
    total = lax.optimization_barrier(jnp.sum(grad_weights * probs, axis=-1, keepdims=True))
    grad_scores = (probs * (grad_weights - total) * HEAD ** (-0.5)).astype(jnp.bfloat16).astype(jnp.float32)
    grad_query = jnp.einsum('nhqk,nkhd->nqhd', grad_scores, keys.astype(jnp.float32))
    grad_keys = jnp.einsum('nhqk,nqhd->nkhd', grad_scores, query.astype(jnp.float32))
    shape_out = (num_windows, win_tokens, channels // 3)
    return jnp.concatenate([grad_query.astype(jnp.bfloat16).reshape(shape_out), grad_keys.astype(jnp.bfloat16).reshape(shape_out), grad_values.astype(jnp.bfloat16).reshape(shape_out)], axis=-1)

def merge_pairs(field):
    levels, lat_rows, lon_cols, features = field.shape
    shaped = field.reshape(levels, lat_rows // 2, 2, lon_cols // 2, 2, features)
    return shaped.transpose(0, 1, 3, 4, 2, 5).reshape(levels, lat_rows // 2, lon_cols // 2, 4 * features)

def split_pairs(field):
    levels, half_rows, half_cols, channels = field.shape
    shaped = field.reshape(levels, half_rows, half_cols, 2, 2, channels // 4)
    return shaped.transpose(0, 1, 4, 2, 3, 5).reshape(levels, 2 * half_rows, 2 * half_cols, channels // 4)

def attend_all(packed_win, labels):

    def one_row(pair):
        return window_forward(pair[0], pair[1])
    return lax.map(one_row, (packed_win, labels))

def attend_back_all(packed_win, labels, upstream_win):

    def one_row(triple):
        return window_backward(triple[0], triple[1], triple[2])
    return lax.map(one_row, (packed_win, labels, upstream_win))

def reference(tokens, window_ids, cotangent, w_qkv, w_out, w_up, w_down, w_merge):
    half_win = WIN // 2
    levels, lat_rows, lon_cols, features = tokens.shape
    normed_in, inverse_in = normalize(tokens)
    first_norm = normed_in.astype(jnp.bfloat16)
    rolled = jnp.roll(first_norm, (-half_win, -half_win), axis=(1, 2))
    packed = matmul(rolled, w_qkv).astype(jnp.bfloat16)
    labels = window_labels(window_ids, levels, WIN)
    packed_win = to_windows(packed, WIN)
    attended = from_windows(attend_all(packed_win, labels), levels, lat_rows, lon_cols, WIN)
    attn_out = matmul(attended, w_out).astype(jnp.bfloat16)
    returned = jnp.roll(attn_out, (half_win, half_win), axis=(1, 2))
    middle = (tokens.astype(jnp.float32) + returned.astype(jnp.float32)).astype(jnp.bfloat16)
    normed_mid, inverse_mid = normalize(middle)
    second_norm = normed_mid.astype(jnp.bfloat16)
    before_act = matmul(second_norm, w_up)
    hidden = jax.nn.gelu(before_act, approximate=False).astype(jnp.bfloat16)
    after_mlp = (middle.astype(jnp.float32) + matmul(hidden, w_down)).astype(jnp.bfloat16)
    merged = merge_pairs(after_mlp)
    normed_out, inverse_out = normalize(merged)
    merged_norm = normed_out.astype(jnp.bfloat16)
    level_two = matmul(merged_norm, w_merge).astype(jnp.bfloat16)
    grad_merge = weight_grad(merged_norm, cotangent)
    grad_merged = norm_back(normed_out, inverse_out, matmul_t(cotangent, w_merge)).astype(jnp.bfloat16)
    grad_after = split_pairs(grad_merged)
    grad_down = weight_grad(hidden, grad_after)
    grad_before = (matmul_t(grad_after, w_down) * gelu_slope(before_act)).astype(jnp.bfloat16)
    grad_up = weight_grad(second_norm, grad_before)
    grad_middle = (grad_after.astype(jnp.float32) + norm_back(normed_mid, inverse_mid, matmul_t(grad_before, w_up))).astype(jnp.bfloat16)
    grad_attn = jnp.roll(grad_middle, (-half_win, -half_win), axis=(1, 2))
    grad_out = weight_grad(attended, grad_attn)
    grad_attended = matmul_t(grad_attn, w_out).astype(jnp.bfloat16)
    grad_packed_win = attend_back_all(packed_win, labels, to_windows(grad_attended, WIN))
    grad_packed = from_windows(grad_packed_win, levels, lat_rows, lon_cols, WIN)
    grad_qkv = weight_grad(rolled, grad_packed)
    grad_rolled = matmul_t(grad_packed, w_qkv).astype(jnp.bfloat16)
    grad_first = jnp.roll(grad_rolled, (half_win, half_win), axis=(1, 2))
    grad_tokens = (grad_middle.astype(jnp.float32) + norm_back(normed_in, inverse_in, grad_first.astype(jnp.float32))).astype(jnp.bfloat16)
    return (level_two, grad_tokens, grad_qkv, grad_out, grad_up, grad_down, grad_merge)
```

```python
import functools

import jax
import jax.numpy as jnp
import numpy as np
from jax import lax
from jax.experimental import pallas as pl
from jax.experimental.pallas import tpu as pltpu
from jax.sharding import PartitionSpec as P

HEAD = 32
WIN = 12
TOKENS = 2 * WIN * WIN
MERGED = TOKENS // 4
EPS = 1e-05
LOG2E = 1.4426950408889634
GRID = ("z", "x_lo", "y", "x_hi", "core")
BF16 = jnp.bfloat16
F32 = jnp.float32

FIRST = {"z": ("z",), "y": ("y",), "x": ("x_lo", "x_hi")}
REST = {
    "z": ("x_lo", "y", "x_hi"),
    "y": ("z", "x_lo", "x_hi"),
    "x": ("z", "y"),
}
SIZES = {"z": 4, "x_lo": 2, "y": 4, "x_hi": 2}


def place_of(chunk, first):
    at = {"core": chunk % 2, "x_hi": chunk // 2 % 2, "y": chunk // 4 % 4}
    at["x_lo"], at["z"] = chunk // 16 % 2, chunk // 32
    lead = rest = 0
    for name in FIRST[first]:
        lead = lead * SIZES[name] + at[name]
    for name in REST[first]:
        rest = rest * SIZES[name] + at[name]
    return at["core"], lead, rest


def row_order(first):
    order = np.zeros((512, 512), np.float32)
    for chunk in range(128):
        core, lead, rest = place_of(chunk, first)
        for row in range(4):
            order[core * 256 + (lead * 16 + rest) * 4 + row, chunk * 4 + row] = 1.0
    return order


def token_order():
    order = np.zeros((4, TOKENS, MERGED), np.float32)
    for quad in range(4):
        for row in range(6):
            for col in range(6):
                for level in range(2):
                    position = (col % 2) * 2 + row % 2
                    patch = quad * 18 + (row // 2 * 3 + col // 2) * 2 + level
                    order[quad, position * MERGED + patch, (row * 6 + col) * 2 + level] = 1.0
    return order


def dot(left, right, left_dim=1, right_dim=0):
    return lax.dot_general(
        left, right, (((left_dim,), (right_dim,)), ((), ())), preferred_element_type=F32
    )


def normalize(wide):
    centered = wide - jnp.mean(wide, axis=-1, keepdims=True)
    inverse_std = lax.rsqrt(jnp.mean(centered * centered, axis=-1, keepdims=True) + EPS)
    return centered * inverse_std, inverse_std


def norm_back(normed, inverse_std, upstream):
    mean_grad = jnp.mean(upstream, axis=-1, keepdims=True)
    mean_cross = jnp.mean(upstream * normed, axis=-1, keepdims=True)
    return inverse_std * (upstream - mean_grad - normed * mean_cross)


def eye(size):
    rows = lax.broadcasted_iota(jnp.int32, (size, size), 0)
    cols = lax.broadcasted_iota(jnp.int32, (size, size), 1)
    return jnp.where(rows == cols, 1.0, 0.0).astype(BF16)


def forward_kernel(
    core_ref, quad0, quad1, quad2, quad3, order_ref, bias_ref, cot_ref, rows_ref, w_qkv, w_qkv_t,
    w_out, w_up, w_down, w_merge,
    level_two_ref, merge_a_keep, merge_a_send, merge_b_keep, merge_b_send, down_keep, down_send,
    up_keep, up_send, tokens_ref, packed_ref, keys_t_ref, probs_ref, attended_ref, middle_grad_ref,
    first_t_ref,
    query_t, values_t, slope_ref, hidden_ref, attended_t,
):
    even = core_ref[0] == 0
    quads = (quad0, quad1, quad2, quad3)
    tokens = sum(dot(order_ref[q], quads[q][...]) for q in range(4))
    tokens_ref[...] = tokens.astype(BF16)
    first_norm = normalize(tokens)[0].astype(BF16)
    first_t_ref[...] = dot(rows_ref[0], first_norm, 1, 1).astype(BF16)
    for part in range(12):
        packed_ref[part] = dot(first_norm, w_qkv[:, part * 128 : part * 128 + 128]).astype(BF16)
    query_t[...] = dot(w_qkv_t[:512], first_norm, 1, 1).astype(BF16)
    keys_t_ref[...] = dot(w_qkv_t[512:1024], first_norm, 1, 1).astype(BF16)
    values_t[...] = dot(w_qkv_t[1024:], first_norm, 1, 1).astype(BF16)

    head_of_row = lax.broadcasted_iota(jnp.int32, (128, TOKENS), 0) // HEAD

    def attend(group, _):
        keys = packed_ref[4 + group]
        queries = query_t[pl.ds(pl.multiple_of(group * 128, 128), 128), :]
        for head in range(4):
            masked = jnp.where(head_of_row == head, queries, jnp.zeros_like(queries))
            scores = dot(keys, masked) * (HEAD ** (-0.5) * LOG2E) + bias_ref[...]
            raised = jnp.exp2(scores - jnp.max(scores, axis=0, keepdims=True))
            inverse = 1.0 / jnp.sum(raised, axis=0, keepdims=True)
            probs = (raised * inverse).astype(BF16)
            probs_ref[group * 4 + head] = probs
            at = pl.ds(pl.multiple_of(group * 128 + head * HEAD, HEAD), HEAD)
            attended_t[at, :] = dot(values_t[at, :], probs).astype(BF16)
        return 0

    lax.fori_loop(0, 4, attend, 0)

    attended_ref[...] = attended_t[...]
    attended = dot(eye(TOKENS), attended_t[...], 1, 1).astype(BF16)
    attn_out = dot(attended, w_out[...]).astype(BF16)
    middle = (tokens + attn_out.astype(F32)).astype(BF16).astype(F32)
    normed_mid, inverse_mid = normalize(middle)
    second_norm = normed_mid.astype(BF16)
    mlp = jnp.zeros((TOKENS, 512), F32)
    for part in range(4):
        cols = slice(part * 512, part * 512 + 512)
        before = dot(second_norm, w_up[:, cols])
        cumulative = 0.5 * (1.0 + lax.erf(before * 0.7071067811865476))
        hidden = (before * cumulative).astype(BF16)
        hidden_ref[:, cols] = hidden
        slope_ref[:, cols] = (
            cumulative + before * jnp.exp(-0.5 * before * before) * 0.3989422804014327
        )
        mlp = mlp + dot(hidden, w_down[cols])
    after_mlp = (middle + mlp).astype(BF16).astype(F32)

    pieces = [after_mlp[p * MERGED : (p + 1) * MERGED] for p in range(4)]
    mean = sum(jnp.sum(v, axis=-1, keepdims=True) for v in pieces) / 2048.0
    pieces = [v - mean for v in pieces]
    inverse_out = lax.rsqrt(
        sum(jnp.sum(v * v, axis=-1, keepdims=True) for v in pieces) / 2048.0 + EPS
    )
    pieces = [v * inverse_out for v in pieces]
    merged_norm = [v.astype(BF16) for v in pieces]
    level_two_ref[...] = sum(
        dot(merged_norm[p], w_merge[p * 512 : p * 512 + 512]) for p in range(4)
    ).astype(BF16)
    cotangent = cot_ref[...]

    def store_blocks(grad, part, first, keep, send):
        narrow = grad.astype(BF16)
        for pair in range(16):
            _, lead, rest = place_of(part * 32 + pair * 2, first)
            low = narrow[pair * 32 : pair * 32 + 16]
            high = narrow[pair * 32 + 16 : pair * 32 + 32]
            keep[lead, rest] = jnp.where(even, low, high)
            send[lead, rest] = jnp.where(even, high, low)

    for part in range(4):
        grad = dot(merged_norm[part], cotangent, 0, 0)
        store_blocks(grad[:, :512], part, "y", merge_a_keep, merge_a_send)
        store_blocks(grad[:, 512:], part, "z", merge_b_keep, merge_b_send)
    upstream = [dot(cotangent, w_merge[p * 512 : p * 512 + 512], 1, 1) for p in range(4)]
    mean_grad = sum(jnp.sum(v, axis=-1, keepdims=True) for v in upstream) / 2048.0
    mean_cross = (
        sum(jnp.sum(v * u, axis=-1, keepdims=True) for v, u in zip(upstream, pieces)) / 2048.0
    )
    grad_after = jnp.concatenate(
        [inverse_out * (v - mean_grad - u * mean_cross) for v, u in zip(upstream, pieces)], axis=0
    ).astype(BF16)

    second_t = dot(rows_ref[1], second_norm, 1, 1).astype(BF16)
    back_up = jnp.zeros((TOKENS, 512), F32)
    for part in range(4):
        cols = slice(part * 512, part * 512 + 512)
        store_blocks(dot(hidden_ref[:, cols], grad_after, 0, 0), part, "x", down_keep, down_send)
        grad_before = (dot(grad_after, w_down[cols], 1, 1) * slope_ref[:, cols]).astype(BF16)
        grad_up = dot(second_t, grad_before).astype(BF16)
        up_keep[:, cols] = jnp.where(even, grad_up[:256], grad_up[256:])
        up_send[:, cols] = jnp.where(even, grad_up[256:], grad_up[:256])
        back_up = back_up + dot(grad_before, w_up[:, cols], 1, 1)
    middle_grad_ref[...] = (
        grad_after.astype(F32) + norm_back(normed_mid, inverse_mid, back_up)
    ).astype(BF16)


def backward_kernel(
    core_ref, tokens_ref, packed_ref, keys_t_ref, probs_ref, attended_ref, middle_grad_ref,
    first_t_ref, rows_ref, order_ref, w_out, w_qkv,
    late_keep, late_send, out0, out1, out2, out3,
    grad_heads, grad_heads_t, products, query_grad_t, packed_grad,
):
    even = core_ref[0] == 0
    middle_grad = middle_grad_ref[...]
    for group in range(4):
        grad_heads[group] = dot(
            middle_grad, w_out[group * 128 : group * 128 + 128], 1, 1
        ).astype(BF16)
    grad_heads_t[...] = dot(w_out[...], middle_grad, 1, 1).astype(BF16)
    products[...] = grad_heads_t[...].astype(F32) * attended_ref[...].astype(F32)

    head_of_row = lax.broadcasted_iota(jnp.int32, (128, TOKENS), 0) // HEAD
    head_of_lane = lax.broadcasted_iota(jnp.int32, (TOKENS, 128), 1) // HEAD

    def attend_back(group, _):
        queries = packed_ref[group]
        values = packed_ref[8 + group]
        upstream = grad_heads[group]
        upstream_t = grad_heads_t[pl.ds(pl.multiple_of(group * 128, 128), 128), :]
        grad_keys = jnp.zeros((TOKENS, 128), F32)
        grad_values = jnp.zeros((TOKENS, 128), F32)
        for head in range(4):
            at = pl.ds(pl.multiple_of(group * 128 + head * HEAD, HEAD), HEAD)
            masked_t = jnp.where(head_of_row == head, upstream_t, jnp.zeros_like(upstream_t))
            weights = probs_ref[group * 4 + head]
            total = jnp.sum(products[at, :], axis=0, keepdims=True)
            grad_weights = dot(values, masked_t)
            scores = (
                weights.astype(F32) * ((grad_weights - total) * HEAD ** (-0.5))
            ).astype(BF16)
            in_head = head_of_lane == head
            grad_keys += dot(scores, jnp.where(in_head, queries, jnp.zeros_like(queries)))
            grad_values += dot(weights, jnp.where(in_head, upstream, jnp.zeros_like(upstream)))
            query_grad_t[at, :] = dot(keys_t_ref[at, :], scores).astype(BF16)
        packed_grad[4 + group] = grad_keys.astype(BF16)
        packed_grad[8 + group] = grad_values.astype(BF16)
        return 0

    lax.fori_loop(0, 4, attend_back, 0)

    identity = eye(TOKENS)
    for group in range(4):
        packed_grad[group] = dot(
            identity, query_grad_t[group * 128 : group * 128 + 128, :], 1, 1
        ).astype(BF16)
    first_t = first_t_ref[...]
    back_qkv = jnp.zeros((TOKENS, 512), F32)
    for part in range(3):
        wide = jnp.concatenate([packed_grad[part * 4 + g] for g in range(4)], axis=1)
        cols = slice(part * 512, part * 512 + 512)
        grad = dot(first_t, wide).astype(BF16)
        late_keep[:, cols] = jnp.where(even, grad[:256], grad[256:])
        late_send[:, cols] = jnp.where(even, grad[256:], grad[:256])
        back_qkv = back_qkv + dot(wide, w_qkv[:, cols], 1, 1)
    attended = dot(rows_ref[0], attended_ref[...]).astype(BF16)
    grad = dot(attended, middle_grad).astype(BF16)
    late_keep[:, 1536:] = jnp.where(even, grad[:256], grad[256:])
    late_send[:, 1536:] = jnp.where(even, grad[256:], grad[:256])

    normed_in, inverse_in = normalize(tokens_ref[...].astype(F32))
    grad_first = back_qkv.astype(BF16).astype(F32)
    grad_tokens = (
        middle_grad.astype(F32) + norm_back(normed_in, inverse_in, grad_first)
    ).astype(BF16)
    for quad, out in enumerate((out0, out1, out2, out3)):
        out[...] = dot(order_ref[quad], grad_tokens).astype(BF16)


LATE, UP = "z", "y"


def call(kernel, inputs, outputs, scratch, flops):
    whole = pl.BlockSpec(memory_space=pltpu.VMEM)
    return pl.pallas_call(
        kernel,
        out_shape=[jax.ShapeDtypeStruct(shape, BF16) for shape in outputs],
        in_specs=[pl.BlockSpec(memory_space=pltpu.SMEM)] + [whole] * (len(inputs) - 1),
        out_specs=[whole] * len(outputs),
        scratch_shapes=scratch,
        compiler_params=pltpu.CompilerParams(vmem_limit_bytes=58 * 2**20),
        cost_estimate=pl.CostEstimate(
            flops=flops, bytes_accessed=25 * 2**20, transcendentals=3 * 2**20
        ),
    )(*inputs)


def window_pass(core, quads, bias, cotangent, w_qkv, w_qkv_t, w_out, w_up, w_down, w_merge):
    order = token_order()
    rows = jnp.asarray(np.stack([row_order(LATE), row_order(UP)]), BF16)
    half, wide = (4, 16, 16, 512), (256, 2048)
    by_feature, field = (512, TOKENS), (TOKENS, 512)
    outs = call(
        forward_kernel,
        [core, *quads, jnp.asarray(order, BF16), bias, cotangent, rows, w_qkv, w_qkv_t,
         w_out, w_up, w_down, w_merge],
        [(MERGED, 1024)] + [half] * 6 + [wide] * 2
        + [field, (12, TOKENS, 128), by_feature, (16, TOKENS, TOKENS), by_feature, field,
           by_feature],
        [pltpu.VMEM(by_feature, BF16), pltpu.VMEM(by_feature, BF16),
         pltpu.VMEM((TOKENS, 2048), F32), pltpu.VMEM((TOKENS, 2048), BF16),
         pltpu.VMEM(by_feature, BF16)],
        24 * 2**30,
    )
    level_two, early, kept = outs[0], outs[1:9], outs[9:]
    late_keep, late_send, *grads = call(
        backward_kernel,
        [core, *kept, rows, jnp.asarray(order.transpose(0, 2, 1), BF16), w_out, w_qkv],
        [wide] * 2 + [(MERGED, 512)] * 4,
        [pltpu.VMEM((4, TOKENS, 128), BF16), pltpu.VMEM(by_feature, BF16),
         pltpu.VMEM(by_feature, F32), pltpu.VMEM(by_feature, BF16),
         pltpu.VMEM((12, TOKENS, 128), BF16)],
        16 * 2**30,
    )
    return level_two, early, late_keep, late_send, grads


def pair_reduce(keep, send):
    arrived = lax.ppermute(send, "core", [(0, 1), (1, 0)])
    return (keep.astype(F32) + arrived.astype(F32)).astype(BF16)


def scatter_grad(keep, send, first, rows):
    blocks = pair_reduce(keep, send)
    cols = blocks.shape[-1]
    blocks = blocks.reshape(4, 16 * rows, cols)
    landed = lax.all_to_all(blocks, FIRST[first], 0, 0, tiled=True)
    blocks = jnp.sum(landed.astype(F32), axis=0).astype(BF16).reshape(16, rows, cols)
    landed = lax.all_to_all(blocks, REST[first], 0, 0, tiled=True)
    return jnp.sum(landed.astype(F32), axis=0)


def shifted_block(block, down, right):
    route = []
    for source in range(128):
        row, col = source // 16, source % 16
        route.append((source, (row + down) % 8 * 16 + (col + right) % 16))
    return lax.ppermute(block, GRID, route)


def quadrants(field):
    field = field.transpose(1, 2, 0, 3)
    rows, cols = field.shape[0] // 2, field.shape[1] // 2
    return field[:rows, :cols], field[:rows, cols:], field[rows:, :cols], field[rows:, cols:]


def roll_back(field):
    upper_left, upper_right, lower_left, lower_right = quadrants(field)
    return [
        lower_right,
        shifted_block(lower_left, 0, -1),
        shifted_block(upper_right, -1, 0),
        shifted_block(upper_left, -1, -1),
    ]


def roll_forth(corners):
    upper_left, upper_right, lower_left, lower_right = corners
    upper = jnp.concatenate(
        [shifted_block(lower_right, 1, 1), shifted_block(lower_left, 1, 0)], axis=1
    )
    lower = jnp.concatenate([shifted_block(upper_right, 0, 1), upper_left], axis=1)
    return jnp.concatenate([upper, lower], axis=0).transpose(2, 0, 1, 3)


def window_bias(window_ids):
    labels = window_ids.reshape(2, 3, 2, 2, 3, 2).transpose(5, 2, 0, 3, 1, 4)
    labels = jnp.broadcast_to(labels[..., None], (2, 2, 2, 2, 3, 3, 2)).reshape(TOKENS)
    return jnp.where(labels[:, None] == labels[None, :], 0.0, -1e30)


def body(tokens, window_ids, cotangent, w_qkv, w_out, w_up, w_down, w_merge):
    quads = [quad.reshape(MERGED, 512) for quad in roll_back(tokens)]
    cot = jnp.concatenate([quad.reshape(18, 1024) for quad in roll_back(cotangent)], axis=0)
    core = lax.axis_index("core").reshape(1)
    level_two, early, late_keep, late_send, grads = window_pass(
        core, quads, window_bias(window_ids), cot, w_qkv, w_qkv.T, w_out, w_up, w_down, w_merge
    )
    merge_a = scatter_grad(early[0], early[1], "y", 16)
    merge_b = scatter_grad(early[2], early[3], "z", 16)
    grad_down = scatter_grad(early[4], early[5], "x", 16)
    grad_up = scatter_grad(early[6], early[7], UP, 4)
    late = scatter_grad(late_keep, late_send, LATE, 4)
    grad_tokens = roll_forth([grad.reshape(6, 6, 2, 512) for grad in grads])
    corners = level_two.reshape(4, 3, 3, 2, 1024)
    level_two = roll_forth([corners[quad] for quad in range(4)])
    grad_merge = jnp.concatenate([merge_a, merge_b], axis=1)
    return (level_two, grad_tokens, late[:, :1536], late[:, 1536:], grad_up, grad_down, grad_merge)


def solution(mesh):
    cube = jax.sharding.Mesh(mesh.devices.reshape(4, 2, 4, 2, 2), GRID)
    lat, lon = GRID[:2], GRID[2:]
    field = P(None, lat, lon, None)
    share = P(GRID, None)
    return jax.shard_map(
        body,
        mesh=cube,
        in_specs=(field, P(lat, lon), field, P(), P(), P(), P(), P()),
        out_specs=(field, field, share, share, share, share, share),
        check_vma=False,
    )
```

```python
import functools

import jax
import jax.numpy as jnp
import numpy as np
from jax import lax
from jax.experimental import pallas as pl
from jax.experimental.pallas import tpu as pltpu
from jax.sharding import PartitionSpec as P

HEAD = 32
WIN = 12
TOKENS = 2 * WIN * WIN
MERGED = TOKENS // 4
EPS = 1e-05
LOG2E = 1.4426950408889634
GRID = ("z", "x_lo", "y", "x_hi", "core")
BF16 = jnp.bfloat16
F32 = jnp.float32

PAIRS = ("z", "x_lo", "y", "x_hi")
NEAR = ("y", "core")
FAR = ("z", "x_lo", "x_hi")


def token_order():
    order = np.zeros((4, TOKENS, MERGED), np.float32)
    for quad in range(4):
        for row in range(6):
            for col in range(6):
                for level in range(2):
                    position = (col % 2) * 2 + row % 2
                    patch = quad * 18 + (row // 2 * 3 + col // 2) * 2 + level
                    order[quad, position * MERGED + patch, (row * 6 + col) * 2 + level] = 1.0
    return order


def dot(left, right, left_dim=1, right_dim=0):
    return lax.dot_general(
        left, right, (((left_dim,), (right_dim,)), ((), ())), preferred_element_type=F32
    )


def normalize(wide):
    centered = wide - jnp.mean(wide, axis=-1, keepdims=True)
    inverse_std = lax.rsqrt(jnp.mean(centered * centered, axis=-1, keepdims=True) + EPS)
    return centered * inverse_std, inverse_std


def norm_back(normed, inverse_std, upstream):
    mean_grad = jnp.mean(upstream, axis=-1, keepdims=True)
    mean_cross = jnp.mean(upstream * normed, axis=-1, keepdims=True)
    return inverse_std * (upstream - mean_grad - normed * mean_cross)


def eye(size):
    rows = lax.broadcasted_iota(jnp.int32, (size, size), 0)
    cols = lax.broadcasted_iota(jnp.int32, (size, size), 1)
    return jnp.where(rows == cols, 1.0, 0.0).astype(BF16)


def weave(even, grads, keep, send, cols):
    tiles = [grad.reshape(64, 8, grad.shape[-1]) for grad in grads]
    turned = [pltpu.roll(tile, 4, 1) for tile in tiles]
    upper = lax.broadcasted_iota(jnp.int32, tiles[0].shape, 1) < 4
    for half in range(2):
        one, two = half * 2, half * 2 + 1
        first = jnp.where(upper, tiles[one], turned[two])
        second = jnp.where(upper, turned[one], tiles[two])
        rows = slice(half * 8, half * 8 + 8)
        keep[:, rows, cols] = jnp.where(even, first, second).astype(BF16)
        send[:, rows, cols] = jnp.where(even, second, first).astype(BF16)


def forward_kernel(
    core_ref, quad0, quad1, quad2, quad3, order_ref, bias_ref, cot_ref, w_qkv, w_qkv_t,
    w_out, w_up, w_down, w_merge,
    level_two_ref, merged_t_ref, keep_ref, send_ref, tokens_ref, packed_ref, keys_t_ref, probs_ref,
    attended_ref, middle_grad_ref, first_t_ref,
    query_t, values_t, slope_ref, hidden_ref, attended_t,
):
    even = core_ref[0] == 0
    quads = (quad0, quad1, quad2, quad3)
    tokens = sum(dot(order_ref[q], quads[q][...]) for q in range(4))
    tokens_ref[...] = tokens.astype(BF16)
    first_norm = normalize(tokens)[0].astype(BF16)
    by_feature = eye(512)
    first_t_ref[...] = dot(by_feature, first_norm, 1, 1).astype(BF16)
    for part in range(12):
        packed_ref[part] = dot(first_norm, w_qkv[:, part * 128 : part * 128 + 128]).astype(BF16)
    query_t[...] = dot(w_qkv_t[:512], first_norm, 1, 1).astype(BF16)
    keys_t_ref[...] = dot(w_qkv_t[512:1024], first_norm, 1, 1).astype(BF16)
    values_t[...] = dot(w_qkv_t[1024:], first_norm, 1, 1).astype(BF16)

    head_of_row = lax.broadcasted_iota(jnp.int32, (128, TOKENS), 0) // HEAD

    def attend(group, _):
        keys = packed_ref[4 + group]
        queries = query_t[pl.ds(pl.multiple_of(group * 128, 128), 128), :]
        for head in range(4):
            masked = jnp.where(head_of_row == head, queries, jnp.zeros_like(queries))
            scores = dot(keys, masked) * (HEAD ** (-0.5) * LOG2E) + bias_ref[...]
            raised = jnp.exp2(scores - jnp.max(scores, axis=0, keepdims=True))
            inverse = 1.0 / jnp.sum(raised, axis=0, keepdims=True)
            probs = (raised * inverse).astype(BF16)
            probs_ref[group * 4 + head] = probs
            at = pl.ds(pl.multiple_of(group * 128 + head * HEAD, HEAD), HEAD)
            attended_t[at, :] = dot(values_t[at, :], probs).astype(BF16)
        return 0

    lax.fori_loop(0, 4, attend, 0)

    attended_ref[...] = attended_t[...]
    attended = dot(eye(TOKENS), attended_t[...], 1, 1).astype(BF16)
    attn_out = dot(attended, w_out[...]).astype(BF16)
    middle = (tokens + attn_out.astype(F32)).astype(BF16).astype(F32)
    normed_mid, inverse_mid = normalize(middle)
    second_norm = normed_mid.astype(BF16)
    mlp = jnp.zeros((TOKENS, 512), F32)
    for part in range(4):
        cols = slice(part * 512, part * 512 + 512)
        before = dot(second_norm, w_up[:, cols])
        cumulative = 0.5 * (1.0 + lax.erf(before * 0.7071067811865476))
        hidden = (before * cumulative).astype(BF16)
        hidden_ref[:, cols] = hidden
        slope_ref[:, cols] = (
            cumulative + before * jnp.exp(-0.5 * before * before) * 0.3989422804014327
        )
        mlp = mlp + dot(hidden, w_down[cols])
    after_mlp = (middle + mlp).astype(BF16).astype(F32)

    pieces = [after_mlp[p * MERGED : (p + 1) * MERGED] for p in range(4)]
    mean = sum(jnp.sum(v, axis=-1, keepdims=True) for v in pieces) / 2048.0
    pieces = [v - mean for v in pieces]
    inverse_out = lax.rsqrt(
        sum(jnp.sum(v * v, axis=-1, keepdims=True) for v in pieces) / 2048.0 + EPS
    )
    pieces = [v * inverse_out for v in pieces]
    merged_norm = [v.astype(BF16) for v in pieces]
    level_two_ref[...] = sum(
        dot(merged_norm[p], w_merge[p * 512 : p * 512 + 512]) for p in range(4)
    ).astype(BF16)
    cotangent = cot_ref[...]

    for part in range(4):
        turned = dot(by_feature, merged_norm[part], 1, 1).astype(BF16)
        for block in range(32):
            x_lo, y, x_hi, core = block // 16, block // 4 % 4, block // 2 % 2, block % 2
            at = (part * 4 + x_lo * 2 + x_hi) * 16
            merged_t_ref[y * 2 + core, at : at + 16] = turned[block * 16 : block * 16 + 16]
    upstream = [dot(cotangent, w_merge[p * 512 : p * 512 + 512], 1, 1) for p in range(4)]
    mean_grad = sum(jnp.sum(v, axis=-1, keepdims=True) for v in upstream) / 2048.0
    mean_cross = (
        sum(jnp.sum(v * u, axis=-1, keepdims=True) for v, u in zip(upstream, pieces)) / 2048.0
    )
    grad_after = jnp.concatenate(
        [inverse_out * (v - mean_grad - u * mean_cross) for v, u in zip(upstream, pieces)], axis=0
    ).astype(BF16)

    second_t = dot(by_feature, second_norm, 1, 1).astype(BF16)
    back_up = jnp.zeros((TOKENS, 512), F32)
    grads_up = []
    for part in range(4):
        cols = slice(part * 512, part * 512 + 512)
        grad = dot(hidden_ref[:, cols], grad_after, 0, 0).astype(BF16)
        for pair in range(16):
            low = grad[pair * 32 : pair * 32 + 16]
            high = grad[pair * 32 + 16 : pair * 32 + 32]
            keep_ref[part * 16 + pair, :, :512] = jnp.where(even, low, high)
            send_ref[part * 16 + pair, :, :512] = jnp.where(even, high, low)
        grad_before = (dot(grad_after, w_down[cols], 1, 1) * slope_ref[:, cols]).astype(BF16)
        grads_up.append(dot(second_t, grad_before))
        back_up = back_up + dot(grad_before, w_up[:, cols], 1, 1)
    weave(even, grads_up, keep_ref, send_ref, slice(512, 1024))
    middle_grad = (
        grad_after.astype(F32) + norm_back(normed_mid, inverse_mid, back_up)
    ).astype(BF16)
    middle_grad_ref[...] = middle_grad
    grad = dot(attended_t[...], middle_grad)
    weave(even, [grad[:, p * 128 : p * 128 + 128] for p in range(4)], keep_ref, send_ref,
          slice(1024, 1152))


def backward_kernel(
    core_ref, tokens_ref, packed_ref, keys_t_ref, probs_ref, attended_ref, middle_grad_ref,
    first_t_ref, order_ref, w_out, w_qkv,
    keep_ref, send_ref, out0, out1, out2, out3,
    grad_heads, grad_heads_t, products, query_grad_t, packed_grad,
):
    even = core_ref[0] == 0
    middle_grad = middle_grad_ref[...]
    for group in range(4):
        grad_heads[group] = dot(
            middle_grad, w_out[group * 128 : group * 128 + 128], 1, 1
        ).astype(BF16)
    grad_heads_t[...] = dot(w_out[...], middle_grad, 1, 1).astype(BF16)
    products[...] = grad_heads_t[...].astype(F32) * attended_ref[...].astype(F32)

    head_of_row = lax.broadcasted_iota(jnp.int32, (128, TOKENS), 0) // HEAD
    head_of_lane = lax.broadcasted_iota(jnp.int32, (TOKENS, 128), 1) // HEAD

    def attend_back(group, _):
        queries = packed_ref[group]
        values = packed_ref[8 + group]
        upstream = grad_heads[group]
        upstream_t = grad_heads_t[pl.ds(pl.multiple_of(group * 128, 128), 128), :]
        grad_keys = jnp.zeros((TOKENS, 128), F32)
        grad_values = jnp.zeros((TOKENS, 128), F32)
        for head in range(4):
            at = pl.ds(pl.multiple_of(group * 128 + head * HEAD, HEAD), HEAD)
            masked_t = jnp.where(head_of_row == head, upstream_t, jnp.zeros_like(upstream_t))
            weights = probs_ref[group * 4 + head]
            total = jnp.sum(products[at, :], axis=0, keepdims=True)
            grad_weights = dot(values, masked_t)
            scores = (
                weights.astype(F32) * ((grad_weights - total) * HEAD ** (-0.5))
            ).astype(BF16)
            in_head = head_of_lane == head
            grad_keys += dot(scores, jnp.where(in_head, queries, jnp.zeros_like(queries)))
            grad_values += dot(weights, jnp.where(in_head, upstream, jnp.zeros_like(upstream)))
            query_grad_t[at, :] = dot(keys_t_ref[at, :], scores).astype(BF16)
        packed_grad[4 + group] = grad_keys.astype(BF16)
        packed_grad[8 + group] = grad_values.astype(BF16)
        return 0

    lax.fori_loop(0, 4, attend_back, 0)

    identity = eye(TOKENS)
    for group in range(4):
        packed_grad[group] = dot(
            identity, query_grad_t[group * 128 : group * 128 + 128, :], 1, 1
        ).astype(BF16)
    first_t = first_t_ref[...]
    back_qkv = jnp.zeros((TOKENS, 512), F32)
    grads = []
    for part in range(3):
        wide = jnp.concatenate([packed_grad[part * 4 + g] for g in range(4)], axis=1)
        grad = dot(first_t, wide)
        grads += [grad[:, q * 128 : q * 128 + 128] for q in range(4)]
        back_qkv = back_qkv + dot(wide, w_qkv[:, part * 512 : part * 512 + 512], 1, 1)
    for part in range(3):
        weave(even, [grads[q * 3 + part] for q in range(4)], keep_ref, send_ref,
              slice(part * 128, part * 128 + 128))

    normed_in, inverse_in = normalize(tokens_ref[...].astype(F32))
    grad_first = back_qkv.astype(BF16).astype(F32)
    grad_tokens = (
        middle_grad.astype(F32) + norm_back(normed_in, inverse_in, grad_first)
    ).astype(BF16)
    for quad, out in enumerate((out0, out1, out2, out3)):
        out[...] = dot(order_ref[quad], grad_tokens).astype(BF16)


def merge_kernel(merged_ref, cots_ref, grad_ref):
    for part in range(4):
        rows = slice(part * 64, part * 64 + 64)
        grad = sum(dot(merged_ref[near, rows], cots_ref[near]) for near in range(8))
        for block in range(4):
            grad_ref[part * 4 + block] = grad[block * 16 : block * 16 + 16].astype(BF16)


def call(kernel, inputs, outputs, scratch, flops):
    whole = pl.BlockSpec(memory_space=pltpu.VMEM)
    return pl.pallas_call(
        kernel,
        out_shape=[jax.ShapeDtypeStruct(shape, BF16) for shape in outputs],
        in_specs=[
            pl.BlockSpec(memory_space=pltpu.SMEM) if value.ndim == 1 else whole for value in inputs
        ],
        out_specs=[whole] * len(outputs),
        scratch_shapes=scratch,
        compiler_params=pltpu.CompilerParams(vmem_limit_bytes=58 * 2**20),
        cost_estimate=pl.CostEstimate(
            flops=flops, bytes_accessed=25 * 2**20, transcendentals=3 * 2**20
        ),
    )(*inputs)


def window_pass(core, quads, bias, cotangent, w_qkv, w_qkv_t, w_out, w_up, w_down, w_merge):
    order = token_order()
    by_feature, field = (512, TOKENS), (TOKENS, 512)
    level_two, merged_t, keep, send, *kept = call(
        forward_kernel,
        [core, *quads, jnp.asarray(order, BF16), bias, cotangent, w_qkv, w_qkv_t,
         w_out, w_up, w_down, w_merge],
        [(MERGED, 1024), (8, 256, MERGED), (64, 16, 1152), (64, 16, 1152),
         field, (12, TOKENS, 128), by_feature, (16, TOKENS, TOKENS), by_feature, field,
         by_feature],
        [pltpu.VMEM(by_feature, BF16), pltpu.VMEM(by_feature, BF16),
         pltpu.VMEM((TOKENS, 2048), F32), pltpu.VMEM((TOKENS, 2048), BF16),
         pltpu.VMEM(by_feature, BF16)],
        24 * 2**30,
    )
    late_keep, late_send, *grads = call(
        backward_kernel,
        [core, *kept, jnp.asarray(order.transpose(0, 2, 1), BF16), w_out, w_qkv],
        [(64, 16, 384)] * 2 + [(MERGED, 512)] * 4,
        [pltpu.VMEM((4, TOKENS, 128), BF16), pltpu.VMEM(by_feature, BF16),
         pltpu.VMEM(by_feature, F32), pltpu.VMEM(by_feature, BF16),
         pltpu.VMEM((12, TOKENS, 128), BF16)],
        16 * 2**30,
    )
    return level_two, merged_t, keep, send, late_keep, late_send, grads


def scatter_grad(keep, send):
    arrived = lax.ppermute(send, "core", [(0, 1), (1, 0)])
    blocks = (keep.astype(F32) + arrived.astype(F32)).astype(BF16)
    landed = lax.all_to_all(blocks, PAIRS, 0, 0, tiled=True)
    return jnp.sum(landed.astype(F32), axis=0)


def unweave(share):
    cols = share.shape[-1]
    return share.reshape(4, 4, cols).transpose(1, 0, 2).reshape(4, 4 * cols)


def scatter_merge(merged_t, cotangents):
    merged = lax.all_to_all(merged_t, NEAR, 0, 0, tiled=True)
    grad, = call(merge_kernel, [merged, cotangents], [(16, 16, 1024)], [], 2**29)
    landed = lax.all_to_all(grad, FAR, 0, 0, tiled=True)
    return jnp.sum(landed.astype(F32), axis=0)


def shifted_block(block, down, right):
    route = []
    for source in range(128):
        row, col = source // 16, source % 16
        route.append((source, (row + down) % 8 * 16 + (col + right) % 16))
    return lax.ppermute(block, GRID, route)


def quadrants(field):
    field = field.transpose(1, 2, 0, 3)
    rows, cols = field.shape[0] // 2, field.shape[1] // 2
    corners = field[:rows, :cols], field[:rows, cols:], field[rows:, :cols], field[rows:, cols:]
    return [corner.reshape(-1, field.shape[-1]) for corner in corners]


def roll_back(field):
    upper_left, upper_right, lower_left, lower_right = quadrants(field)
    return [
        lower_right,
        shifted_block(lower_left, 0, -1),
        shifted_block(upper_right, -1, 0),
        shifted_block(upper_left, -1, -1),
    ]


def roll_forth(corners, side):
    upper_left, upper_right, lower_left, lower_right = corners
    moved = [
        shifted_block(lower_right, 1, 1),
        shifted_block(lower_left, 1, 0),
        shifted_block(upper_right, 0, 1),
        upper_left,
    ]
    moved = [corner.reshape(side, side, 2, corner.shape[-1]) for corner in moved]
    upper = jnp.concatenate(moved[:2], axis=1)
    lower = jnp.concatenate(moved[2:], axis=1)
    return jnp.concatenate([upper, lower], axis=0).transpose(2, 0, 1, 3)


def window_bias(window_ids):
    labels = window_ids.reshape(2, 3, 2, 2, 3, 2).transpose(5, 2, 0, 3, 1, 4)
    labels = jnp.broadcast_to(labels[..., None], (2, 2, 2, 2, 3, 3, 2)).reshape(TOKENS)
    return jnp.where(labels[:, None] == labels[None, :], 0.0, -1e30)


def body(tokens, window_ids, cotangent, w_qkv, w_out, w_up, w_down, w_merge):
    quads = roll_back(tokens)
    cot = jnp.concatenate(roll_back(cotangent), axis=0)
    cotangents = lax.all_gather(cot, NEAR)
    core = lax.axis_index("core").reshape(1)
    level_two, merged_t, keep, send, late_keep, late_send, grads = window_pass(
        core, quads, window_bias(window_ids), cot, w_qkv, w_qkv.T, w_out, w_up, w_down, w_merge
    )
    grad_merge = scatter_merge(merged_t, cotangents)
    share = scatter_grad(keep, send)
    grad_qkv = unweave(scatter_grad(late_keep, late_send))
    grad_down, grad_up = share[:, :512], unweave(share[:, 512:1024])
    grad_out = unweave(share[:, 1024:])
    grad_tokens = roll_forth(grads, 6)
    level_two = roll_forth([level_two[quad * 18 : quad * 18 + 18] for quad in range(4)], 3)
    return (level_two, grad_tokens, grad_qkv, grad_out, grad_up, grad_down, grad_merge)


def solution(mesh):
    cube = jax.sharding.Mesh(mesh.devices.reshape(4, 2, 4, 2, 2), GRID)
    lat, lon = GRID[:2], GRID[2:]
    field = P(None, lat, lon, None)
    share = P(GRID, None)
    return jax.shard_map(
        body,
        mesh=cube,
        in_specs=(field, P(lat, lon), field, P(), P(), P(), P(), P()),
        out_specs=(field, field, share, share, share, share, share),
        check_vma=False,
    )
```

```python
import functools

import jax
import jax.numpy as jnp
import numpy as np
from jax import lax
from jax.experimental import pallas as pl
from jax.experimental.pallas import tpu as pltpu
from jax.sharding import PartitionSpec as P

HEAD = 32
WIN = 12
TOKENS = 2 * WIN * WIN
MERGED = TOKENS // 4
EPS = 1e-05
LOG2E = 1.4426950408889634
GRID = ("z", "x_lo", "y", "x_hi", "core")
BF16 = jnp.bfloat16
F32 = jnp.float32

PAIRS = ("z", "x_lo", "y", "x_hi")
NEAR = ("y", "core")
FAR = ("z", "x_lo", "x_hi")


def token_order():
    order = np.zeros((4, TOKENS, MERGED), np.float32)
    for quad in range(4):
        for row in range(6):
            for col in range(6):
                for level in range(2):
                    position = (col % 2) * 2 + row % 2
                    patch = quad * 18 + (row // 2 * 3 + col // 2) * 2 + level
                    order[quad, position * MERGED + patch, (row * 6 + col) * 2 + level] = 1.0
    return order


def dot(left, right, left_dim=1, right_dim=0):
    return lax.dot_general(
        left, right, (((left_dim,), (right_dim,)), ((), ())), preferred_element_type=F32
    )


def normalize(wide):
    centered = wide - jnp.mean(wide, axis=-1, keepdims=True)
    inverse_std = lax.rsqrt(jnp.mean(centered * centered, axis=-1, keepdims=True) + EPS)
    return centered * inverse_std, inverse_std


def norm_back(normed, inverse_std, upstream):
    mean_grad = jnp.mean(upstream, axis=-1, keepdims=True)
    mean_cross = jnp.mean(upstream * normed, axis=-1, keepdims=True)
    return inverse_std * (upstream - mean_grad - normed * mean_cross)


def eye(size):
    rows = lax.broadcasted_iota(jnp.int32, (size, size), 0)
    cols = lax.broadcasted_iota(jnp.int32, (size, size), 1)
    return jnp.where(rows == cols, 1.0, 0.0).astype(BF16)


def weave(even, grads, keep, send, cols):
    tiles = [grad.reshape(64, 8, grad.shape[-1]) for grad in grads]
    turned = [pltpu.roll(tile, 4, 1) for tile in tiles]
    upper = lax.broadcasted_iota(jnp.int32, tiles[0].shape, 1) < 4
    for half in range(2):
        one, two = half * 2, half * 2 + 1
        first = jnp.where(upper, tiles[one], turned[two])
        second = jnp.where(upper, turned[one], tiles[two])
        rows = slice(half * 8, half * 8 + 8)
        keep[:, rows, cols] = jnp.where(even, first, second).astype(BF16)
        send[:, rows, cols] = jnp.where(even, second, first).astype(BF16)


def load(pairs, sems):
    copies = [pltpu.make_async_copy(*pair, sems.at[at]) for at, pair in enumerate(pairs)]
    for copy in copies:
        copy.start()
    return copies


def merge_norm(after_mlp):
    pieces = [after_mlp[p * MERGED : (p + 1) * MERGED] for p in range(4)]
    mean = sum(jnp.sum(v, axis=-1, keepdims=True) for v in pieces) / 2048.0
    pieces = [v - mean for v in pieces]
    inverse_out = lax.rsqrt(
        sum(jnp.sum(v * v, axis=-1, keepdims=True) for v in pieces) / 2048.0 + EPS
    )
    return [v * inverse_out for v in pieces], inverse_out


def near_order():
    source = lax.broadcasted_iota(jnp.int32, (512, 512), 0)
    target = lax.broadcasted_iota(jnp.int32, (512, 512), 1)
    block = source // 16
    near = block // 4 % 4 * 2 + block % 2
    far = block // 16 * 2 + block // 2 % 2
    return jnp.where(target == near * 64 + far * 16 + source % 16, 1.0, 0.0).astype(BF16)


def forward_kernel(
    quad0, quad1, quad2, quad3, order_ref, bias_ref, w_qkv, w_qkv_t,
    w_out_hbm, w_up_hbm, w_down_hbm, w_merge_hbm,
    level_two_ref, merged_ref, tokens_ref, packed_ref, keys_t_ref, attended_ref, first_t_ref,
    middle_ref, after_mlp_ref, probs_hbm, hidden_hbm, slope_hbm,
    query_t, values_t, slope_ref, hidden_ref, probs_ref, w_out, w_up, w_down, w_merge,
    in_sems, out_sems,
):
    weights = load(
        [(w_out_hbm, w_out), (w_up_hbm, w_up), (w_down_hbm, w_down), (w_merge_hbm, w_merge)],
        in_sems,
    )
    quads = (quad0, quad1, quad2, quad3)
    tokens = sum(dot(order_ref[q], quads[q][...]) for q in range(4))
    tokens_ref[...] = tokens.astype(BF16)
    first_norm = normalize(tokens)[0].astype(BF16)
    first_t_ref[...] = dot(eye(512), first_norm, 1, 1).astype(BF16)
    for part in range(12):
        packed_ref[part] = dot(first_norm, w_qkv[:, part * 128 : part * 128 + 128]).astype(BF16)
    query_t[...] = dot(w_qkv_t[:512], first_norm, 1, 1).astype(BF16)
    keys_t_ref[...] = dot(w_qkv_t[512:1024], first_norm, 1, 1).astype(BF16)
    values_t[...] = dot(w_qkv_t[1024:], first_norm, 1, 1).astype(BF16)

    head_of_row = lax.broadcasted_iota(jnp.int32, (128, TOKENS), 0) // HEAD

    def attend(group, _):
        keys = packed_ref[4 + group]
        queries = query_t[pl.ds(pl.multiple_of(group * 128, 128), 128), :]
        for head in range(4):
            masked = jnp.where(head_of_row == head, queries, jnp.zeros_like(queries))
            scores = dot(keys, masked) * (HEAD ** (-0.5) * LOG2E) + bias_ref[...]
            raised = jnp.exp2(scores - jnp.max(scores, axis=0, keepdims=True))
            inverse = 1.0 / jnp.sum(raised, axis=0, keepdims=True)
            probs = (raised * inverse).astype(BF16)
            probs_ref[group * 4 + head] = probs
            at = pl.ds(pl.multiple_of(group * 128 + head * HEAD, HEAD), HEAD)
            attended_ref[at, :] = dot(values_t[at, :], probs).astype(BF16)
        return 0

    lax.fori_loop(0, 4, attend, 0)
    saves = load([(probs_ref, probs_hbm)], out_sems.at[pl.ds(0, 1)])

    attended = dot(eye(TOKENS), attended_ref[...], 1, 1).astype(BF16)
    weights[0].wait()
    attn_out = dot(attended, w_out[...]).astype(BF16)
    narrow_middle = (tokens + attn_out.astype(F32)).astype(BF16)
    middle_ref[...] = narrow_middle
    middle = narrow_middle.astype(F32)
    second_norm = normalize(middle)[0].astype(BF16)
    mlp = jnp.zeros((TOKENS, 512), F32)
    weights[1].wait()
    weights[2].wait()
    for part in range(4):
        cols = slice(part * 512, part * 512 + 512)
        before = dot(second_norm, w_up[:, cols])
        cumulative = 0.5 * (1.0 + lax.erf(before * 0.7071067811865476))
        hidden = (before * cumulative).astype(BF16)
        hidden_ref[:, cols] = hidden
        slope_ref[:, cols] = (
            cumulative + before * jnp.exp(-0.5 * before * before) * 0.3989422804014327
        ).astype(BF16)
        mlp = mlp + dot(hidden, w_down[cols])
    saves += load([(hidden_ref, hidden_hbm), (slope_ref, slope_hbm)], out_sems.at[pl.ds(1, 2)])
    after_mlp = (middle + mlp).astype(BF16)
    after_mlp_ref[...] = after_mlp
    merged_norm = [v.astype(BF16) for v in merge_norm(after_mlp.astype(F32))[0]]
    order = near_order()
    spread = [dot(v, order) for v in merged_norm]
    for near in range(8):
        at = slice(near * 64, near * 64 + 64)
        merged_ref[near] = jnp.concatenate([v[:, at] for v in spread], axis=1).astype(BF16)
    weights[3].wait()
    level_two_ref[...] = sum(
        dot(merged_norm[p], w_merge[p * 512 : p * 512 + 512]) for p in range(4)
    ).astype(BF16)
    for save in saves:
        save.wait()


def middle_kernel(
    core_ref, cot_ref, middle_ref, after_mlp_ref, attended_ref,
    w_merge_hbm, hidden_hbm, w_down_hbm, slope_hbm, w_up_hbm,
    keep_ref, send_ref, middle_grad_ref,
    w_merge, hidden_ref, w_down, slope_ref, w_up, sems,
):
    loads = load(
        [(w_merge_hbm, w_merge), (hidden_hbm, hidden_ref), (w_down_hbm, w_down),
         (slope_hbm, slope_ref), (w_up_hbm, w_up)],
        sems,
    )
    even = core_ref[0] == 0
    cotangent = cot_ref[...]
    pieces, inverse_out = merge_norm(after_mlp_ref[...].astype(F32))
    normed_mid, inverse_mid = normalize(middle_ref[...].astype(F32))
    second_t = dot(eye(512), normed_mid.astype(BF16), 1, 1).astype(BF16)
    loads[0].wait()
    upstream = [dot(cotangent, w_merge[p * 512 : p * 512 + 512], 1, 1) for p in range(4)]
    mean_grad = sum(jnp.sum(v, axis=-1, keepdims=True) for v in upstream) / 2048.0
    mean_cross = (
        sum(jnp.sum(v * u, axis=-1, keepdims=True) for v, u in zip(upstream, pieces)) / 2048.0
    )
    grad_after = jnp.concatenate(
        [inverse_out * (v - mean_grad - u * mean_cross) for v, u in zip(upstream, pieces)], axis=0
    ).astype(BF16)

    back_up = jnp.zeros((TOKENS, 512), F32)
    grads_up = []
    for copy in loads[1:]:
        copy.wait()
    for part in range(4):
        cols = slice(part * 512, part * 512 + 512)
        grad = dot(hidden_ref[:, cols], grad_after, 0, 0).astype(BF16)
        for pair in range(16):
            low = grad[pair * 32 : pair * 32 + 16]
            high = grad[pair * 32 + 16 : pair * 32 + 32]
            keep_ref[part * 16 + pair, :, :512] = jnp.where(even, low, high)
            send_ref[part * 16 + pair, :, :512] = jnp.where(even, high, low)
        grad_before = (
            dot(grad_after, w_down[cols], 1, 1) * slope_ref[:, cols].astype(F32)
        ).astype(BF16)
        grads_up.append(dot(second_t, grad_before))
        back_up = back_up + dot(grad_before, w_up[:, cols], 1, 1)
    weave(even, grads_up, keep_ref, send_ref, slice(512, 1024))
    middle_grad = (
        grad_after.astype(F32) + norm_back(normed_mid, inverse_mid, back_up)
    ).astype(BF16)
    middle_grad_ref[...] = middle_grad
    grad = dot(attended_ref[...], middle_grad)
    weave(even, [grad[:, p * 128 : p * 128 + 128] for p in range(4)], keep_ref, send_ref,
          slice(1024, 1152))


def backward_kernel(
    core_ref, tokens_ref, packed_ref, keys_t_ref, attended_ref, middle_grad_ref,
    first_t_ref, order_ref, w_out, probs_hbm, w_qkv_hbm,
    keep_ref, send_ref, out0, out1, out2, out3,
    grad_heads, grad_heads_t, products, query_grad_t, packed_grad, probs_ref, w_qkv, sems,
):
    loads = load(
        [(probs_hbm.at[pl.ds(g * 4, 4)], probs_ref.at[pl.ds(g * 4, 4)]) for g in range(4)]
        + [(w_qkv_hbm, w_qkv)],
        sems,
    )
    even = core_ref[0] == 0
    middle_grad = middle_grad_ref[...]
    for group in range(4):
        grad_heads[group] = dot(
            middle_grad, w_out[group * 128 : group * 128 + 128], 1, 1
        ).astype(BF16)
    grad_heads_t[...] = dot(w_out[...], middle_grad, 1, 1).astype(BF16)
    products[...] = grad_heads_t[...].astype(F32) * attended_ref[...].astype(F32)

    head_of_row = lax.broadcasted_iota(jnp.int32, (128, TOKENS), 0) // HEAD
    head_of_lane = lax.broadcasted_iota(jnp.int32, (TOKENS, 128), 1) // HEAD

    def attend_back(group):
        loads[group].wait()
        queries = packed_ref[group]
        values = packed_ref[8 + group]
        upstream = grad_heads[group]
        upstream_t = grad_heads_t[slice(group * 128, group * 128 + 128), :]
        grad_keys = jnp.zeros((TOKENS, 128), F32)
        grad_values = jnp.zeros((TOKENS, 128), F32)
        for head in range(4):
            at = slice(group * 128 + head * HEAD, group * 128 + head * HEAD + HEAD)
            masked_t = jnp.where(head_of_row == head, upstream_t, jnp.zeros_like(upstream_t))
            weights = probs_ref[group * 4 + head]
            total = jnp.sum(products[at, :], axis=0, keepdims=True)
            grad_weights = dot(values, masked_t)
            scores = (
                weights.astype(F32) * ((grad_weights - total) * HEAD ** (-0.5))
            ).astype(BF16)
            in_head = head_of_lane == head
            grad_keys += dot(scores, jnp.where(in_head, queries, jnp.zeros_like(queries)))
            grad_values += dot(weights, jnp.where(in_head, upstream, jnp.zeros_like(upstream)))
            query_grad_t[at, :] = dot(keys_t_ref[at, :], scores).astype(BF16)
        packed_grad[4 + group] = grad_keys.astype(BF16)
        packed_grad[8 + group] = grad_values.astype(BF16)

    for group in range(4):
        attend_back(group)

    identity = eye(TOKENS)
    for group in range(4):
        packed_grad[group] = dot(
            identity, query_grad_t[group * 128 : group * 128 + 128, :], 1, 1
        ).astype(BF16)
    first_t = first_t_ref[...]
    loads[4].wait()
    back_qkv = jnp.zeros((TOKENS, 512), F32)
    grads = []
    for part in range(3):
        wide = jnp.concatenate([packed_grad[part * 4 + g] for g in range(4)], axis=1)
        grad = dot(first_t, wide)
        grads += [grad[:, q * 128 : q * 128 + 128] for q in range(4)]
        back_qkv = back_qkv + dot(wide, w_qkv[:, part * 512 : part * 512 + 512], 1, 1)
    for part in range(3):
        weave(even, [grads[q * 3 + part] for q in range(4)], keep_ref, send_ref,
              slice(part * 128, part * 128 + 128))

    normed_in, inverse_in = normalize(tokens_ref[...].astype(F32))
    grad_first = back_qkv.astype(BF16).astype(F32)
    grad_tokens = (
        middle_grad.astype(F32) + norm_back(normed_in, inverse_in, grad_first)
    ).astype(BF16)
    for quad, out in enumerate((out0, out1, out2, out3)):
        out[...] = dot(order_ref[quad], grad_tokens).astype(BF16)


def merge_kernel(merged_ref, cots_ref, grad_ref):
    grad = dot(merged_ref[...], cots_ref[...], 0, 0)
    for block in range(16):
        grad_ref[block] = grad[block * 16 : block * 16 + 16].astype(BF16)


def call(kernel, inputs, held, outputs, saved, scratch, micros):
    whole, there = pl.BlockSpec(memory_space=pltpu.VMEM), pl.BlockSpec(memory_space=pl.ANY)
    specs = [whole if at < held else there for at in range(len(inputs))]
    if inputs[0].ndim == 1:
        specs[0] = pl.BlockSpec(memory_space=pltpu.SMEM)
    return pl.pallas_call(
        kernel,
        out_shape=[jax.ShapeDtypeStruct(shape, BF16) for shape in outputs],
        in_specs=specs,
        out_specs=[whole if at < saved else there for at in range(len(outputs))],
        scratch_shapes=scratch,
        compiler_params=pltpu.CompilerParams(vmem_limit_bytes=56 * 2**20),
        cost_estimate=pl.CostEstimate(
            flops=micros * 10**9, bytes_accessed=micros * 10**6, transcendentals=0
        ),
    )(*inputs)


def vmem(*shape):
    return pltpu.VMEM(shape, BF16)


def add_kernel(keep_ref, arrived_ref, blocks_ref):
    blocks_ref[...] = (keep_ref[...].astype(F32) + arrived_ref[...].astype(F32)).astype(BF16)


def add_into_kernel(keep_ref, arrived_ref, _, blocks_ref):
    add_kernel(keep_ref, arrived_ref, blocks_ref)


def pair_sum(keep, send, blocks, place):
    arrived = lax.ppermute(send, "core", [(0, 1), (1, 0)])
    tile = (16, 16, keep.shape[-1])
    taken = pl.BlockSpec(tile, lambda step: (step, 0, 0))
    inputs, specs, aliases = [keep, arrived], [taken, taken], {}
    if blocks is not None:
        inputs, specs = inputs + [blocks], specs + [pl.BlockSpec(memory_space=pl.ANY)]
        aliases = {2: 0}
    return pl.pallas_call(
        add_kernel if blocks is None else add_into_kernel,
        grid=(4,),
        out_shape=jax.ShapeDtypeStruct((64, 16, 1536), BF16),
        in_specs=specs,
        out_specs=pl.BlockSpec(tile, lambda step: (step, 0, place)),
        input_output_aliases=aliases,
        compiler_params=pltpu.CompilerParams(vmem_limit_bytes=16 * 2**20),
        cost_estimate=pl.CostEstimate(
            flops=keep.size, bytes_accessed=6 * keep.size, transcendentals=0
        ),
    )(*inputs)


def unweave(share):
    cols = share.shape[-1]
    return share.reshape(4, 4, cols).transpose(1, 0, 2).reshape(4, 4 * cols)


def shifted_block(block, down, right):
    route = []
    for source in range(128):
        row, col = source // 16, source % 16
        route.append((source, (row + down) % 8 * 16 + (col + right) % 16))
    return lax.ppermute(block, GRID, route)


def quadrants(field):
    field = field.transpose(1, 2, 0, 3)
    rows, cols = field.shape[0] // 2, field.shape[1] // 2
    corners = field[:rows, :cols], field[:rows, cols:], field[rows:, :cols], field[rows:, cols:]
    return [corner.reshape(-1, field.shape[-1]) for corner in corners]


def roll_back(field):
    upper_left, upper_right, lower_left, lower_right = quadrants(field)
    return [
        lower_right,
        shifted_block(lower_left, 0, -1),
        shifted_block(upper_right, -1, 0),
        shifted_block(upper_left, -1, -1),
    ]


def roll_forth(corners):
    upper_left, upper_right, lower_left, lower_right = corners
    moved = [
        shifted_block(lower_right, 1, 1),
        shifted_block(lower_left, 1, 0),
        shifted_block(upper_right, 0, 1),
        upper_left,
    ]
    upper = jnp.concatenate(moved[:2], axis=1)
    lower = jnp.concatenate(moved[2:], axis=1)
    return jnp.concatenate([upper, lower], axis=0).transpose(2, 0, 1, 3)


def window_bias(window_ids):
    labels = window_ids.reshape(2, 3, 2, 2, 3, 2).transpose(5, 2, 0, 3, 1, 4)
    labels = jnp.broadcast_to(labels[..., None], (2, 2, 2, 2, 3, 3, 2)).reshape(TOKENS)
    return jnp.where(labels[:, None] == labels[None, :], 0.0, -1e30)


def body(tokens, window_ids, cotangent, w_qkv, w_out, w_up, w_down, w_merge):
    order = token_order()
    by_feature, field, hidden_shape = (512, TOKENS), (TOKENS, 512), (TOKENS, 2048)
    all_probs = (16, TOKENS, TOKENS)
    core = lax.axis_index("core").reshape(1)
    quads = roll_back(tokens)
    cot = jnp.concatenate(roll_back(cotangent), axis=0)
    cotangents = lax.all_gather(cot, NEAR, tiled=True)

    (level_two, merged, tokens_in, packed, keys_t, attended, first_t, middle, after_mlp, probs,
     hidden, slope) = call(
        forward_kernel,
        [*quads, jnp.asarray(order, BF16), window_bias(window_ids), w_qkv, w_qkv.T,
         w_out, w_up, w_down, w_merge], 8,
        [(MERGED, 1024), (8, MERGED, 256), field, (12, TOKENS, 128), by_feature, by_feature,
         by_feature, field, field, all_probs, hidden_shape, hidden_shape], 9,
        [vmem(*by_feature), vmem(*by_feature), vmem(*hidden_shape), vmem(*hidden_shape),
         vmem(*all_probs), vmem(*w_out.shape), vmem(*w_up.shape), vmem(*w_down.shape),
         vmem(*w_merge.shape), pltpu.SemaphoreType.DMA((4,)), pltpu.SemaphoreType.DMA((3,))],
        15,
    )
    keep, send, middle_grad = call(
        middle_kernel,
        [core, cot, middle, after_mlp, attended, w_merge, hidden, w_down, slope, w_up], 5,
        [(64, 16, 1152), (64, 16, 1152), field], 3,
        [vmem(*w_merge.shape), vmem(*hidden_shape), vmem(*w_down.shape), vmem(*hidden_shape),
         vmem(*w_up.shape), pltpu.SemaphoreType.DMA((5,))],
        12,
    )
    merged = lax.all_to_all(merged, NEAR, 0, 0, tiled=True).reshape(8 * MERGED, 256)
    merge_part, = call(merge_kernel, [merged, cotangents], 2, [(16, 16, 1024)], 1, [], 3)
    merge_part, middle_grad = lax.optimization_barrier((merge_part, middle_grad))
    late_keep, late_send, *grads = call(
        backward_kernel,
        [core, tokens_in, packed, keys_t, attended, middle_grad, first_t,
         jnp.asarray(order.transpose(0, 2, 1), BF16), w_out, probs, w_qkv], 9,
        [(64, 16, 384)] * 2 + [(MERGED, 512)] * 4, 6,
        [vmem(4, TOKENS, 128), vmem(*by_feature), pltpu.VMEM(by_feature, F32), vmem(*by_feature),
         vmem(12, TOKENS, 128), vmem(*all_probs), vmem(*w_qkv.shape),
         pltpu.SemaphoreType.DMA((5,))],
        12,
    )
    merge_landed = lax.all_to_all(merge_part, FAR, 0, 0, tiled=True)
    grad_merge = jnp.sum(merge_landed.astype(F32), axis=0)
    level_two = level_two.reshape(4, 3, 3, 2, 1024)
    level_two = roll_forth([level_two[quad] for quad in range(4)])

    blocks = pair_sum(keep, send, None, 0)
    blocks = pair_sum(late_keep, late_send, blocks, 3)
    blocks, grad_merge, level_two = lax.optimization_barrier((blocks, grad_merge, level_two))
    landed = lax.all_to_all(blocks, PAIRS, 0, 0, tiled=True)
    share = jnp.sum(landed.astype(F32), axis=0)
    grad_down, grad_up = share[:, :512], unweave(share[:, 512:1024])
    grad_out, grad_qkv = unweave(share[:, 1024:1152]), unweave(share[:, 1152:])
    grad_tokens = roll_forth([grad.reshape(6, 6, 2, 512) for grad in grads])
    return (level_two, grad_tokens, grad_qkv, grad_out, grad_up, grad_down, grad_merge)


def solution(mesh):
    cube = jax.sharding.Mesh(mesh.devices.reshape(4, 2, 4, 2, 2), GRID)
    lat, lon = GRID[:2], GRID[2:]
    field = P(None, lat, lon, None)
    share = P(GRID, None)
    return jax.shard_map(
        body,
        mesh=cube,
        in_specs=(field, P(lat, lon), field, P(), P(), P(), P(), P()),
        out_specs=(field, field, share, share, share, share, share),
        check_vma=False,
    )
```

```python
import functools

import jax
import jax.numpy as jnp
import numpy as np
from jax import lax
from jax.experimental import pallas as pl
from jax.experimental.pallas import tpu as pltpu
from jax.sharding import PartitionSpec as P

HEAD = 32
WIN = 12
TOKENS = 2 * WIN * WIN
MERGED = TOKENS // 4
EPS = 1e-05
LOG2E = 1.4426950408889634
GRID = ("z", "x_lo", "y", "x_hi", "core")
BF16 = jnp.bfloat16
F32 = jnp.float32

PAIRS = ("z", "x_lo", "y", "x_hi")
NEAR = ("y", "core")


PACKED = MERGED + 36


def token_order():
    order = np.zeros((4, TOKENS, PACKED), np.float32)
    for quad in range(4):
        for row in range(6):
            for col in range(6):
                for level in range(2):
                    position = (col % 2) * 2 + row % 2
                    patch = quad * 18 + (row // 2 * 3 + col // 2) * 2 + level
                    order[quad, position * MERGED + patch, (row * 6 + col) * 2 + level] = 1.0
    return order


def cotangent_order():
    order = np.zeros((4, 2 * MERGED, PACKED), np.float32)
    for quad in range(4):
        for half in range(2):
            for patch in range(18):
                order[quad, half * MERGED + quad * 18 + patch, MERGED + half * 18 + patch] = 1.0
    return order


def dot(left, right, left_dim=1, right_dim=0):
    return lax.dot_general(
        left, right, (((left_dim,), (right_dim,)), ((), ())), preferred_element_type=F32
    )


def normalize(wide):
    centered = wide - jnp.mean(wide, axis=-1, keepdims=True)
    inverse_std = lax.rsqrt(jnp.mean(centered * centered, axis=-1, keepdims=True) + EPS)
    return centered * inverse_std, inverse_std


def norm_back(normed, inverse_std, upstream):
    mean_grad = jnp.mean(upstream, axis=-1, keepdims=True)
    mean_cross = jnp.mean(upstream * normed, axis=-1, keepdims=True)
    return inverse_std * (upstream - mean_grad - normed * mean_cross)


def eye(size):
    rows = lax.broadcasted_iota(jnp.int32, (size, size), 0)
    cols = lax.broadcasted_iota(jnp.int32, (size, size), 1)
    return jnp.where(rows == cols, 1.0, 0.0).astype(BF16)


def weave(even, grads, keep, send, cols):
    tiles = [grad.reshape(64, 8, grad.shape[-1]) for grad in grads]
    turned = [pltpu.roll(tile, 4, 1) for tile in tiles]
    upper = lax.broadcasted_iota(jnp.int32, tiles[0].shape, 1) < 4
    for half in range(2):
        one, two = half * 2, half * 2 + 1
        first = jnp.where(upper, tiles[one], turned[two])
        second = jnp.where(upper, turned[one], tiles[two])
        rows = slice(half * 8, half * 8 + 8)
        keep[:, rows, cols] = jnp.where(even, first, second).astype(BF16)
        send[:, rows, cols] = jnp.where(even, second, first).astype(BF16)


def weave_all(grads):
    tiles = [grad.reshape(32, 8, grad.shape[-1]) for grad in grads]
    turned = [pltpu.roll(tile, 4, 1) for tile in tiles]
    upper = lax.broadcasted_iota(jnp.int32, tiles[0].shape, 1) < 4
    halves = []
    for one, two in ((0, 1), (2, 3)):
        first = jnp.where(upper, tiles[one], turned[two])
        second = jnp.where(upper, turned[one], tiles[two])
        halves.append(jnp.stack([first, second], axis=1))
    return jnp.stack(halves, axis=2).reshape(64, 16, grads[0].shape[-1]).astype(BF16)


def load(pairs, sems):
    copies = [pltpu.make_async_copy(*pair, sems.at[at]) for at, pair in enumerate(pairs)]
    for copy in copies:
        copy.start()
    return copies


def merge_norm(after_mlp):
    pieces = [after_mlp[p * MERGED : (p + 1) * MERGED] for p in range(4)]
    mean = sum(jnp.sum(v, axis=-1, keepdims=True) for v in pieces) / 2048.0
    pieces = [v - mean for v in pieces]
    inverse_out = lax.rsqrt(
        sum(jnp.sum(v * v, axis=-1, keepdims=True) for v in pieces) / 2048.0 + EPS
    )
    return [v * inverse_out for v in pieces], inverse_out


def near_order():
    source = lax.broadcasted_iota(jnp.int32, (512, 512), 0)
    target = lax.broadcasted_iota(jnp.int32, (512, 512), 1)
    near = source // 4 % 4 * 2 + source // 16 % 2
    place = near * 64 + source // 32 * 4 + source % 4
    return jnp.where(target == place, 1.0, 0.0).astype(BF16)


def forward_kernel(
    quad0, quad1, quad2, quad3, order_ref, cot_order_ref, bias_ref, w_qkv, w_qkv_t,
    w_out_hbm, w_up_hbm, w_down_hbm, w_merge_hbm,
    cot_ref, level_two_ref, merged_ref, tokens_ref, packed_ref, keys_t_ref, attended_ref, first_t_ref,
    middle_ref, after_mlp_ref, probs_hbm, hidden_hbm, slope_hbm,
    query_t, values_t, slope_ref, hidden_ref, probs_ref, w_out, w_up, w_down, w_merge,
    in_sems, out_sems,
):
    weights = load(
        [(w_out_hbm, w_out), (w_up_hbm, w_up), (w_down_hbm, w_down), (w_merge_hbm, w_merge)],
        in_sems,
    )
    quads = (quad0, quad1, quad2, quad3)
    tokens = sum(dot(order_ref[q], quads[q][...]) for q in range(4))
    tokens_ref[...] = tokens.astype(BF16)
    halves = sum(dot(cot_order_ref[q], quads[q][...]) for q in range(4))
    cot_ref[:, :512] = halves[:MERGED].astype(BF16)
    cot_ref[:, 512:] = halves[MERGED:].astype(BF16)
    first_norm = normalize(tokens)[0].astype(BF16)
    first_t_ref[...] = dot(eye(512), first_norm, 1, 1).astype(BF16)
    for part in range(12):
        packed_ref[part] = dot(first_norm, w_qkv[:, part * 128 : part * 128 + 128]).astype(BF16)
    query_t[...] = dot(w_qkv_t[:512], first_norm, 1, 1).astype(BF16)
    keys_t_ref[...] = dot(w_qkv_t[512:1024], first_norm, 1, 1).astype(BF16)
    values_t[...] = dot(w_qkv_t[1024:], first_norm, 1, 1).astype(BF16)

    head_of_row = lax.broadcasted_iota(jnp.int32, (128, TOKENS), 0) // HEAD

    def attend(group, _):
        keys = packed_ref[4 + group]
        queries = query_t[pl.ds(pl.multiple_of(group * 128, 128), 128), :]
        for head in range(4):
            masked = jnp.where(head_of_row == head, queries, jnp.zeros_like(queries))
            scores = dot(keys, masked) * (HEAD ** (-0.5) * LOG2E) + bias_ref[...]
            raised = jnp.exp2(scores - jnp.max(scores, axis=0, keepdims=True))
            inverse = 1.0 / jnp.sum(raised, axis=0, keepdims=True)
            probs = (raised * inverse).astype(BF16)
            probs_ref[group * 4 + head] = probs
            at = pl.ds(pl.multiple_of(group * 128 + head * HEAD, HEAD), HEAD)
            attended_ref[at, :] = dot(values_t[at, :], probs).astype(BF16)
        return 0

    lax.fori_loop(0, 4, attend, 0)
    saves = load([(probs_ref, probs_hbm)], out_sems.at[pl.ds(0, 1)])

    attended = dot(eye(TOKENS), attended_ref[...], 1, 1).astype(BF16)
    weights[0].wait()
    attn_out = dot(attended, w_out[...]).astype(BF16)
    narrow_middle = (tokens + attn_out.astype(F32)).astype(BF16)
    middle_ref[...] = narrow_middle
    middle = narrow_middle.astype(F32)
    second_norm = normalize(middle)[0].astype(BF16)
    mlp = jnp.zeros((TOKENS, 512), F32)
    weights[1].wait()
    weights[2].wait()
    for part in range(4):
        cols = slice(part * 512, part * 512 + 512)
        before = dot(second_norm, w_up[:, cols])
        cumulative = 0.5 * (1.0 + lax.erf(before * 0.7071067811865476))
        hidden = (before * cumulative).astype(BF16)
        hidden_ref[:, cols] = hidden
        slope_ref[:, cols] = (
            cumulative + before * jnp.exp(-0.5 * before * before) * 0.3989422804014327
        ).astype(BF16)
        mlp = mlp + dot(hidden, w_down[cols])
    saves += load([(hidden_ref, hidden_hbm), (slope_ref, slope_hbm)], out_sems.at[pl.ds(1, 2)])
    after_mlp = (middle + mlp).astype(BF16)
    after_mlp_ref[...] = after_mlp
    merged_norm = [v.astype(BF16) for v in merge_norm(after_mlp.astype(F32))[0]]
    order = near_order()
    spread = [dot(v, order) for v in merged_norm]
    for near in range(8):
        at = slice(near * 64, near * 64 + 64)
        merged_ref[near] = jnp.concatenate([v[:, at] for v in spread], axis=1).astype(BF16)
    weights[3].wait()
    level_two_ref[...] = sum(
        dot(merged_norm[p], w_merge[p * 512 : p * 512 + 512]) for p in range(4)
    ).astype(BF16)
    for save in saves:
        save.wait()


def middle_kernel(
    core_ref, cot_ref, middle_ref, after_mlp_ref, attended_ref,
    w_merge_hbm, hidden_hbm, w_down_hbm, slope_hbm, w_up_hbm,
    keep_ref, send_ref, middle_grad_ref,
    w_merge, hidden_ref, w_down, slope_ref, w_up, sems,
):
    loads = load(
        [(w_merge_hbm, w_merge), (hidden_hbm, hidden_ref), (w_down_hbm, w_down),
         (slope_hbm, slope_ref), (w_up_hbm, w_up)],
        sems,
    )
    even = core_ref[0] == 0
    cotangent = cot_ref[...]
    pieces, inverse_out = merge_norm(after_mlp_ref[...].astype(F32))
    normed_mid, inverse_mid = normalize(middle_ref[...].astype(F32))
    second_t = dot(eye(512), normed_mid.astype(BF16), 1, 1).astype(BF16)
    loads[0].wait()
    upstream = [dot(cotangent, w_merge[p * 512 : p * 512 + 512], 1, 1) for p in range(4)]
    mean_grad = sum(jnp.sum(v, axis=-1, keepdims=True) for v in upstream) / 2048.0
    mean_cross = (
        sum(jnp.sum(v * u, axis=-1, keepdims=True) for v, u in zip(upstream, pieces)) / 2048.0
    )
    grad_after = jnp.concatenate(
        [inverse_out * (v - mean_grad - u * mean_cross) for v, u in zip(upstream, pieces)], axis=0
    ).astype(BF16)

    back_up = jnp.zeros((TOKENS, 512), F32)
    grads_up = []
    for copy in loads[1:]:
        copy.wait()
    for part in range(4):
        cols = slice(part * 512, part * 512 + 512)
        grad = dot(hidden_ref[:, cols], grad_after, 0, 0).astype(BF16)
        for pair in range(16):
            low = grad[pair * 32 : pair * 32 + 16]
            high = grad[pair * 32 + 16 : pair * 32 + 32]
            keep_ref[part * 16 + pair, :, :512] = jnp.where(even, low, high)
            send_ref[part * 16 + pair, :, :512] = jnp.where(even, high, low)
        grad_before = (
            dot(grad_after, w_down[cols], 1, 1) * slope_ref[:, cols].astype(F32)
        ).astype(BF16)
        grads_up.append(dot(second_t, grad_before))
        back_up = back_up + dot(grad_before, w_up[:, cols], 1, 1)
    weave(even, grads_up, keep_ref, send_ref, slice(512, 1024))
    middle_grad = (
        grad_after.astype(F32) + norm_back(normed_mid, inverse_mid, back_up)
    ).astype(BF16)
    middle_grad_ref[...] = middle_grad
    grad = dot(attended_ref[...], middle_grad)
    weave(even, [grad[:, p * 128 : p * 128 + 128] for p in range(4)], keep_ref, send_ref,
          slice(1024, 1152))


def backward_kernel(
    core_ref, tokens_ref, packed_ref, keys_t_ref, attended_ref, middle_grad_ref,
    first_t_ref, order_ref, w_out, probs_hbm, w_qkv_hbm,
    keep_ref, send_ref, out0, out1, out2, out3,
    grad_heads, grad_heads_t, products, query_grad_t, packed_grad, probs_ref, w_qkv, sems,
):
    loads = load(
        [(probs_hbm.at[pl.ds(g * 4, 4)], probs_ref.at[pl.ds(g * 4, 4)]) for g in range(4)]
        + [(w_qkv_hbm, w_qkv)],
        sems,
    )
    even = core_ref[0] == 0
    middle_grad = middle_grad_ref[...]
    for group in range(4):
        grad_heads[group] = dot(
            middle_grad, w_out[group * 128 : group * 128 + 128], 1, 1
        ).astype(BF16)
    grad_heads_t[...] = dot(w_out[...], middle_grad, 1, 1).astype(BF16)
    products[...] = grad_heads_t[...].astype(F32) * attended_ref[...].astype(F32)

    head_of_row = lax.broadcasted_iota(jnp.int32, (128, TOKENS), 0) // HEAD
    head_of_lane = lax.broadcasted_iota(jnp.int32, (TOKENS, 128), 1) // HEAD

    def attend_back(group):
        loads[group].wait()
        queries = packed_ref[group]
        values = packed_ref[8 + group]
        upstream = grad_heads[group]
        upstream_t = grad_heads_t[slice(group * 128, group * 128 + 128), :]
        grad_keys = jnp.zeros((TOKENS, 128), F32)
        grad_values = jnp.zeros((TOKENS, 128), F32)
        for head in range(4):
            at = slice(group * 128 + head * HEAD, group * 128 + head * HEAD + HEAD)
            masked_t = jnp.where(head_of_row == head, upstream_t, jnp.zeros_like(upstream_t))
            weights = probs_ref[group * 4 + head]
            total = jnp.sum(products[at, :], axis=0, keepdims=True)
            grad_weights = dot(values, masked_t)
            scores = (
                weights.astype(F32) * ((grad_weights - total) * HEAD ** (-0.5))
            ).astype(BF16)
            in_head = head_of_lane == head
            grad_keys += dot(scores, jnp.where(in_head, queries, jnp.zeros_like(queries)))
            grad_values += dot(weights, jnp.where(in_head, upstream, jnp.zeros_like(upstream)))
            query_grad_t[at, :] = dot(keys_t_ref[at, :], scores).astype(BF16)
        packed_grad[4 + group] = grad_keys.astype(BF16)
        packed_grad[8 + group] = grad_values.astype(BF16)

    for group in range(4):
        attend_back(group)

    identity = eye(TOKENS)
    for group in range(4):
        packed_grad[group] = dot(
            identity, query_grad_t[group * 128 : group * 128 + 128, :], 1, 1
        ).astype(BF16)
    first_t = first_t_ref[...]
    loads[4].wait()
    back_qkv = jnp.zeros((TOKENS, 512), F32)
    grads = []
    for part in range(3):
        wide = jnp.concatenate([packed_grad[part * 4 + g] for g in range(4)], axis=1)
        grad = dot(first_t, wide)
        grads += [grad[:, q * 128 : q * 128 + 128] for q in range(4)]
        back_qkv = back_qkv + dot(wide, w_qkv[:, part * 512 : part * 512 + 512], 1, 1)
    for part in range(3):
        weave(even, [grads[q * 3 + part] for q in range(4)], keep_ref, send_ref,
              slice(part * 128, part * 128 + 128))

    normed_in, inverse_in = normalize(tokens_ref[...].astype(F32))
    grad_first = back_qkv.astype(BF16).astype(F32)
    grad_tokens = (
        middle_grad.astype(F32) + norm_back(normed_in, inverse_in, grad_first)
    ).astype(BF16)
    for quad, out in enumerate((out0, out1, out2, out3)):
        out[...] = dot(order_ref[quad], grad_tokens).astype(BF16)


def assemble_kernel(
    merged_ref, cots_ref, keep_hbm, arrived_hbm, blocks_hbm, keep_ref, arrived_ref, merge_ref,
    keep_sems, arrived_sems, out_sems,
):
    parts = [pl.ds(p * 16, 16) for p in range(4)]
    keeps = load([(keep_hbm.at[p], keep_ref.at[p]) for p in parts], keep_sems)
    arrivals = load([(arrived_hbm.at[p], arrived_ref.at[p]) for p in parts], arrived_sems)
    grad = dot(merged_ref[...], cots_ref[...], 0, 0)
    merge_ref[...] = weave_all([grad[:, q * 256 : q * 256 + 256] for q in range(4)])
    saves = load(
        [(merge_ref, blocks_hbm.at[:, :, pl.ds(1536, 256)])], out_sems.at[pl.ds(4, 1)]
    )
    for part, rows in enumerate(parts):
        keeps[part].wait()
        arrivals[part].wait()
        total = keep_ref[rows].astype(F32) + arrived_ref[rows].astype(F32)
        keep_ref[rows] = total.astype(BF16)
        saves += load(
            [(keep_ref.at[rows], blocks_hbm.at[rows, :, pl.ds(0, 1152)])],
            out_sems.at[pl.ds(part, 1)],
        )
    for save in saves:
        save.wait()


def late_kernel(keep_ref, arrived_ref, _, blocks_hbm, total_ref, sem):
    total = keep_ref[...].astype(F32) + arrived_ref[...].astype(F32)
    total_ref[...] = total.astype(BF16)
    save, = load([(total_ref, blocks_hbm.at[:, :, pl.ds(1152, 384)])], sem)
    save.wait()


def share_kernel(landed_hbm, qkv_ref, out_ref, up_ref, down_ref, merge_ref, landed_ref, sems):
    loads = load(
        [(landed_hbm.at[pl.ds(p * 16, 16)], landed_ref.at[pl.ds(p * 16, 16)]) for p in range(4)],
        sems,
    )
    shared = jnp.zeros((16, 1536), F32)
    merge = [jnp.zeros((16, 256), F32) for _ in range(4)]
    for part in range(4):
        loads[part].wait()
        for chip in range(part * 16, part * 16 + 16):
            y = chip // 2 % 4
            shared = shared + landed_ref[chip, :, :1536].astype(F32)
            merge[y] = merge[y] + landed_ref[chip, :, 1536:].astype(F32)
    down_ref[...] = shared[:, :512]
    for block in range(4):
        rows = shared[block * 4 : block * 4 + 4]
        up_ref[:, block * 512 : block * 512 + 512] = rows[:, 512:1024]
        out_ref[:, block * 128 : block * 128 + 128] = rows[:, 1024:1152]
        qkv_ref[:, block * 384 : block * 384 + 384] = rows[:, 1152:]
        for y in range(4):
            merge_ref[y * 4 : y * 4 + 4, block * 256 : block * 256 + 256] = merge[y][
                block * 4 : block * 4 + 4
            ]


def call(kernel, inputs, held, outputs, saved, scratch, micros, kind=BF16, aliases=()):
    whole, there = pl.BlockSpec(memory_space=pltpu.VMEM), pl.BlockSpec(memory_space=pl.ANY)
    specs = [whole if at < held else there for at in range(len(inputs))]
    if inputs[0].ndim == 1:
        specs[0] = pl.BlockSpec(memory_space=pltpu.SMEM)
    return pl.pallas_call(
        kernel,
        out_shape=[jax.ShapeDtypeStruct(shape, kind) for shape in outputs],
        in_specs=specs,
        out_specs=[whole if at < saved else there for at in range(len(outputs))],
        scratch_shapes=scratch,
        input_output_aliases=dict(aliases),
        compiler_params=pltpu.CompilerParams(vmem_limit_bytes=(56 if micros > 9 else 24) * 2**20),
        cost_estimate=pl.CostEstimate(
            flops=micros * 10**9, bytes_accessed=micros * 10**6, transcendentals=0
        ),
    )(*inputs)


def vmem(*shape):
    return pltpu.VMEM(shape, BF16)


def dmas(count):
    return pltpu.SemaphoreType.DMA((count,))


def from_pair(send):
    return lax.ppermute(send, "core", [(0, 1), (1, 0)])


def shifted_block(block, down, right):
    route = []
    for source in range(128):
        row, col = source // 16, source % 16
        route.append((source, (row + down) % 8 * 16 + (col + right) % 16))
    return lax.ppermute(block, GRID, route)


def quadrants(field):
    field = field.transpose(1, 2, 0, 3)
    rows, cols = field.shape[0] // 2, field.shape[1] // 2
    corners = field[:rows, :cols], field[:rows, cols:], field[rows:, :cols], field[rows:, cols:]
    return [corner.reshape(-1, field.shape[-1]) for corner in corners]


def roll_back(tokens, cotangent):
    corners = [
        jnp.concatenate([corner, cot[:, :512], cot[:, 512:]], axis=0)
        for corner, cot in zip(quadrants(tokens), quadrants(cotangent))
    ]
    upper_left, upper_right, lower_left, lower_right = corners
    return [
        lower_right,
        shifted_block(lower_left, 0, -1),
        shifted_block(upper_right, -1, 0),
        shifted_block(upper_left, -1, -1),
    ]


def roll_forth(corners):
    upper_left, upper_right, lower_left, lower_right = corners
    moved = [
        shifted_block(lower_right, 1, 1),
        shifted_block(lower_left, 1, 0),
        shifted_block(upper_right, 0, 1),
        upper_left,
    ]
    upper = jnp.concatenate(moved[:2], axis=1)
    lower = jnp.concatenate(moved[2:], axis=1)
    return jnp.concatenate([upper, lower], axis=0).transpose(2, 0, 1, 3)


def window_bias(window_ids):
    labels = window_ids.reshape(2, 3, 2, 2, 3, 2).transpose(5, 2, 0, 3, 1, 4)
    labels = jnp.broadcast_to(labels[..., None], (2, 2, 2, 2, 3, 3, 2)).reshape(TOKENS)
    return jnp.where(labels[:, None] == labels[None, :], 0.0, -1e30)


def body(tokens, window_ids, cotangent, w_qkv, w_out, w_up, w_down, w_merge):
    order = token_order()
    by_feature, field, hidden_shape = (512, TOKENS), (TOKENS, 512), (TOKENS, 2048)
    all_probs = (16, TOKENS, TOKENS)
    core = lax.axis_index("core").reshape(1)
    quads = roll_back(tokens, cotangent)

    (cot, level_two, merged, tokens_in, packed, keys_t, attended, first_t, middle, after_mlp, probs,
     hidden, slope) = call(
        forward_kernel,
        [*quads, jnp.asarray(order, BF16), jnp.asarray(cotangent_order(), BF16),
         window_bias(window_ids), w_qkv, w_qkv.T, w_out, w_up, w_down, w_merge], 9,
        [(MERGED, 1024), (MERGED, 1024), (8, MERGED, 256), field, (12, TOKENS, 128), by_feature, by_feature,
         by_feature, field, field, all_probs, hidden_shape, hidden_shape], 10,
        [vmem(*by_feature), vmem(*by_feature), vmem(*hidden_shape), vmem(*hidden_shape),
         vmem(*all_probs), vmem(*w_out.shape), vmem(*w_up.shape), vmem(*w_down.shape),
         vmem(*w_merge.shape), dmas(4), dmas(3)],
        15,
    )
    cotangents = lax.all_gather(cot, NEAR, tiled=True)
    merged = lax.all_to_all(merged, NEAR, 0, 0, tiled=True).reshape(8 * MERGED, 256)
    keep, send, middle_grad = call(
        middle_kernel,
        [core, cot, middle, after_mlp, attended, w_merge, hidden, w_down, slope, w_up], 5,
        [(64, 16, 1152), (64, 16, 1152), field], 3,
        [vmem(*w_merge.shape), vmem(*hidden_shape), vmem(*w_down.shape), vmem(*hidden_shape),
         vmem(*w_up.shape), dmas(5)],
        12,
    )
    late_keep, late_send, *grads = call(
        backward_kernel,
        [core, tokens_in, packed, keys_t, attended, middle_grad, first_t,
         jnp.asarray(order[:, :, :MERGED].transpose(0, 2, 1), BF16), w_out, probs, w_qkv], 9,
        [(64, 16, 384)] * 2 + [(MERGED, 512)] * 4, 6,
        [vmem(4, TOKENS, 128), vmem(*by_feature), pltpu.VMEM(by_feature, F32), vmem(*by_feature),
         vmem(12, TOKENS, 128), vmem(*all_probs), vmem(*w_qkv.shape),
         dmas(5)],
        12,
    )
    blocks, = call(
        assemble_kernel, [merged, cotangents, keep, from_pair(send)], 2,
        [(64, 16, 1792)], 0,
        [vmem(64, 16, 1152), vmem(64, 16, 1152), vmem(64, 16, 256), dmas(4), dmas(4), dmas(5)],
        4,
    )
    blocks, = call(
        late_kernel, [late_keep, from_pair(late_send), blocks], 2, [blocks.shape], 0,
        [vmem(64, 16, 384), dmas(1)], 2, aliases={2: 0},
    )
    landed = lax.all_to_all(blocks, PAIRS, 0, 0, tiled=True)
    grad_qkv, grad_out, grad_up, grad_down, grad_merge = call(
        share_kernel, [landed], 0,
        [(4, 1536), (4, 512), (4, 2048), (16, 512), (16, 1024)], 5,
        [vmem(*blocks.shape), dmas(4)], 3, kind=F32,
    )
    level_two = level_two.reshape(4, 3, 3, 2, 1024)
    level_two = roll_forth([level_two[quad] for quad in range(4)])
    grad_tokens = roll_forth([grad.reshape(6, 6, 2, 512) for grad in grads])
    return (level_two, grad_tokens, grad_qkv, grad_out, grad_up, grad_down, grad_merge)


def solution(mesh):
    cube = jax.sharding.Mesh(mesh.devices.reshape(4, 2, 4, 2, 2), GRID)
    lat, lon = GRID[:2], GRID[2:]
    field = P(None, lat, lon, None)
    share = P(GRID, None)
    return jax.shard_map(
        body,
        mesh=cube,
        in_specs=(field, P(lat, lon), field, P(), P(), P(), P(), P()),
        out_specs=(field, field, share, share, share, share, share),
        check_vma=False,
    )
```

```python
import functools

import jax
import jax.numpy as jnp
import numpy as np
from jax import lax
from jax.experimental import pallas as pl
from jax.experimental.pallas import tpu as pltpu
from jax.sharding import PartitionSpec as P

HEAD = 32
WIN = 12
TOKENS = 2 * WIN * WIN
MERGED = TOKENS // 4
EPS = 1e-05
LOG2E = 1.4426950408889634
GRID = ("z", "x_lo", "y", "x_hi", "core")
BF16 = jnp.bfloat16
F32 = jnp.float32

PAIRS = ("z", "x_lo", "y", "x_hi")


PACKED = MERGED + 36


def token_order():
    order = np.zeros((4, TOKENS, PACKED), np.float32)
    for quad in range(4):
        for row in range(6):
            for col in range(6):
                for level in range(2):
                    position = (col % 2) * 2 + row % 2
                    patch = quad * 18 + (row // 2 * 3 + col // 2) * 2 + level
                    order[quad, position * MERGED + patch, (row * 6 + col) * 2 + level] = 1.0
    return order


def cotangent_order():
    order = np.zeros((4, 2 * MERGED, PACKED), np.float32)
    for quad in range(4):
        for half in range(2):
            for patch in range(18):
                order[quad, half * MERGED + quad * 18 + patch, MERGED + half * 18 + patch] = 1.0
    return order


def dot(left, right, left_dim=1, right_dim=0):
    return lax.dot_general(
        left, right, (((left_dim,), (right_dim,)), ((), ())), preferred_element_type=F32
    )


def normalize(wide):
    centered = wide - jnp.mean(wide, axis=-1, keepdims=True)
    inverse_std = lax.rsqrt(jnp.mean(centered * centered, axis=-1, keepdims=True) + EPS)
    return centered * inverse_std, inverse_std


def norm_back(normed, inverse_std, upstream):
    mean_grad = jnp.mean(upstream, axis=-1, keepdims=True)
    mean_cross = jnp.mean(upstream * normed, axis=-1, keepdims=True)
    return inverse_std * (upstream - mean_grad - normed * mean_cross)


def eye(size):
    rows = lax.broadcasted_iota(jnp.int32, (size, size), 0)
    cols = lax.broadcasted_iota(jnp.int32, (size, size), 1)
    return jnp.where(rows == cols, 1.0, 0.0).astype(BF16)


def weave(grads, slots, cols):
    tiles = [grad.reshape(64, 8, grad.shape[-1]) for grad in grads]
    turned = [pltpu.roll(tile, 4, 1) for tile in tiles]
    upper = lax.broadcasted_iota(jnp.int32, tiles[0].shape, 1) < 4
    for half in range(2):
        one, two = half * 2, half * 2 + 1
        rows = slice(half * 8, half * 8 + 8)
        slots[0, :, rows, cols] = jnp.where(upper, tiles[one], turned[two]).astype(BF16)
        slots[1, :, rows, cols] = jnp.where(upper, turned[one], tiles[two]).astype(BF16)


def load(pairs, sems):
    copies = [pltpu.make_async_copy(*pair, sems.at[at]) for at, pair in enumerate(pairs)]
    for copy in copies:
        copy.start()
    return copies


def merge_norm(after_mlp):
    pieces = [after_mlp[p * MERGED : (p + 1) * MERGED] for p in range(4)]
    mean = sum(jnp.sum(v, axis=-1, keepdims=True) for v in pieces) / 2048.0
    pieces = [v - mean for v in pieces]
    inverse_out = lax.rsqrt(
        sum(jnp.sum(v * v, axis=-1, keepdims=True) for v in pieces) / 2048.0 + EPS
    )
    return [v * inverse_out for v in pieces], inverse_out


def near_order():
    source = lax.broadcasted_iota(jnp.int32, (512, 512), 0)
    target = lax.broadcasted_iota(jnp.int32, (512, 512), 1)
    place = source // 4 % 4 * 128 + source // 16 * 4 + source % 4
    return jnp.where(target == place, 1.0, 0.0).astype(BF16)


def gelu_parts(values):
    density = jnp.exp2(values * values * (-0.5 * LOG2E))
    inverse = 1.0 / (1.0 + jnp.abs(values) * (0.3275911 * 0.7071067811865476))
    series = 0.5 * 1.061405429
    for term in (-1.453152027, 1.421413741, -0.284496736, 0.254829592):
        series = series * inverse + 0.5 * term
    tail = series * inverse * density
    return jnp.where(values < 0.0, tail, 1.0 - tail), density


def forward_kernel(
    where_ref, quad0, quad1, quad2, quad3, order_ref, cot_order_ref, bias_ref, w_qkv, w_qkv_t,
    w_out_hbm, w_up_hbm, w_down_hbm, w_merge_hbm,
    cot_ref, level_two_ref, near0, near1, near2, near3, tokens_ref, packed_ref, keys_t_ref, attended_ref, first_t_ref,
    middle_ref, after_mlp_ref, probs_hbm, hidden_hbm, slope_hbm,
    query_t, values_t, slope_ref, hidden_ref, probs_ref, w_out, w_up, w_down, w_merge,
    in_sems, out_sems,
):
    weights = load(
        [(w_out_hbm, w_out), (w_up_hbm, w_up), (w_down_hbm, w_down), (w_merge_hbm, w_merge)],
        in_sems,
    )
    quads = (quad0, quad1, quad2, quad3)
    tokens = sum(dot(order_ref[q], quads[q][...]) for q in range(4))
    tokens_ref[...] = tokens.astype(BF16)
    halves = sum(dot(cot_order_ref[q], quads[q][...]) for q in range(4))
    cot_ref[:, :512] = halves[:MERGED].astype(BF16)
    cot_ref[:, 512:] = halves[MERGED:].astype(BF16)
    first_norm = normalize(tokens)[0].astype(BF16)
    first_t_ref[...] = dot(eye(512), first_norm, 1, 1).astype(BF16)
    for part in range(12):
        packed_ref[part] = dot(first_norm, w_qkv[:, part * 128 : part * 128 + 128]).astype(BF16)
    queries = dot(w_qkv_t[:512], first_norm, 1, 1)
    query_t[...] = (queries * (HEAD ** (-0.5) * LOG2E)).astype(BF16)
    keys_t_ref[...] = dot(w_qkv_t[512:1024], first_norm, 1, 1).astype(BF16)
    values_t[...] = dot(w_qkv_t[1024:], first_norm, 1, 1).astype(BF16)

    head_of_row = lax.broadcasted_iota(jnp.int32, (128, TOKENS), 0) // HEAD

    def attend(group, _):
        keys = packed_ref[4 + group]
        queries = query_t[pl.ds(pl.multiple_of(group * 128, 128), 128), :]
        for head in range(4):
            masked = jnp.where(head_of_row == head, queries, jnp.zeros_like(queries))
            scores = dot(keys, masked) + bias_ref[...]
            raised = jnp.exp2(scores - jnp.max(scores, axis=0, keepdims=True))
            inverse = 1.0 / jnp.sum(raised, axis=0, keepdims=True)
            probs = (raised * inverse).astype(BF16)
            probs_ref[group * 4 + head] = probs
            at = pl.ds(pl.multiple_of(group * 128 + head * HEAD, HEAD), HEAD)
            attended_ref[at, :] = dot(values_t[at, :], probs).astype(BF16)
        return 0

    lax.fori_loop(0, 4, attend, 0)
    saves = load([(probs_ref, probs_hbm)], out_sems.at[pl.ds(0, 1)])

    attended = dot(eye(TOKENS), attended_ref[...], 1, 1).astype(BF16)
    weights[0].wait()
    attn_out = dot(attended, w_out[...]).astype(BF16)
    narrow_middle = (tokens + attn_out.astype(F32)).astype(BF16)
    middle_ref[...] = narrow_middle
    middle = narrow_middle.astype(F32)
    second_norm = normalize(middle)[0].astype(BF16)
    mlp = jnp.zeros((TOKENS, 512), F32)
    weights[1].wait()
    weights[2].wait()
    for part in range(4):
        cols = slice(part * 512, part * 512 + 512)
        before = dot(second_norm, w_up[:, cols])
        cumulative, density = gelu_parts(before)
        hidden = (before * cumulative).astype(BF16)
        hidden_ref[:, cols] = hidden
        slope_ref[:, cols] = (cumulative + before * density * 0.3989422804014327).astype(BF16)
        mlp = mlp + dot(hidden, w_down[cols])
    saves += load([(hidden_ref, hidden_hbm), (slope_ref, slope_hbm)], out_sems.at[pl.ds(1, 2)])
    after_mlp = (middle + mlp).astype(BF16)
    after_mlp_ref[...] = after_mlp
    merged_norm = [v.astype(BF16) for v in merge_norm(after_mlp.astype(F32))[0]]
    order = near_order()
    spread = [dot(v, order) for v in merged_norm]
    blocks = [
        jnp.concatenate([v[:, at * 128 : at * 128 + 128] for v in spread], axis=1).astype(BF16)
        for at in range(4)
    ]
    y = where_ref[1]
    for step, near in enumerate((near0, near1, near2, near3)):
        block = blocks[step]
        for own in range(1, 4):
            block = jnp.where(y == own, blocks[(own + step) % 4], block)
        near[...] = block
    weights[3].wait()
    level_two_ref[...] = sum(
        dot(merged_norm[p], w_merge[p * 512 : p * 512 + 512]) for p in range(4)
    ).astype(BF16)
    for save in saves:
        save.wait()


def middle_kernel(
    where_ref, cot_ref, middle_ref, after_mlp_ref, attended_ref,
    w_merge_hbm, hidden_hbm, w_down_hbm, slope_hbm, w_up_hbm,
    middle_grad_ref, keep_hbm, send_hbm,
    w_merge, hidden_ref, w_down, slope_ref, w_up, slots, sems, out_sems,
):
    loads = load(
        [(w_merge_hbm, w_merge), (hidden_hbm, hidden_ref), (w_down_hbm, w_down),
         (slope_hbm, slope_ref), (w_up_hbm, w_up)],
        sems,
    )
    core = where_ref[0]
    cotangent = cot_ref[...]
    pieces, inverse_out = merge_norm(after_mlp_ref[...].astype(F32))
    normed_mid, inverse_mid = normalize(middle_ref[...].astype(F32))
    second_t = dot(eye(512), normed_mid.astype(BF16), 1, 1).astype(BF16)
    loads[0].wait()
    upstream = [dot(cotangent, w_merge[p * 512 : p * 512 + 512], 1, 1) for p in range(4)]
    mean_grad = sum(jnp.sum(v, axis=-1, keepdims=True) for v in upstream) / 2048.0
    mean_cross = (
        sum(jnp.sum(v * u, axis=-1, keepdims=True) for v, u in zip(upstream, pieces)) / 2048.0
    )
    grad_after = jnp.concatenate(
        [inverse_out * (v - mean_grad - u * mean_cross) for v, u in zip(upstream, pieces)], axis=0
    ).astype(BF16)

    def save(cols, at):
        return load(
            [(slots.at[core, :, :, cols], keep_hbm.at[:, :, cols]),
             (slots.at[1 - core, :, :, cols], send_hbm.at[:, :, cols])],
            out_sems.at[pl.ds(at, 2)],
        )

    loads[1].wait()
    for part in range(4):
        grad = dot(hidden_ref[:, part * 512 : part * 512 + 512], grad_after, 0, 0).astype(BF16)
        for block in range(32):
            slots[block % 2, part * 16 + block // 2, :, :512] = grad[block * 16 : block * 16 + 16]
    saves = save(pl.ds(0, 512), 0)
    back_up = jnp.zeros((TOKENS, 512), F32)
    grads_up = []
    for copy in loads[2:]:
        copy.wait()
    for part in range(4):
        cols = slice(part * 512, part * 512 + 512)
        grad_before = (
            dot(grad_after, w_down[cols], 1, 1) * slope_ref[:, cols].astype(F32)
        ).astype(BF16)
        grads_up.append(dot(second_t, grad_before))
        back_up = back_up + dot(grad_before, w_up[:, cols], 1, 1)
    weave(grads_up, slots, slice(512, 1024))
    middle_grad = (
        grad_after.astype(F32) + norm_back(normed_mid, inverse_mid, back_up)
    ).astype(BF16)
    middle_grad_ref[...] = middle_grad
    grad = dot(attended_ref[...], middle_grad)
    weave([grad[:, p * 128 : p * 128 + 128] for p in range(4)], slots, slice(1024, 1152))
    saves += save(pl.ds(512, 640), 2)
    for copy in saves:
        copy.wait()


def backward_kernel(
    where_ref, tokens_ref, packed_ref, keys_t_ref, attended_ref, middle_grad_ref,
    first_t_ref, order_ref, level_order_ref, level_two_ref, near0, near1, near2, near3, cots_ref,
    w_out, probs_hbm, w_qkv_hbm,
    out0, out1, out2, out3, keep_hbm, send_hbm,
    grad_heads, grad_heads_t, products, query_grad_t, packed_grad, probs_ref, w_qkv, slots, sems,
    out_sems,
):
    loads = load(
        [(probs_hbm.at[pl.ds(g * 4, 4)], probs_ref.at[pl.ds(g * 4, 4)]) for g in range(4)]
        + [(w_qkv_hbm, w_qkv)],
        sems,
    )
    core, y = where_ref[0], where_ref[1]

    near = [near0[...], near1[...], near2[...], near3[...]]
    near = jnp.concatenate([v.astype(F32) for v in near], axis=0).astype(BF16)
    cots = [cots_ref[lax.rem(y + 4 - step, 4)].astype(F32) for step in range(4)]
    grad = dot(near, jnp.concatenate(cots, axis=0).astype(BF16), 0, 0)
    weave([grad[:, q * 256 : q * 256 + 256] for q in range(4)], slots, slice(384, 640))

    middle_grad = middle_grad_ref[...]
    for group in range(4):
        grad_heads[group] = dot(
            middle_grad, w_out[group * 128 : group * 128 + 128], 1, 1
        ).astype(BF16)
    grad_heads_t[...] = dot(w_out[...], middle_grad, 1, 1).astype(BF16)
    products[...] = grad_heads_t[...].astype(F32) * attended_ref[...].astype(F32)

    head_of_row = lax.broadcasted_iota(jnp.int32, (128, TOKENS), 0) // HEAD
    head_of_lane = lax.broadcasted_iota(jnp.int32, (TOKENS, 128), 1) // HEAD

    def attend_back(group):
        loads[group].wait()
        queries = packed_ref[group]
        values = packed_ref[8 + group]
        upstream = grad_heads[group]
        upstream_t = grad_heads_t[slice(group * 128, group * 128 + 128), :]
        grad_keys = jnp.zeros((TOKENS, 128), F32)
        grad_values = jnp.zeros((TOKENS, 128), F32)
        for head in range(4):
            at = slice(group * 128 + head * HEAD, group * 128 + head * HEAD + HEAD)
            masked_t = jnp.where(head_of_row == head, upstream_t, jnp.zeros_like(upstream_t))
            weights = probs_ref[group * 4 + head]
            total = jnp.sum(products[at, :], axis=0, keepdims=True)
            grad_weights = dot(values, masked_t)
            scores = (
                weights.astype(F32) * ((grad_weights - total) * HEAD ** (-0.5))
            ).astype(BF16)
            in_head = head_of_lane == head
            grad_keys += dot(scores, jnp.where(in_head, queries, jnp.zeros_like(queries)))
            grad_values += dot(weights, jnp.where(in_head, upstream, jnp.zeros_like(upstream)))
            query_grad_t[at, :] = dot(keys_t_ref[at, :], scores).astype(BF16)
        packed_grad[4 + group] = grad_keys.astype(BF16)
        packed_grad[8 + group] = grad_values.astype(BF16)

    for group in range(4):
        attend_back(group)

    identity = eye(TOKENS)
    for group in range(4):
        packed_grad[group] = dot(
            identity, query_grad_t[group * 128 : group * 128 + 128, :], 1, 1
        ).astype(BF16)
    first_t = first_t_ref[...]
    loads[4].wait()
    back_qkv = jnp.zeros((TOKENS, 512), F32)
    grads = []
    for part in range(3):
        wide = jnp.concatenate([packed_grad[part * 4 + g] for g in range(4)], axis=1)
        grad = dot(first_t, wide)
        grads += [grad[:, q * 128 : q * 128 + 128] for q in range(4)]
        back_qkv = back_qkv + dot(wide, w_qkv[:, part * 512 : part * 512 + 512], 1, 1)
    for part in range(3):
        weave([grads[q * 3 + part] for q in range(4)], slots, slice(part * 128, part * 128 + 128))
    saves = load([(slots.at[core], keep_hbm), (slots.at[1 - core], send_hbm)], out_sems)

    normed_in, inverse_in = normalize(tokens_ref[...].astype(F32))
    grad_first = back_qkv.astype(BF16).astype(F32)
    grad_tokens = (
        middle_grad.astype(F32) + norm_back(normed_in, inverse_in, grad_first)
    ).astype(BF16)
    for quad, out in enumerate((out0, out1, out2, out3)):
        rows = dot(order_ref[quad], grad_tokens)
        for half in range(2):
            level_two = level_two_ref[:, half * 512 : half * 512 + 512]
            rows = rows + dot(level_order_ref[half * 4 + quad], level_two)
        out[...] = rows.astype(BF16)
    for copy in saves:
        copy.wait()


def pair_kernel(keep_hbm, arrived_hbm, *refs, place):
    blocks_hbm, keep_ref, arrived_ref, keep_sems, arrived_sems, out_sems = refs[-6:]
    cols = pl.ds(place, keep_hbm.shape[-1])
    parts = [pl.ds(p * 16, 16) for p in range(4)]
    keeps = load([(keep_hbm.at[p], keep_ref.at[p]) for p in parts], keep_sems)
    arrivals = load([(arrived_hbm.at[p], arrived_ref.at[p]) for p in parts], arrived_sems)
    saves = []
    for part, rows in enumerate(parts):
        keeps[part].wait()
        arrivals[part].wait()
        total = keep_ref[rows].astype(F32) + arrived_ref[rows].astype(F32)
        keep_ref[rows] = total.astype(BF16)
        saves += load(
            [(keep_ref.at[rows], blocks_hbm.at[rows, :, cols])], out_sems.at[pl.ds(part, 1)]
        )
    for save in saves:
        save.wait()


def share_kernel(landed_hbm, qkv_ref, out_ref, up_ref, down_ref, merge_ref, landed_ref, sems):
    loads = load(
        [(landed_hbm.at[pl.ds(p * 16, 16)], landed_ref.at[pl.ds(p * 16, 16)]) for p in range(4)],
        sems,
    )
    shared = jnp.zeros((16, 1536), F32)
    merge = [jnp.zeros((16, 256), F32) for _ in range(4)]
    for part in range(4):
        loads[part].wait()
        for chip in range(part * 16, part * 16 + 16):
            y = chip // 2 % 4
            shared = shared + landed_ref[chip, :, :1536].astype(F32)
            merge[y] = merge[y] + landed_ref[chip, :, 1536:].astype(F32)
    down_ref[...] = shared[:, :512]
    for block in range(4):
        rows = shared[block * 4 : block * 4 + 4]
        up_ref[:, block * 512 : block * 512 + 512] = rows[:, 512:1024]
        out_ref[:, block * 128 : block * 128 + 128] = rows[:, 1024:1152]
        qkv_ref[:, block * 384 : block * 384 + 384] = rows[:, 1152:]
        for y in range(4):
            merge_ref[y * 4 : y * 4 + 4, block * 256 : block * 256 + 256] = merge[y][
                block * 4 : block * 4 + 4
            ]


def call(kernel, inputs, held, outputs, saved, scratch, micros, kind=BF16, aliases=()):
    whole, there = pl.BlockSpec(memory_space=pltpu.VMEM), pl.BlockSpec(memory_space=pltpu.HBM)
    specs = [whole if at < held else there for at in range(len(inputs))]
    if held == 0 and len(inputs) > 1:
        specs[1] = pl.BlockSpec(memory_space=pl.ANY)
    if inputs[0].ndim == 1:
        specs[0] = pl.BlockSpec(memory_space=pltpu.SMEM)
    return pl.pallas_call(
        kernel,
        out_shape=[jax.ShapeDtypeStruct(shape, kind) for shape in outputs],
        in_specs=specs,
        out_specs=[whole if at < saved else there for at in range(len(outputs))],
        scratch_shapes=scratch,
        input_output_aliases=dict(aliases),
        compiler_params=pltpu.CompilerParams(vmem_limit_bytes=56 * 2**20),
        cost_estimate=pl.CostEstimate(
            flops=micros * 10**9, bytes_accessed=micros * 10**6, transcendentals=0
        ),
    )(*inputs)


def vmem(*shape):
    return pltpu.VMEM(shape, BF16)


def dmas(count):
    return pltpu.SemaphoreType.DMA((count,))


def from_pair(send):
    return lax.ppermute(send, "core", [(0, 1), (1, 0)])


def shifted_block(block, down, right):
    route = []
    for source in range(128):
        row, col = source // 16, source % 16
        route.append((source, (row + down) % 8 * 16 + (col + right) % 16))
    return lax.ppermute(block, GRID, route)


def quadrants(field):
    field = field.transpose(1, 2, 0, 3)
    rows, cols = field.shape[0] // 2, field.shape[1] // 2
    corners = field[:rows, :cols], field[:rows, cols:], field[rows:, :cols], field[rows:, cols:]
    return [corner.reshape(-1, field.shape[-1]) for corner in corners]


def roll_back(tokens, cotangent):
    corners = [
        jnp.concatenate([corner, cot[:, :512], cot[:, 512:]], axis=0)
        for corner, cot in zip(quadrants(tokens), quadrants(cotangent))
    ]
    upper_left, upper_right, lower_left, lower_right = corners
    return [
        lower_right,
        shifted_block(lower_left, 0, -1),
        shifted_block(upper_right, -1, 0),
        shifted_block(upper_left, -1, -1),
    ]


def send_forth(corners):
    upper_left, upper_right, lower_left, lower_right = corners
    return [
        shifted_block(lower_right, 1, 1),
        shifted_block(lower_left, 1, 0),
        shifted_block(upper_right, 0, 1),
        upper_left,
    ]


def from_corners(corners):
    upper = jnp.concatenate(corners[:2], axis=1)
    lower = jnp.concatenate(corners[2:], axis=1)
    return jnp.concatenate([upper, lower], axis=0).transpose(2, 0, 1, 3)


def window_bias(window_ids):
    labels = window_ids.reshape(2, 3, 2, 2, 3, 2).transpose(5, 2, 0, 3, 1, 4)
    labels = jnp.broadcast_to(labels[..., None], (2, 2, 2, 2, 3, 3, 2)).reshape(TOKENS)
    return jnp.where(labels[:, None] == labels[None, :], 0.0, -1e30)


def body(tokens, window_ids, cotangent, w_qkv, w_out, w_up, w_down, w_merge):
    order, cot_order = token_order(), cotangent_order()
    level_order = np.concatenate([cot_order[:, :MERGED], cot_order[:, MERGED:]]).transpose(0, 2, 1)
    by_feature, field, hidden_shape = (512, TOKENS), (TOKENS, 512), (TOKENS, 2048)
    all_probs, near_shape, corner = (16, TOKENS, TOKENS), (MERGED, 512), (PACKED, 512)
    where = jnp.stack([lax.axis_index("core"), lax.axis_index("y")])
    quads = roll_back(tokens, cotangent)

    (cot, level_two, near0, near1, near2, near3, tokens_in, packed, keys_t, attended, first_t,
     middle, after_mlp, probs, hidden, slope) = call(
        forward_kernel,
        [where, *quads, jnp.asarray(order, BF16), jnp.asarray(cot_order, BF16),
         window_bias(window_ids), w_qkv, w_qkv.T, w_out, w_up, w_down, w_merge], 10,
        [(MERGED, 1024), (MERGED, 1024)] + [near_shape] * 4 + [field, (12, TOKENS, 128),
         by_feature, by_feature, by_feature, field, field, all_probs, hidden_shape, hidden_shape],
        13,
        [vmem(*by_feature), vmem(*by_feature), vmem(*hidden_shape), vmem(*hidden_shape),
         vmem(*all_probs), vmem(*w_out.shape), vmem(*w_up.shape), vmem(*w_down.shape),
         vmem(*w_merge.shape), dmas(4), dmas(3)],
        15,
    )
    cotangents = lax.all_gather(cot, "y")
    near = [near0]
    for step, block in ((1, near1), (2, near2), (3, near3)):
        near.append(lax.ppermute(block, "y", [(i, (i + step) % 4) for i in range(4)]))
    middle_grad, keep, send = call(
        middle_kernel,
        [where, cot, middle, after_mlp, attended, w_merge, hidden, w_down, slope, w_up], 5,
        [field, (64, 16, 1152), (64, 16, 1152)], 1,
        [vmem(*w_merge.shape), vmem(*hidden_shape), vmem(*w_down.shape), vmem(*hidden_shape),
         vmem(*w_up.shape), vmem(2, 64, 16, 1152), dmas(5), dmas(4)],
        12,
    )
    *corners, late_keep, late_send = call(
        backward_kernel,
        [where, tokens_in, packed, keys_t, attended, middle_grad, first_t,
         jnp.asarray(order.transpose(0, 2, 1), BF16), jnp.asarray(level_order, BF16), level_two,
         *near, cotangents, w_out, probs, w_qkv], 16,
        [corner] * 4 + [(64, 16, 640)] * 2, 4,
        [vmem(4, TOKENS, 128), vmem(*by_feature), pltpu.VMEM(by_feature, F32), vmem(*by_feature),
         vmem(12, TOKENS, 128), vmem(*all_probs), vmem(*w_qkv.shape), vmem(2, 64, 16, 640),
         dmas(5), dmas(2)],
        12,
    )
    blocks = None
    for kept, sent, place in ((keep, send, 0), (late_keep, late_send, 1152)):
        blocks, = call(
            functools.partial(pair_kernel, place=place),
            [kept, from_pair(sent)] + ([] if blocks is None else [blocks]), 0,
            [(64, 16, 1792)], 0,
            [vmem(*kept.shape), vmem(*kept.shape), dmas(4), dmas(4), dmas(4)],
            2, aliases={} if blocks is None else {2: 0},
        )
    corners = send_forth(corners)
    blocks, *corners = lax.optimization_barrier((blocks, *corners))
    landed = lax.all_to_all(blocks, PAIRS, 0, 0, tiled=True)
    grad_qkv, grad_out, grad_up, grad_down, grad_merge = call(
        share_kernel, [landed], 0,
        [(4, 1536), (4, 512), (4, 2048), (16, 512), (16, 1024)], 5,
        [vmem(*blocks.shape), dmas(4)], 3, kind=F32,
    )
    grad_tokens = from_corners([c[:MERGED].reshape(6, 6, 2, 512) for c in corners])
    halves = [(c[MERGED : MERGED + 18], c[MERGED + 18 :]) for c in corners]
    level_two = from_corners(
        [jnp.concatenate(pair, axis=1).reshape(3, 3, 2, 1024) for pair in halves]
    )
    return (level_two, grad_tokens, grad_qkv, grad_out, grad_up, grad_down, grad_merge)


def solution(mesh):
    cube = jax.sharding.Mesh(mesh.devices.reshape(4, 2, 4, 2, 2), GRID)
    lat, lon = GRID[:2], GRID[2:]
    field = P(None, lat, lon, None)
    share = P(GRID, None)
    return jax.shard_map(
        body,
        mesh=cube,
        in_specs=(field, P(lat, lon), field, P(), P(), P(), P(), P()),
        out_specs=(field, field, share, share, share, share, share),
        check_vma=False,
    )
```

```python
import functools

import jax
import jax.numpy as jnp
import numpy as np
from jax import lax
from jax.experimental import pallas as pl
from jax.experimental.pallas import tpu as pltpu
from jax.sharding import PartitionSpec as P

HEAD = 32
WIN = 12
TOKENS = 2 * WIN * WIN
MERGED = TOKENS // 4
EPS = 1e-05
LOG2E = 1.4426950408889634
QUERY_SCALE = HEAD ** (-0.5) * LOG2E
GRID = ("z", "x_lo", "y", "x_hi", "core")
BF16 = jnp.bfloat16
F32 = jnp.float32

PAIRS = ("z", "x_lo", "y", "x_hi")


PACKED = MERGED + 36


def token_order():
    order = np.zeros((4, TOKENS, PACKED), np.float32)
    for quad in range(4):
        for row in range(6):
            for col in range(6):
                for level in range(2):
                    position = (col % 2) * 2 + row % 2
                    patch = quad * 18 + (row // 2 * 3 + col // 2) * 2 + level
                    order[quad, position * MERGED + patch, (row * 6 + col) * 2 + level] = 1.0
    return order


def window_places():
    places = np.zeros((2, TOKENS, WIN), np.float32)
    for row in range(WIN):
        for col in range(WIN):
            position = (col % 2) * 2 + row % 2
            quad = row // 6 * 2 + col // 6
            patch = quad * 18 + (row % 6 // 2 * 3 + col % 6 // 2) * 2
            for level in range(2):
                places[0, position * MERGED + patch + level, row] = 1.0
                places[1, position * MERGED + patch + level, col] = 1.0
    return places


def cotangent_order():
    order = np.zeros((4, 2 * MERGED, PACKED), np.float32)
    for quad in range(4):
        for half in range(2):
            for patch in range(18):
                order[quad, half * MERGED + quad * 18 + patch, MERGED + half * 18 + patch] = 1.0
    return order


def dot(left, right, left_dim=1, right_dim=0):
    return lax.dot_general(
        left, right, (((left_dim,), (right_dim,)), ((), ())), preferred_element_type=F32
    )


def normalize(wide):
    centered = wide - jnp.mean(wide, axis=-1, keepdims=True)
    inverse_std = lax.rsqrt(jnp.mean(centered * centered, axis=-1, keepdims=True) + EPS)
    return centered * inverse_std, inverse_std


def norm_back(normed, inverse_std, upstream):
    mean_grad = jnp.mean(upstream, axis=-1, keepdims=True)
    mean_cross = jnp.mean(upstream * normed, axis=-1, keepdims=True)
    return inverse_std * (upstream - mean_grad - normed * mean_cross)


def eye(size):
    rows = lax.broadcasted_iota(jnp.int32, (size, 1), 0)
    cols = lax.broadcasted_iota(jnp.int32, (1, size), 1)
    return jnp.where(rows == cols, 1.0, 0.0).astype(BF16)


def weave(grads, slots, cols):
    tiles = [grad.reshape(64, 8, grad.shape[-1]) for grad in grads]
    turned = [pltpu.roll(tile, 4, 1) for tile in tiles]
    upper = lax.broadcasted_iota(jnp.int32, tiles[0].shape, 1) < 4
    for half in range(2):
        one, two = half * 2, half * 2 + 1
        rows = slice(half * 8, half * 8 + 8)
        slots[0, :, rows, cols] = jnp.where(upper, tiles[one], turned[two]).astype(BF16)
        slots[1, :, rows, cols] = jnp.where(upper, turned[one], tiles[two]).astype(BF16)


def load(pairs, sems):
    copies = [pltpu.make_async_copy(*pair, sems.at[at]) for at, pair in enumerate(pairs)]
    for copy in copies:
        copy.start()
    return copies


def merge_norm(after_mlp):
    pieces = [after_mlp[p * MERGED : (p + 1) * MERGED] for p in range(4)]
    mean = sum(jnp.sum(v, axis=-1, keepdims=True) for v in pieces) / 2048.0
    pieces = [v - mean for v in pieces]
    inverse_out = lax.rsqrt(
        sum(jnp.sum(v * v, axis=-1, keepdims=True) for v in pieces) / 2048.0 + EPS
    )
    return [v * inverse_out for v in pieces], inverse_out


def near_order():
    source = lax.broadcasted_iota(jnp.int32, (512, 1), 0)
    target = lax.broadcasted_iota(jnp.int32, (1, 512), 1)
    place = ((source >> 2) & 3) * 128 + (source >> 4) * 4 + (source & 3)
    return jnp.where(target == place, 1.0, 0.0).astype(BF16)


def gelu_parts(values):
    density = jnp.exp2(values * values * (-0.5 * LOG2E))
    inverse = 1.0 / (1.0 + jnp.abs(values) * (0.3275911 * 0.7071067811865476))
    series = 0.5 * 1.061405429
    for term in (-1.453152027, 1.421413741, -0.284496736, 0.254829592):
        series = series * inverse + 0.5 * term
    tail = series * inverse * density
    return jnp.where(values < 0.0, tail, 1.0 - tail), density


def forward_kernel(
    where_ref, order_ref, cot_order_ref, ids_ref, places_ref, cols_t_ref, w_qkv,
    quad0_hbm, quad1_hbm, quad2_hbm, quad3_hbm, w_out_hbm, w_up_hbm, w_down_hbm, w_merge_hbm,
    cot_ref, level_two_ref, near0, near1, near2, near3, tokens_ref, packed_ref, keys_t_ref,
    attended_ref, first_t_ref, middle_ref, after_mlp_ref, probs_hbm, hidden_hbm, slope_hbm,
    quads_ref, bias_ref, query_t, values_t, slope_ref, hidden_ref, probs_ref, w_out, w_up, w_down,
    w_merge, quad_sems, in_sems, out_sems,
):
    quads = (quad0_hbm, quad1_hbm, quad2_hbm, quad3_hbm)
    quads = load([(quads[q], quads_ref.at[q]) for q in range(4)], quad_sems)
    weights = load(
        [(w_out_hbm, w_out), (w_up_hbm, w_up), (w_down_hbm, w_down), (w_merge_hbm, w_merge)],
        in_sems,
    )
    ids = ids_ref[...].astype(F32).astype(BF16)
    by_row = dot(places_ref[0], ids) * places_ref[1].astype(F32)
    by_col = dot(ids, places_ref[0], 0, 1) * cols_t_ref[...]
    alike = jnp.sum(by_row, axis=1, keepdims=True) == jnp.sum(by_col, axis=0, keepdims=True)
    bias_ref[...] = jnp.where(alike, 0.0, -1e30)
    for quad in quads:
        quad.wait()
    tokens = sum(dot(order_ref[q], quads_ref[q]) for q in range(4))
    tokens_ref[...] = tokens.astype(BF16)
    halves = sum(dot(cot_order_ref[q], quads_ref[q]) for q in range(4))
    cotangent = jnp.concatenate([halves[:MERGED], halves[MERGED:]], axis=1).astype(BF16)
    cot_ref[...] = cotangent
    first_norm = normalize(tokens)[0].astype(BF16)
    first_t_ref[...] = dot(eye(512), first_norm, 1, 1).astype(BF16)
    by_lane = eye(128)
    for part in range(12):
        grid = dot(first_norm, w_qkv[:, part * 128 : part * 128 + 128])
        grid = (grid * QUERY_SCALE if part < 4 else grid).astype(BF16)
        packed_ref[part] = grid
        turned = (query_t, keys_t_ref, values_t)[part // 4]
        rows = slice(part % 4 * 128, part % 4 * 128 + 128)
        turned[rows, :] = dot(by_lane, grid, 1, 1).astype(BF16)

    head_of_row = lax.broadcasted_iota(jnp.int32, (128, TOKENS), 0) >> 5

    def attend(group, _):
        keys = packed_ref[4 + group]
        queries = query_t[pl.ds(pl.multiple_of(group * 128, 128), 128), :]
        for head in range(4):
            masked = jnp.where(head_of_row == head, queries, jnp.zeros_like(queries))
            scores = dot(keys, masked) + bias_ref[...]
            raised = jnp.exp2(scores - jnp.max(scores, axis=0, keepdims=True))
            inverse = 1.0 / jnp.sum(raised, axis=0, keepdims=True)
            probs = (raised * inverse).astype(BF16)
            probs_ref[group * 4 + head] = probs
            at = pl.ds(pl.multiple_of(group * 128 + head * HEAD, HEAD), HEAD)
            attended_ref[at, :] = dot(values_t[at, :], probs).astype(BF16)
        return 0

    lax.fori_loop(0, 4, attend, 0)
    saves = load([(probs_ref, probs_hbm)], out_sems.at[pl.ds(0, 1)])

    attended = dot(eye(TOKENS), attended_ref[...], 1, 1).astype(BF16)
    weights[0].wait()
    attn_out = dot(attended, w_out[...]).astype(BF16)
    narrow_middle = (tokens + attn_out.astype(F32)).astype(BF16)
    middle_ref[...] = narrow_middle
    middle = narrow_middle.astype(F32)
    second_norm = normalize(middle)[0].astype(BF16)
    mlp = jnp.zeros((TOKENS, 512), F32)
    weights[1].wait()
    weights[2].wait()
    for part in range(4):
        cols = slice(part * 512, part * 512 + 512)
        before = dot(second_norm, w_up[:, cols])
        cumulative, density = gelu_parts(before)
        hidden = (before * cumulative).astype(BF16)
        hidden_ref[:, cols] = hidden
        slope_ref[:, cols] = (cumulative + before * density * 0.3989422804014327).astype(BF16)
        mlp = mlp + dot(hidden, w_down[cols])
    saves += load([(hidden_ref, hidden_hbm), (slope_ref, slope_hbm)], out_sems.at[pl.ds(1, 2)])
    after_mlp = (middle + mlp).astype(BF16)
    after_mlp_ref[...] = after_mlp
    merged_norm = [v.astype(BF16) for v in merge_norm(after_mlp.astype(F32))[0]]
    order = near_order()
    spread = [dot(v, order) for v in merged_norm]
    blocks = [
        jnp.concatenate([v[:, at * 128 : at * 128 + 128] for v in spread], axis=1).astype(BF16)
        for at in range(4)
    ]
    y = where_ref[0] >> 1
    for step, near in enumerate((near0, near1, near2, near3)):
        block = blocks[step]
        for own in range(1, 4):
            block = jnp.where(y == own, blocks[(own + step) % 4], block)
        near[:, :512] = block
        near[:, 512:] = cotangent
    weights[3].wait()
    level_two_ref[...] = sum(
        dot(merged_norm[p], w_merge[p * 512 : p * 512 + 512]) for p in range(4)
    ).astype(BF16)
    for save in saves:
        save.wait()


def middle_kernel(
    where_ref, cot_ref, middle_ref, after_mlp_ref, attended_ref,
    w_merge_hbm, hidden_hbm, w_down_hbm, slope_hbm, w_up_hbm,
    middle_grad_ref, keep_hbm, send_hbm,
    w_merge, hidden_ref, w_down, slope_ref, w_up, slots, sems, out_sems,
):
    loads = load(
        [(w_merge_hbm, w_merge), (hidden_hbm, hidden_ref), (w_down_hbm, w_down),
         (slope_hbm, slope_ref), (w_up_hbm, w_up)],
        sems,
    )
    core = where_ref[0] & 1
    cotangent = cot_ref[...]
    pieces, inverse_out = merge_norm(after_mlp_ref[...].astype(F32))
    normed_mid, inverse_mid = normalize(middle_ref[...].astype(F32))
    second_t = dot(eye(512), normed_mid.astype(BF16), 1, 1).astype(BF16)
    loads[0].wait()
    upstream = [dot(cotangent, w_merge[p * 512 : p * 512 + 512], 1, 1) for p in range(4)]
    mean_grad = sum(jnp.sum(v, axis=-1, keepdims=True) for v in upstream) / 2048.0
    mean_cross = (
        sum(jnp.sum(v * u, axis=-1, keepdims=True) for v, u in zip(upstream, pieces)) / 2048.0
    )
    grad_after = jnp.concatenate(
        [inverse_out * (v - mean_grad - u * mean_cross) for v, u in zip(upstream, pieces)], axis=0
    ).astype(BF16)

    def save(cols, at):
        return load(
            [(slots.at[core, :, :, cols], keep_hbm.at[:, :, cols]),
             (slots.at[1 - core, :, :, cols], send_hbm.at[:, :, cols])],
            out_sems.at[pl.ds(at, 2)],
        )

    loads[1].wait()
    for part in range(4):
        grad = dot(hidden_ref[:, part * 512 : part * 512 + 512], grad_after, 0, 0).astype(BF16)
        for block in range(32):
            slots[block % 2, part * 16 + block // 2, :, :512] = grad[block * 16 : block * 16 + 16]
    saves = save(pl.ds(0, 512), 0)
    back_up = jnp.zeros((TOKENS, 512), F32)
    grads_up = []
    for copy in loads[2:]:
        copy.wait()
    for part in range(4):
        cols = slice(part * 512, part * 512 + 512)
        grad_before = (
            dot(grad_after, w_down[cols], 1, 1) * slope_ref[:, cols].astype(F32)
        ).astype(BF16)
        grads_up.append(dot(second_t, grad_before))
        back_up = back_up + dot(grad_before, w_up[:, cols], 1, 1)
    weave(grads_up, slots, slice(512, 1024))
    middle_grad = (
        grad_after.astype(F32) + norm_back(normed_mid, inverse_mid, back_up)
    ).astype(BF16)
    middle_grad_ref[...] = middle_grad
    grad = dot(attended_ref[...], middle_grad)
    weave([grad[:, p * 128 : p * 128 + 128] for p in range(4)], slots, slice(1024, 1152))
    saves += save(pl.ds(512, 640), 2)
    for copy in saves:
        copy.wait()


def backward_kernel(
    where_ref, tokens_ref, packed_ref, keys_t_ref, attended_ref, middle_grad_ref,
    first_t_ref, order_ref, level_order_ref, level_two_ref, w_out,
    near0_hbm, near1_hbm, near2_hbm, near3_hbm, probs_hbm, w_qkv_hbm,
    out0, out1, out2, out3, keep_hbm, send_hbm,
    grad_heads, grad_heads_t, products, query_grad_t, packed_grad, probs_ref, w_qkv, near_ref,
    slots, near_sems, sems, out_sems,
):
    loads = load(
        [(probs_hbm.at[pl.ds(g * 4, 4)], probs_ref.at[pl.ds(g * 4, 4)]) for g in range(4)]
        + [(w_qkv_hbm, w_qkv)],
        sems,
    )
    nears = (near0_hbm, near1_hbm, near2_hbm, near3_hbm)
    nears = load([(nears[step], near_ref.at[step]) for step in range(4)], near_sems)
    core = where_ref[0] & 1
    middle_grad = middle_grad_ref[...]
    for group in range(4):
        grad_heads[group] = dot(
            middle_grad, w_out[group * 128 : group * 128 + 128], 1, 1
        ).astype(BF16)
    grad_heads_t[...] = dot(w_out[...], middle_grad, 1, 1).astype(BF16)
    products[...] = grad_heads_t[...].astype(F32) * attended_ref[...].astype(F32)

    head_of_row = lax.broadcasted_iota(jnp.int32, (128, TOKENS), 0) >> 5
    head_of_lane = lax.broadcasted_iota(jnp.int32, (TOKENS, 128), 1) >> 5

    def attend_back(group):
        loads[group].wait()
        queries = packed_ref[group]
        values = packed_ref[8 + group]
        upstream = grad_heads[group]
        upstream_t = grad_heads_t[slice(group * 128, group * 128 + 128), :]
        grad_keys = jnp.zeros((TOKENS, 128), F32)
        grad_values = jnp.zeros((TOKENS, 128), F32)
        for head in range(4):
            at = slice(group * 128 + head * HEAD, group * 128 + head * HEAD + HEAD)
            masked_t = jnp.where(head_of_row == head, upstream_t, jnp.zeros_like(upstream_t))
            weights = probs_ref[group * 4 + head]
            total = jnp.sum(products[at, :], axis=0, keepdims=True)
            grad_weights = dot(values, masked_t)
            scores = (weights.astype(F32) * ((grad_weights - total) * (1 / LOG2E))).astype(BF16)
            in_head = head_of_lane == head
            grad_keys += dot(scores, jnp.where(in_head, queries, jnp.zeros_like(queries)))
            grad_values += dot(weights, jnp.where(in_head, upstream, jnp.zeros_like(upstream)))
            query_grad_t[at, :] = (dot(keys_t_ref[at, :], scores) * QUERY_SCALE).astype(BF16)
        packed_grad[4 + group] = grad_keys.astype(BF16)
        packed_grad[8 + group] = grad_values.astype(BF16)

    for group in range(4):
        attend_back(group)

    for copy in nears:
        copy.wait()
    near = jnp.concatenate([near_ref[step].astype(F32) for step in range(4)], axis=0).astype(BF16)
    grad = dot(near[:, :512], near[:, 512:], 0, 0)
    weave([grad[:, q * 256 : q * 256 + 256] for q in range(4)], slots, slice(384, 640))

    identity = eye(TOKENS)
    for group in range(4):
        packed_grad[group] = dot(
            identity, query_grad_t[group * 128 : group * 128 + 128, :], 1, 1
        ).astype(BF16)
    first_t = first_t_ref[...]
    loads[4].wait()
    back_qkv = jnp.zeros((TOKENS, 512), F32)
    grads = []
    for part in range(3):
        wide = jnp.concatenate([packed_grad[part * 4 + g] for g in range(4)], axis=1)
        grad = dot(first_t, wide)
        grads += [grad[:, q * 128 : q * 128 + 128] for q in range(4)]
        back_qkv = back_qkv + dot(wide, w_qkv[:, part * 512 : part * 512 + 512], 1, 1)
    for part in range(3):
        weave([grads[q * 3 + part] for q in range(4)], slots, slice(part * 128, part * 128 + 128))
    saves = load([(slots.at[core], keep_hbm), (slots.at[1 - core], send_hbm)], out_sems)

    normed_in, inverse_in = normalize(tokens_ref[...].astype(F32))
    grad_first = back_qkv.astype(BF16).astype(F32)
    grad_tokens = (
        middle_grad.astype(F32) + norm_back(normed_in, inverse_in, grad_first)
    ).astype(BF16)
    for quad, out in enumerate((out0, out1, out2, out3)):
        rows = dot(order_ref[quad], grad_tokens)
        for half in range(2):
            level_two = level_two_ref[:, half * 512 : half * 512 + 512]
            rows = rows + dot(level_order_ref[half * 4 + quad], level_two)
        out[...] = rows.astype(BF16)
    for copy in saves:
        copy.wait()


def pair_kernel(keep_hbm, arrived_hbm, *refs, place):
    blocks_hbm, keep_ref, arrived_ref, keep_sems, arrived_sems, out_sems = refs[-6:]
    cols = pl.ds(place, keep_hbm.shape[-1])
    parts = [pl.ds(p * 16, 16) for p in range(4)]
    keeps = load([(keep_hbm.at[p], keep_ref.at[p]) for p in parts], keep_sems)
    arrivals = load([(arrived_hbm.at[p], arrived_ref.at[p]) for p in parts], arrived_sems)
    saves = []
    for part, rows in enumerate(parts):
        keeps[part].wait()
        arrivals[part].wait()
        total = keep_ref[rows].astype(F32) + arrived_ref[rows].astype(F32)
        keep_ref[rows] = total.astype(BF16)
        saves += load(
            [(keep_ref.at[rows], blocks_hbm.at[rows, :, cols])], out_sems.at[pl.ds(part, 1)]
        )
    for save in saves:
        save.wait()


def share_kernel(landed_hbm, qkv_ref, out_ref, up_ref, down_ref, merge_ref, landed_ref, sems):
    loads = load(
        [(landed_hbm.at[pl.ds(p * 16, 16)], landed_ref.at[pl.ds(p * 16, 16)]) for p in range(4)],
        sems,
    )
    shared = jnp.zeros((16, 1536), F32)
    merge = [jnp.zeros((16, 256), F32) for _ in range(4)]
    for part in range(4):
        loads[part].wait()
        for chip in range(part * 16, part * 16 + 16):
            y = chip // 2 % 4
            shared = shared + landed_ref[chip, :, :1536].astype(F32)
            merge[y] = merge[y] + landed_ref[chip, :, 1536:].astype(F32)
    down_ref[...] = shared[:, :512]
    for block in range(4):
        rows = shared[block * 4 : block * 4 + 4]
        up_ref[:, block * 512 : block * 512 + 512] = rows[:, 512:1024]
        out_ref[:, block * 128 : block * 128 + 128] = rows[:, 1024:1152]
        qkv_ref[:, block * 384 : block * 384 + 384] = rows[:, 1152:]
        for y in range(4):
            merge_ref[y * 4 : y * 4 + 4, block * 256 : block * 256 + 256] = merge[y][
                block * 4 : block * 4 + 4
            ]


def call(kernel, inputs, held, outputs, saved, scratch, micros, kind=BF16, free=(), aliases=()):
    whole, there = pl.BlockSpec(memory_space=pltpu.VMEM), pl.BlockSpec(memory_space=pltpu.HBM)
    specs = [whole if at < held else there for at in range(len(inputs))]
    for at in free:
        specs[at] = pl.BlockSpec(memory_space=pl.ANY)
    if inputs[0].ndim == 1:
        specs[0] = pl.BlockSpec(memory_space=pltpu.SMEM)
    return pl.pallas_call(
        kernel,
        out_shape=[jax.ShapeDtypeStruct(shape, kind) for shape in outputs],
        in_specs=specs,
        out_specs=[whole if at < saved else there for at in range(len(outputs))],
        scratch_shapes=scratch,
        input_output_aliases=dict(aliases),
        compiler_params=pltpu.CompilerParams(vmem_limit_bytes=(40 if micros > 9 else 14) * 2**20),
        cost_estimate=pl.CostEstimate(
            flops=micros * 10**9, bytes_accessed=micros * 10**6, transcendentals=0
        ),
    )(*inputs)


def vmem(*shape):
    return pltpu.VMEM(shape, BF16)


def dmas(count):
    return pltpu.SemaphoreType.DMA((count,))


def from_pair(send):
    return lax.ppermute(send, "core", [(0, 1), (1, 0)])


def shifted_block(block, down, right):
    route = []
    for source in range(128):
        row, col = source // 16, source % 16
        route.append((source, (row + down) % 8 * 16 + (col + right) % 16))
    return lax.ppermute(block, GRID, route)


def quadrants(field):
    field = field.transpose(1, 2, 0, 3)
    rows, cols = field.shape[0] // 2, field.shape[1] // 2
    corners = field[:rows, :cols], field[:rows, cols:], field[rows:, :cols], field[rows:, cols:]
    return [corner.reshape(-1, field.shape[-1]) for corner in corners]


def roll_back(tokens, cotangent):
    corners = [
        jnp.concatenate([corner, cot[:, :512], cot[:, 512:]], axis=0)
        for corner, cot in zip(quadrants(tokens), quadrants(cotangent))
    ]
    upper_left, upper_right, lower_left, lower_right = corners
    return [
        lower_right,
        shifted_block(lower_left, 0, -1),
        shifted_block(upper_right, -1, 0),
        shifted_block(upper_left, -1, -1),
    ]


def send_forth(corners):
    upper_left, upper_right, lower_left, lower_right = corners
    return [
        shifted_block(lower_right, 1, 1),
        shifted_block(lower_left, 1, 0),
        shifted_block(upper_right, 0, 1),
        upper_left,
    ]


def from_corners(corners):
    upper = jnp.concatenate(corners[:2], axis=1)
    lower = jnp.concatenate(corners[2:], axis=1)
    return jnp.concatenate([upper, lower], axis=0).transpose(2, 0, 1, 3)


def body(tokens, window_ids, cotangent, w_qkv, w_out, w_up, w_down, w_merge):
    order, cot_order = token_order(), cotangent_order()
    level_order = np.concatenate([cot_order[:, :MERGED], cot_order[:, MERGED:]]).transpose(0, 2, 1)
    by_feature, field, hidden_shape = (512, TOKENS), (TOKENS, 512), (TOKENS, 2048)
    all_probs, near_shape, corner = (16, TOKENS, TOKENS), (MERGED, 1536), (PACKED, 512)
    places = window_places()
    where = lax.axis_index(("y", "core")).reshape(1)
    quads = roll_back(tokens, cotangent)

    (cot, level_two, near0, near1, near2, near3, tokens_in, packed, keys_t, attended, first_t,
     middle, after_mlp, probs, hidden, slope) = call(
        forward_kernel,
        [where, jnp.asarray(order, BF16), jnp.asarray(cot_order, BF16), window_ids,
         jnp.asarray(places, BF16), jnp.asarray(places[1].T, F32), w_qkv, *quads,
         w_out, w_up, w_down, w_merge], 7,
        [(MERGED, 1024), (MERGED, 1024)] + [near_shape] * 4 + [field, (12, TOKENS, 128),
         by_feature, by_feature, by_feature, field, field, all_probs, hidden_shape, hidden_shape],
        13,
        [vmem(4, *corner), pltpu.VMEM((TOKENS, TOKENS), F32), vmem(*by_feature), vmem(*by_feature),
         vmem(*hidden_shape), vmem(*hidden_shape), vmem(*all_probs), vmem(*w_out.shape),
         vmem(*w_up.shape), vmem(*w_down.shape), vmem(*w_merge.shape), dmas(4), dmas(4), dmas(3)],
        15, free=range(7, 11),
    )
    near = [near0]
    for step, block in ((1, near1), (2, near2), (3, near3)):
        near.append(lax.ppermute(block, "y", [(i, (i + step) % 4) for i in range(4)]))
    middle_grad, keep, send = call(
        middle_kernel,
        [where, cot, middle, after_mlp, attended, w_merge, hidden, w_down, slope, w_up], 5,
        [field, (64, 16, 1152), (64, 16, 1152)], 1,
        [vmem(*w_merge.shape), vmem(*hidden_shape), vmem(*w_down.shape), vmem(*hidden_shape),
         vmem(*w_up.shape), vmem(2, 64, 16, 1152), dmas(5), dmas(4)],
        12,
    )
    *corners, late_keep, late_send = call(
        backward_kernel,
        [where, tokens_in, packed, keys_t, attended, middle_grad, first_t,
         jnp.asarray(order.transpose(0, 2, 1), BF16), jnp.asarray(level_order, BF16), level_two,
         w_out, *near, probs, w_qkv], 11,
        [corner] * 4 + [(64, 16, 640)] * 2, 4,
        [vmem(4, TOKENS, 128), vmem(*by_feature), pltpu.VMEM(by_feature, F32), vmem(*by_feature),
         vmem(12, TOKENS, 128), vmem(*all_probs), vmem(*w_qkv.shape), vmem(4, *near_shape),
         vmem(2, 64, 16, 640), dmas(4), dmas(5), dmas(2)],
        12, free=range(12, 15),
    )
    blocks = None
    for kept, sent, place in ((keep, send, 0), (late_keep, late_send, 1152)):
        blocks, = call(
            functools.partial(pair_kernel, place=place),
            [kept, from_pair(sent)] + ([] if blocks is None else [blocks]), 0,
            [(64, 16, 1792)], 0,
            [vmem(*kept.shape), vmem(*kept.shape), dmas(4), dmas(4), dmas(4)],
            2, free=(1,), aliases={} if blocks is None else {2: 0},
        )
    corners = send_forth(corners)
    blocks, *corners = lax.optimization_barrier((blocks, *corners))
    landed = lax.all_to_all(blocks, PAIRS, 0, 0, tiled=True)
    grad_qkv, grad_out, grad_up, grad_down, grad_merge = call(
        share_kernel, [landed], 0,
        [(4, 1536), (4, 512), (4, 2048), (16, 512), (16, 1024)], 5,
        [vmem(*blocks.shape), dmas(4)], 3, kind=F32,
    )
    grad_tokens = from_corners([c[:MERGED].reshape(6, 6, 2, 512) for c in corners])
    halves = [(c[MERGED : MERGED + 18], c[MERGED + 18 :]) for c in corners]
    level_two = from_corners(
        [jnp.concatenate(pair, axis=1).reshape(3, 3, 2, 1024) for pair in halves]
    )
    return (level_two, grad_tokens, grad_qkv, grad_out, grad_up, grad_down, grad_merge)


def solution(mesh):
    cube = jax.sharding.Mesh(mesh.devices.reshape(4, 2, 4, 2, 2), GRID)
    lat, lon = GRID[:2], GRID[2:]
    field = P(None, lat, lon, None)
    share = P(GRID, None)
    return jax.shard_map(
        body,
        mesh=cube,
        in_specs=(field, P(lat, lon), field, P(), P(), P(), P(), P()),
        out_specs=(field, field, share, share, share, share, share),
        check_vma=False,
    )
```

```python
import functools

import jax
import jax.numpy as jnp
import numpy as np
from jax import lax
from jax.experimental import pallas as pl
from jax.experimental.pallas import tpu as pltpu
from jax.sharding import PartitionSpec as P

HEAD = 32
WIN = 12
TOKENS = 2 * WIN * WIN
MERGED = TOKENS // 4
EPS = 1e-05
LOG2E = 1.4426950408889634
QUERY_SCALE = HEAD ** (-0.5) * LOG2E
GRID = ("z", "x_lo", "y", "x_hi", "core")
BF16 = jnp.bfloat16
F32 = jnp.float32

PAIRS = ("z", "x_lo", "y", "x_hi")


PACKED = MERGED + 36


def token_order():
    order = np.zeros((4, TOKENS, PACKED), np.float32)
    for quad in range(4):
        for row in range(6):
            for col in range(6):
                for level in range(2):
                    position = (col % 2) * 2 + row % 2
                    patch = quad * 18 + (row // 2 * 3 + col // 2) * 2 + level
                    order[quad, position * MERGED + patch, (row * 6 + col) * 2 + level] = 1.0
    return order


def window_places():
    places = np.zeros((2, TOKENS, WIN), np.float32)
    for row in range(WIN):
        for col in range(WIN):
            position = (col % 2) * 2 + row % 2
            quad = row // 6 * 2 + col // 6
            patch = quad * 18 + (row % 6 // 2 * 3 + col % 6 // 2) * 2
            for level in range(2):
                places[0, position * MERGED + patch + level, row] = 1.0
                places[1, position * MERGED + patch + level, col] = 1.0
    return places


def cotangent_order():
    order = np.zeros((4, 2 * MERGED, PACKED), np.float32)
    for quad in range(4):
        for half in range(2):
            for patch in range(18):
                order[quad, half * MERGED + quad * 18 + patch, MERGED + half * 18 + patch] = 1.0
    return order


def dot(left, right, left_dim=1, right_dim=0):
    return lax.dot_general(
        left, right, (((left_dim,), (right_dim,)), ((), ())), preferred_element_type=F32
    )


def normalize(wide):
    centered = wide - jnp.mean(wide, axis=-1, keepdims=True)
    inverse_std = lax.rsqrt(jnp.mean(centered * centered, axis=-1, keepdims=True) + EPS)
    return centered * inverse_std, inverse_std


def norm_back(normed, inverse_std, upstream):
    mean_grad = jnp.mean(upstream, axis=-1, keepdims=True)
    mean_cross = jnp.mean(upstream * normed, axis=-1, keepdims=True)
    return inverse_std * (upstream - mean_grad - normed * mean_cross)


def eye(size):
    rows = lax.broadcasted_iota(jnp.int32, (size, 1), 0)
    cols = lax.broadcasted_iota(jnp.int32, (1, size), 1)
    return jnp.where(rows == cols, 1.0, 0.0).astype(BF16)


def weave(grads, slots, cols):
    tiles = [grad.reshape(64, 8, grad.shape[-1]) for grad in grads]
    turned = [pltpu.roll(tile, 4, 1) for tile in tiles]
    upper = lax.broadcasted_iota(jnp.int32, tiles[0].shape, 1) < 4
    for half in range(2):
        one, two = half * 2, half * 2 + 1
        rows = slice(half * 8, half * 8 + 8)
        slots[0, :, rows, cols] = jnp.where(upper, tiles[one], turned[two]).astype(BF16)
        slots[1, :, rows, cols] = jnp.where(upper, turned[one], tiles[two]).astype(BF16)


def load(pairs, sems):
    copies = [pltpu.make_async_copy(*pair, sems.at[at]) for at, pair in enumerate(pairs)]
    for copy in copies:
        copy.start()
    return copies


def merge_norm(after_mlp):
    pieces = [after_mlp[p * MERGED : (p + 1) * MERGED] for p in range(4)]
    mean = sum(jnp.sum(v, axis=-1, keepdims=True) for v in pieces) / 2048.0
    pieces = [v - mean for v in pieces]
    inverse_out = lax.rsqrt(
        sum(jnp.sum(v * v, axis=-1, keepdims=True) for v in pieces) / 2048.0 + EPS
    )
    return [v * inverse_out for v in pieces], inverse_out


def near_order():
    source = lax.broadcasted_iota(jnp.int32, (512, 1), 0)
    target = lax.broadcasted_iota(jnp.int32, (1, 512), 1)
    place = ((source >> 2) & 3) * 128 + (source >> 4) * 4 + (source & 3)
    return jnp.where(target == place, 1.0, 0.0).astype(BF16)


def gelu_parts(values):
    density = jnp.exp2(values * values * (-0.5 * LOG2E))
    inverse = 1.0 / (1.0 + jnp.abs(values) * (0.3275911 * 0.7071067811865476))
    series = 0.5 * 1.061405429
    for term in (-1.453152027, 1.421413741, -0.284496736, 0.254829592):
        series = series * inverse + 0.5 * term
    tail = series * inverse * density
    return jnp.where(values < 0.0, tail, 1.0 - tail), density


def forward_kernel(
    where_ref, order_ref, cot_order_ref, ids_ref, places_ref, cols_t_ref, w_qkv,
    quad0_hbm, quad1_hbm, quad2_hbm, quad3_hbm, w_out_hbm, w_up_hbm, w_down_hbm, w_merge_hbm,
    level_two_ref, near0, near1, near2, near3, tokens_ref, packed_ref, keys_t_ref,
    attended_ref, first_t_ref, middle_ref, grad_after_ref, probs_hbm, slope_hbm, keep_hbm, send_hbm,
    quads_ref, bias_ref, query_t, values_t, slope_ref, hidden_ref, probs_ref, w_out, w_up, w_down,
    w_merge, slots, quad_sems, in_sems, out_sems,
):
    quads = (quad0_hbm, quad1_hbm, quad2_hbm, quad3_hbm)
    quads = load([(quads[q], quads_ref.at[q]) for q in range(4)], quad_sems)
    weights = load(
        [(w_out_hbm, w_out), (w_up_hbm, w_up), (w_down_hbm, w_down), (w_merge_hbm, w_merge)],
        in_sems,
    )
    ids = ids_ref[...].astype(F32).astype(BF16)
    by_row = dot(places_ref[0], ids) * places_ref[1].astype(F32)
    by_col = dot(ids, places_ref[0], 0, 1) * cols_t_ref[...]
    alike = jnp.sum(by_row, axis=1, keepdims=True) == jnp.sum(by_col, axis=0, keepdims=True)
    bias_ref[...] = jnp.where(alike, 0.0, -1e30)
    for quad in quads:
        quad.wait()
    tokens = sum(dot(order_ref[q], quads_ref[q]) for q in range(4))
    tokens_ref[...] = tokens.astype(BF16)
    halves = sum(dot(cot_order_ref[q], quads_ref[q]) for q in range(4))
    cotangent = jnp.concatenate([halves[:MERGED], halves[MERGED:]], axis=1).astype(BF16)
    first_norm = normalize(tokens)[0].astype(BF16)
    first_t_ref[...] = dot(eye(512), first_norm, 1, 1).astype(BF16)
    by_lane = eye(128)
    for part in range(3):
        wide = dot(first_norm, w_qkv[:, part * 512 : part * 512 + 512])
        wide = (wide * QUERY_SCALE if part == 0 else wide).astype(BF16)
        for group in range(4):
            grid = wide[:, group * 128 : group * 128 + 128]
            packed_ref[part * 4 + group] = grid
            turned = (query_t, keys_t_ref, values_t)[part]
            turned[group * 128 : group * 128 + 128, :] = dot(by_lane, grid, 1, 1).astype(BF16)

    head_of_row = lax.broadcasted_iota(jnp.int32, (128, TOKENS), 0) >> 5

    def scores_of(head):
        queries = query_t[head // 4 * 128 : head // 4 * 128 + 128, :]
        masked = jnp.where(head_of_row == head % 4, queries, jnp.zeros_like(queries))
        return dot(packed_ref[4 + head // 4], masked)

    ahead = scores_of(0)
    for head in range(16):
        scores = ahead + bias_ref[...]
        if head < 15:
            ahead = scores_of(head + 1)
        raised = jnp.exp2(scores - jnp.max(scores, axis=0, keepdims=True))
        inverse = 1.0 / jnp.sum(raised, axis=0, keepdims=True)
        probs = (raised * inverse).astype(BF16)
        probs_ref[head] = probs
        at = slice(head * HEAD, head * HEAD + HEAD)
        attended_ref[at, :] = dot(values_t[at, :], probs).astype(BF16)
    saves = load([(probs_ref, probs_hbm)], out_sems.at[pl.ds(0, 1)])

    attended = dot(eye(TOKENS), attended_ref[...], 1, 1).astype(BF16)
    weights[0].wait()
    attn_out = dot(attended, w_out[...]).astype(BF16)
    narrow_middle = (tokens + attn_out.astype(F32)).astype(BF16)
    middle_ref[...] = narrow_middle
    middle = narrow_middle.astype(F32)
    second_norm = normalize(middle)[0].astype(BF16)
    mlp = jnp.zeros((TOKENS, 512), F32)
    weights[1].wait()
    weights[2].wait()
    ahead = dot(second_norm, w_up[:, :512])
    for part in range(4):
        cols = slice(part * 512, part * 512 + 512)
        before = ahead
        if part < 3:
            ahead = dot(second_norm, w_up[:, part * 512 + 512 : part * 512 + 1024])
        cumulative, density = gelu_parts(before)
        hidden = (before * cumulative).astype(BF16)
        hidden_ref[:, cols] = hidden
        slope_ref[:, cols] = (cumulative + before * density * 0.3989422804014327).astype(BF16)
        mlp = mlp + dot(hidden, w_down[cols])
    saves += load([(slope_ref, slope_hbm)], out_sems.at[pl.ds(1, 1)])
    after_mlp = (middle + mlp).astype(BF16)
    pieces, inverse_out = merge_norm(after_mlp.astype(F32))
    merged_norm = [v.astype(BF16) for v in pieces]
    order = near_order()
    spread = [dot(v, order) for v in merged_norm]
    blocks = [
        jnp.concatenate([v[:, at * 128 : at * 128 + 128] for v in spread], axis=1).astype(BF16)
        for at in range(4)
    ]
    y = where_ref[0] >> 1
    for step, near in enumerate((near0, near1, near2, near3)):
        block = blocks[step]
        for own in range(1, 4):
            block = jnp.where(y == own, blocks[(own + step) % 4], block)
        near[:, :512] = block
        near[:, 512:] = cotangent

    weights[3].wait()
    level_two_ref[...] = sum(
        dot(merged_norm[p], w_merge[p * 512 : p * 512 + 512]) for p in range(4)
    ).astype(BF16)
    upstream = [dot(cotangent, w_merge[p * 512 : p * 512 + 512], 1, 1) for p in range(4)]
    mean_grad = sum(jnp.sum(v, axis=-1, keepdims=True) for v in upstream) / 2048.0
    mean_cross = (
        sum(jnp.sum(v * u, axis=-1, keepdims=True) for v, u in zip(upstream, pieces)) / 2048.0
    )
    grad_after = jnp.concatenate(
        [inverse_out * (v - mean_grad - u * mean_cross) for v, u in zip(upstream, pieces)], axis=0
    ).astype(BF16)
    grad_after_ref[...] = grad_after
    core = where_ref[0] & 1
    for part in range(4):
        grad = dot(hidden_ref[:, part * 512 : part * 512 + 512], grad_after, 0, 0).astype(BF16)
        for block in range(32):
            slots[block % 2, part * 16 + block // 2] = grad[block * 16 : block * 16 + 16]
    saves += load(
        [(slots.at[core], keep_hbm), (slots.at[1 - core], send_hbm)], out_sems.at[pl.ds(2, 2)]
    )
    for save in saves:
        save.wait()


def middle_kernel(
    where_ref, grad_after_ref, middle_ref, attended_ref, w_down_hbm, slope_hbm, w_up_hbm,
    middle_grad_ref, keep_hbm, send_hbm,
    w_down, slope_ref, w_up, slots, sems, out_sems,
):
    loads = load([(w_down_hbm, w_down), (slope_hbm, slope_ref), (w_up_hbm, w_up)], sems)
    core = where_ref[0] & 1
    grad_after = grad_after_ref[...]
    normed_mid, inverse_mid = normalize(middle_ref[...].astype(F32))
    second_t = dot(eye(512), normed_mid.astype(BF16), 1, 1).astype(BF16)

    def save(cols, at):
        return load(
            [(slots.at[core, :, :, cols], keep_hbm.at[:, :, cols]),
             (slots.at[1 - core, :, :, cols], send_hbm.at[:, :, cols])],
            out_sems.at[pl.ds(at, 2)],
        )

    back_up = jnp.zeros((TOKENS, 512), F32)
    grads_up = []
    for copy in loads:
        copy.wait()
    for part in range(4):
        cols = slice(part * 512, part * 512 + 512)
        grad_before = (
            dot(grad_after, w_down[cols], 1, 1) * slope_ref[:, cols].astype(F32)
        ).astype(BF16)
        grads_up.append(dot(second_t, grad_before))
        back_up = back_up + dot(grad_before, w_up[:, cols], 1, 1)
    weave(grads_up, slots, slice(0, 512))
    saves = save(pl.ds(0, 512), 0)
    middle_grad = (
        grad_after.astype(F32) + norm_back(normed_mid, inverse_mid, back_up)
    ).astype(BF16)
    middle_grad_ref[...] = middle_grad
    grad = dot(attended_ref[...], middle_grad)
    weave([grad[:, p * 128 : p * 128 + 128] for p in range(4)], slots, slice(512, 640))
    saves += save(pl.ds(512, 128), 2)
    for copy in saves:
        copy.wait()


def backward_kernel(
    where_ref, tokens_ref, packed_ref, keys_t_ref, attended_ref, middle_grad_ref,
    first_t_ref, order_ref, level_order_ref, level_two_ref, w_out,
    near0_hbm, near1_hbm, near2_hbm, near3_hbm, probs_hbm, w_qkv_hbm,
    out0, out1, out2, out3, keep_hbm, send_hbm,
    grad_heads, grad_heads_t, products, query_grad_t, packed_grad, probs_ref, w_qkv, near_ref,
    slots, near_sems, sems, out_sems,
):
    loads = load(
        [(probs_hbm.at[pl.ds(g * 4, 4)], probs_ref.at[pl.ds(g * 4, 4)]) for g in range(4)]
        + [(w_qkv_hbm, w_qkv)],
        sems,
    )
    nears = (near0_hbm, near1_hbm, near2_hbm, near3_hbm)
    nears = load([(nears[step], near_ref.at[step]) for step in range(4)], near_sems)
    core = where_ref[0] & 1
    middle_grad = middle_grad_ref[...]
    wide = dot(middle_grad, w_out[...], 1, 1).astype(BF16)
    for group in range(4):
        grad_heads[group] = wide[:, group * 128 : group * 128 + 128]
    grad_heads_t[...] = dot(w_out[...], middle_grad, 1, 1).astype(BF16)
    products[...] = grad_heads_t[...].astype(F32) * attended_ref[...].astype(F32)

    head_of_row = lax.broadcasted_iota(jnp.int32, (128, TOKENS), 0) >> 5
    head_of_lane = lax.broadcasted_iota(jnp.int32, (TOKENS, 128), 1) >> 5

    def attend_back(group):
        loads[group].wait()
        queries = packed_ref[group]
        values = packed_ref[8 + group]
        upstream = grad_heads[group]
        upstream_t = grad_heads_t[slice(group * 128, group * 128 + 128), :]
        grad_keys = jnp.zeros((TOKENS, 128), F32)
        grad_values = jnp.zeros((TOKENS, 128), F32)
        for head in range(4):
            at = slice(group * 128 + head * HEAD, group * 128 + head * HEAD + HEAD)
            masked_t = jnp.where(head_of_row == head, upstream_t, jnp.zeros_like(upstream_t))
            weights = probs_ref[group * 4 + head]
            total = jnp.sum(products[at, :], axis=0, keepdims=True)
            grad_weights = dot(values, masked_t)
            scores = (weights.astype(F32) * ((grad_weights - total) * (1 / LOG2E))).astype(BF16)
            in_head = head_of_lane == head
            grad_keys += dot(scores, jnp.where(in_head, queries, jnp.zeros_like(queries)))
            grad_values += dot(weights, jnp.where(in_head, upstream, jnp.zeros_like(upstream)))
            query_grad_t[at, :] = (dot(keys_t_ref[at, :], scores) * QUERY_SCALE).astype(BF16)
        packed_grad[4 + group] = grad_keys.astype(BF16)
        packed_grad[8 + group] = grad_values.astype(BF16)

    for group in range(4):
        attend_back(group)

    for copy in nears:
        copy.wait()
    near = jnp.concatenate([near_ref[step].astype(F32) for step in range(4)], axis=0).astype(BF16)
    grad = dot(near[:, :512], near[:, 512:], 0, 0)
    weave([grad[:, q * 256 : q * 256 + 256] for q in range(4)], slots, slice(384, 640))

    identity = eye(TOKENS)
    for group in range(4):
        packed_grad[group] = dot(
            identity, query_grad_t[group * 128 : group * 128 + 128, :], 1, 1
        ).astype(BF16)
    first_t = first_t_ref[...]
    loads[4].wait()
    back_qkv = jnp.zeros((TOKENS, 512), F32)
    grads = []
    for part in range(3):
        wide = jnp.concatenate([packed_grad[part * 4 + g] for g in range(4)], axis=1)
        grad = dot(first_t, wide)
        grads += [grad[:, q * 128 : q * 128 + 128] for q in range(4)]
        back_qkv = back_qkv + dot(wide, w_qkv[:, part * 512 : part * 512 + 512], 1, 1)
    for part in range(3):
        weave([grads[q * 3 + part] for q in range(4)], slots, slice(part * 128, part * 128 + 128))
    saves = load([(slots.at[core], keep_hbm), (slots.at[1 - core], send_hbm)], out_sems)

    normed_in, inverse_in = normalize(tokens_ref[...].astype(F32))
    grad_first = back_qkv.astype(BF16).astype(F32)
    grad_tokens = (
        middle_grad.astype(F32) + norm_back(normed_in, inverse_in, grad_first)
    ).astype(BF16)
    for quad, out in enumerate((out0, out1, out2, out3)):
        rows = dot(order_ref[quad], grad_tokens)
        for half in range(2):
            level_two = level_two_ref[:, half * 512 : half * 512 + 512]
            rows = rows + dot(level_order_ref[half * 4 + quad], level_two)
        out[...] = rows.astype(BF16)
    for copy in saves:
        copy.wait()


def pair_kernel(keep_hbm, arrived_hbm, *refs, place):
    blocks_hbm, keep_ref, arrived_ref, keep_sems, arrived_sems, out_sems = refs[-6:]
    cols = pl.ds(place, keep_hbm.shape[-1])
    parts = [pl.ds(p * 16, 16) for p in range(4)]
    keeps = load([(keep_hbm.at[p], keep_ref.at[p]) for p in parts], keep_sems)
    arrivals = load([(arrived_hbm.at[p], arrived_ref.at[p]) for p in parts], arrived_sems)
    saves = []
    for part, rows in enumerate(parts):
        keeps[part].wait()
        arrivals[part].wait()
        total = keep_ref[rows].astype(F32) + arrived_ref[rows].astype(F32)
        keep_ref[rows] = total.astype(BF16)
        saves += load(
            [(keep_ref.at[rows], blocks_hbm.at[rows, :, cols])], out_sems.at[pl.ds(part, 1)]
        )
    for save in saves:
        save.wait()


def arrive(landed_hbm, landed_ref, sems):
    parts = [pl.ds(p * 16, 16) for p in range(4)]
    loads = load([(landed_hbm.at[p], landed_ref.at[p]) for p in parts], sems)
    for chip in range(64):
        if chip % 16 == 0:
            loads[chip // 16].wait()
        yield chip, landed_ref[chip].astype(F32)


def down_kernel(landed_hbm, down_ref, landed_ref, sems):
    down_ref[...] = sum(block for _, block in arrive(landed_hbm, landed_ref, sems))


def share_kernel(landed_hbm, qkv_ref, out_ref, up_ref, merge_ref, landed_ref, sems):
    shared = jnp.zeros((16, 1024), F32)
    merge = [jnp.zeros((16, 256), F32) for _ in range(4)]
    for chip, block in arrive(landed_hbm, landed_ref, sems):
        y = chip // 2 % 4
        shared = shared + block[:, :1024]
        merge[y] = merge[y] + block[:, 1024:]
    for block in range(4):
        rows = shared[block * 4 : block * 4 + 4]
        up_ref[:, block * 512 : block * 512 + 512] = rows[:, :512]
        out_ref[:, block * 128 : block * 128 + 128] = rows[:, 512:640]
        qkv_ref[:, block * 384 : block * 384 + 384] = rows[:, 640:]
        for y in range(4):
            merge_ref[y * 4 : y * 4 + 4, block * 256 : block * 256 + 256] = merge[y][
                block * 4 : block * 4 + 4
            ]


def call(kernel, inputs, held, outputs, saved, scratch, micros, kind=BF16, free=(), aliases=()):
    whole, there = pl.BlockSpec(memory_space=pltpu.VMEM), pl.BlockSpec(memory_space=pltpu.HBM)
    specs = [whole if at < held else there for at in range(len(inputs))]
    for at in free:
        specs[at] = pl.BlockSpec(memory_space=pl.ANY)
    if inputs[0].ndim == 1:
        specs[0] = pl.BlockSpec(memory_space=pltpu.SMEM)
    return pl.pallas_call(
        kernel,
        out_shape=[jax.ShapeDtypeStruct(shape, kind) for shape in outputs],
        in_specs=specs,
        out_specs=[whole if at < saved else there for at in range(len(outputs))],
        scratch_shapes=scratch,
        input_output_aliases=dict(aliases),
        compiler_params=pltpu.CompilerParams(vmem_limit_bytes=(56 if micros > 5 else 14) * 2**20),
        cost_estimate=pl.CostEstimate(
            flops=micros * 10**9, bytes_accessed=micros * 10**6, transcendentals=0
        ),
    )(*inputs)


def vmem(*shape):
    return pltpu.VMEM(shape, BF16)


def dmas(count):
    return pltpu.SemaphoreType.DMA((count,))


def pair_sum(keep, send, width, place, blocks=None):
    arrived = lax.ppermute(send, "core", [(0, 1), (1, 0)])
    blocks, = call(
        functools.partial(pair_kernel, place=place),
        [keep, arrived] + ([] if blocks is None else [blocks]), 0, [(64, 16, width)], 0,
        [vmem(*keep.shape), vmem(*keep.shape), dmas(4), dmas(4), dmas(4)],
        2, free=(1,), aliases={} if blocks is None else {2: 0},
    )
    return blocks


def shifted_block(block, down, right):
    route = []
    for source in range(128):
        row, col = source // 16, source % 16
        route.append((source, (row + down) % 8 * 16 + (col + right) % 16))
    return lax.ppermute(block, GRID, route)


def quadrants(field):
    field = field.transpose(1, 2, 0, 3)
    rows, cols = field.shape[0] // 2, field.shape[1] // 2
    corners = field[:rows, :cols], field[:rows, cols:], field[rows:, :cols], field[rows:, cols:]
    return [corner.reshape(-1, field.shape[-1]) for corner in corners]


def roll_back(tokens, cotangent):
    corners = [
        jnp.concatenate([corner, cot[:, :512], cot[:, 512:]], axis=0)
        for corner, cot in zip(quadrants(tokens), quadrants(cotangent))
    ]
    upper_left, upper_right, lower_left, lower_right = corners
    return [
        lower_right,
        shifted_block(lower_left, 0, -1),
        shifted_block(upper_right, -1, 0),
        shifted_block(upper_left, -1, -1),
    ]


def send_forth(corners):
    upper_left, upper_right, lower_left, lower_right = corners
    return [
        shifted_block(lower_right, 1, 1),
        shifted_block(lower_left, 1, 0),
        shifted_block(upper_right, 0, 1),
        upper_left,
    ]


def from_corners(corners):
    upper = jnp.concatenate(corners[:2], axis=1)
    lower = jnp.concatenate(corners[2:], axis=1)
    return jnp.concatenate([upper, lower], axis=0).transpose(2, 0, 1, 3)


def body(tokens, window_ids, cotangent, w_qkv, w_out, w_up, w_down, w_merge):
    order, cot_order = token_order(), cotangent_order()
    level_order = np.concatenate([cot_order[:, :MERGED], cot_order[:, MERGED:]]).transpose(0, 2, 1)
    by_feature, field, hidden_shape = (512, TOKENS), (TOKENS, 512), (TOKENS, 2048)
    all_probs, near_shape, corner = (16, TOKENS, TOKENS), (MERGED, 1536), (PACKED, 512)
    places = window_places()
    where = lax.axis_index(("y", "core")).reshape(1)
    quads = roll_back(tokens, cotangent)

    (level_two, near0, near1, near2, near3, tokens_in, packed, keys_t, attended, first_t,
     middle, grad_after, probs, slope, down_keep, down_send) = call(
        forward_kernel,
        [where, jnp.asarray(order, BF16), jnp.asarray(cot_order, BF16), window_ids,
         jnp.asarray(places, BF16), jnp.asarray(places[1].T, F32), w_qkv, *quads,
         w_out, w_up, w_down, w_merge], 7,
        [(MERGED, 1024)] + [near_shape] * 4 + [field, (12, TOKENS, 128), by_feature, by_feature,
         by_feature, field, field, all_probs, hidden_shape, (64, 16, 512), (64, 16, 512)], 12,
        [vmem(4, *corner), pltpu.VMEM((TOKENS, TOKENS), F32), vmem(*by_feature), vmem(*by_feature),
         vmem(*hidden_shape), vmem(*hidden_shape), vmem(*all_probs), vmem(*w_out.shape),
         vmem(*w_up.shape), vmem(*w_down.shape), vmem(*w_merge.shape), vmem(2, 64, 16, 512),
         dmas(4), dmas(4), dmas(4)],
        20, free=range(7, 11),
    )
    near = [near0]
    for step, block in ((1, near1), (2, near2), (3, near3)):
        near.append(lax.ppermute(block, "y", [(i, (i + step) % 4) for i in range(4)]))
    middle_grad, keep, send = call(
        middle_kernel,
        [where, grad_after, middle, attended, w_down, slope, w_up], 4,
        [field, (64, 16, 640), (64, 16, 640)], 1,
        [vmem(*w_down.shape), vmem(*hidden_shape), vmem(*w_up.shape), vmem(2, 64, 16, 640),
         dmas(3), dmas(4)],
        7,
    )
    down_blocks = pair_sum(down_keep, down_send, 512, 0)
    middle_grad, down_blocks = lax.optimization_barrier((middle_grad, down_blocks))
    landed = lax.all_to_all(down_blocks, PAIRS, 0, 0, tiled=True)
    grad_down, = call(
        down_kernel, [landed], 0, [(16, 512)], 1, [vmem(64, 16, 512), dmas(4)], 1, kind=F32
    )
    *corners, late_keep, late_send = call(
        backward_kernel,
        [where, tokens_in, packed, keys_t, attended, middle_grad, first_t,
         jnp.asarray(order.transpose(0, 2, 1), BF16), jnp.asarray(level_order, BF16), level_two,
         w_out, *near, probs, w_qkv], 11,
        [corner] * 4 + [(64, 16, 640)] * 2, 4,
        [vmem(4, TOKENS, 128), vmem(*by_feature), pltpu.VMEM(by_feature, F32), vmem(*by_feature),
         vmem(12, TOKENS, 128), vmem(*all_probs), vmem(*w_qkv.shape), vmem(4, *near_shape),
         vmem(2, 64, 16, 640), dmas(4), dmas(5), dmas(2)],
        12, free=range(12, 15),
    )
    blocks = pair_sum(keep, send, 1280, 0)
    late_keep, grad_down = lax.optimization_barrier((late_keep, grad_down))
    blocks = pair_sum(late_keep, late_send, 1280, 640, blocks)
    corners = send_forth(corners)
    blocks, *corners = lax.optimization_barrier((blocks, *corners))
    landed = lax.all_to_all(blocks, PAIRS, 0, 0, tiled=True)
    grad_qkv, grad_out, grad_up, grad_merge = call(
        share_kernel, [landed], 0, [(4, 1536), (4, 512), (4, 2048), (16, 1024)], 4,
        [vmem(*blocks.shape), dmas(4)], 3, kind=F32,
    )
    grad_tokens = from_corners([c[:MERGED].reshape(6, 6, 2, 512) for c in corners])
    halves = [(c[MERGED : MERGED + 18], c[MERGED + 18 :]) for c in corners]
    level_two = from_corners(
        [jnp.concatenate(pair, axis=1).reshape(3, 3, 2, 1024) for pair in halves]
    )
    return (level_two, grad_tokens, grad_qkv, grad_out, grad_up, grad_down, grad_merge)


def solution(mesh):
    cube = jax.sharding.Mesh(mesh.devices.reshape(4, 2, 4, 2, 2), GRID)
    lat, lon = GRID[:2], GRID[2:]
    field = P(None, lat, lon, None)
    share = P(GRID, None)
    return jax.shard_map(
        body,
        mesh=cube,
        in_specs=(field, P(lat, lon), field, P(), P(), P(), P(), P()),
        out_specs=(field, field, share, share, share, share, share),
        check_vma=False,
    )
```

```python
import functools

import jax
import jax.numpy as jnp
import numpy as np
from jax import lax
from jax.experimental import pallas as pl
from jax.experimental.pallas import tpu as pltpu
from jax.sharding import PartitionSpec as P

HEAD = 32
WIN = 12
TOKENS = 2 * WIN * WIN
MERGED = TOKENS // 4
EPS = 1e-05
LOG2E = 1.4426950408889634
QUERY_SCALE = HEAD ** (-0.5) * LOG2E
GRID = ("z", "x_lo", "y", "x_hi", "core")
BF16 = jnp.bfloat16
F32 = jnp.float32

PAIRS = ("z", "x_lo", "y", "x_hi")


PACKED = MERGED + 36


def token_order():
    order = np.zeros((4, TOKENS, PACKED), np.float32)
    for quad in range(4):
        for row in range(6):
            for col in range(6):
                for level in range(2):
                    position = (col % 2) * 2 + row % 2
                    patch = quad * 18 + (row // 2 * 3 + col // 2) * 2 + level
                    order[quad, position * MERGED + patch, (row * 6 + col) * 2 + level] = 1.0
    return order


def window_places():
    places = np.zeros((2, TOKENS, WIN), np.float32)
    for row in range(WIN):
        for col in range(WIN):
            position = (col % 2) * 2 + row % 2
            quad = row // 6 * 2 + col // 6
            patch = quad * 18 + (row % 6 // 2 * 3 + col % 6 // 2) * 2
            for level in range(2):
                places[0, position * MERGED + patch + level, row] = 1.0
                places[1, position * MERGED + patch + level, col] = 1.0
    return places


def cotangent_order():
    order = np.zeros((4, 2 * MERGED, PACKED), np.float32)
    for quad in range(4):
        for half in range(2):
            for patch in range(18):
                order[quad, half * MERGED + quad * 18 + patch, MERGED + half * 18 + patch] = 1.0
    return order


def dot(left, right, left_dim=1, right_dim=0):
    return lax.dot_general(
        left, right, (((left_dim,), (right_dim,)), ((), ())), preferred_element_type=F32
    )


def normalize(wide):
    centered = wide - jnp.mean(wide, axis=-1, keepdims=True)
    inverse_std = lax.rsqrt(jnp.mean(centered * centered, axis=-1, keepdims=True) + EPS)
    return centered * inverse_std, inverse_std


def norm_back(normed, inverse_std, upstream):
    mean_grad = jnp.mean(upstream, axis=-1, keepdims=True)
    mean_cross = jnp.mean(upstream * normed, axis=-1, keepdims=True)
    return inverse_std * (upstream - mean_grad - normed * mean_cross)


def eye(size):
    rows = lax.broadcasted_iota(jnp.int32, (size, 1), 0)
    cols = lax.broadcasted_iota(jnp.int32, (1, size), 1)
    return jnp.where(rows == cols, 1.0, 0.0).astype(BF16)


def weave(grads, slots, cols):
    tiles = [grad.reshape(64, 8, grad.shape[-1]) for grad in grads]
    turned = [pltpu.roll(tile, 4, 1) for tile in tiles]
    upper = lax.broadcasted_iota(jnp.int32, tiles[0].shape, 1) < 4
    for half in range(2):
        one, two = half * 2, half * 2 + 1
        rows = slice(half * 8, half * 8 + 8)
        slots[0, :, rows, cols] = jnp.where(upper, tiles[one], turned[two]).astype(BF16)
        slots[1, :, rows, cols] = jnp.where(upper, turned[one], tiles[two]).astype(BF16)


def load(pairs, sems):
    copies = [pltpu.make_async_copy(*pair, sems.at[at]) for at, pair in enumerate(pairs)]
    for copy in copies:
        copy.start()
    return copies


def merge_norm(after_mlp):
    pieces = [after_mlp[p * MERGED : (p + 1) * MERGED] for p in range(4)]
    mean = sum(jnp.sum(v, axis=-1, keepdims=True) for v in pieces) / 2048.0
    pieces = [v - mean for v in pieces]
    inverse_out = lax.rsqrt(
        sum(jnp.sum(v * v, axis=-1, keepdims=True) for v in pieces) / 2048.0 + EPS
    )
    return [v * inverse_out for v in pieces], inverse_out


def near_order():
    source = lax.broadcasted_iota(jnp.int32, (512, 1), 0)
    target = lax.broadcasted_iota(jnp.int32, (1, 512), 1)
    place = ((source >> 2) & 3) * 128 + (source >> 4) * 4 + (source & 3)
    return jnp.where(target == place, 1.0, 0.0).astype(BF16)


def gelu_parts(values):
    density = jnp.exp2(values * values * (-0.5 * LOG2E))
    inverse = 1.0 / (1.0 + jnp.abs(values) * (0.3275911 * 0.7071067811865476))
    series = 0.5 * 1.061405429
    for term in (-1.453152027, 1.421413741, -0.284496736, 0.254829592):
        series = series * inverse + 0.5 * term
    tail = series * inverse * density
    return jnp.where(values < 0.0, tail, 1.0 - tail), density


def forward_kernel(
    where_ref, order_ref, cot_order_ref, ids_ref, places_ref, cols_t_ref, w_qkv,
    quad0_hbm, quad1_hbm, quad2_hbm, quad3_hbm, w_out_hbm, w_up_hbm, w_down_hbm, w_merge_hbm,
    level_two_ref, near0, near1, near2, near3, tokens_ref, packed_ref, keys_t_ref,
    attended_ref, first_t_ref, middle_ref, grad_after_ref, probs_hbm, slope_hbm, keep_hbm, send_hbm,
    quads_ref, bias_ref, query_t, values_t, slope_ref, hidden_ref, probs_ref, w_out, w_up, w_down,
    w_merge, slots, quad_sems, in_sems, out_sems,
):
    quads = (quad0_hbm, quad1_hbm, quad2_hbm, quad3_hbm)
    quads = load([(quads[q], quads_ref.at[q]) for q in range(4)], quad_sems)
    weights = load(
        [(w_out_hbm, w_out), (w_up_hbm, w_up), (w_down_hbm, w_down), (w_merge_hbm, w_merge)],
        in_sems,
    )
    ids = ids_ref[...].astype(F32).astype(BF16)
    by_row = dot(places_ref[0], ids) * places_ref[1].astype(F32)
    by_col = dot(ids, places_ref[0], 0, 1) * cols_t_ref[...]
    alike = jnp.sum(by_row, axis=1, keepdims=True) == jnp.sum(by_col, axis=0, keepdims=True)
    bias_ref[...] = jnp.where(alike, 0.0, -1e30)
    for quad in quads:
        quad.wait()
    tokens = sum(dot(order_ref[q], quads_ref[q]) for q in range(4))
    tokens_ref[...] = tokens.astype(BF16)
    halves = sum(dot(cot_order_ref[q], quads_ref[q]) for q in range(4))
    cotangent = jnp.concatenate([halves[:MERGED], halves[MERGED:]], axis=1).astype(BF16)
    first_norm = normalize(tokens)[0].astype(BF16)
    first_t_ref[...] = dot(eye(512), first_norm, 1, 1).astype(BF16)
    by_lane = eye(128)
    for part in range(3):
        wide = dot(first_norm, w_qkv[:, part * 512 : part * 512 + 512])
        wide = (wide * QUERY_SCALE if part == 0 else wide).astype(BF16)
        for group in range(4):
            grid = wide[:, group * 128 : group * 128 + 128]
            packed_ref[part * 4 + group] = grid
            turned = (query_t, keys_t_ref, values_t)[part]
            turned[group * 128 : group * 128 + 128, :] = dot(by_lane, grid, 1, 1).astype(BF16)

    head_of_row = lax.broadcasted_iota(jnp.int32, (128, TOKENS), 0) >> 5

    def scores_of(head):
        queries = query_t[head // 4 * 128 : head // 4 * 128 + 128, :]
        masked = jnp.where(head_of_row == head % 4, queries, jnp.zeros_like(queries))
        return dot(packed_ref[4 + head // 4], masked)

    ahead = scores_of(0)
    for head in range(16):
        scores = ahead + bias_ref[...]
        if head < 15:
            ahead = scores_of(head + 1)
        raised = jnp.exp2(scores - jnp.max(scores, axis=0, keepdims=True))
        inverse = 1.0 / jnp.sum(raised, axis=0, keepdims=True)
        probs = (raised * inverse).astype(BF16)
        probs_ref[head] = probs
        at = slice(head * HEAD, head * HEAD + HEAD)
        attended_ref[at, :] = dot(values_t[at, :], probs).astype(BF16)
    saves = load([(probs_ref, probs_hbm)], out_sems.at[pl.ds(0, 1)])

    attended = dot(eye(TOKENS), attended_ref[...], 1, 1).astype(BF16)
    weights[0].wait()
    attn_out = dot(attended, w_out[...]).astype(BF16)
    narrow_middle = (tokens + attn_out.astype(F32)).astype(BF16)
    middle_ref[...] = narrow_middle
    middle = narrow_middle.astype(F32)
    second_norm = normalize(middle)[0].astype(BF16)
    mlp = jnp.zeros((TOKENS, 512), F32)
    weights[1].wait()
    weights[2].wait()
    ahead = dot(second_norm, w_up[:, :512])
    for part in range(4):
        cols = slice(part * 512, part * 512 + 512)
        before = ahead
        if part < 3:
            ahead = dot(second_norm, w_up[:, part * 512 + 512 : part * 512 + 1024])
        cumulative, density = gelu_parts(before)
        hidden = (before * cumulative).astype(BF16)
        hidden_ref[:, cols] = hidden
        slope_ref[:, cols] = (cumulative + before * density * 0.3989422804014327).astype(BF16)
        mlp = mlp + dot(hidden, w_down[cols])
    saves += load([(slope_ref, slope_hbm)], out_sems.at[pl.ds(1, 1)])
    after_mlp = (middle + mlp).astype(BF16)
    pieces, inverse_out = merge_norm(after_mlp.astype(F32))
    merged_norm = [v.astype(BF16) for v in pieces]
    order = near_order()
    spread = [dot(v, order) for v in merged_norm]
    blocks = [
        jnp.concatenate([v[:, at * 128 : at * 128 + 128] for v in spread], axis=1).astype(BF16)
        for at in range(4)
    ]
    y = where_ref[0] >> 1
    for step, near in enumerate((near0, near1, near2, near3)):
        block = blocks[step]
        for own in range(1, 4):
            block = jnp.where(y == own, blocks[(own + step) % 4], block)
        near[:, :512] = block
        near[:, 512:] = cotangent

    weights[3].wait()
    level_two_ref[...] = sum(
        dot(merged_norm[p], w_merge[p * 512 : p * 512 + 512]) for p in range(4)
    ).astype(BF16)
    upstream = [dot(cotangent, w_merge[p * 512 : p * 512 + 512], 1, 1) for p in range(4)]
    mean_grad = sum(jnp.sum(v, axis=-1, keepdims=True) for v in upstream) / 2048.0
    mean_cross = (
        sum(jnp.sum(v * u, axis=-1, keepdims=True) for v, u in zip(upstream, pieces)) / 2048.0
    )
    grad_after = jnp.concatenate(
        [inverse_out * (v - mean_grad - u * mean_cross) for v, u in zip(upstream, pieces)], axis=0
    ).astype(BF16)
    grad_after_ref[...] = grad_after
    core = where_ref[0] & 1
    for part in range(4):
        grad = dot(hidden_ref[:, part * 512 : part * 512 + 512], grad_after, 0, 0).astype(BF16)
        for block in range(32):
            slots[block % 2, part * 16 + block // 2] = grad[block * 16 : block * 16 + 16]
    saves += load(
        [(slots.at[core], keep_hbm), (slots.at[1 - core], send_hbm)], out_sems.at[pl.ds(2, 2)]
    )
    for save in saves:
        save.wait()


def middle_kernel(
    where_ref, grad_after_ref, middle_ref, attended_ref, w_down_hbm, slope_hbm, w_up_hbm,
    middle_grad_ref, keep_hbm, send_hbm,
    w_down, slope_ref, w_up, slots, sems, out_sems,
):
    loads = load([(w_down_hbm, w_down), (slope_hbm, slope_ref), (w_up_hbm, w_up)], sems)
    core = where_ref[0] & 1
    grad_after = grad_after_ref[...]
    normed_mid, inverse_mid = normalize(middle_ref[...].astype(F32))
    second_t = dot(eye(512), normed_mid.astype(BF16), 1, 1).astype(BF16)

    def save(cols, at):
        return load(
            [(slots.at[core, :, :, cols], keep_hbm.at[:, :, cols]),
             (slots.at[1 - core, :, :, cols], send_hbm.at[:, :, cols])],
            out_sems.at[pl.ds(at, 2)],
        )

    back_up = jnp.zeros((TOKENS, 512), F32)
    grads_up = []
    for copy in loads:
        copy.wait()
    for part in range(4):
        cols = slice(part * 512, part * 512 + 512)
        grad_before = (
            dot(grad_after, w_down[cols], 1, 1) * slope_ref[:, cols].astype(F32)
        ).astype(BF16)
        grads_up.append(dot(second_t, grad_before))
        back_up = back_up + dot(grad_before, w_up[:, cols], 1, 1)
    weave(grads_up, slots, slice(0, 512))
    saves = save(pl.ds(0, 512), 0)
    middle_grad = (
        grad_after.astype(F32) + norm_back(normed_mid, inverse_mid, back_up)
    ).astype(BF16)
    middle_grad_ref[...] = middle_grad
    grad = dot(attended_ref[...], middle_grad)
    weave([grad[:, p * 128 : p * 128 + 128] for p in range(4)], slots, slice(512, 640))
    saves += save(pl.ds(512, 128), 2)
    for copy in saves:
        copy.wait()


def backward_kernel(
    where_ref, tokens_ref, packed_ref, keys_t_ref, attended_ref, middle_grad_ref,
    first_t_ref, order_ref, level_order_ref, level_two_ref, w_out,
    near0_hbm, near1_hbm, near2_hbm, near3_hbm, probs_hbm, w_qkv_hbm,
    out0, out1, out2, out3, keep_hbm, send_hbm,
    grad_heads, grad_heads_t, products, query_grad_t, packed_grad, probs_ref, w_qkv, near_ref,
    slots, near_sems, sems, out_sems,
):
    loads = load(
        [(probs_hbm.at[pl.ds(g * 4, 4)], probs_ref.at[pl.ds(g * 4, 4)]) for g in range(4)]
        + [(w_qkv_hbm, w_qkv)],
        sems,
    )
    nears = (near0_hbm, near1_hbm, near2_hbm, near3_hbm)
    nears = load([(nears[step], near_ref.at[step]) for step in range(4)], near_sems)
    core = where_ref[0] & 1
    middle_grad = middle_grad_ref[...]
    wide = dot(middle_grad, w_out[...], 1, 1).astype(BF16)
    for group in range(4):
        grad_heads[group] = wide[:, group * 128 : group * 128 + 128]
    grad_heads_t[...] = dot(w_out[...], middle_grad, 1, 1).astype(BF16)
    products[...] = grad_heads_t[...].astype(F32) * attended_ref[...].astype(F32)

    head_of_row = lax.broadcasted_iota(jnp.int32, (128, TOKENS), 0) >> 5
    head_of_lane = lax.broadcasted_iota(jnp.int32, (TOKENS, 128), 1) >> 5

    def attend_back(group):
        loads[group].wait()
        queries = packed_ref[group]
        values = packed_ref[8 + group]
        upstream = grad_heads[group]
        upstream_t = grad_heads_t[slice(group * 128, group * 128 + 128), :]
        grad_keys = jnp.zeros((TOKENS, 128), F32)
        grad_values = jnp.zeros((TOKENS, 128), F32)
        for head in range(4):
            at = slice(group * 128 + head * HEAD, group * 128 + head * HEAD + HEAD)
            masked_t = jnp.where(head_of_row == head, upstream_t, jnp.zeros_like(upstream_t))
            weights = probs_ref[group * 4 + head]
            total = jnp.sum(products[at, :], axis=0, keepdims=True)
            grad_weights = dot(values, masked_t)
            scores = (weights.astype(F32) * ((grad_weights - total) * (1 / LOG2E))).astype(BF16)
            in_head = head_of_lane == head
            grad_keys += dot(scores, jnp.where(in_head, queries, jnp.zeros_like(queries)))
            grad_values += dot(weights, jnp.where(in_head, upstream, jnp.zeros_like(upstream)))
            query_grad_t[at, :] = (dot(keys_t_ref[at, :], scores) * QUERY_SCALE).astype(BF16)
        packed_grad[4 + group] = grad_keys.astype(BF16)
        packed_grad[8 + group] = grad_values.astype(BF16)

    for group in range(4):
        attend_back(group)

    for copy in nears:
        copy.wait()
    near = jnp.concatenate([near_ref[step].astype(F32) for step in range(4)], axis=0).astype(BF16)
    grad = dot(near[:, :512], near[:, 512:], 0, 0)
    weave([grad[:, q * 256 : q * 256 + 256] for q in range(4)], slots, slice(384, 640))

    identity = eye(TOKENS)
    for group in range(4):
        packed_grad[group] = dot(
            identity, query_grad_t[group * 128 : group * 128 + 128, :], 1, 1
        ).astype(BF16)
    first_t = first_t_ref[...]
    loads[4].wait()
    back_qkv = jnp.zeros((TOKENS, 512), F32)
    grads = []
    for part in range(3):
        wide = jnp.concatenate([packed_grad[part * 4 + g] for g in range(4)], axis=1)
        grad = dot(first_t, wide)
        grads += [grad[:, q * 128 : q * 128 + 128] for q in range(4)]
        back_qkv = back_qkv + dot(wide, w_qkv[:, part * 512 : part * 512 + 512], 1, 1)
    for part in range(3):
        weave([grads[q * 3 + part] for q in range(4)], slots, slice(part * 128, part * 128 + 128))
    saves = load([(slots.at[core], keep_hbm), (slots.at[1 - core], send_hbm)], out_sems)

    normed_in, inverse_in = normalize(tokens_ref[...].astype(F32))
    grad_first = back_qkv.astype(BF16).astype(F32)
    grad_tokens = (
        middle_grad.astype(F32) + norm_back(normed_in, inverse_in, grad_first)
    ).astype(BF16)
    for quad, out in enumerate((out0, out1, out2, out3)):
        rows = dot(order_ref[quad], grad_tokens)
        for half in range(2):
            level_two = level_two_ref[:, half * 512 : half * 512 + 512]
            rows = rows + dot(level_order_ref[half * 4 + quad], level_two)
        out[...] = rows.astype(BF16)
    for copy in saves:
        copy.wait()


def pair_kernel(keep_hbm, arrived_hbm, *refs, place):
    blocks_hbm, keep_ref, arrived_ref, keep_sems, arrived_sems, out_sems = refs[-6:]
    cols = pl.ds(place, keep_hbm.shape[-1])
    parts = [pl.ds(p * 16, 16) for p in range(4)]
    keeps = load([(keep_hbm.at[p], keep_ref.at[p]) for p in parts], keep_sems)
    arrivals = load([(arrived_hbm.at[p], arrived_ref.at[p]) for p in parts], arrived_sems)
    saves = []
    for part, rows in enumerate(parts):
        keeps[part].wait()
        arrivals[part].wait()
        total = keep_ref[rows].astype(F32) + arrived_ref[rows].astype(F32)
        keep_ref[rows] = total.astype(BF16)
        saves += load(
            [(keep_ref.at[rows], blocks_hbm.at[rows, :, cols])], out_sems.at[pl.ds(part, 1)]
        )
    for save in saves:
        save.wait()


def arrive(landed_hbm, landed_ref, sems):
    parts = [pl.ds(p * 16, 16) for p in range(4)]
    loads = load([(landed_hbm.at[p], landed_ref.at[p]) for p in parts], sems)
    for chip in range(64):
        if chip % 16 == 0:
            loads[chip // 16].wait()
        yield chip, landed_ref[chip].astype(F32)


def down_kernel(landed_hbm, down_ref, landed_ref, sems):
    down_ref[...] = sum(block for _, block in arrive(landed_hbm, landed_ref, sems))


def share_kernel(landed_hbm, qkv_ref, out_ref, up_ref, merge_ref, landed_ref, sems):
    shared = jnp.zeros((16, 1024), F32)
    merge = [jnp.zeros((16, 256), F32) for _ in range(4)]
    for chip, block in arrive(landed_hbm, landed_ref, sems):
        y = chip // 2 % 4
        shared = shared + block[:, :1024]
        merge[y] = merge[y] + block[:, 1024:]
    for block in range(4):
        rows = shared[block * 4 : block * 4 + 4]
        up_ref[:, block * 512 : block * 512 + 512] = rows[:, :512]
        out_ref[:, block * 128 : block * 128 + 128] = rows[:, 512:640]
        qkv_ref[:, block * 384 : block * 384 + 384] = rows[:, 640:]
        for y in range(4):
            merge_ref[y * 4 : y * 4 + 4, block * 256 : block * 256 + 256] = merge[y][
                block * 4 : block * 4 + 4
            ]


def call(kernel, inputs, held, outputs, saved, scratch, micros, kind=BF16, free=(), aliases=(),
         weight=1):
    whole, there = pl.BlockSpec(memory_space=pltpu.VMEM), pl.BlockSpec(memory_space=pltpu.HBM)
    specs = [whole if at < held else there for at in range(len(inputs))]
    for at in free:
        specs[at] = pl.BlockSpec(memory_space=pl.ANY)
    if inputs[0].ndim == 1:
        specs[0] = pl.BlockSpec(memory_space=pltpu.SMEM)
    return pl.pallas_call(
        kernel,
        out_shape=[jax.ShapeDtypeStruct(shape, kind) for shape in outputs],
        in_specs=specs,
        out_specs=[whole if at < saved else there for at in range(len(outputs))],
        scratch_shapes=scratch,
        input_output_aliases=dict(aliases),
        compiler_params=pltpu.CompilerParams(vmem_limit_bytes=(56 if micros > 5 else 14) * 2**20),
        cost_estimate=pl.CostEstimate(
            flops=weight * micros * 10**9, bytes_accessed=micros * 10**6, transcendentals=0
        ),
    )(*inputs)


def vmem(*shape):
    return pltpu.VMEM(shape, BF16)


def dmas(count):
    return pltpu.SemaphoreType.DMA((count,))


def pair_sum(keep, send, width, place, blocks=None):
    arrived = lax.ppermute(send, "core", [(0, 1), (1, 0)])
    blocks, = call(
        functools.partial(pair_kernel, place=place),
        [keep, arrived] + ([] if blocks is None else [blocks]), 0, [(64, 16, width)], 0,
        [vmem(*keep.shape), vmem(*keep.shape), dmas(4), dmas(4), dmas(4)],
        2, free=(1,), aliases={} if blocks is None else {2: 0},
    )
    return blocks


def shifted_block(block, down, right):
    route = []
    for source in range(128):
        row, col = source // 16, source % 16
        route.append((source, (row + down) % 8 * 16 + (col + right) % 16))
    return lax.ppermute(block, GRID, route)


def quadrants(field):
    field = field.transpose(1, 2, 0, 3)
    rows, cols = field.shape[0] // 2, field.shape[1] // 2
    corners = field[:rows, :cols], field[:rows, cols:], field[rows:, :cols], field[rows:, cols:]
    return [corner.reshape(-1, field.shape[-1]) for corner in corners]


def roll_back(tokens, cotangent):
    corners = [
        jnp.concatenate([corner, cot[:, :512], cot[:, 512:]], axis=0)
        for corner, cot in zip(quadrants(tokens), quadrants(cotangent))
    ]
    upper_left, upper_right, lower_left, lower_right = corners
    return [
        lower_right,
        shifted_block(lower_left, 0, -1),
        shifted_block(upper_right, -1, 0),
        shifted_block(upper_left, -1, -1),
    ]


def send_forth(corners):
    upper_left, upper_right, lower_left, lower_right = corners
    return [
        shifted_block(lower_right, 1, 1),
        shifted_block(lower_left, 1, 0),
        shifted_block(upper_right, 0, 1),
        upper_left,
    ]


def from_corners(corners):
    upper = jnp.concatenate(corners[:2], axis=1)
    lower = jnp.concatenate(corners[2:], axis=1)
    return jnp.concatenate([upper, lower], axis=0).transpose(2, 0, 1, 3)


def body(tokens, window_ids, cotangent, w_qkv, w_out, w_up, w_down, w_merge):
    order, cot_order = token_order(), cotangent_order()
    level_order = np.concatenate([cot_order[:, :MERGED], cot_order[:, MERGED:]]).transpose(0, 2, 1)
    by_feature, field, hidden_shape = (512, TOKENS), (TOKENS, 512), (TOKENS, 2048)
    all_probs, near_shape, corner = (16, TOKENS, TOKENS), (MERGED, 1536), (PACKED, 512)
    places = window_places()
    where = lax.axis_index(("y", "core")).reshape(1)
    quads = roll_back(tokens, cotangent)

    (level_two, near0, near1, near2, near3, tokens_in, packed, keys_t, attended, first_t,
     middle, grad_after, probs, slope, down_keep, down_send) = call(
        forward_kernel,
        [where, jnp.asarray(order, BF16), jnp.asarray(cot_order, BF16), window_ids,
         jnp.asarray(places, BF16), jnp.asarray(places[1].T, F32), w_qkv, *quads,
         w_out, w_up, w_down, w_merge], 7,
        [(MERGED, 1024)] + [near_shape] * 4 + [field, (12, TOKENS, 128), by_feature, by_feature,
         by_feature, field, field, all_probs, hidden_shape, (64, 16, 512), (64, 16, 512)], 12,
        [vmem(4, *corner), pltpu.VMEM((TOKENS, TOKENS), F32), vmem(*by_feature), vmem(*by_feature),
         vmem(*hidden_shape), vmem(*hidden_shape), vmem(*all_probs), vmem(*w_out.shape),
         vmem(*w_up.shape), vmem(*w_down.shape), vmem(*w_merge.shape), vmem(2, 64, 16, 512),
         dmas(4), dmas(4), dmas(4)],
        20, free=range(7, 11),
    )
    near = [near0]
    for step, block in ((1, near1), (2, near2), (3, near3)):
        near.append(lax.ppermute(block, "y", [(i, (i + step) % 4) for i in range(4)]))
    middle_grad, keep, send = call(
        middle_kernel,
        [where, grad_after, middle, attended, w_down, slope, w_up], 4,
        [field, (64, 16, 640), (64, 16, 640)], 1,
        [vmem(*w_down.shape), vmem(*hidden_shape), vmem(*w_up.shape), vmem(2, 64, 16, 640),
         dmas(3), dmas(4)],
        7,
    )
    down_blocks = pair_sum(down_keep, down_send, 512, 0)
    middle_grad, down_blocks = lax.optimization_barrier((middle_grad, down_blocks))
    landed = lax.all_to_all(down_blocks, PAIRS, 0, 0, tiled=True)
    grad_down, = call(
        down_kernel, [landed], 0, [(16, 512)], 1, [vmem(64, 16, 512), dmas(4)], 1, kind=F32,
        weight=60,
    )
    *corners, late_keep, late_send = call(
        backward_kernel,
        [where, tokens_in, packed, keys_t, attended, middle_grad, first_t,
         jnp.asarray(order.transpose(0, 2, 1), BF16), jnp.asarray(level_order, BF16), level_two,
         w_out, *near, probs, w_qkv], 11,
        [corner] * 4 + [(64, 16, 640)] * 2, 4,
        [vmem(4, TOKENS, 128), vmem(*by_feature), pltpu.VMEM(by_feature, F32), vmem(*by_feature),
         vmem(12, TOKENS, 128), vmem(*all_probs), vmem(*w_qkv.shape), vmem(4, *near_shape),
         vmem(2, 64, 16, 640), dmas(4), dmas(5), dmas(2)],
        12, free=range(12, 15),
    )
    blocks = pair_sum(keep, send, 1280, 0)
    late_keep, grad_down = lax.optimization_barrier((late_keep, grad_down))
    blocks = pair_sum(late_keep, late_send, 1280, 640, blocks)
    corners = send_forth(corners)
    blocks, *corners = lax.optimization_barrier((blocks, *corners))
    landed = lax.all_to_all(blocks, PAIRS, 0, 0, tiled=True)
    grad_qkv, grad_out, grad_up, grad_merge = call(
        share_kernel, [landed], 0, [(4, 1536), (4, 512), (4, 2048), (16, 1024)], 4,
        [vmem(*blocks.shape), dmas(4)], 3, kind=F32,
    )
    grad_tokens = from_corners([c[:MERGED].reshape(6, 6, 2, 512) for c in corners])
    halves = [(c[MERGED : MERGED + 18], c[MERGED + 18 :]) for c in corners]
    level_two = from_corners(
        [jnp.concatenate(pair, axis=1).reshape(3, 3, 2, 1024) for pair in halves]
    )
    return (level_two, grad_tokens, grad_qkv, grad_out, grad_up, grad_down, grad_merge)


def solution(mesh):
    cube = jax.sharding.Mesh(mesh.devices.reshape(4, 2, 4, 2, 2), GRID)
    lat, lon = GRID[:2], GRID[2:]
    field = P(None, lat, lon, None)
    share = P(GRID, None)
    return jax.shard_map(
        body,
        mesh=cube,
        in_specs=(field, P(lat, lon), field, P(), P(), P(), P(), P()),
        out_specs=(field, field, share, share, share, share, share),
        check_vma=False,
    )
```

```python
import functools

import jax
import jax.numpy as jnp
import numpy as np
from jax import lax
from jax.experimental import pallas as pl
from jax.experimental.pallas import tpu as pltpu
from jax.sharding import PartitionSpec as P

HEAD = 32
WIN = 12
TOKENS = 2 * WIN * WIN
MERGED = TOKENS // 4
EPS = 1e-05
LOG2E = 1.4426950408889634
QUERY_SCALE = HEAD ** (-0.5) * LOG2E
GRID = ("z", "x_lo", "y", "x_hi", "core")
BF16 = jnp.bfloat16
F32 = jnp.float32

PAIRS = ("z", "x_lo", "y", "x_hi")


PACKED = MERGED + 36


def token_order():
    order = np.zeros((4, TOKENS, PACKED), np.float32)
    for quad in range(4):
        for row in range(6):
            for col in range(6):
                for level in range(2):
                    position = (col % 2) * 2 + row % 2
                    patch = quad * 18 + (row // 2 * 3 + col // 2) * 2 + level
                    order[quad, position * MERGED + patch, (row * 6 + col) * 2 + level] = 1.0
    return order


def window_places():
    places = np.zeros((2, TOKENS, WIN), np.float32)
    for row in range(WIN):
        for col in range(WIN):
            position = (col % 2) * 2 + row % 2
            quad = row // 6 * 2 + col // 6
            patch = quad * 18 + (row % 6 // 2 * 3 + col % 6 // 2) * 2
            for level in range(2):
                places[0, position * MERGED + patch + level, row] = 1.0
                places[1, position * MERGED + patch + level, col] = 1.0
    return places


def cotangent_order():
    order = np.zeros((4, 2 * MERGED, PACKED), np.float32)
    for quad in range(4):
        for half in range(2):
            for patch in range(18):
                order[quad, half * MERGED + quad * 18 + patch, MERGED + half * 18 + patch] = 1.0
    return order


def dot(left, right, left_dim=1, right_dim=0):
    return lax.dot_general(
        left, right, (((left_dim,), (right_dim,)), ((), ())), preferred_element_type=F32
    )


def normalize(wide):
    centered = wide - jnp.mean(wide, axis=-1, keepdims=True)
    inverse_std = lax.rsqrt(jnp.mean(centered * centered, axis=-1, keepdims=True) + EPS)
    return centered * inverse_std, inverse_std


def norm_back(normed, inverse_std, upstream):
    mean_grad = jnp.mean(upstream, axis=-1, keepdims=True)
    mean_cross = jnp.mean(upstream * normed, axis=-1, keepdims=True)
    return inverse_std * (upstream - mean_grad - normed * mean_cross)


def eye(size):
    rows = lax.broadcasted_iota(jnp.int32, (size, 1), 0)
    cols = lax.broadcasted_iota(jnp.int32, (1, size), 1)
    return jnp.where(rows == cols, 1.0, 0.0).astype(BF16)


def weave(grads, slots, cols):
    tiles = [grad.reshape(64, 8, grad.shape[-1]) for grad in grads]
    turned = [pltpu.roll(tile, 4, 1) for tile in tiles]
    upper = lax.broadcasted_iota(jnp.int32, tiles[0].shape, 1) < 4
    for half in range(2):
        one, two = half * 2, half * 2 + 1
        rows = slice(half * 8, half * 8 + 8)
        slots[0, :, rows, cols] = jnp.where(upper, tiles[one], turned[two]).astype(BF16)
        slots[1, :, rows, cols] = jnp.where(upper, turned[one], tiles[two]).astype(BF16)


def load(pairs, sems):
    copies = [pltpu.make_async_copy(*pair, sems.at[at]) for at, pair in enumerate(pairs)]
    for copy in copies:
        copy.start()
    return copies


def merge_norm(after_mlp):
    pieces = [after_mlp[p * MERGED : (p + 1) * MERGED] for p in range(4)]
    mean = sum(jnp.sum(v, axis=-1, keepdims=True) for v in pieces) / 2048.0
    pieces = [v - mean for v in pieces]
    inverse_out = lax.rsqrt(
        sum(jnp.sum(v * v, axis=-1, keepdims=True) for v in pieces) / 2048.0 + EPS
    )
    return [v * inverse_out for v in pieces], inverse_out


def near_order():
    source = lax.broadcasted_iota(jnp.int32, (512, 1), 0)
    target = lax.broadcasted_iota(jnp.int32, (1, 512), 1)
    place = ((source >> 2) & 3) * 128 + (source >> 4) * 4 + (source & 3)
    return jnp.where(target == place, 1.0, 0.0).astype(BF16)


def gelu_parts(values):
    density = jnp.exp2(values * values * (-0.5 * LOG2E))
    inverse = 1.0 / (1.0 + jnp.abs(values) * (0.3275911 * 0.7071067811865476))
    series = 0.5 * 1.061405429
    for term in (-1.453152027, 1.421413741, -0.284496736, 0.254829592):
        series = series * inverse + 0.5 * term
    tail = series * inverse * density
    return jnp.where(values < 0.0, tail, 1.0 - tail), density


def forward_kernel(
    where_ref, order_ref, cot_order_ref, ids_ref, places_ref, cols_t_ref, w_qkv,
    quad0_hbm, quad1_hbm, quad2_hbm, quad3_hbm, w_out_hbm, w_up_hbm, w_down_hbm, w_merge_hbm,
    level_two_ref, near0, near1, near2, near3, tokens_ref, packed_ref, keys_t_ref,
    attended_ref, first_t_ref, middle_ref, grad_after_ref, probs_hbm, slope_hbm, keep_hbm, send_hbm,
    quads_ref, bias_ref, query_t, values_t, slope_ref, hidden_ref, probs_ref, w_out, w_up, w_down,
    w_merge, slots, quad_sems, in_sems, out_sems,
):
    quads = (quad0_hbm, quad1_hbm, quad2_hbm, quad3_hbm)
    quads = load([(quads[q], quads_ref.at[q]) for q in range(4)], quad_sems)
    weights = load(
        [(w_out_hbm, w_out), (w_up_hbm, w_up), (w_down_hbm, w_down), (w_merge_hbm, w_merge)],
        in_sems,
    )
    ids = ids_ref[...].astype(F32).astype(BF16)
    by_row = dot(places_ref[0], ids) * places_ref[1].astype(F32)
    by_col = dot(ids, places_ref[0], 0, 1) * cols_t_ref[...]
    alike = jnp.sum(by_row, axis=1, keepdims=True) == jnp.sum(by_col, axis=0, keepdims=True)
    bias_ref[...] = jnp.where(alike, 0.0, -1e30)
    for quad in quads:
        quad.wait()
    tokens = sum(dot(order_ref[q], quads_ref[q]) for q in range(4))
    tokens_ref[...] = tokens.astype(BF16)
    halves = sum(dot(cot_order_ref[q], quads_ref[q]) for q in range(4))
    cotangent = jnp.concatenate([halves[:MERGED], halves[MERGED:]], axis=1).astype(BF16)
    first_norm = normalize(tokens)[0].astype(BF16)
    first_t_ref[...] = dot(eye(512), first_norm, 1, 1).astype(BF16)
    by_lane = eye(128)
    for part in range(3):
        wide = dot(first_norm, w_qkv[:, part * 512 : part * 512 + 512])
        wide = (wide * QUERY_SCALE if part == 0 else wide).astype(BF16)
        for group in range(4):
            grid = wide[:, group * 128 : group * 128 + 128]
            packed_ref[part * 4 + group] = grid
            turned = (query_t, keys_t_ref, values_t)[part]
            turned[group * 128 : group * 128 + 128, :] = dot(by_lane, grid, 1, 1).astype(BF16)

    head_of_row = lax.broadcasted_iota(jnp.int32, (128, TOKENS), 0) >> 5

    def scores_of(head):
        queries = query_t[head // 4 * 128 : head // 4 * 128 + 128, :]
        masked = jnp.where(head_of_row == head % 4, queries, jnp.zeros_like(queries))
        return dot(packed_ref[4 + head // 4], masked)

    ahead = scores_of(0)
    for head in range(16):
        scores = ahead + bias_ref[...]
        if head < 15:
            ahead = scores_of(head + 1)
        raised = jnp.exp2(scores - jnp.max(scores, axis=0, keepdims=True))
        inverse = 1.0 / jnp.sum(raised, axis=0, keepdims=True)
        probs = (raised * inverse).astype(BF16)
        probs_ref[head] = probs
        at = slice(head * HEAD, head * HEAD + HEAD)
        attended_ref[at, :] = dot(values_t[at, :], probs).astype(BF16)
    saves = load([(probs_ref, probs_hbm)], out_sems.at[pl.ds(0, 1)])

    attended = dot(eye(TOKENS), attended_ref[...], 1, 1).astype(BF16)
    weights[0].wait()
    attn_out = dot(attended, w_out[...]).astype(BF16)
    narrow_middle = (tokens + attn_out.astype(F32)).astype(BF16)
    middle_ref[...] = narrow_middle
    middle = narrow_middle.astype(F32)
    second_norm = normalize(middle)[0].astype(BF16)
    mlp = jnp.zeros((TOKENS, 512), F32)
    weights[1].wait()
    weights[2].wait()
    ahead = dot(second_norm, w_up[:, :512])
    for part in range(4):
        cols = slice(part * 512, part * 512 + 512)
        before = ahead
        if part < 3:
            ahead = dot(second_norm, w_up[:, part * 512 + 512 : part * 512 + 1024])
        cumulative, density = gelu_parts(before)
        hidden = (before * cumulative).astype(BF16)
        hidden_ref[:, cols] = hidden
        slope_ref[:, cols] = (cumulative + before * density * 0.3989422804014327).astype(BF16)
        mlp = mlp + dot(hidden, w_down[cols])
    saves += load([(slope_ref, slope_hbm)], out_sems.at[pl.ds(1, 1)])
    after_mlp = (middle + mlp).astype(BF16)
    pieces, inverse_out = merge_norm(after_mlp.astype(F32))
    merged_norm = [v.astype(BF16) for v in pieces]
    order = near_order()
    spread = [dot(v, order) for v in merged_norm]
    blocks = [
        jnp.concatenate([v[:, at * 128 : at * 128 + 128] for v in spread], axis=1).astype(BF16)
        for at in range(4)
    ]
    y = (where_ref[0] >> 1) & 3
    for step, near in enumerate((near0, near1, near2, near3)):
        block = blocks[step]
        for own in range(1, 4):
            block = jnp.where(y == own, blocks[(own + step) % 4], block)
        near[:, :512] = block
        near[:, 512:] = cotangent

    weights[3].wait()
    level_two_ref[...] = sum(
        dot(merged_norm[p], w_merge[p * 512 : p * 512 + 512]) for p in range(4)
    ).astype(BF16)
    upstream = [dot(cotangent, w_merge[p * 512 : p * 512 + 512], 1, 1) for p in range(4)]
    mean_grad = sum(jnp.sum(v, axis=-1, keepdims=True) for v in upstream) / 2048.0
    mean_cross = (
        sum(jnp.sum(v * u, axis=-1, keepdims=True) for v, u in zip(upstream, pieces)) / 2048.0
    )
    grad_after = jnp.concatenate(
        [inverse_out * (v - mean_grad - u * mean_cross) for v, u in zip(upstream, pieces)], axis=0
    ).astype(BF16)
    grad_after_ref[...] = grad_after
    core = where_ref[0] & 1
    for part in range(4):
        grad = dot(hidden_ref[:, part * 512 : part * 512 + 512], grad_after, 0, 0).astype(BF16)
        grad = grad.reshape(16, 2, 16, 512)
        for unit in range(4):
            for parity in range(2):
                slots[parity, unit, part * 16 : part * 16 + 16] = grad[
                    :, parity, :, unit * 128 : unit * 128 + 128
                ]
    saves += load(
        [(slots.at[core], keep_hbm), (slots.at[1 - core], send_hbm)], out_sems.at[pl.ds(2, 2)]
    )
    for save in saves:
        save.wait()


def middle_kernel(
    where_ref, grad_after_ref, middle_ref, attended_ref, w_down_hbm, slope_hbm, w_up_hbm,
    middle_grad_ref, keep_hbm, send_hbm,
    w_down, slope_ref, w_up, slots, sems, out_sems,
):
    loads = load([(w_down_hbm, w_down), (slope_hbm, slope_ref), (w_up_hbm, w_up)], sems)
    core = where_ref[0] & 1
    grad_after = grad_after_ref[...]
    normed_mid, inverse_mid = normalize(middle_ref[...].astype(F32))
    second_t = dot(eye(512), normed_mid.astype(BF16), 1, 1).astype(BF16)

    def save(units, at):
        return load(
            [(slots.at[core, units], keep_hbm.at[units]),
             (slots.at[1 - core, units], send_hbm.at[units])],
            out_sems.at[pl.ds(at, 2)],
        )

    back_up = jnp.zeros((TOKENS, 512), F32)
    grads_up = []
    for copy in loads:
        copy.wait()
    for part in range(4):
        cols = slice(part * 512, part * 512 + 512)
        grad_before = (
            dot(grad_after, w_down[cols], 1, 1) * slope_ref[:, cols].astype(F32)
        ).astype(BF16)
        grads_up.append(dot(second_t, grad_before))
        back_up = back_up + dot(grad_before, w_up[:, cols], 1, 1)
    for unit in range(4):
        cols = slice(unit * 128, unit * 128 + 128)
        weave([grad[:, cols] for grad in grads_up], slots.at[:, unit], slice(0, 128))
    saves = save(pl.ds(0, 4), 0)
    middle_grad = (
        grad_after.astype(F32) + norm_back(normed_mid, inverse_mid, back_up)
    ).astype(BF16)
    middle_grad_ref[...] = middle_grad
    grad = dot(attended_ref[...], middle_grad)
    columns = [grad[:, p * 128 : p * 128 + 128] for p in range(4)]
    weave(columns, slots.at[:, 4], slice(0, 128))
    saves += save(pl.ds(4, 1), 2)
    for copy in saves:
        copy.wait()


def backward_kernel(
    where_ref, tokens_ref, packed_ref, keys_t_ref, attended_ref, middle_grad_ref,
    first_t_ref, order_ref, level_order_ref, level_two_ref, w_out,
    near0_hbm, near1_hbm, near2_hbm, near3_hbm, probs_hbm, w_qkv_hbm,
    out0, out1, out2, out3, keep_hbm, send_hbm,
    grad_heads, grad_heads_t, products, query_grad_t, packed_grad, probs_ref, w_qkv, near_ref,
    slots, near_sems, sems, out_sems,
):
    loads = load(
        [(probs_hbm.at[pl.ds(g * 4, 4)], probs_ref.at[pl.ds(g * 4, 4)]) for g in range(4)]
        + [(w_qkv_hbm, w_qkv)],
        sems,
    )
    nears = (near0_hbm, near1_hbm, near2_hbm, near3_hbm)
    nears = load([(nears[step], near_ref.at[step]) for step in range(4)], near_sems)
    core = where_ref[0] & 1
    middle_grad = middle_grad_ref[...]
    wide = dot(middle_grad, w_out[...], 1, 1).astype(BF16)
    for group in range(4):
        grad_heads[group] = wide[:, group * 128 : group * 128 + 128]
    grad_heads_t[...] = dot(w_out[...], middle_grad, 1, 1).astype(BF16)
    products[...] = grad_heads_t[...].astype(F32) * attended_ref[...].astype(F32)

    head_of_row = lax.broadcasted_iota(jnp.int32, (128, TOKENS), 0) >> 5
    head_of_lane = lax.broadcasted_iota(jnp.int32, (TOKENS, 128), 1) >> 5

    def attend_back(group):
        loads[group].wait()
        queries = packed_ref[group]
        values = packed_ref[8 + group]
        upstream = grad_heads[group]
        upstream_t = grad_heads_t[slice(group * 128, group * 128 + 128), :]
        grad_keys = jnp.zeros((TOKENS, 128), F32)
        grad_values = jnp.zeros((TOKENS, 128), F32)
        for head in range(4):
            at = slice(group * 128 + head * HEAD, group * 128 + head * HEAD + HEAD)
            masked_t = jnp.where(head_of_row == head, upstream_t, jnp.zeros_like(upstream_t))
            weights = probs_ref[group * 4 + head]
            total = jnp.sum(products[at, :], axis=0, keepdims=True)
            grad_weights = dot(values, masked_t)
            scores = (weights.astype(F32) * ((grad_weights - total) * (1 / LOG2E))).astype(BF16)
            in_head = head_of_lane == head
            grad_keys += dot(scores, jnp.where(in_head, queries, jnp.zeros_like(queries)))
            grad_values += dot(weights, jnp.where(in_head, upstream, jnp.zeros_like(upstream)))
            query_grad_t[at, :] = (dot(keys_t_ref[at, :], scores) * QUERY_SCALE).astype(BF16)
        packed_grad[4 + group] = grad_keys.astype(BF16)
        packed_grad[8 + group] = grad_values.astype(BF16)

    for group in range(4):
        attend_back(group)

    for copy in nears:
        copy.wait()
    near = jnp.concatenate([near_ref[step].astype(F32) for step in range(4)], axis=0).astype(BF16)
    grad = dot(near[:, :512], near[:, 512:], 0, 0)
    weave([grad[:, q * 256 : q * 256 + 256] for q in range(4)], slots, slice(384, 640))

    identity = eye(TOKENS)
    for group in range(4):
        packed_grad[group] = dot(
            identity, query_grad_t[group * 128 : group * 128 + 128, :], 1, 1
        ).astype(BF16)
    first_t = first_t_ref[...]
    loads[4].wait()
    back_qkv = jnp.zeros((TOKENS, 512), F32)
    grads = []
    for part in range(3):
        wide = jnp.concatenate([packed_grad[part * 4 + g] for g in range(4)], axis=1)
        grad = dot(first_t, wide)
        grads += [grad[:, q * 128 : q * 128 + 128] for q in range(4)]
        back_qkv = back_qkv + dot(wide, w_qkv[:, part * 512 : part * 512 + 512], 1, 1)
    for part in range(3):
        weave([grads[q * 3 + part] for q in range(4)], slots, slice(part * 128, part * 128 + 128))
    saves = load([(slots.at[core], keep_hbm), (slots.at[1 - core], send_hbm)], out_sems)

    normed_in, inverse_in = normalize(tokens_ref[...].astype(F32))
    grad_first = back_qkv.astype(BF16).astype(F32)
    grad_tokens = (
        middle_grad.astype(F32) + norm_back(normed_in, inverse_in, grad_first)
    ).astype(BF16)
    for quad, out in enumerate((out0, out1, out2, out3)):
        rows = dot(order_ref[quad], grad_tokens)
        for half in range(2):
            level_two = level_two_ref[:, half * 512 : half * 512 + 512]
            rows = rows + dot(level_order_ref[half * 4 + quad], level_two)
        out[...] = rows.astype(BF16)
    for copy in saves:
        copy.wait()


def pair_kernel(keep_hbm, arrived_hbm, *refs, place):
    blocks_hbm, keep_ref, arrived_ref, keep_sems, arrived_sems, out_sems = refs[-6:]
    cols = pl.ds(place, keep_hbm.shape[-1])
    parts = [pl.ds(p * 16, 16) for p in range(4)]
    keeps = load([(keep_hbm.at[p], keep_ref.at[p]) for p in parts], keep_sems)
    arrivals = load([(arrived_hbm.at[p], arrived_ref.at[p]) for p in parts], arrived_sems)
    saves = []
    for part, rows in enumerate(parts):
        keeps[part].wait()
        arrivals[part].wait()
        total = keep_ref[rows].astype(F32) + arrived_ref[rows].astype(F32)
        keep_ref[rows] = total.astype(BF16)
        saves += load(
            [(keep_ref.at[rows], blocks_hbm.at[rows, :, cols])], out_sems.at[pl.ds(part, 1)]
        )
    for save in saves:
        save.wait()


def ring_kernel(where_ref, keep_hbm, arrived_hbm, *refs, shift):
    *outs, keep_ref, arrived_ref, keep_sems, arrived_sems = refs
    me = (where_ref[0] >> shift) & 3
    units = [(me + step) & 3 for step in range(4)] + list(range(4, len(outs)))
    keeps = [(keep_hbm.at[unit], keep_ref.at[at]) for at, unit in enumerate(units)]
    arrivals = [(arrived_hbm.at[unit], arrived_ref.at[at]) for at, unit in enumerate(units)]
    copies = list(zip(load(keeps, keep_sems), load(arrivals, arrived_sems)))
    for at, out in enumerate(outs):
        for copy in copies[at]:
            copy.wait()
        out[...] = (keep_ref[at].astype(F32) + arrived_ref[at].astype(F32)).astype(BF16)


def assemble_kernel(*refs):
    blocks_hbm, parts_ref, total_ref, sems, out_sem = refs[9:]
    copies = load([(refs[at], parts_ref.at[at]) for at in range(9)], sems)
    for unit, first in enumerate((0, 4)):
        for copy in copies[first : first + 4]:
            copy.wait()
        total = sum(parts_ref[first + step].astype(F32) for step in range(4))
        total_ref[:, :, unit * 128 : unit * 128 + 128] = total.astype(BF16)
    copies[8].wait()
    total_ref[:, :, 256:] = parts_ref[8]
    save, = load([(total_ref, blocks_hbm.at[:, :, pl.ds(0, 384)])], out_sem)
    save.wait()


def share_kernel(landed_hbm, qkv_ref, out_ref, up_ref, down_ref, merge_ref, landed_ref, sems):
    parts = [pl.ds(p * 16, 16) for p in range(4)]
    loads = load([(landed_hbm.at[p], landed_ref.at[p]) for p in parts], sems)
    down, up, merge = ([0.0] * 4 for _ in range(3))
    shared = 0.0
    for chip in range(64):
        z, y = chip // 16, chip // 2 % 4
        if chip % 16 == 0:
            loads[z].wait()
        block = landed_ref[chip].astype(F32)
        down[z] = down[z] + block[:, :128]
        up[y] = up[y] + block[:, 128:256]
        shared = shared + block[:, 256:768]
        merge[y] = merge[y] + block[:, 768:]
    for block in range(4):
        down_ref[:, block * 128 : block * 128 + 128] = down[block]
        rows = slice(block * 4, block * 4 + 4)
        out_ref[:, block * 128 : block * 128 + 128] = shared[rows, :128]
        qkv_ref[:, block * 384 : block * 384 + 384] = shared[rows, 128:]
        for y in range(4):
            at = block * 512 + y * 128
            up_ref[:, at : at + 128] = up[y][rows]
            merge_ref[y * 4 : y * 4 + 4, block * 256 : block * 256 + 256] = merge[y][rows]


def call(kernel, inputs, held, outputs, saved, scratch, micros, kind=BF16, free=(), aliases=(),
         weight=1):
    whole, there = pl.BlockSpec(memory_space=pltpu.VMEM), pl.BlockSpec(memory_space=pltpu.HBM)
    specs = [whole if at < held else there for at in range(len(inputs))]
    for at in free:
        specs[at] = pl.BlockSpec(memory_space=pl.ANY)
    if inputs[0].ndim == 1:
        specs[0] = pl.BlockSpec(memory_space=pltpu.SMEM)
    return pl.pallas_call(
        kernel,
        out_shape=[jax.ShapeDtypeStruct(shape, kind) for shape in outputs],
        in_specs=specs,
        out_specs=[whole if at < saved else there for at in range(len(outputs))],
        scratch_shapes=scratch,
        input_output_aliases=dict(aliases),
        compiler_params=pltpu.CompilerParams(vmem_limit_bytes=(56 if micros > 5 else 14) * 2**20),
        cost_estimate=pl.CostEstimate(
            flops=weight * micros * 10**9, bytes_accessed=micros * 10**6, transcendentals=0
        ),
    )(*inputs)


def vmem(*shape):
    return pltpu.VMEM(shape, BF16)


def dmas(count):
    return pltpu.SemaphoreType.DMA((count,))


def exchanged(send):
    return lax.ppermute(send, "core", [(0, 1), (1, 0)])


def ring_parts(where, keep, send, axis, shift):
    count = keep.shape[0]
    outs = call(
        functools.partial(ring_kernel, shift=shift),
        [where, keep, exchanged(send)], 1, [(64, 16, 128)] * count, count,
        [vmem(*keep.shape), vmem(*keep.shape), dmas(count), dmas(count)], 2, free=(2,),
    )
    moved = [
        lax.ppermute(outs[step], axis, [(i, (i + step) % 4) for i in range(4)])
        for step in (1, 2, 3)
    ]
    return outs, [outs[0], *moved, *outs[4:]]


def shifted_block(block, down, right):
    route = []
    for source in range(128):
        row, col = source // 16, source % 16
        route.append((source, (row + down) % 8 * 16 + (col + right) % 16))
    return lax.ppermute(block, GRID, route)


def quadrants(field):
    field = field.transpose(1, 2, 0, 3)
    rows, cols = field.shape[0] // 2, field.shape[1] // 2
    corners = field[:rows, :cols], field[:rows, cols:], field[rows:, :cols], field[rows:, cols:]
    return [corner.reshape(-1, field.shape[-1]) for corner in corners]


def roll_back(tokens, cotangent):
    corners = [
        jnp.concatenate([corner, cot[:, :512], cot[:, 512:]], axis=0)
        for corner, cot in zip(quadrants(tokens), quadrants(cotangent))
    ]
    upper_left, upper_right, lower_left, lower_right = corners
    return [
        lower_right,
        shifted_block(lower_left, 0, -1),
        shifted_block(upper_right, -1, 0),
        shifted_block(upper_left, -1, -1),
    ]


def send_forth(corners):
    upper_left, upper_right, lower_left, lower_right = corners
    return [
        shifted_block(lower_right, 1, 1),
        shifted_block(lower_left, 1, 0),
        shifted_block(upper_right, 0, 1),
        upper_left,
    ]


def from_corners(corners):
    upper = jnp.concatenate(corners[:2], axis=1)
    lower = jnp.concatenate(corners[2:], axis=1)
    return jnp.concatenate([upper, lower], axis=0).transpose(2, 0, 1, 3)


def body(tokens, window_ids, cotangent, w_qkv, w_out, w_up, w_down, w_merge):
    order, cot_order = token_order(), cotangent_order()
    level_order = np.concatenate([cot_order[:, :MERGED], cot_order[:, MERGED:]]).transpose(0, 2, 1)
    by_feature, field, hidden_shape = (512, TOKENS), (TOKENS, 512), (TOKENS, 2048)
    all_probs, near_shape, corner = (16, TOKENS, TOKENS), (MERGED, 1536), (PACKED, 512)
    places = window_places()
    where = lax.axis_index(("z", "y", "core")).reshape(1)
    quads = roll_back(tokens, cotangent)

    (level_two, near0, near1, near2, near3, tokens_in, packed, keys_t, attended, first_t,
     middle, grad_after, probs, slope, down_keep, down_send) = call(
        forward_kernel,
        [where, jnp.asarray(order, BF16), jnp.asarray(cot_order, BF16), window_ids,
         jnp.asarray(places, BF16), jnp.asarray(places[1].T, F32), w_qkv, *quads,
         w_out, w_up, w_down, w_merge], 7,
        [(MERGED, 1024)] + [near_shape] * 4 + [field, (12, TOKENS, 128), by_feature, by_feature,
         by_feature, field, field, all_probs, hidden_shape, (4, 64, 16, 128), (4, 64, 16, 128)],
        12,
        [vmem(4, *corner), pltpu.VMEM((TOKENS, TOKENS), F32), vmem(*by_feature), vmem(*by_feature),
         vmem(*hidden_shape), vmem(*hidden_shape), vmem(*all_probs), vmem(*w_out.shape),
         vmem(*w_up.shape), vmem(*w_down.shape), vmem(*w_merge.shape), vmem(2, 4, 64, 16, 128),
         dmas(4), dmas(4), dmas(4)],
        20, free=range(7, 11),
    )
    near = [near0]
    for step, block in ((1, near1), (2, near2), (3, near3)):
        near.append(lax.ppermute(block, "y", [(i, (i + step) % 4) for i in range(4)]))
    middle_grad, keep, send = call(
        middle_kernel,
        [where, grad_after, middle, attended, w_down, slope, w_up], 4,
        [field, (5, 64, 16, 128), (5, 64, 16, 128)], 1,
        [vmem(*w_down.shape), vmem(*hidden_shape), vmem(*w_up.shape), vmem(2, 5, 64, 16, 128),
         dmas(3), dmas(4)],
        7,
    )
    down_sums, down_parts = ring_parts(where, down_keep, down_send, "z", 3)
    up_sums, up_parts = ring_parts(where, keep, send, "y", 1)
    middle_grad, *_ = lax.optimization_barrier((middle_grad, down_sums[0], up_sums[0]))
    *corners, late_keep, late_send = call(
        backward_kernel,
        [where, tokens_in, packed, keys_t, attended, middle_grad, first_t,
         jnp.asarray(order.transpose(0, 2, 1), BF16), jnp.asarray(level_order, BF16), level_two,
         w_out, *near, probs, w_qkv], 11,
        [corner] * 4 + [(64, 16, 640)] * 2, 4,
        [vmem(4, TOKENS, 128), vmem(*by_feature), pltpu.VMEM(by_feature, F32), vmem(*by_feature),
         vmem(12, TOKENS, 128), vmem(*all_probs), vmem(*w_qkv.shape), vmem(4, *near_shape),
         vmem(2, 64, 16, 640), dmas(4), dmas(5), dmas(2)],
        12, free=range(12, 15),
    )
    blocks, = call(
        assemble_kernel, [*down_parts, *up_parts], 0, [(64, 16, 1024)], 0,
        [vmem(9, 64, 16, 128), vmem(64, 16, 384), dmas(9), dmas(1)], 2, free=range(9), weight=60,
    )
    blocks, = call(
        functools.partial(pair_kernel, place=384),
        [late_keep, exchanged(late_send), blocks], 0, [blocks.shape], 0,
        [vmem(64, 16, 640), vmem(64, 16, 640), dmas(4), dmas(4), dmas(4)], 2, free=(1,),
        aliases={2: 0},
    )
    corners = send_forth(corners)
    blocks, *corners = lax.optimization_barrier((blocks, *corners))
    landed = lax.all_to_all(blocks, PAIRS, 0, 0, tiled=True)
    grad_qkv, grad_out, grad_up, grad_down, grad_merge = call(
        share_kernel, [landed], 0, [(4, 1536), (4, 512), (4, 2048), (16, 512), (16, 1024)], 5,
        [vmem(*blocks.shape), dmas(4)], 3, kind=F32,
    )
    grad_tokens = from_corners([c[:MERGED].reshape(6, 6, 2, 512) for c in corners])
    halves = [(c[MERGED : MERGED + 18], c[MERGED + 18 :]) for c in corners]
    level_two = from_corners(
        [jnp.concatenate(pair, axis=1).reshape(3, 3, 2, 1024) for pair in halves]
    )
    return (level_two, grad_tokens, grad_qkv, grad_out, grad_up, grad_down, grad_merge)


def solution(mesh):
    cube = jax.sharding.Mesh(mesh.devices.reshape(4, 2, 4, 2, 2), GRID)
    lat, lon = GRID[:2], GRID[2:]
    field = P(None, lat, lon, None)
    share = P(GRID, None)
    return jax.shard_map(
        body,
        mesh=cube,
        in_specs=(field, P(lat, lon), field, P(), P(), P(), P(), P()),
        out_specs=(field, field, share, share, share, share, share),
        check_vma=False,
    )
```

```python
import functools

import jax
import jax.numpy as jnp
import numpy as np
from jax import lax
from jax.experimental import pallas as pl
from jax.experimental.pallas import tpu as pltpu
from jax.sharding import PartitionSpec as P

HEAD = 32
WIN = 12
TOKENS = 2 * WIN * WIN
MERGED = TOKENS // 4
EPS = 1e-05
LOG2E = 1.4426950408889634
QUERY_SCALE = HEAD ** (-0.5) * LOG2E
GRID = ("z", "x_lo", "y", "x_hi", "core")
BF16 = jnp.bfloat16
F32 = jnp.float32

PAIRS = ("z", "x_lo", "y", "x_hi")


PACKED = MERGED + 36


def token_order():
    order = np.zeros((4, TOKENS, PACKED), np.float32)
    for quad in range(4):
        for row in range(6):
            for col in range(6):
                for level in range(2):
                    position = (col % 2) * 2 + row % 2
                    patch = quad * 18 + (row // 2 * 3 + col // 2) * 2 + level
                    order[quad, position * MERGED + patch, (row * 6 + col) * 2 + level] = 1.0
    return order


def window_places():
    places = np.zeros((2, TOKENS, WIN), np.float32)
    for row in range(WIN):
        for col in range(WIN):
            position = (col % 2) * 2 + row % 2
            quad = row // 6 * 2 + col // 6
            patch = quad * 18 + (row % 6 // 2 * 3 + col % 6 // 2) * 2
            for level in range(2):
                places[0, position * MERGED + patch + level, row] = 1.0
                places[1, position * MERGED + patch + level, col] = 1.0
    return places


def cotangent_order():
    order = np.zeros((4, 2 * MERGED, PACKED), np.float32)
    for quad in range(4):
        for half in range(2):
            for patch in range(18):
                order[quad, half * MERGED + quad * 18 + patch, MERGED + half * 18 + patch] = 1.0
    return order


def dot(left, right, left_dim=1, right_dim=0):
    return lax.dot_general(
        left, right, (((left_dim,), (right_dim,)), ((), ())), preferred_element_type=F32
    )


def normalize(wide):
    centered = wide - jnp.mean(wide, axis=-1, keepdims=True)
    inverse_std = lax.rsqrt(jnp.mean(centered * centered, axis=-1, keepdims=True) + EPS)
    return centered * inverse_std, inverse_std


def norm_back(normed, inverse_std, upstream):
    mean_grad = jnp.mean(upstream, axis=-1, keepdims=True)
    mean_cross = jnp.mean(upstream * normed, axis=-1, keepdims=True)
    return inverse_std * (upstream - mean_grad - normed * mean_cross)


def eye(size):
    rows = lax.broadcasted_iota(jnp.int32, (size, 1), 0)
    cols = lax.broadcasted_iota(jnp.int32, (1, size), 1)
    return jnp.where(rows == cols, 1.0, 0.0).astype(BF16)


def weave(grads, slots, cols):
    tiles = [grad.reshape(64, 8, grad.shape[-1]) for grad in grads]
    turned = [pltpu.roll(tile, 4, 1) for tile in tiles]
    upper = lax.broadcasted_iota(jnp.int32, tiles[0].shape, 1) < 4
    for half in range(2):
        one, two = half * 2, half * 2 + 1
        rows = slice(half * 8, half * 8 + 8)
        slots[0, :, rows, cols] = jnp.where(upper, tiles[one], turned[two]).astype(BF16)
        slots[1, :, rows, cols] = jnp.where(upper, turned[one], tiles[two]).astype(BF16)


def load(pairs, sems):
    copies = [pltpu.make_async_copy(*pair, sems.at[at]) for at, pair in enumerate(pairs)]
    for copy in copies:
        copy.start()
    return copies


def merge_norm(after_mlp):
    pieces = [after_mlp[p * MERGED : (p + 1) * MERGED] for p in range(4)]
    mean = sum(jnp.sum(v, axis=-1, keepdims=True) for v in pieces) / 2048.0
    pieces = [v - mean for v in pieces]
    inverse_out = lax.rsqrt(
        sum(jnp.sum(v * v, axis=-1, keepdims=True) for v in pieces) / 2048.0 + EPS
    )
    return [v * inverse_out for v in pieces], inverse_out


def near_order():
    source = lax.broadcasted_iota(jnp.int32, (512, 1), 0)
    target = lax.broadcasted_iota(jnp.int32, (1, 512), 1)
    place = ((source >> 2) & 3) * 128 + (source >> 4) * 4 + (source & 3)
    return jnp.where(target == place, 1.0, 0.0).astype(BF16)


def gelu_parts(values):
    density = jnp.exp2(values * values * (-0.5 * LOG2E))
    inverse = 1.0 / (1.0 + jnp.abs(values) * (0.3275911 * 0.7071067811865476))
    series = 0.5 * 1.061405429
    for term in (-1.453152027, 1.421413741, -0.284496736, 0.254829592):
        series = series * inverse + 0.5 * term
    tail = series * inverse * density
    return jnp.where(values < 0.0, tail, 1.0 - tail), density


def forward_kernel(
    where_ref, order_ref, cot_order_ref, ids_ref, places_ref, cols_t_ref,
    quad0_hbm, quad1_hbm, quad2_hbm, quad3_hbm, w_qkv_hbm, w_out_hbm, w_up_hbm, w_down_hbm, w_merge_hbm,
    level_two_ref, near0, near1, near2, near3, tokens_ref, packed_ref, keys_t_ref,
    attended_ref, first_t_ref, middle_ref, grad_after_ref, probs_hbm, slope_hbm, keep_hbm, send_hbm,
    quads_ref, bias_ref, query_t, values_t, slope_ref, hidden_ref, probs_ref, w_qkv, w_out, w_up, w_down,
    w_merge, slots, quad_sems, in_sems, out_sems,
):
    quads = (quad0_hbm, quad1_hbm, quad2_hbm, quad3_hbm)
    quads = load([(quads[q], quads_ref.at[q]) for q in range(4)], quad_sems)
    weights = load(
        [(w_qkv_hbm, w_qkv), (w_out_hbm, w_out), (w_up_hbm, w_up), (w_down_hbm, w_down),
         (w_merge_hbm, w_merge)],
        in_sems,
    )
    query_t[...] = jnp.zeros_like(query_t)
    ids = ids_ref[...].astype(F32).astype(BF16)
    by_row = dot(places_ref[0], ids) * places_ref[1].astype(F32)
    by_col = dot(ids, places_ref[0], 0, 1) * cols_t_ref[...]
    alike = jnp.sum(by_row, axis=1, keepdims=True) == jnp.sum(by_col, axis=0, keepdims=True)
    bias_ref[...] = jnp.where(alike, 0.0, -1e30)
    for quad in quads:
        quad.wait()
    tokens = sum(dot(order_ref[q], quads_ref[q]) for q in range(4))
    tokens_ref[...] = tokens.astype(BF16)
    halves = sum(dot(cot_order_ref[q], quads_ref[q]) for q in range(4))
    cotangent = jnp.concatenate([halves[:MERGED], halves[MERGED:]], axis=1).astype(BF16)
    first_norm = normalize(tokens)[0].astype(BF16)
    first_t_ref[...] = dot(eye(512), first_norm, 1, 1).astype(BF16)
    by_lane = eye(128)
    weights[0].wait()
    for part in range(3):
        wide = dot(first_norm, w_qkv[:, part * 512 : part * 512 + 512])
        wide = (wide * QUERY_SCALE if part == 0 else wide).astype(BF16)
        for group in range(4):
            grid = wide[:, group * 128 : group * 128 + 128]
            packed_ref[part * 4 + group] = grid
            turned = dot(by_lane, grid, 1, 1).astype(BF16)
            if part:
                (keys_t_ref, values_t)[part - 1][group * 128 : group * 128 + 128, :] = turned
                continue
            for head in range(4):
                rows = slice(head * HEAD, head * HEAD + HEAD)
                query_t[group * 4 + head, rows, :] = turned[rows]

    def scores_of(head):
        return dot(packed_ref[4 + head // 4], query_t[head])

    ahead = scores_of(0)
    for head in range(16):
        scores = ahead + bias_ref[...]
        if head < 15:
            ahead = scores_of(head + 1)
        raised = jnp.exp2(scores - jnp.max(scores, axis=0, keepdims=True))
        inverse = 1.0 / jnp.sum(raised, axis=0, keepdims=True)
        probs = (raised * inverse).astype(BF16)
        probs_ref[head] = probs
        at = slice(head * HEAD, head * HEAD + HEAD)
        attended_ref[at, :] = dot(values_t[at, :], probs).astype(BF16)
    saves = load([(probs_ref, probs_hbm)], out_sems.at[pl.ds(0, 1)])

    attended = dot(eye(TOKENS), attended_ref[...], 1, 1).astype(BF16)
    weights[1].wait()
    attn_out = dot(attended, w_out[...]).astype(BF16)
    narrow_middle = (tokens + attn_out.astype(F32)).astype(BF16)
    middle_ref[...] = narrow_middle
    middle = narrow_middle.astype(F32)
    second_norm = normalize(middle)[0].astype(BF16)
    mlp = jnp.zeros((TOKENS, 512), F32)
    weights[2].wait()
    weights[3].wait()
    ahead = dot(second_norm, w_up[:, :512])
    for part in range(4):
        cols = slice(part * 512, part * 512 + 512)
        before = ahead
        if part < 3:
            ahead = dot(second_norm, w_up[:, part * 512 + 512 : part * 512 + 1024])
        cumulative, density = gelu_parts(before)
        hidden = (before * cumulative).astype(BF16)
        hidden_ref[:, cols] = hidden
        slope_ref[:, cols] = (cumulative + before * density * 0.3989422804014327).astype(BF16)
        mlp = mlp + dot(hidden, w_down[cols])
    saves += load([(slope_ref, slope_hbm)], out_sems.at[pl.ds(1, 1)])
    after_mlp = (middle + mlp).astype(BF16)
    pieces, inverse_out = merge_norm(after_mlp.astype(F32))
    merged_norm = [v.astype(BF16) for v in pieces]
    order = near_order()
    spread = [dot(v, order) for v in merged_norm]
    blocks = [
        jnp.concatenate([v[:, at * 128 : at * 128 + 128] for v in spread], axis=1).astype(BF16)
        for at in range(4)
    ]
    y = (where_ref[0] >> 1) & 3
    for step, near in enumerate((near0, near1, near2, near3)):
        block = blocks[step]
        for own in range(1, 4):
            block = jnp.where(y == own, blocks[(own + step) % 4], block)
        near[:, :512] = block
        near[:, 512:] = cotangent

    weights[4].wait()
    level_two_ref[...] = sum(
        dot(merged_norm[p], w_merge[p * 512 : p * 512 + 512]) for p in range(4)
    ).astype(BF16)
    upstream = [dot(cotangent, w_merge[p * 512 : p * 512 + 512], 1, 1) for p in range(4)]
    mean_grad = sum(jnp.sum(v, axis=-1, keepdims=True) for v in upstream) / 2048.0
    mean_cross = (
        sum(jnp.sum(v * u, axis=-1, keepdims=True) for v, u in zip(upstream, pieces)) / 2048.0
    )
    grad_after = jnp.concatenate(
        [inverse_out * (v - mean_grad - u * mean_cross) for v, u in zip(upstream, pieces)], axis=0
    ).astype(BF16)
    grad_after_ref[...] = grad_after
    core = where_ref[0] & 1
    for part in range(4):
        grad = dot(hidden_ref[:, part * 512 : part * 512 + 512], grad_after, 0, 0).astype(BF16)
        grad = grad.reshape(16, 2, 16, 512)
        for unit in range(4):
            for parity in range(2):
                slots[parity, unit, part * 16 : part * 16 + 16] = grad[
                    :, parity, :, unit * 128 : unit * 128 + 128
                ]
    saves += load(
        [(slots.at[core], keep_hbm), (slots.at[1 - core], send_hbm)], out_sems.at[pl.ds(2, 2)]
    )
    for save in saves:
        save.wait()


def middle_kernel(
    where_ref, grad_after_ref, middle_ref, attended_ref, w_down_hbm, slope_hbm, w_up_hbm,
    middle_grad_ref, keep_hbm, send_hbm,
    w_down, slope_ref, w_up, slots, sems, out_sems,
):
    loads = load([(w_down_hbm, w_down), (slope_hbm, slope_ref), (w_up_hbm, w_up)], sems)
    core = where_ref[0] & 1
    grad_after = grad_after_ref[...]
    normed_mid, inverse_mid = normalize(middle_ref[...].astype(F32))
    second_t = dot(eye(512), normed_mid.astype(BF16), 1, 1).astype(BF16)

    def save(units, at):
        return load(
            [(slots.at[core, units], keep_hbm.at[units]),
             (slots.at[1 - core, units], send_hbm.at[units])],
            out_sems.at[pl.ds(at, 2)],
        )

    back_up = jnp.zeros((TOKENS, 512), F32)
    grads_up = []
    for copy in loads:
        copy.wait()
    for part in range(4):
        cols = slice(part * 512, part * 512 + 512)
        grad_before = (
            dot(grad_after, w_down[cols], 1, 1) * slope_ref[:, cols].astype(F32)
        ).astype(BF16)
        grads_up.append(dot(second_t, grad_before))
        back_up = back_up + dot(grad_before, w_up[:, cols], 1, 1)
    for unit in range(4):
        cols = slice(unit * 128, unit * 128 + 128)
        weave([grad[:, cols] for grad in grads_up], slots.at[:, unit], slice(0, 128))
    saves = save(pl.ds(0, 4), 0)
    middle_grad = (
        grad_after.astype(F32) + norm_back(normed_mid, inverse_mid, back_up)
    ).astype(BF16)
    middle_grad_ref[...] = middle_grad
    grad = dot(attended_ref[...], middle_grad)
    columns = [grad[:, p * 128 : p * 128 + 128] for p in range(4)]
    weave(columns, slots.at[:, 4], slice(0, 128))
    saves += save(pl.ds(4, 1), 2)
    for copy in saves:
        copy.wait()


def backward_kernel(
    where_ref, tokens_ref, packed_ref, keys_t_ref, attended_ref, middle_grad_ref,
    first_t_ref, order_ref, level_order_ref, level_two_ref, w_out,
    near0_hbm, near1_hbm, near2_hbm, near3_hbm, probs_hbm, w_qkv_hbm,
    out0, out1, out2, out3, keep_hbm, send_hbm,
    grad_heads, grad_heads_t, products, query_grad_t, packed_grad, probs_ref, w_qkv, near_ref,
    slots, near_sems, sems, out_sems,
):
    loads = load(
        [(probs_hbm.at[pl.ds(g * 4, 4)], probs_ref.at[pl.ds(g * 4, 4)]) for g in range(4)]
        + [(w_qkv_hbm, w_qkv)],
        sems,
    )
    nears = (near0_hbm, near1_hbm, near2_hbm, near3_hbm)
    nears = load([(nears[step], near_ref.at[step]) for step in range(4)], near_sems)
    core = where_ref[0] & 1
    middle_grad = middle_grad_ref[...]
    wide = dot(middle_grad, w_out[...], 1, 1).astype(BF16)
    for group in range(4):
        grad_heads[group] = wide[:, group * 128 : group * 128 + 128]
    upstream_t = dot(w_out[...], middle_grad, 1, 1).astype(BF16)
    products[...] = upstream_t.astype(F32) * attended_ref[...].astype(F32)
    grad_heads_t[...] = jnp.zeros_like(grad_heads_t)
    for head in range(16):
        rows = slice(head % 4 * HEAD, head % 4 * HEAD + HEAD)
        grad_heads_t[head, rows, :] = upstream_t[head * HEAD : head * HEAD + HEAD]

    head_of_lane = lax.broadcasted_iota(jnp.int32, (TOKENS, 128), 1) >> 5

    for group in range(4):
        loads[group].wait()
        queries = packed_ref[group]
        values = packed_ref[8 + group]
        upstream = grad_heads[group]
        grad_keys = jnp.zeros((TOKENS, 128), F32)
        grad_values = jnp.zeros((TOKENS, 128), F32)
        for part in range(4):
            head = group * 4 + part
            at = slice(head * HEAD, head * HEAD + HEAD)
            weights = probs_ref[head]
            total = jnp.sum(products[at, :], axis=0, keepdims=True)
            grad_weights = dot(values, grad_heads_t[head])
            scores = (weights.astype(F32) * (grad_weights - total)).astype(BF16)
            in_head = head_of_lane == part
            grad_keys = jnp.where(in_head, dot(scores, queries), grad_keys)
            grad_values = jnp.where(in_head, dot(weights, upstream), grad_values)
            query_grad_t[at, :] = (dot(keys_t_ref[at, :], scores) * HEAD ** (-0.5)).astype(BF16)
        packed_grad[4 + group] = (grad_keys * (1 / LOG2E)).astype(BF16)
        packed_grad[8 + group] = grad_values.astype(BF16)

    for copy in nears:
        copy.wait()
    near = jnp.concatenate([near_ref[step].astype(F32) for step in range(4)], axis=0).astype(BF16)
    grad = dot(near[:, :512], near[:, 512:], 0, 0)
    weave([grad[:, q * 256 : q * 256 + 256] for q in range(4)], slots, slice(384, 640))

    identity = eye(TOKENS)
    for group in range(4):
        packed_grad[group] = dot(
            identity, query_grad_t[group * 128 : group * 128 + 128, :], 1, 1
        ).astype(BF16)
    first_t = first_t_ref[...]
    loads[4].wait()
    back_qkv = jnp.zeros((TOKENS, 512), F32)
    grads = []
    for part in range(3):
        wide = jnp.concatenate([packed_grad[part * 4 + g] for g in range(4)], axis=1)
        grad = dot(first_t, wide)
        grads += [grad[:, q * 128 : q * 128 + 128] for q in range(4)]
        back_qkv = back_qkv + dot(wide, w_qkv[:, part * 512 : part * 512 + 512], 1, 1)
    for part in range(3):
        weave([grads[q * 3 + part] for q in range(4)], slots, slice(part * 128, part * 128 + 128))
    saves = load([(slots.at[core], keep_hbm), (slots.at[1 - core], send_hbm)], out_sems)

    normed_in, inverse_in = normalize(tokens_ref[...].astype(F32))
    grad_first = back_qkv.astype(BF16).astype(F32)
    grad_tokens = (
        middle_grad.astype(F32) + norm_back(normed_in, inverse_in, grad_first)
    ).astype(BF16)
    for quad, out in enumerate((out0, out1, out2, out3)):
        rows = dot(order_ref[quad], grad_tokens)
        for half in range(2):
            level_two = level_two_ref[:, half * 512 : half * 512 + 512]
            rows = rows + dot(level_order_ref[half * 4 + quad], level_two)
        out[...] = rows.astype(BF16)
    for copy in saves:
        copy.wait()


def pair_kernel(keep_hbm, arrived_hbm, *refs, place):
    blocks_hbm, keep_ref, arrived_ref, keep_sems, arrived_sems, out_sems = refs[-6:]
    cols = pl.ds(place, keep_hbm.shape[-1])
    parts = [pl.ds(p * 16, 16) for p in range(4)]
    keeps = load([(keep_hbm.at[p], keep_ref.at[p]) for p in parts], keep_sems)
    arrivals = load([(arrived_hbm.at[p], arrived_ref.at[p]) for p in parts], arrived_sems)
    saves = []
    for part, rows in enumerate(parts):
        keeps[part].wait()
        arrivals[part].wait()
        total = keep_ref[rows].astype(F32) + arrived_ref[rows].astype(F32)
        keep_ref[rows] = total.astype(BF16)
        saves += load(
            [(keep_ref.at[rows], blocks_hbm.at[rows, :, cols])], out_sems.at[pl.ds(part, 1)]
        )
    for save in saves:
        save.wait()


def ring_kernel(where_ref, keep_hbm, arrived_hbm, *refs, shift):
    *outs, keep_ref, arrived_ref, keep_sems, arrived_sems = refs
    me = (where_ref[0] >> shift) & 3
    units = [(me + step) & 3 for step in range(4)] + list(range(4, len(outs)))
    keeps = [(keep_hbm.at[unit], keep_ref.at[at]) for at, unit in enumerate(units)]
    arrivals = [(arrived_hbm.at[unit], arrived_ref.at[at]) for at, unit in enumerate(units)]
    copies = list(zip(load(keeps, keep_sems), load(arrivals, arrived_sems)))
    for at, out in enumerate(outs):
        for copy in copies[at]:
            copy.wait()
        out[...] = (keep_ref[at].astype(F32) + arrived_ref[at].astype(F32)).astype(BF16)


def assemble_kernel(*refs):
    blocks_hbm, parts_ref, total_ref, sems, out_sem = refs[9:]
    copies = load([(refs[at], parts_ref.at[at]) for at in range(9)], sems)
    for unit, first in enumerate((0, 4)):
        for copy in copies[first : first + 4]:
            copy.wait()
        total = sum(parts_ref[first + step].astype(F32) for step in range(4))
        total_ref[:, :, unit * 128 : unit * 128 + 128] = total.astype(BF16)
    copies[8].wait()
    total_ref[:, :, 256:] = parts_ref[8]
    save, = load([(total_ref, blocks_hbm.at[:, :, pl.ds(0, 384)])], out_sem)
    save.wait()


def share_kernel(landed_hbm, qkv_ref, out_ref, up_ref, down_ref, merge_ref, landed_ref, sems):
    parts = [pl.ds(p * 16, 16) for p in range(4)]
    loads = load([(landed_hbm.at[p], landed_ref.at[p]) for p in parts], sems)
    down, up, merge = ([0.0] * 4 for _ in range(3))
    shared = 0.0
    for chip in range(64):
        z, y = chip // 16, chip // 2 % 4
        if chip % 16 == 0:
            loads[z].wait()
        block = landed_ref[chip].astype(F32)
        down[z] = down[z] + block[:, :128]
        up[y] = up[y] + block[:, 128:256]
        shared = shared + block[:, 256:768]
        merge[y] = merge[y] + block[:, 768:]
    for block in range(4):
        down_ref[:, block * 128 : block * 128 + 128] = down[block]
        rows = slice(block * 4, block * 4 + 4)
        out_ref[:, block * 128 : block * 128 + 128] = shared[rows, :128]
        qkv_ref[:, block * 384 : block * 384 + 384] = shared[rows, 128:]
        for y in range(4):
            at = block * 512 + y * 128
            up_ref[:, at : at + 128] = up[y][rows]
            merge_ref[y * 4 : y * 4 + 4, block * 256 : block * 256 + 256] = merge[y][rows]


def call(kernel, inputs, held, outputs, saved, scratch, micros, kind=BF16, free=(), aliases=(),
         weight=1, loose=False):
    whole, there = pl.BlockSpec(memory_space=pltpu.VMEM), pl.BlockSpec(memory_space=pltpu.HBM)
    specs = [whole if at < held else there for at in range(len(inputs))]
    for at in free:
        specs[at] = pl.BlockSpec(memory_space=pl.ANY)
    if inputs[0].ndim == 1:
        specs[0] = pl.BlockSpec(memory_space=pltpu.SMEM)
    return pl.pallas_call(
        kernel,
        out_shape=[jax.ShapeDtypeStruct(shape, kind) for shape in outputs],
        in_specs=specs,
        out_specs=[
            pl.BlockSpec(memory_space=pl.ANY) if loose else whole if at < saved else there
            for at in range(len(outputs))
        ],
        scratch_shapes=scratch,
        input_output_aliases=dict(aliases),
        compiler_params=pltpu.CompilerParams(vmem_limit_bytes=(56 if micros > 5 else 14) * 2**20),
        cost_estimate=pl.CostEstimate(
            flops=weight * micros * 10**9, bytes_accessed=micros * 10**6, transcendentals=0
        ),
    )(*inputs)


def vmem(*shape):
    return pltpu.VMEM(shape, BF16)


def dmas(count):
    return pltpu.SemaphoreType.DMA((count,))


def exchanged(send):
    return lax.ppermute(send, "core", [(0, 1), (1, 0)])


def ring_parts(where, keep, arrived, axis, shift, weight):
    count = keep.shape[0]
    outs = call(
        functools.partial(ring_kernel, shift=shift),
        [where, keep, arrived], 1, [(64, 16, 128)] * count, count,
        [vmem(*keep.shape), vmem(*keep.shape), dmas(count), dmas(count)], 2, free=(2,), weight=weight,
    )
    moved = [
        lax.ppermute(outs[step], axis, [(i, (i + step) % 4) for i in range(4)])
        for step in (1, 2, 3)
    ]
    return outs, [outs[0], *moved, *outs[4:]]


def shifted_block(block, down, right):
    route = []
    for source in range(128):
        row, col = source // 16, source % 16
        route.append((source, (row + down) % 8 * 16 + (col + right) % 16))
    return lax.ppermute(block, GRID, route)


def quadrants(field):
    field = field.transpose(1, 2, 0, 3)
    rows, cols = field.shape[0] // 2, field.shape[1] // 2
    corners = field[:rows, :cols], field[:rows, cols:], field[rows:, :cols], field[rows:, cols:]
    return [corner.reshape(-1, field.shape[-1]) for corner in corners]


def roll_back(tokens, cotangent):
    corners = [
        jnp.concatenate([corner, cot[:, :512], cot[:, 512:]], axis=0)
        for corner, cot in zip(quadrants(tokens), quadrants(cotangent))
    ]
    upper_left, upper_right, lower_left, lower_right = corners
    return [
        lower_right,
        shifted_block(lower_left, 0, -1),
        shifted_block(upper_right, -1, 0),
        shifted_block(upper_left, -1, -1),
    ]


def send_forth(corners):
    upper_left, upper_right, lower_left, lower_right = corners
    return [
        shifted_block(lower_right, 1, 1),
        shifted_block(lower_left, 1, 0),
        shifted_block(upper_right, 0, 1),
        upper_left,
    ]


def from_corners(corners):
    upper = jnp.concatenate(corners[:2], axis=1)
    lower = jnp.concatenate(corners[2:], axis=1)
    return jnp.concatenate([upper, lower], axis=0).transpose(2, 0, 1, 3)


def body(tokens, window_ids, cotangent, w_qkv, w_out, w_up, w_down, w_merge):
    order, cot_order = token_order(), cotangent_order()
    level_order = np.concatenate([cot_order[:, :MERGED], cot_order[:, MERGED:]]).transpose(0, 2, 1)
    by_feature, field, hidden_shape = (512, TOKENS), (TOKENS, 512), (TOKENS, 2048)
    all_probs, near_shape, corner = (16, TOKENS, TOKENS), (MERGED, 1536), (PACKED, 512)
    places = window_places()
    where = lax.axis_index(("z", "y", "core")).reshape(1)
    quads = roll_back(tokens, cotangent)

    (level_two, near0, near1, near2, near3, tokens_in, packed, keys_t, attended, first_t,
     middle, grad_after, probs, slope, down_keep, down_send) = call(
        forward_kernel,
        [where, jnp.asarray(order, BF16), jnp.asarray(cot_order, BF16), window_ids,
         jnp.asarray(places, BF16), jnp.asarray(places[1].T, F32), *quads, w_qkv,
         w_out, w_up, w_down, w_merge], 6,
        [(MERGED, 1024)] + [near_shape] * 4 + [field, (12, TOKENS, 128), by_feature, by_feature,
         by_feature, field, field, all_probs, hidden_shape, (4, 64, 16, 128), (4, 64, 16, 128)],
        12,
        [vmem(4, *corner), pltpu.VMEM((TOKENS, TOKENS), F32), vmem(16, 128, TOKENS), vmem(*by_feature),
         vmem(*hidden_shape), vmem(*hidden_shape), vmem(*all_probs), vmem(*w_qkv.shape), vmem(*w_out.shape),
         vmem(*w_up.shape), vmem(*w_down.shape), vmem(*w_merge.shape), vmem(2, 4, 64, 16, 128),
         dmas(4), dmas(5), dmas(4)],
        20, free=range(6, 10),
    )
    near = [near0]
    for step, block in ((1, near1), (2, near2), (3, near3)):
        near.append(lax.ppermute(block, "y", [(i, (i + step) % 4) for i in range(4)]))
    middle_grad, keep, send = call(
        middle_kernel,
        [where, grad_after, middle, attended, w_down, slope, w_up], 4,
        [field, (5, 64, 16, 128), (5, 64, 16, 128)], 1,
        [vmem(*w_down.shape), vmem(*hidden_shape), vmem(*w_up.shape), vmem(2, 5, 64, 16, 128),
         dmas(3), dmas(4)],
        7,
    )
    down_keep, *near = lax.optimization_barrier((down_keep, *near))
    down_sums, down_parts = ring_parts(where, down_keep, exchanged(down_send), "z", 3, 60)
    up_sums, up_parts = ring_parts(where, keep, exchanged(send), "y", 1, 1)
    middle_grad, *_ = lax.optimization_barrier((middle_grad, down_sums[0], up_sums[0]))
    *corners, late_keep, late_send = call(
        backward_kernel,
        [where, tokens_in, packed, keys_t, attended, middle_grad, first_t,
         jnp.asarray(order.transpose(0, 2, 1), BF16), jnp.asarray(level_order, BF16), level_two,
         w_out, *near, probs, w_qkv], 11,
        [corner] * 4 + [(64, 16, 640)] * 2, 4,
        [vmem(4, TOKENS, 128), vmem(16, 128, TOKENS), pltpu.VMEM(by_feature, F32), vmem(*by_feature),
         vmem(12, TOKENS, 128), vmem(*all_probs), vmem(*w_qkv.shape), vmem(4, *near_shape),
         vmem(2, 64, 16, 640), dmas(4), dmas(5), dmas(2)],
        12, free=range(12, 15),
    )
    blocks, = call(
        assemble_kernel, [*down_parts, *up_parts], 0, [(64, 16, 1024)], 0,
        [vmem(9, 64, 16, 128), vmem(64, 16, 384), dmas(9), dmas(1)], 2, free=range(9), weight=60,
        loose=True,
    )
    blocks, = call(
        functools.partial(pair_kernel, place=384),
        [late_keep, exchanged(late_send), blocks], 0, [blocks.shape], 0,
        [vmem(64, 16, 640), vmem(64, 16, 640), dmas(4), dmas(4), dmas(4)], 2, free=(1, 2),
        aliases={2: 0}, loose=True,
    )
    corners = send_forth(corners)
    blocks, *corners = lax.optimization_barrier((blocks, *corners))
    landed = lax.all_to_all(blocks, PAIRS, 0, 0, tiled=True)
    grad_qkv, grad_out, grad_up, grad_down, grad_merge = call(
        share_kernel, [landed], 0, [(4, 1536), (4, 512), (4, 2048), (16, 512), (16, 1024)], 5,
        [vmem(*blocks.shape), dmas(4)], 3, kind=F32,
    )
    grad_tokens = from_corners([c[:MERGED].reshape(6, 6, 2, 512) for c in corners])
    halves = [(c[MERGED : MERGED + 18], c[MERGED + 18 :]) for c in corners]
    level_two = from_corners(
        [jnp.concatenate(pair, axis=1).reshape(3, 3, 2, 1024) for pair in halves]
    )
    return (level_two, grad_tokens, grad_qkv, grad_out, grad_up, grad_down, grad_merge)


def solution(mesh):
    cube = jax.sharding.Mesh(mesh.devices.reshape(4, 2, 4, 2, 2), GRID)
    lat, lon = GRID[:2], GRID[2:]
    field = P(None, lat, lon, None)
    share = P(GRID, None)
    return jax.shard_map(
        body,
        mesh=cube,
        in_specs=(field, P(lat, lon), field, P(), P(), P(), P(), P()),
        out_specs=(field, field, share, share, share, share, share),
        check_vma=False,
    )
```

```python
import functools

import jax
import jax.numpy as jnp
import numpy as np
from jax import lax
from jax.experimental import pallas as pl
from jax.experimental.pallas import tpu as pltpu
from jax.sharding import PartitionSpec as P

HEAD = 32
WIN = 12
TOKENS = 2 * WIN * WIN
MERGED = TOKENS // 4
EPS = 1e-05
LOG2E = 1.4426950408889634
QUERY_SCALE = HEAD ** (-0.5) * LOG2E
GRID = ("z", "x_lo", "y", "x_hi", "core")
BF16 = jnp.bfloat16
F32 = jnp.float32

PAIRS = ("z", "x_lo", "y", "x_hi")


PACKED = MERGED + 36


def token_order():
    order = np.zeros((4, TOKENS, PACKED), np.float32)
    for quad in range(4):
        for row in range(6):
            for col in range(6):
                for level in range(2):
                    position = (col % 2) * 2 + row % 2
                    patch = quad * 18 + (row // 2 * 3 + col // 2) * 2 + level
                    order[quad, position * MERGED + patch, (row * 6 + col) * 2 + level] = 1.0
    return order


def window_places():
    places = np.zeros((2, TOKENS, WIN), np.float32)
    for row in range(WIN):
        for col in range(WIN):
            position = (col % 2) * 2 + row % 2
            quad = row // 6 * 2 + col // 6
            patch = quad * 18 + (row % 6 // 2 * 3 + col % 6 // 2) * 2
            for level in range(2):
                places[0, position * MERGED + patch + level, row] = 1.0
                places[1, position * MERGED + patch + level, col] = 1.0
    return places


def cotangent_order():
    order = np.zeros((4, 2 * MERGED, PACKED), np.float32)
    for quad in range(4):
        for half in range(2):
            for patch in range(18):
                order[quad, half * MERGED + quad * 18 + patch, MERGED + half * 18 + patch] = 1.0
    return order


def dot(left, right, left_dim=1, right_dim=0):
    return lax.dot_general(
        left, right, (((left_dim,), (right_dim,)), ((), ())), preferred_element_type=F32
    )


def normalize(wide):
    centered = wide - jnp.mean(wide, axis=-1, keepdims=True)
    inverse_std = lax.rsqrt(jnp.mean(centered * centered, axis=-1, keepdims=True) + EPS)
    return centered * inverse_std, inverse_std


def norm_back(normed, inverse_std, upstream):
    mean_grad = jnp.mean(upstream, axis=-1, keepdims=True)
    mean_cross = jnp.mean(upstream * normed, axis=-1, keepdims=True)
    return inverse_std * (upstream - mean_grad - normed * mean_cross)


def turned(values):
    return jnp.swapaxes(values.astype(F32), 0, 1).astype(BF16)


def weave(grads, slots, cols):
    tiles = [grad.reshape(64, 8, grad.shape[-1]) for grad in grads]
    turned = [pltpu.roll(tile, 4, 1) for tile in tiles]
    upper = lax.broadcasted_iota(jnp.int32, tiles[0].shape, 1) < 4
    for half in range(2):
        one, two = half * 2, half * 2 + 1
        rows = slice(half * 8, half * 8 + 8)
        slots[0, :, rows, cols] = jnp.where(upper, tiles[one], turned[two]).astype(BF16)
        slots[1, :, rows, cols] = jnp.where(upper, turned[one], tiles[two]).astype(BF16)


def load(pairs, sems):
    copies = [pltpu.make_async_copy(*pair, sems.at[at]) for at, pair in enumerate(pairs)]
    for copy in copies:
        copy.start()
    return copies


def merge_norm(after_mlp):
    pieces = [after_mlp[p * MERGED : (p + 1) * MERGED] for p in range(4)]
    mean = sum(jnp.sum(v, axis=-1, keepdims=True) for v in pieces) / 2048.0
    pieces = [v - mean for v in pieces]
    inverse_out = lax.rsqrt(
        sum(jnp.sum(v * v, axis=-1, keepdims=True) for v in pieces) / 2048.0 + EPS
    )
    return [v * inverse_out for v in pieces], inverse_out


def near_order():
    source = lax.broadcasted_iota(jnp.int32, (512, 1), 0)
    target = lax.broadcasted_iota(jnp.int32, (1, 512), 1)
    place = ((source >> 2) & 3) * 128 + (source >> 4) * 4 + (source & 3)
    return jnp.where(target == place, 1.0, 0.0).astype(BF16)


def gelu_parts(values):
    density = jnp.exp2(values * values * (-0.5 * LOG2E))
    inverse = 1.0 / (1.0 + jnp.abs(values) * (0.3275911 * 0.7071067811865476))
    series = 0.5 * 1.061405429
    for term in (-1.453152027, 1.421413741, -0.284496736, 0.254829592):
        series = series * inverse + 0.5 * term
    tail = series * inverse * density
    return jnp.where(values < 0.0, tail, 1.0 - tail), density


def forward_kernel(
    where_ref, order_ref, cot_order_ref, ids_ref, places_ref, cols_t_ref,
    quad0_hbm, quad1_hbm, quad2_hbm, quad3_hbm, w_qkv_hbm, w_out_hbm, w_up_hbm, w_down_hbm, w_merge_hbm,
    level_two_ref, near0, near1, near2, near3, tokens_ref, packed_ref, keys_t_ref,
    attended_ref, first_t_ref, middle_ref, grad_after_ref, probs_hbm, slope_hbm, keep_hbm, send_hbm,
    quads_ref, bias_ref, query_t, values_t, slope_ref, hidden_ref, probs_ref, w_qkv, w_out, w_up, w_down,
    w_merge, slots, quad_sems, in_sems, out_sems,
):
    quads = (quad0_hbm, quad1_hbm, quad2_hbm, quad3_hbm)
    quads = load([(quads[q], quads_ref.at[q]) for q in range(4)], quad_sems)
    weights = load(
        [(w_qkv_hbm, w_qkv), (w_out_hbm, w_out), (w_up_hbm, w_up), (w_down_hbm, w_down),
         (w_merge_hbm, w_merge)],
        in_sems,
    )
    query_t[...] = jnp.zeros_like(query_t)
    ids = ids_ref[...].astype(F32).astype(BF16)
    by_row = dot(places_ref[0], ids) * places_ref[1].astype(F32)
    by_col = dot(ids, places_ref[0], 0, 1) * cols_t_ref[...]
    alike = jnp.sum(by_row, axis=1, keepdims=True) == jnp.sum(by_col, axis=0, keepdims=True)
    bias_ref[...] = jnp.where(alike, 0.0, -1e30)
    for quad in quads:
        quad.wait()
    tokens = sum(dot(order_ref[q], quads_ref[q]) for q in range(4))
    tokens_ref[...] = tokens.astype(BF16)
    halves = sum(dot(cot_order_ref[q], quads_ref[q]) for q in range(4))
    cotangent = jnp.concatenate([halves[:MERGED], halves[MERGED:]], axis=1).astype(BF16)
    normed_in = normalize(tokens)[0]
    first_norm = normed_in.astype(BF16)
    first_t_ref[...] = turned(normed_in)
    weights[0].wait()
    for part in range(3):
        wide = dot(first_norm, w_qkv[:, part * 512 : part * 512 + 512])
        wide = wide * QUERY_SCALE if part == 0 else wide
        for group in range(4):
            packed_ref[part * 4 + group] = wide[:, group * 128 : group * 128 + 128].astype(BF16)
        by_feature = turned(wide)
        if part:
            (keys_t_ref, values_t)[part - 1][...] = by_feature
            continue
        for head in range(16):
            rows = slice(head % 4 * HEAD, head % 4 * HEAD + HEAD)
            query_t[head, rows, :] = by_feature[head * HEAD : head * HEAD + HEAD]

    def scores_of(head):
        return dot(packed_ref[4 + head // 4], query_t[head])

    ahead = scores_of(0)
    for head in range(16):
        scores = ahead + bias_ref[...]
        if head < 15:
            ahead = scores_of(head + 1)
        raised = jnp.exp2(scores - jnp.max(scores, axis=0, keepdims=True))
        inverse = 1.0 / jnp.sum(raised, axis=0, keepdims=True)
        probs = (raised * inverse).astype(BF16)
        probs_ref[head] = probs
        at = slice(head * HEAD, head * HEAD + HEAD)
        attended_ref[at, :] = dot(values_t[at, :], probs).astype(BF16)
    saves = load([(probs_ref, probs_hbm)], out_sems.at[pl.ds(0, 1)])

    attended = turned(attended_ref[...])
    weights[1].wait()
    attn_out = dot(attended, w_out[...]).astype(BF16)
    narrow_middle = (tokens + attn_out.astype(F32)).astype(BF16)
    middle_ref[...] = narrow_middle
    middle = narrow_middle.astype(F32)
    second_norm = normalize(middle)[0].astype(BF16)
    mlp = jnp.zeros((TOKENS, 512), F32)
    weights[2].wait()
    weights[3].wait()
    ahead = dot(second_norm, w_up[:, :512])
    for part in range(4):
        cols = slice(part * 512, part * 512 + 512)
        before = ahead
        if part < 3:
            ahead = dot(second_norm, w_up[:, part * 512 + 512 : part * 512 + 1024])
        cumulative, density = gelu_parts(before)
        hidden = (before * cumulative).astype(BF16)
        hidden_ref[:, cols] = hidden
        slope_ref[:, cols] = (cumulative + before * density * 0.3989422804014327).astype(BF16)
        mlp = mlp + dot(hidden, w_down[cols])
    saves += load([(slope_ref, slope_hbm)], out_sems.at[pl.ds(1, 1)])
    after_mlp = (middle + mlp).astype(BF16)
    pieces, inverse_out = merge_norm(after_mlp.astype(F32))
    merged_norm = [v.astype(BF16) for v in pieces]
    order = near_order()
    spread = [dot(v, order) for v in merged_norm]
    blocks = [
        jnp.concatenate([v[:, at * 128 : at * 128 + 128] for v in spread], axis=1).astype(BF16)
        for at in range(4)
    ]
    y = (where_ref[0] >> 1) & 3
    for step, near in enumerate((near0, near1, near2, near3)):
        block = blocks[step]
        for own in range(1, 4):
            block = jnp.where(y == own, blocks[(own + step) % 4], block)
        near[:, :512] = block
        near[:, 512:] = cotangent

    weights[4].wait()
    level_two_ref[...] = sum(
        dot(merged_norm[p], w_merge[p * 512 : p * 512 + 512]) for p in range(4)
    ).astype(BF16)
    upstream = [dot(cotangent, w_merge[p * 512 : p * 512 + 512], 1, 1) for p in range(4)]
    mean_grad = sum(jnp.sum(v, axis=-1, keepdims=True) for v in upstream) / 2048.0
    mean_cross = (
        sum(jnp.sum(v * u, axis=-1, keepdims=True) for v, u in zip(upstream, pieces)) / 2048.0
    )
    grad_after = jnp.concatenate(
        [inverse_out * (v - mean_grad - u * mean_cross) for v, u in zip(upstream, pieces)], axis=0
    ).astype(BF16)
    grad_after_ref[...] = grad_after
    core = where_ref[0] & 1
    for part in range(4):
        grad = dot(hidden_ref[:, part * 512 : part * 512 + 512], grad_after, 0, 0).astype(BF16)
        grad = grad.reshape(16, 2, 16, 512)
        for unit in range(4):
            for parity in range(2):
                slots[parity, unit, part * 16 : part * 16 + 16] = grad[
                    :, parity, :, unit * 128 : unit * 128 + 128
                ]
    saves += load(
        [(slots.at[core], keep_hbm), (slots.at[1 - core], send_hbm)], out_sems.at[pl.ds(2, 2)]
    )
    for save in saves:
        save.wait()


def middle_kernel(
    where_ref, grad_after_ref, middle_ref, attended_ref, w_down_hbm, slope_hbm, w_up_hbm,
    middle_grad_ref, keep_hbm, send_hbm,
    w_down, slope_ref, w_up, slots, sems, out_sems,
):
    loads = load([(w_down_hbm, w_down), (slope_hbm, slope_ref), (w_up_hbm, w_up)], sems)
    core = where_ref[0] & 1
    grad_after = grad_after_ref[...]
    normed_mid, inverse_mid = normalize(middle_ref[...].astype(F32))
    second_t = turned(normed_mid)

    def save(units, at):
        return load(
            [(slots.at[core, units], keep_hbm.at[units]),
             (slots.at[1 - core, units], send_hbm.at[units])],
            out_sems.at[pl.ds(at, 2)],
        )

    back_up = jnp.zeros((TOKENS, 512), F32)
    grads_up = []
    for copy in loads:
        copy.wait()
    for part in range(4):
        cols = slice(part * 512, part * 512 + 512)
        grad_before = (
            dot(grad_after, w_down[cols], 1, 1) * slope_ref[:, cols].astype(F32)
        ).astype(BF16)
        grads_up.append(dot(second_t, grad_before))
        back_up = back_up + dot(grad_before, w_up[:, cols], 1, 1)
    for unit in range(4):
        cols = slice(unit * 128, unit * 128 + 128)
        weave([grad[:, cols] for grad in grads_up], slots.at[:, unit], slice(0, 128))
    saves = save(pl.ds(0, 4), 0)
    middle_grad = (
        grad_after.astype(F32) + norm_back(normed_mid, inverse_mid, back_up)
    ).astype(BF16)
    middle_grad_ref[...] = middle_grad
    grad = dot(attended_ref[...], middle_grad)
    columns = [grad[:, p * 128 : p * 128 + 128] for p in range(4)]
    weave(columns, slots.at[:, 4], slice(0, 128))
    saves += save(pl.ds(4, 1), 2)
    for copy in saves:
        copy.wait()


def backward_kernel(
    where_ref, tokens_ref, packed_ref, keys_t_ref, attended_ref, middle_grad_ref,
    first_t_ref, order_ref, level_order_ref, level_two_ref, w_out,
    near0_hbm, near1_hbm, near2_hbm, near3_hbm, probs_hbm, w_qkv_hbm,
    out0, out1, out2, out3, keep_hbm, send_hbm,
    grad_heads, grad_heads_t, products, query_grad_t, packed_grad, probs_ref, w_qkv, near_ref,
    slots, near_sems, sems, out_sems,
):
    loads = load(
        [(probs_hbm.at[pl.ds(g * 4, 4)], probs_ref.at[pl.ds(g * 4, 4)]) for g in range(4)]
        + [(w_qkv_hbm, w_qkv)],
        sems,
    )
    nears = (near0_hbm, near1_hbm, near2_hbm, near3_hbm)
    nears = load([(nears[step], near_ref.at[step]) for step in range(4)], near_sems)
    core = where_ref[0] & 1
    middle_grad = middle_grad_ref[...]
    wide = dot(middle_grad, w_out[...], 1, 1).astype(BF16)
    for group in range(4):
        grad_heads[group] = wide[:, group * 128 : group * 128 + 128]
    upstream_t = dot(w_out[...], middle_grad, 1, 1).astype(BF16)
    products[...] = upstream_t.astype(F32) * attended_ref[...].astype(F32)
    grad_heads_t[...] = jnp.zeros_like(grad_heads_t)
    for head in range(16):
        rows = slice(head % 4 * HEAD, head % 4 * HEAD + HEAD)
        grad_heads_t[head, rows, :] = upstream_t[head * HEAD : head * HEAD + HEAD]

    head_of_lane = lax.broadcasted_iota(jnp.int32, (TOKENS, 128), 1) >> 5

    for group in range(4):
        loads[group].wait()
        queries = packed_ref[group]
        values = packed_ref[8 + group]
        upstream = grad_heads[group]
        grad_keys = jnp.zeros((TOKENS, 128), F32)
        grad_values = jnp.zeros((TOKENS, 128), F32)
        for part in range(4):
            head = group * 4 + part
            at = slice(head * HEAD, head * HEAD + HEAD)
            weights = probs_ref[head]
            total = jnp.sum(products[at, :], axis=0, keepdims=True)
            grad_weights = dot(values, grad_heads_t[head])
            scores = (weights.astype(F32) * (grad_weights - total)).astype(BF16)
            in_head = head_of_lane == part
            grad_keys = jnp.where(in_head, dot(scores, queries), grad_keys)
            grad_values = jnp.where(in_head, dot(weights, upstream), grad_values)
            query_grad_t[at, :] = (dot(keys_t_ref[at, :], scores) * HEAD ** (-0.5)).astype(BF16)
        packed_grad[4 + group] = (grad_keys * (1 / LOG2E)).astype(BF16)
        packed_grad[8 + group] = grad_values.astype(BF16)

    for copy in nears:
        copy.wait()
    near = jnp.concatenate([near_ref[step].astype(F32) for step in range(4)], axis=0).astype(BF16)
    grad = dot(near[:, :512], near[:, 512:], 0, 0)
    weave([grad[:, q * 256 : q * 256 + 256] for q in range(4)], slots, slice(384, 640))

    for group in range(4):
        packed_grad[group] = turned(query_grad_t[group * 128 : group * 128 + 128, :])
    first_t = first_t_ref[...]
    loads[4].wait()
    back_qkv = jnp.zeros((TOKENS, 512), F32)
    grads = []
    for part in range(3):
        wide = jnp.concatenate([packed_grad[part * 4 + g] for g in range(4)], axis=1)
        grad = dot(first_t, wide)
        grads += [grad[:, q * 128 : q * 128 + 128] for q in range(4)]
        back_qkv = back_qkv + dot(wide, w_qkv[:, part * 512 : part * 512 + 512], 1, 1)
    for part in range(3):
        weave([grads[q * 3 + part] for q in range(4)], slots, slice(part * 128, part * 128 + 128))
    saves = load([(slots.at[core], keep_hbm), (slots.at[1 - core], send_hbm)], out_sems)

    normed_in, inverse_in = normalize(tokens_ref[...].astype(F32))
    grad_first = back_qkv.astype(BF16).astype(F32)
    grad_tokens = (
        middle_grad.astype(F32) + norm_back(normed_in, inverse_in, grad_first)
    ).astype(BF16)
    for quad, out in enumerate((out0, out1, out2, out3)):
        rows = dot(order_ref[quad], grad_tokens)
        for half in range(2):
            level_two = level_two_ref[:, half * 512 : half * 512 + 512]
            rows = rows + dot(level_order_ref[half * 4 + quad], level_two)
        out[...] = rows.astype(BF16)
    for copy in saves:
        copy.wait()


def pair_kernel(keep_hbm, arrived_hbm, *refs, place):
    blocks_hbm, keep_ref, arrived_ref, keep_sems, arrived_sems, out_sems = refs[-6:]
    cols = pl.ds(place, keep_hbm.shape[-1])
    parts = [pl.ds(p * 16, 16) for p in range(4)]
    keeps = load([(keep_hbm.at[p], keep_ref.at[p]) for p in parts], keep_sems)
    arrivals = load([(arrived_hbm.at[p], arrived_ref.at[p]) for p in parts], arrived_sems)
    saves = []
    for part, rows in enumerate(parts):
        keeps[part].wait()
        arrivals[part].wait()
        total = keep_ref[rows].astype(F32) + arrived_ref[rows].astype(F32)
        keep_ref[rows] = total.astype(BF16)
        saves += load(
            [(keep_ref.at[rows], blocks_hbm.at[rows, :, cols])], out_sems.at[pl.ds(part, 1)]
        )
    for save in saves:
        save.wait()


def pair_total(keep_hbm, arrived_hbm, units, keep_ref, arrived_ref, keep_sems, arrived_sems):
    keeps = [(keep_hbm.at[unit], keep_ref.at[at]) for at, unit in enumerate(units)]
    arrivals = [(arrived_hbm.at[unit], arrived_ref.at[at]) for at, unit in enumerate(units)]
    copies = list(zip(load(keeps, keep_sems), load(arrivals, arrived_sems)))
    for at in range(len(units)):
        for copy in copies[at]:
            copy.wait()
        yield at, (keep_ref[at].astype(F32) + arrived_ref[at].astype(F32)).astype(BF16)


def ring_kernel(where_ref, keep_hbm, arrived_hbm, own, send1, send2, send3, *scratch):
    z = where_ref[0] >> 3
    units = [(z + step) & 3 for step in range(4)]
    for at, total in pair_total(keep_hbm, arrived_hbm, units, *scratch):
        (own, send1, send2, send3)[at][...] = total


def halves_kernel(where_ref, keep_hbm, arrived_hbm, own, send, out, *scratch):
    half = (where_ref[0] >> 1) & 1
    units = [half * 2, half * 2 + 1, 2 - half * 2, 3 - half * 2, 4]
    for at, total in pair_total(keep_hbm, arrived_hbm, units, *scratch):
        if at == 4:
            out[...] = total
        else:
            (own, send)[at // 2][:, :, at % 2 * 128 : at % 2 * 128 + 128] = total


def assemble_kernel(*refs):
    downs, ups, out_hbm, blocks_hbm = refs[:4], refs[4:6], refs[6], refs[7]
    down_ref, up_ref, total_ref, sems, out_sem = refs[8:]
    copies = load(
        [(downs[at], down_ref.at[at]) for at in range(4)]
        + [(ups[at], up_ref.at[at]) for at in range(2)]
        + [(out_hbm, total_ref.at[:, :, pl.ds(384, 128)])],
        sems,
    )
    for copy in copies[:4]:
        copy.wait()
    total = sum(down_ref[step].astype(F32) for step in range(4))
    total_ref[:, :, :128] = total.astype(BF16)
    for copy in copies[4:]:
        copy.wait()
    total_ref[:, :, 128:384] = (up_ref[0].astype(F32) + up_ref[1].astype(F32)).astype(BF16)
    save, = load([(total_ref, blocks_hbm.at[:, :, pl.ds(0, 512)])], out_sem)
    save.wait()


def share_kernel(landed_hbm, qkv_ref, out_ref, up_ref, down_ref, merge_ref, landed_ref, sems):
    parts = [pl.ds(p * 16, 16) for p in range(4)]
    loads = load([(landed_hbm.at[p], landed_ref.at[p]) for p in parts], sems)
    down, up, merge = [0.0] * 4, [0.0] * 2, [0.0] * 4
    shared = 0.0
    for chip in range(64):
        z, y = chip // 16, chip // 2 % 4
        if chip % 16 == 0:
            loads[z].wait()
        block = landed_ref[chip].astype(F32)
        down[z] = down[z] + block[:, :128]
        up[y % 2] = up[y % 2] + block[:, 128:384]
        shared = shared + block[:, 384:896]
        merge[y] = merge[y] + block[:, 896:]
    for block in range(4):
        down_ref[:, block * 128 : block * 128 + 128] = down[block]
        rows = slice(block * 4, block * 4 + 4)
        out_ref[:, block * 128 : block * 128 + 128] = shared[rows, :128]
        qkv_ref[:, block * 384 : block * 384 + 384] = shared[rows, 128:]
        for half in range(2):
            at = block * 512 + half * 256
            up_ref[:, at : at + 256] = up[half][rows]
        for y in range(4):
            merge_ref[y * 4 : y * 4 + 4, block * 256 : block * 256 + 256] = merge[y][rows]


def call(kernel, inputs, held, outputs, saved, scratch, micros, kind=BF16, free=(), aliases=(),
         weight=1, loose=False):
    whole, there = pl.BlockSpec(memory_space=pltpu.VMEM), pl.BlockSpec(memory_space=pltpu.HBM)
    specs = [whole if at < held else there for at in range(len(inputs))]
    for at in free:
        specs[at] = pl.BlockSpec(memory_space=pl.ANY)
    if inputs[0].ndim == 1:
        specs[0] = pl.BlockSpec(memory_space=pltpu.SMEM)
    return pl.pallas_call(
        kernel,
        out_shape=[jax.ShapeDtypeStruct(shape, kind) for shape in outputs],
        in_specs=specs,
        out_specs=[
            pl.BlockSpec(memory_space=pl.ANY) if loose else whole if at < saved else there
            for at in range(len(outputs))
        ],
        scratch_shapes=scratch,
        input_output_aliases=dict(aliases),
        compiler_params=pltpu.CompilerParams(vmem_limit_bytes=(56 if micros > 5 else 14) * 2**20),
        cost_estimate=pl.CostEstimate(
            flops=weight * micros * 10**9, bytes_accessed=micros * 10**6, transcendentals=0
        ),
    )(*inputs)


def vmem(*shape):
    return pltpu.VMEM(shape, BF16)


def dmas(count):
    return pltpu.SemaphoreType.DMA((count,))


def exchanged(send):
    return lax.ppermute(send, "core", [(0, 1), (1, 0)])


def pair_scratch(count):
    return [vmem(count, 64, 16, 128), vmem(count, 64, 16, 128), dmas(count), dmas(count)]


def shifted_block(block, down, right):
    route = []
    for source in range(128):
        row, col = source // 16, source % 16
        route.append((source, (row + down) % 8 * 16 + (col + right) % 16))
    return lax.ppermute(block, GRID, route)


def quadrants(field):
    field = field.transpose(1, 2, 0, 3)
    rows, cols = field.shape[0] // 2, field.shape[1] // 2
    corners = field[:rows, :cols], field[:rows, cols:], field[rows:, :cols], field[rows:, cols:]
    return [corner.reshape(-1, field.shape[-1]) for corner in corners]


def roll_back(tokens, cotangent):
    corners = [
        jnp.concatenate([corner, cot[:, :512], cot[:, 512:]], axis=0)
        for corner, cot in zip(quadrants(tokens), quadrants(cotangent))
    ]
    upper_left, upper_right, lower_left, lower_right = corners
    return [
        lower_right,
        shifted_block(lower_left, 0, -1),
        shifted_block(upper_right, -1, 0),
        shifted_block(upper_left, -1, -1),
    ]


def send_forth(corners):
    upper_left, upper_right, lower_left, lower_right = corners
    return [
        shifted_block(lower_right, 1, 1),
        shifted_block(lower_left, 1, 0),
        shifted_block(upper_right, 0, 1),
        upper_left,
    ]


def from_corners(corners):
    upper = jnp.concatenate(corners[:2], axis=1)
    lower = jnp.concatenate(corners[2:], axis=1)
    return jnp.concatenate([upper, lower], axis=0).transpose(2, 0, 1, 3)


def body(tokens, window_ids, cotangent, w_qkv, w_out, w_up, w_down, w_merge):
    order, cot_order = token_order(), cotangent_order()
    level_order = np.concatenate([cot_order[:, :MERGED], cot_order[:, MERGED:]]).transpose(0, 2, 1)
    by_feature, field, hidden_shape = (512, TOKENS), (TOKENS, 512), (TOKENS, 2048)
    all_probs, near_shape, corner = (16, TOKENS, TOKENS), (MERGED, 1536), (PACKED, 512)
    places = window_places()
    where = lax.axis_index(("z", "y", "core")).reshape(1)
    quads = roll_back(tokens, cotangent)

    (level_two, near0, near1, near2, near3, tokens_in, packed, keys_t, attended, first_t,
     middle, grad_after, probs, slope, down_keep, down_send) = call(
        forward_kernel,
        [where, jnp.asarray(order, BF16), jnp.asarray(cot_order, BF16), window_ids,
         jnp.asarray(places, BF16), jnp.asarray(places[1].T, F32), *quads, w_qkv,
         w_out, w_up, w_down, w_merge], 6,
        [(MERGED, 1024)] + [near_shape] * 4 + [field, (12, TOKENS, 128), by_feature, by_feature,
         by_feature, field, field, all_probs, hidden_shape, (4, 64, 16, 128), (4, 64, 16, 128)],
        12,
        [vmem(4, *corner), pltpu.VMEM((TOKENS, TOKENS), F32), vmem(16, 128, TOKENS), vmem(*by_feature),
         vmem(*hidden_shape), vmem(*hidden_shape), vmem(*all_probs), vmem(*w_qkv.shape), vmem(*w_out.shape),
         vmem(*w_up.shape), vmem(*w_down.shape), vmem(*w_merge.shape), vmem(2, 4, 64, 16, 128),
         dmas(4), dmas(5), dmas(4)],
        20, free=range(6, 10),
    )
    near = [near0]
    for step, block in ((1, near1), (2, near2), (3, near3)):
        near.append(lax.ppermute(block, "y", [(i, (i + step) % 4) for i in range(4)]))
    middle_grad, keep, send = call(
        middle_kernel,
        [where, grad_after, middle, attended, w_down, slope, w_up], 4,
        [field, (5, 64, 16, 128), (5, 64, 16, 128)], 1,
        [vmem(*w_down.shape), vmem(*hidden_shape), vmem(*w_up.shape), vmem(2, 5, 64, 16, 128),
         dmas(3), dmas(4)],
        7,
    )
    down_keep, *near = lax.optimization_barrier((down_keep, *near))
    down_own, *down_sends = call(
        ring_kernel, [where, down_keep, exchanged(down_send)], 1, [(64, 16, 128)] * 4, 4,
        pair_scratch(4), 2, free=(2,), weight=60,
    )
    downs = [down_own]
    for step, block in enumerate(down_sends, 1):
        downs.append(lax.ppermute(block, "z", [(i, (i + step) % 4) for i in range(4)]))
    up_own, up_send, out_sum = call(
        halves_kernel, [where, keep, exchanged(send)], 1,
        [(64, 16, 256), (64, 16, 256), (64, 16, 128)], 3, pair_scratch(5), 2, free=(2,),
    )
    up_arrived = lax.ppermute(up_send, "y", [(i, i ^ 1) for i in range(4)])
    middle_grad, *_ = lax.optimization_barrier((middle_grad, down_own, up_own))
    *corners, late_keep, late_send = call(
        backward_kernel,
        [where, tokens_in, packed, keys_t, attended, middle_grad, first_t,
         jnp.asarray(order.transpose(0, 2, 1), BF16), jnp.asarray(level_order, BF16), level_two,
         w_out, *near, probs, w_qkv], 11,
        [corner] * 4 + [(64, 16, 640)] * 2, 4,
        [vmem(4, TOKENS, 128), vmem(16, 128, TOKENS), pltpu.VMEM(by_feature, F32), vmem(*by_feature),
         vmem(12, TOKENS, 128), vmem(*all_probs), vmem(*w_qkv.shape), vmem(4, *near_shape),
         vmem(2, 64, 16, 640), dmas(4), dmas(5), dmas(2)],
        12, free=range(12, 15),
    )
    blocks, = call(
        assemble_kernel, [*downs, up_own, up_arrived, out_sum], 0, [(64, 16, 1152)], 0,
        [vmem(4, 64, 16, 128), vmem(2, 64, 16, 256), vmem(64, 16, 512), dmas(7), dmas(1)], 2,
        free=range(7), weight=60,
        loose=True,
    )
    blocks, = call(
        functools.partial(pair_kernel, place=512),
        [late_keep, exchanged(late_send), blocks], 0, [blocks.shape], 0,
        [vmem(64, 16, 640), vmem(64, 16, 640), dmas(4), dmas(4), dmas(4)], 2, free=(1, 2),
        aliases={2: 0}, loose=True,
    )
    corners = send_forth(corners)
    blocks, *corners = lax.optimization_barrier((blocks, *corners))
    landed = lax.all_to_all(blocks, PAIRS, 0, 0, tiled=True)
    grad_qkv, grad_out, grad_up, grad_down, grad_merge = call(
        share_kernel, [landed], 0, [(4, 1536), (4, 512), (4, 2048), (16, 512), (16, 1024)], 5,
        [vmem(*blocks.shape), dmas(4)], 3, kind=F32,
    )
    grad_tokens = from_corners([c[:MERGED].reshape(6, 6, 2, 512) for c in corners])
    halves = [(c[MERGED : MERGED + 18], c[MERGED + 18 :]) for c in corners]
    level_two = from_corners(
        [jnp.concatenate(pair, axis=1).reshape(3, 3, 2, 1024) for pair in halves]
    )
    return (level_two, grad_tokens, grad_qkv, grad_out, grad_up, grad_down, grad_merge)


def solution(mesh):
    cube = jax.sharding.Mesh(mesh.devices.reshape(4, 2, 4, 2, 2), GRID)
    lat, lon = GRID[:2], GRID[2:]
    field = P(None, lat, lon, None)
    share = P(GRID, None)
    return jax.shard_map(
        body,
        mesh=cube,
        in_specs=(field, P(lat, lon), field, P(), P(), P(), P(), P()),
        out_specs=(field, field, share, share, share, share, share),
        check_vma=False,
    )
```

```python
import functools

import jax
import jax.numpy as jnp
import numpy as np
from jax import lax
from jax.experimental import pallas as pl
from jax.experimental.pallas import tpu as pltpu
from jax.sharding import PartitionSpec as P

HEAD = 32
WIN = 12
TOKENS = 2 * WIN * WIN
MERGED = TOKENS // 4
MAIN = 256
EPS = 1e-05
LOG2E = 1.4426950408889634
QUERY_SCALE = HEAD ** (-0.5) * LOG2E
GRID = ("z", "x_lo", "y", "x_hi", "core")
BF16 = jnp.bfloat16
F32 = jnp.float32

PAIRS = ("z", "x_lo", "y", "x_hi")


PACKED = MERGED + 36


def token_order():
    order = np.zeros((4, TOKENS, PACKED), np.float32)
    for quad in range(4):
        for row in range(6):
            for col in range(6):
                for level in range(2):
                    position = (col % 2) * 2 + row % 2
                    patch = quad * 18 + (row // 2 * 3 + col // 2) * 2 + level
                    order[quad, position * MERGED + patch, (row * 6 + col) * 2 + level] = 1.0
    return order


def window_places():
    places = np.zeros((2, TOKENS, WIN), np.float32)
    for row in range(WIN):
        for col in range(WIN):
            position = (col % 2) * 2 + row % 2
            quad = row // 6 * 2 + col // 6
            patch = quad * 18 + (row % 6 // 2 * 3 + col % 6 // 2) * 2
            for level in range(2):
                places[0, position * MERGED + patch + level, row] = 1.0
                places[1, position * MERGED + patch + level, col] = 1.0
    return places


def cotangent_order():
    order = np.zeros((4, 2 * MERGED, PACKED), np.float32)
    for quad in range(4):
        for half in range(2):
            for patch in range(18):
                order[quad, half * MERGED + quad * 18 + patch, MERGED + half * 18 + patch] = 1.0
    return order


def dot(left, right, left_dim=1, right_dim=0):
    return lax.dot_general(
        left, right, (((left_dim,), (right_dim,)), ((), ())), preferred_element_type=F32
    )


def normalize(wide):
    centered = wide - jnp.mean(wide, axis=-1, keepdims=True)
    inverse_std = lax.rsqrt(jnp.mean(centered * centered, axis=-1, keepdims=True) + EPS)
    return centered * inverse_std, inverse_std


def norm_back(normed, inverse_std, upstream):
    mean_grad = jnp.mean(upstream, axis=-1, keepdims=True)
    mean_cross = jnp.mean(upstream * normed, axis=-1, keepdims=True)
    return inverse_std * (upstream - mean_grad - normed * mean_cross)


def turned(values):
    return jnp.swapaxes(values.astype(F32), 0, 1).astype(BF16)


def own_block(shape):
    rows = lax.broadcasted_iota(jnp.int32, shape, 0) >> 5
    return rows == lax.broadcasted_iota(jnp.int32, shape, 1) >> 5


def spread_rest(values):
    wide = jnp.concatenate([values] * 4, axis=1)
    return jnp.where(own_block(wide.shape), wide, 0.0).astype(BF16)


def gather_rest(blocks):
    kept = jnp.where(own_block(blocks.shape), blocks, 0.0)
    kept = kept + pltpu.roll(kept, 64, 1)
    kept = kept + pltpu.roll(kept, 32, 1)
    return kept[:, :HEAD]


def stack_rest(values):
    tall = jnp.concatenate([values[MAIN:]] * 4, axis=0)
    return jnp.where(own_block(tall.shape), tall, jnp.zeros_like(tall))


def weave(grads, slots, cols):
    tiles = [grad.reshape(64, 8, grad.shape[-1]) for grad in grads]
    turned = [pltpu.roll(tile, 4, 1) for tile in tiles]
    upper = lax.broadcasted_iota(jnp.int32, tiles[0].shape, 1) < 4
    for half in range(2):
        one, two = half * 2, half * 2 + 1
        rows = slice(half * 8, half * 8 + 8)
        slots[0, :, rows, cols] = jnp.where(upper, tiles[one], turned[two]).astype(BF16)
        slots[1, :, rows, cols] = jnp.where(upper, turned[one], tiles[two]).astype(BF16)


def load(pairs, sems):
    copies = [pltpu.make_async_copy(*pair, sems.at[at]) for at, pair in enumerate(pairs)]
    for copy in copies:
        copy.start()
    return copies


def merge_norm(after_mlp):
    pieces = [after_mlp[p * MERGED : (p + 1) * MERGED] for p in range(4)]
    mean = sum(jnp.sum(v, axis=-1, keepdims=True) for v in pieces) / 2048.0
    pieces = [v - mean for v in pieces]
    inverse_out = lax.rsqrt(
        sum(jnp.sum(v * v, axis=-1, keepdims=True) for v in pieces) / 2048.0 + EPS
    )
    return [v * inverse_out for v in pieces], inverse_out


def near_order():
    source = lax.broadcasted_iota(jnp.int32, (512, 1), 0)
    target = lax.broadcasted_iota(jnp.int32, (1, 512), 1)
    place = ((source >> 2) & 3) * 128 + (source >> 4) * 4 + (source & 3)
    return jnp.where(target == place, 1.0, 0.0).astype(BF16)


def gelu_parts(values):
    density = jnp.exp2(values * values * (-0.5 * LOG2E))
    inverse = 1.0 / (1.0 + jnp.abs(values) * (0.3275911 * 0.7071067811865476))
    series = 0.5 * 1.061405429
    for term in (-1.453152027, 1.421413741, -0.284496736, 0.254829592):
        series = series * inverse + 0.5 * term
    tail = series * inverse * density
    return jnp.where(values < 0.0, tail, 1.0 - tail), density


def forward_kernel(
    where_ref, order_ref, cot_order_ref, ids_ref, places_ref, cols_t_ref,
    quad0_hbm, quad1_hbm, quad2_hbm, quad3_hbm, w_qkv_hbm, w_out_hbm, w_up_hbm, w_down_hbm,
    w_merge_hbm,
    level_two_ref, grad_after_ref, near0, near1, near2, near3, tokens_hbm, packed_hbm, keys_t_hbm,
    attended_hbm, first_t_hbm, middle_hbm, probs_hbm, rest_hbm, slope_hbm, keep_hbm, send_hbm,
    quads_ref, bias_ref, bias_rest, query_t, query_rest, values_t, slope_ref, hidden_ref,
    probs_ref, rest_ref, w_qkv, w_out, w_up, w_down, w_merge, slots, near_ref, tokens_ref,
    packed_ref, keys_t_ref, attended_ref, first_t_ref, middle_ref, quad_sems, in_sems, out_sems,
):
    saves = []

    def save(*pairs):
        saves.extend(load(pairs, out_sems.at[pl.ds(len(saves), len(pairs))]))

    quads = (quad0_hbm, quad1_hbm, quad2_hbm, quad3_hbm)
    quads = load([(quads[q], quads_ref.at[q]) for q in range(4)], quad_sems)
    weights = load(
        [(w_qkv_hbm, w_qkv), (w_out_hbm, w_out), (w_up_hbm, w_up), (w_down_hbm, w_down),
         (w_merge_hbm, w_merge)],
        in_sems,
    )
    query_t[...] = jnp.zeros_like(query_t)
    ids = ids_ref[...].astype(F32).astype(BF16)
    by_row = dot(places_ref[0], ids) * places_ref[1].astype(F32)
    by_col = dot(ids, places_ref[0], 0, 1) * cols_t_ref[...]
    by_row = jnp.sum(by_row, axis=1, keepdims=True)
    by_col = jnp.sum(by_col, axis=0, keepdims=True)
    rest = jnp.concatenate([by_col[:, MAIN:]] * 4, axis=1)
    bias_ref[...] = jnp.where(by_row == by_col[:, :MAIN], 0.0, -1e30)
    bias_rest[...] = jnp.where(by_row == rest, 0.0, -1e30)
    for quad in quads:
        quad.wait()
    tokens = sum(dot(order_ref[q], quads_ref[q]) for q in range(4))
    tokens_ref[...] = tokens.astype(BF16)
    halves = sum(dot(cot_order_ref[q], quads_ref[q]) for q in range(4))
    cotangent = jnp.concatenate([halves[:MERGED], halves[MERGED:]], axis=1).astype(BF16)
    normed_in = normalize(tokens)[0]
    first_norm = normed_in.astype(BF16)
    first_t_ref[...] = turned(normed_in)
    save((tokens_ref, tokens_hbm), (first_t_ref, first_t_hbm))
    weights[0].wait()
    for part in range(3):
        wide = dot(first_norm, w_qkv[:, part * 512 : part * 512 + 512])
        wide = wide * QUERY_SCALE if part == 0 else wide
        for group in range(4):
            packed_ref[part * 4 + group] = wide[:, group * 128 : group * 128 + 128].astype(BF16)
        by_feature = jnp.swapaxes(wide, 0, 1)
        if part:
            (keys_t_ref, values_t)[part - 1][...] = by_feature.astype(BF16)
            continue
        for head in range(16):
            rows = slice(head % 4 * HEAD, head % 4 * HEAD + HEAD)
            own = by_feature[head * HEAD : head * HEAD + HEAD, :MAIN]
            query_t[head, rows, :] = own.astype(BF16)
        for group in range(4):
            rest = by_feature[group * 128 : group * 128 + 128, MAIN:]
            query_rest[group] = spread_rest(rest)
    save((packed_ref, packed_hbm), (keys_t_ref, keys_t_hbm))

    def scores_of(at):
        group, head = at // 5, at % 5
        turn = query_rest[group] if head == 4 else query_t[group * 4 + head]
        return dot(packed_ref[4 + group], turn)

    ahead = scores_of(0)
    for at in range(20):
        group, head = at // 5, at % 5
        scores = ahead + (bias_rest if head == 4 else bias_ref)[...]
        if at < 19:
            ahead = scores_of(at + 1)
        raised = jnp.exp2(scores - jnp.max(scores, axis=0, keepdims=True))
        inverse = 1.0 / jnp.sum(raised, axis=0, keepdims=True)
        probs = (raised * inverse).astype(BF16)
        if head == 4:
            rest_ref[group] = probs
            rows = slice(group * 128, group * 128 + 128)
            rest = gather_rest(dot(values_t[rows, :], probs))
            attended_ref[rows, MAIN:] = rest.astype(BF16)
        else:
            probs_ref[group * 4 + head] = probs
            rows = slice(group * 128 + head * HEAD, group * 128 + head * HEAD + HEAD)
            attended_ref[rows, :MAIN] = dot(values_t[rows, :], probs).astype(BF16)
    save((probs_ref, probs_hbm), (rest_ref, rest_hbm), (attended_ref, attended_hbm))

    attended = turned(attended_ref[...])
    weights[1].wait()
    attn_out = dot(attended, w_out[...]).astype(BF16)
    narrow_middle = (tokens + attn_out.astype(F32)).astype(BF16)
    middle_ref[...] = narrow_middle
    save((middle_ref, middle_hbm))
    middle = narrow_middle.astype(F32)
    second_norm = normalize(middle)[0].astype(BF16)
    mlp = jnp.zeros((TOKENS, 512), F32)
    weights[2].wait()
    weights[3].wait()
    ahead = dot(second_norm, w_up[:, :512])
    for part in range(4):
        cols = slice(part * 512, part * 512 + 512)
        before = ahead
        if part < 3:
            ahead = dot(second_norm, w_up[:, part * 512 + 512 : part * 512 + 1024])
        cumulative, density = gelu_parts(before)
        hidden = (before * cumulative).astype(BF16)
        hidden_ref[:, cols] = hidden
        slope_ref[:, cols] = (cumulative + before * density * 0.3989422804014327).astype(BF16)
        mlp = mlp + dot(hidden, w_down[cols])
    save((slope_ref, slope_hbm))
    after_mlp = (middle + mlp).astype(BF16)
    pieces, inverse_out = merge_norm(after_mlp.astype(F32))
    merged_norm = [v.astype(BF16) for v in pieces]
    order = near_order()
    spread = [dot(v, order) for v in merged_norm]
    blocks = [
        jnp.concatenate([v[:, at * 128 : at * 128 + 128] for v in spread], axis=1).astype(BF16)
        for at in range(4)
    ]
    y = (where_ref[0] >> 1) & 3
    for step, near in enumerate((near0, near1, near2, near3)):
        block = blocks[step]
        for own in range(1, 4):
            block = jnp.where(y == own, blocks[(own + step) % 4], block)
        near_ref[step, :, :512] = block
        near_ref[step, :, 512:] = cotangent
        save((near_ref.at[step], near))

    weights[4].wait()
    level_two_ref[...] = sum(
        dot(merged_norm[p], w_merge[p * 512 : p * 512 + 512]) for p in range(4)
    ).astype(BF16)
    upstream = [dot(cotangent, w_merge[p * 512 : p * 512 + 512], 1, 1) for p in range(4)]
    mean_grad = sum(jnp.sum(v, axis=-1, keepdims=True) for v in upstream) / 2048.0
    mean_cross = (
        sum(jnp.sum(v * u, axis=-1, keepdims=True) for v, u in zip(upstream, pieces)) / 2048.0
    )
    grad_after = jnp.concatenate(
        [inverse_out * (v - mean_grad - u * mean_cross) for v, u in zip(upstream, pieces)], axis=0
    ).astype(BF16)
    grad_after_ref[...] = grad_after
    core = where_ref[0] & 1
    for part in range(4):
        grad = dot(hidden_ref[:, part * 512 : part * 512 + 512], grad_after, 0, 0).astype(BF16)
        grad = grad.reshape(16, 2, 16, 512)
        for unit in range(4):
            for parity in range(2):
                slots[parity, unit, part * 16 : part * 16 + 16] = grad[
                    :, parity, :, unit * 128 : unit * 128 + 128
                ]
    save((slots.at[core], keep_hbm), (slots.at[1 - core], send_hbm))
    for copy in saves:
        copy.wait()


def middle_kernel(
    where_ref, grad_after_ref, middle_ref, attended_ref, w_down_hbm, slope_hbm, w_up_hbm,
    middle_grad_ref, keep_hbm, send_hbm,
    w_down, slope_ref, w_up, slots, sems, out_sems,
):
    loads = []
    for part in range(4):
        cols = pl.ds(part * 512, 512)
        pairs = [(w_down_hbm.at[cols], w_down.at[cols])]
        pairs += [(slope_hbm.at[:, cols], slope_ref.at[part])]
        pairs += [(w_up_hbm.at[:, cols], w_up.at[part])]
        loads.append(load(pairs, sems.at[pl.ds(part * 3, 3)]))
    core = where_ref[0] & 1
    grad_after = grad_after_ref[...]
    normed_mid, inverse_mid = normalize(middle_ref[...].astype(F32))
    second_t = turned(normed_mid)

    def save(units, at):
        return load(
            [(slots.at[core, units], keep_hbm.at[units]),
             (slots.at[1 - core, units], send_hbm.at[units])],
            out_sems.at[pl.ds(at, 2)],
        )

    back_up = jnp.zeros((TOKENS, 512), F32)
    grads_up = []
    for part in range(4):
        cols = slice(part * 512, part * 512 + 512)
        for copy in loads[part]:
            copy.wait()
        grad_before = (
            dot(grad_after, w_down[cols], 1, 1) * slope_ref[part].astype(F32)
        ).astype(BF16)
        grads_up.append(dot(second_t, grad_before))
        back_up = back_up + dot(grad_before, w_up[part], 1, 1)
    for unit in range(4):
        cols = slice(unit * 128, unit * 128 + 128)
        weave([grad[:, cols] for grad in grads_up], slots.at[:, unit], slice(0, 128))
    saves = save(pl.ds(0, 4), 0)
    middle_grad = (
        grad_after.astype(F32) + norm_back(normed_mid, inverse_mid, back_up)
    ).astype(BF16)
    middle_grad_ref[...] = middle_grad
    grad = dot(attended_ref[...], middle_grad)
    columns = [grad[:, p * 128 : p * 128 + 128] for p in range(4)]
    weave(columns, slots.at[:, 4], slice(0, 128))
    saves += save(pl.ds(4, 1), 2)
    for copy in saves:
        copy.wait()


def backward_kernel(
    where_ref, middle_grad_ref, attended_ref, w_out,
    near0_hbm, near1_hbm, near2_hbm, near3_hbm, packed_hbm, keys_t_hbm, probs_hbm, rest_hbm,
    w_qkv_hbm, first_t_hbm, tokens_hbm, order_hbm, level_order_hbm, level_two_hbm,
    out0, out1, out2, out3, keep_hbm, send_hbm,
    grad_heads, grad_heads_t, grad_heads_rest, products, query_grad_t, packed_grad, probs_ref,
    near_ref, packed_ref, keys_t_ref, rest_ref, w_qkv, first_t_ref, tokens_ref, order_ref,
    level_order_ref, level_two_ref, slots, near_sems, sems, out_sems,
):
    loads = load(
        [(packed_hbm, packed_ref), (keys_t_hbm, keys_t_ref), (rest_hbm, rest_ref)]
        + [(probs_hbm.at[pl.ds(g * 4, 4)], probs_ref.at[pl.ds(g * 4, 4)]) for g in range(4)]
        + [(w_qkv_hbm, w_qkv), (first_t_hbm, first_t_ref), (tokens_hbm, tokens_ref),
           (order_hbm, order_ref), (level_order_hbm, level_order_ref),
           (level_two_hbm, level_two_ref)],
        sems,
    )
    nears = (near0_hbm, near1_hbm, near2_hbm, near3_hbm)
    nears = load([(nears[step], near_ref.at[step]) for step in range(4)], near_sems)
    core = where_ref[0] & 1
    middle_grad = middle_grad_ref[...]
    wide = dot(middle_grad, w_out[...], 1, 1).astype(BF16)
    for group in range(4):
        grad_heads[group] = wide[:, group * 128 : group * 128 + 128]
    upstream_t = dot(w_out[...], middle_grad, 1, 1).astype(BF16)
    products[...] = upstream_t.astype(F32) * attended_ref[...].astype(F32)
    grad_heads_t[...] = jnp.zeros_like(grad_heads_t)
    for head in range(16):
        rows = slice(head % 4 * HEAD, head % 4 * HEAD + HEAD)
        grad_heads_t[head, rows, :] = upstream_t[head * HEAD : head * HEAD + HEAD, :MAIN]
    for group in range(4):
        rest = upstream_t[group * 128 : group * 128 + 128].astype(F32)
        grad_heads_rest[group] = spread_rest(rest[:, MAIN:])

    head_of_lane = lax.broadcasted_iota(jnp.int32, (TOKENS, 128), 1) >> 5
    for copy in loads[:3]:
        copy.wait()
    for group in range(4):
        loads[3 + group].wait()
        rows = slice(group * 128, group * 128 + 128)
        queries = packed_ref[group]
        values = packed_ref[8 + group]
        upstream = grad_heads[group]
        grad_keys = jnp.zeros((TOKENS, 128), F32)
        grad_values = jnp.zeros((TOKENS, 128), F32)
        totals = []
        for part in range(4):
            head = group * 4 + part
            at = slice(head * HEAD, head * HEAD + HEAD)
            weights = probs_ref[head]
            total = jnp.sum(products[at, :], axis=0, keepdims=True)
            totals.append(total[:, MAIN:])
            grad_weights = dot(values, grad_heads_t[head])
            scores = (weights.astype(F32) * (grad_weights - total[:, :MAIN])).astype(BF16)
            in_head = head_of_lane == part
            grad_keys = jnp.where(in_head, dot(scores, queries[:MAIN]), grad_keys)
            grad_values = jnp.where(in_head, dot(weights, upstream[:MAIN]), grad_values)
            query_grad = dot(keys_t_ref[at, :], scores) * HEAD ** (-0.5)
            query_grad_t[at, :MAIN] = query_grad.astype(BF16)
        weights = rest_ref[group]
        total = jnp.concatenate(totals, axis=1)
        grad_weights = dot(values, grad_heads_rest[group])
        scores = (weights.astype(F32) * (grad_weights - total)).astype(BF16)
        grad_keys = grad_keys + dot(scores, stack_rest(queries))
        grad_values = grad_values + dot(weights, stack_rest(upstream))
        query_grad = gather_rest(dot(keys_t_ref[rows, :], scores)) * HEAD ** (-0.5)
        query_grad_t[rows, MAIN:] = query_grad.astype(BF16)
        packed_grad[4 + group] = (grad_keys * (1 / LOG2E)).astype(BF16)
        packed_grad[8 + group] = grad_values.astype(BF16)

    for copy in nears:
        copy.wait()
    near = jnp.concatenate([near_ref[step].astype(F32) for step in range(4)], axis=0).astype(BF16)
    grad = dot(near[:, :512], near[:, 512:], 0, 0)
    weave([grad[:, q * 256 : q * 256 + 256] for q in range(4)], slots, slice(384, 640))

    for group in range(4):
        packed_grad[group] = turned(query_grad_t[group * 128 : group * 128 + 128, :])
    for copy in loads[7:]:
        copy.wait()
    first_t = first_t_ref[...]
    back_qkv = jnp.zeros((TOKENS, 512), F32)
    grads = []
    for part in range(3):
        wide = jnp.concatenate([packed_grad[part * 4 + g] for g in range(4)], axis=1)
        grad = dot(first_t, wide)
        grads += [grad[:, q * 128 : q * 128 + 128] for q in range(4)]
        back_qkv = back_qkv + dot(wide, w_qkv[:, part * 512 : part * 512 + 512], 1, 1)
    for part in range(3):
        weave([grads[q * 3 + part] for q in range(4)], slots, slice(part * 128, part * 128 + 128))
    saves = load([(slots.at[core], keep_hbm), (slots.at[1 - core], send_hbm)], out_sems)

    normed_in, inverse_in = normalize(tokens_ref[...].astype(F32))
    grad_first = back_qkv.astype(BF16).astype(F32)
    grad_tokens = (
        middle_grad.astype(F32) + norm_back(normed_in, inverse_in, grad_first)
    ).astype(BF16)
    for quad, out in enumerate((out0, out1, out2, out3)):
        rows = dot(order_ref[quad], grad_tokens)
        for half in range(2):
            level_two = level_two_ref[:, half * 512 : half * 512 + 512]
            rows = rows + dot(level_order_ref[half * 4 + quad], level_two)
        out[...] = rows.astype(BF16)
    for copy in saves:
        copy.wait()


def pair_kernel(keep_hbm, arrived_hbm, *refs, place):
    blocks_hbm, keep_ref, arrived_ref, keep_sems, arrived_sems, out_sems = refs[-6:]
    cols = pl.ds(place, keep_hbm.shape[-1])
    parts = [pl.ds(p * 16, 16) for p in range(4)]
    keeps = load([(keep_hbm.at[p], keep_ref.at[p]) for p in parts], keep_sems)
    arrivals = load([(arrived_hbm.at[p], arrived_ref.at[p]) for p in parts], arrived_sems)
    saves = []
    for part, rows in enumerate(parts):
        keeps[part].wait()
        arrivals[part].wait()
        total = keep_ref[rows].astype(F32) + arrived_ref[rows].astype(F32)
        keep_ref[rows] = total.astype(BF16)
        saves += load(
            [(keep_ref.at[rows], blocks_hbm.at[rows, :, cols])], out_sems.at[pl.ds(part, 1)]
        )
    for save in saves:
        save.wait()


def pair_total(keep_hbm, arrived_hbm, units, keep_ref, arrived_ref, keep_sems, arrived_sems):
    keeps = [(keep_hbm.at[unit], keep_ref.at[at]) for at, unit in enumerate(units)]
    arrivals = [(arrived_hbm.at[unit], arrived_ref.at[at]) for at, unit in enumerate(units)]
    copies = list(zip(load(keeps, keep_sems), load(arrivals, arrived_sems)))
    for at in range(len(units)):
        for copy in copies[at]:
            copy.wait()
        yield at, (keep_ref[at].astype(F32) + arrived_ref[at].astype(F32)).astype(BF16)


def ring_kernel(where_ref, keep_hbm, arrived_hbm, own, send1, send2, send3, *scratch):
    z = where_ref[0] >> 3
    units = [(z + step) & 3 for step in range(4)]
    for at, total in pair_total(keep_hbm, arrived_hbm, units, *scratch):
        (own, send1, send2, send3)[at][...] = total


def halves_kernel(where_ref, keep_hbm, arrived_hbm, own, send, out, *scratch):
    half = (where_ref[0] >> 1) & 1
    units = [half * 2, half * 2 + 1, 2 - half * 2, 3 - half * 2, 4]
    for at, total in pair_total(keep_hbm, arrived_hbm, units, *scratch):
        if at == 4:
            out[...] = total
        else:
            (own, send)[at // 2][:, :, at % 2 * 128 : at % 2 * 128 + 128] = total


def assemble_kernel(*refs):
    downs, ups, out_hbm, blocks_hbm = refs[:4], refs[4:6], refs[6], refs[7]
    down_ref, up_ref, total_ref, sems, out_sem = refs[8:]
    copies = load(
        [(downs[at], down_ref.at[at]) for at in range(4)]
        + [(ups[at], up_ref.at[at]) for at in range(2)]
        + [(out_hbm, total_ref.at[:, :, pl.ds(384, 128)])],
        sems,
    )
    for copy in copies[:4]:
        copy.wait()
    total = sum(down_ref[step].astype(F32) for step in range(4))
    total_ref[:, :, :128] = total.astype(BF16)
    for copy in copies[4:]:
        copy.wait()
    total_ref[:, :, 128:384] = (up_ref[0].astype(F32) + up_ref[1].astype(F32)).astype(BF16)
    save, = load([(total_ref, blocks_hbm.at[:, :, pl.ds(0, 512)])], out_sem)
    save.wait()


def share_kernel(landed_hbm, qkv_ref, out_ref, up_ref, down_ref, merge_ref, landed_ref, sems):
    parts = [pl.ds(p * 16, 16) for p in range(4)]
    loads = load([(landed_hbm.at[p], landed_ref.at[p]) for p in parts], sems)
    down, up, merge = [0.0] * 4, [0.0] * 2, [0.0] * 4
    shared = 0.0
    for chip in range(64):
        z, y = chip // 16, chip // 2 % 4
        if chip % 16 == 0:
            loads[z].wait()
        block = landed_ref[chip].astype(F32)
        down[z] = down[z] + block[:, :128]
        up[y % 2] = up[y % 2] + block[:, 128:384]
        shared = shared + block[:, 384:896]
        merge[y] = merge[y] + block[:, 896:]
    for block in range(4):
        down_ref[:, block * 128 : block * 128 + 128] = down[block]
        rows = slice(block * 4, block * 4 + 4)
        out_ref[:, block * 128 : block * 128 + 128] = shared[rows, :128]
        qkv_ref[:, block * 384 : block * 384 + 384] = shared[rows, 128:]
        for half in range(2):
            at = block * 512 + half * 256
            up_ref[:, at : at + 256] = up[half][rows]
        for y in range(4):
            merge_ref[y * 4 : y * 4 + 4, block * 256 : block * 256 + 256] = merge[y][rows]


def call(kernel, inputs, held, outputs, saved, scratch, micros, kind=BF16, free=(), aliases=(),
         weight=1, loose=False):
    whole, there = pl.BlockSpec(memory_space=pltpu.VMEM), pl.BlockSpec(memory_space=pltpu.HBM)
    specs = [whole if at < held else there for at in range(len(inputs))]
    for at in free:
        specs[at] = pl.BlockSpec(memory_space=pl.ANY)
    if inputs[0].ndim == 1:
        specs[0] = pl.BlockSpec(memory_space=pltpu.SMEM)
    return pl.pallas_call(
        kernel,
        out_shape=[jax.ShapeDtypeStruct(shape, kind) for shape in outputs],
        in_specs=specs,
        out_specs=[
            pl.BlockSpec(memory_space=pl.ANY) if loose else whole if at < saved else there
            for at in range(len(outputs))
        ],
        scratch_shapes=scratch,
        input_output_aliases=dict(aliases),
        compiler_params=pltpu.CompilerParams(vmem_limit_bytes=(56 if micros > 5 else 14) * 2**20),
        cost_estimate=pl.CostEstimate(
            flops=weight * micros * 10**9, bytes_accessed=micros * 10**6, transcendentals=0
        ),
    )(*inputs)


def vmem(*shape):
    return pltpu.VMEM(shape, BF16)


def dmas(count):
    return pltpu.SemaphoreType.DMA((count,))


def exchanged(send):
    return lax.ppermute(send, "core", [(0, 1), (1, 0)])


def pair_scratch(count):
    return [vmem(count, 64, 16, 128), vmem(count, 64, 16, 128), dmas(count), dmas(count)]


def shifted_block(block, down, right):
    route = []
    for source in range(128):
        row, col = source // 16, source % 16
        route.append((source, (row + down) % 8 * 16 + (col + right) % 16))
    return lax.ppermute(block, GRID, route)


def quadrants(field):
    field = field.transpose(1, 2, 0, 3)
    rows, cols = field.shape[0] // 2, field.shape[1] // 2
    corners = field[:rows, :cols], field[:rows, cols:], field[rows:, :cols], field[rows:, cols:]
    return [corner.reshape(-1, field.shape[-1]) for corner in corners]


def roll_back(tokens, cotangent):
    corners = [
        jnp.concatenate([corner, cot[:, :512], cot[:, 512:]], axis=0)
        for corner, cot in zip(quadrants(tokens), quadrants(cotangent))
    ]
    upper_left, upper_right, lower_left, lower_right = corners
    return [
        lower_right,
        shifted_block(lower_left, 0, -1),
        shifted_block(upper_right, -1, 0),
        shifted_block(upper_left, -1, -1),
    ]


def send_forth(corners):
    upper_left, upper_right, lower_left, lower_right = corners
    return [
        shifted_block(lower_right, 1, 1),
        shifted_block(lower_left, 1, 0),
        shifted_block(upper_right, 0, 1),
        upper_left,
    ]


def from_corners(corners):
    upper = jnp.concatenate(corners[:2], axis=1)
    lower = jnp.concatenate(corners[2:], axis=1)
    return jnp.concatenate([upper, lower], axis=0).transpose(2, 0, 1, 3)


def body(tokens, window_ids, cotangent, w_qkv, w_out, w_up, w_down, w_merge):
    order, cot_order = token_order(), cotangent_order()
    level_order = np.concatenate([cot_order[:, :MERGED], cot_order[:, MERGED:]]).transpose(0, 2, 1)
    by_feature, field, hidden_shape = (512, TOKENS), (TOKENS, 512), (TOKENS, 2048)
    near_shape, corner = (MERGED, 1536), (PACKED, 512)
    places = window_places()
    where = lax.axis_index(("z", "y", "core")).reshape(1)
    quads = roll_back(tokens, cotangent)

    probs_shape, rest_shape = (16, TOKENS, MAIN), (4, TOKENS, 128)
    packed_shape, down_shape = (12, TOKENS, 128), (4, 64, 16, 128)
    (level_two, grad_after, near0, near1, near2, near3, tokens_in, packed, keys_t, attended,
     first_t, middle, probs, rest, slope, down_keep, down_send) = call(
        forward_kernel,
        [where, jnp.asarray(order, BF16), jnp.asarray(cot_order, BF16), window_ids,
         jnp.asarray(places, BF16), jnp.asarray(places[1].T, F32), *quads, w_qkv,
         w_out, w_up, w_down, w_merge], 6,
        [(MERGED, 1024), field] + [near_shape] * 4 + [field, packed_shape, by_feature, by_feature,
         by_feature, field, probs_shape, rest_shape, hidden_shape, down_shape, down_shape], 2,
        [vmem(4, *corner), pltpu.VMEM((TOKENS, MAIN), F32), pltpu.VMEM((TOKENS, 128), F32),
         vmem(16, 128, MAIN), vmem(4, 128, 128), vmem(*by_feature), vmem(*hidden_shape),
         vmem(*hidden_shape), vmem(*probs_shape), vmem(*rest_shape), vmem(*w_qkv.shape),
         vmem(*w_out.shape), vmem(*w_up.shape), vmem(*w_down.shape), vmem(*w_merge.shape),
         vmem(2, *down_shape), vmem(4, *near_shape), vmem(*field), vmem(*packed_shape),
         vmem(*by_feature), vmem(*by_feature), vmem(*by_feature), vmem(*field),
         dmas(4), dmas(5), dmas(15)],
        20, free=range(6, 10),
    )
    near = [near0]
    for step, block in ((1, near1), (2, near2), (3, near3)):
        near.append(lax.ppermute(block, "y", [(i, (i + step) % 4) for i in range(4)]))
    middle_grad, keep, send = call(
        middle_kernel,
        [where, grad_after, middle, attended, w_down, slope, w_up], 4,
        [field, (5, 64, 16, 128), (5, 64, 16, 128)], 1,
        [vmem(*w_down.shape), vmem(4, TOKENS, 512), vmem(4, 512, 512), vmem(2, 5, 64, 16, 128),
         dmas(12), dmas(4)],
        7,
    )
    down_keep, *near = lax.optimization_barrier((down_keep, *near))
    down_own, *down_sends = call(
        ring_kernel, [where, down_keep, exchanged(down_send)], 1, [(64, 16, 128)] * 4, 4,
        pair_scratch(4), 2, free=(2,), weight=60,
    )
    downs = [down_own]
    for step, block in enumerate(down_sends, 1):
        downs.append(lax.ppermute(block, "z", [(i, (i + step) % 4) for i in range(4)]))
    up_own, up_send, out_sum = call(
        halves_kernel, [where, keep, exchanged(send)], 1,
        [(64, 16, 256), (64, 16, 256), (64, 16, 128)], 3, pair_scratch(5), 2, free=(2,),
    )
    up_arrived = lax.ppermute(up_send, "y", [(i, i ^ 1) for i in range(4)])
    middle_grad, *_ = lax.optimization_barrier((middle_grad, down_own, up_own))
    *corners, late_keep, late_send = call(
        backward_kernel,
        [where, middle_grad, attended, w_out, *near, packed, keys_t, probs, rest, w_qkv, first_t,
         tokens_in, jnp.asarray(order.transpose(0, 2, 1), BF16), jnp.asarray(level_order, BF16),
         level_two], 4,
        [corner] * 4 + [(64, 16, 640)] * 2, 4,
        [vmem(4, TOKENS, 128), vmem(16, 128, MAIN), vmem(4, 128, 128),
         pltpu.VMEM(by_feature, F32), vmem(*by_feature), vmem(*packed_shape), vmem(*probs_shape),
         vmem(4, *near_shape), vmem(*packed_shape), vmem(*by_feature), vmem(*rest_shape),
         vmem(*w_qkv.shape), vmem(*by_feature), vmem(*field), vmem(4, PACKED, TOKENS),
         vmem(8, PACKED, MERGED), vmem(MERGED, 1024), vmem(2, 64, 16, 640),
         dmas(4), dmas(13), dmas(2)],
        12, free=range(5, 8),
    )
    blocks, = call(
        assemble_kernel, [*downs, up_own, up_arrived, out_sum], 0, [(64, 16, 1152)], 0,
        [vmem(4, 64, 16, 128), vmem(2, 64, 16, 256), vmem(64, 16, 512), dmas(7), dmas(1)], 2,
        free=range(7), weight=60,
        loose=True,
    )
    blocks, = call(
        functools.partial(pair_kernel, place=512),
        [late_keep, exchanged(late_send), blocks], 0, [blocks.shape], 0,
        [vmem(64, 16, 640), vmem(64, 16, 640), dmas(4), dmas(4), dmas(4)], 2, free=(1, 2),
        aliases={2: 0}, loose=True,
    )
    corners = send_forth(corners)
    blocks, *corners = lax.optimization_barrier((blocks, *corners))
    landed = lax.all_to_all(blocks, PAIRS, 0, 0, tiled=True)
    grad_qkv, grad_out, grad_up, grad_down, grad_merge = call(
        share_kernel, [landed], 0, [(4, 1536), (4, 512), (4, 2048), (16, 512), (16, 1024)], 5,
        [vmem(*blocks.shape), dmas(4)], 3, kind=F32,
    )
    grad_tokens = from_corners([c[:MERGED].reshape(6, 6, 2, 512) for c in corners])
    halves = [(c[MERGED : MERGED + 18], c[MERGED + 18 :]) for c in corners]
    level_two = from_corners(
        [jnp.concatenate(pair, axis=1).reshape(3, 3, 2, 1024) for pair in halves]
    )
    return (level_two, grad_tokens, grad_qkv, grad_out, grad_up, grad_down, grad_merge)


def solution(mesh):
    cube = jax.sharding.Mesh(mesh.devices.reshape(4, 2, 4, 2, 2), GRID)
    lat, lon = GRID[:2], GRID[2:]
    field = P(None, lat, lon, None)
    share = P(GRID, None)
    return jax.shard_map(
        body,
        mesh=cube,
        in_specs=(field, P(lat, lon), field, P(), P(), P(), P(), P()),
        out_specs=(field, field, share, share, share, share, share),
        check_vma=False,
    )
```

```python
import functools

import jax
import jax.numpy as jnp
import numpy as np
from jax import lax
from jax.experimental import pallas as pl
from jax.experimental.pallas import tpu as pltpu
from jax.sharding import PartitionSpec as P

HEAD = 32
WIN = 12
TOKENS = 2 * WIN * WIN
MERGED = TOKENS // 4
MAIN = 256
EPS = 1e-05
LOG2E = 1.4426950408889634
QUERY_SCALE = HEAD ** (-0.5) * LOG2E
GRID = ("z", "x_lo", "y", "x_hi", "core")
BF16 = jnp.bfloat16
F32 = jnp.float32

PAIRS = ("z", "x_lo", "y", "x_hi")


PACKED = MERGED + 36


def token_order():
    order = np.zeros((4, TOKENS, PACKED), np.float32)
    for quad in range(4):
        for row in range(6):
            for col in range(6):
                for level in range(2):
                    position = (col % 2) * 2 + row % 2
                    patch = quad * 18 + (row // 2 * 3 + col // 2) * 2 + level
                    order[quad, position * MERGED + patch, (row * 6 + col) * 2 + level] = 1.0
    return order


def window_places():
    places = np.zeros((2, TOKENS, WIN), np.float32)
    for row in range(WIN):
        for col in range(WIN):
            position = (col % 2) * 2 + row % 2
            quad = row // 6 * 2 + col // 6
            patch = quad * 18 + (row % 6 // 2 * 3 + col % 6 // 2) * 2
            for level in range(2):
                places[0, position * MERGED + patch + level, row] = 1.0
                places[1, position * MERGED + patch + level, col] = 1.0
    return places


def cotangent_order():
    order = np.zeros((4, 2 * MERGED, PACKED), np.float32)
    for quad in range(4):
        for half in range(2):
            for patch in range(18):
                order[quad, half * MERGED + quad * 18 + patch, MERGED + half * 18 + patch] = 1.0
    return order


def dot(left, right, left_dim=1, right_dim=0):
    return lax.dot_general(
        left, right, (((left_dim,), (right_dim,)), ((), ())), preferred_element_type=F32
    )


def normalize(wide):
    centered = wide - jnp.mean(wide, axis=-1, keepdims=True)
    inverse_std = lax.rsqrt(jnp.mean(centered * centered, axis=-1, keepdims=True) + EPS)
    return centered * inverse_std, inverse_std


def norm_back(normed, inverse_std, upstream):
    mean_grad = jnp.mean(upstream, axis=-1, keepdims=True)
    mean_cross = jnp.mean(upstream * normed, axis=-1, keepdims=True)
    return inverse_std * (upstream - mean_grad - normed * mean_cross)


def turned(values):
    return jnp.swapaxes(values.astype(F32), 0, 1).astype(BF16)


def block_of(at, size):
    return pl.ds(pl.multiple_of(at * size, size), size)


def own_block(shape):
    rows = lax.broadcasted_iota(jnp.int32, shape, 0) >> 5
    return rows == lax.broadcasted_iota(jnp.int32, shape, 1) >> 5


def spread_rest(values):
    wide = jnp.concatenate([values] * 4, axis=1)
    return jnp.where(own_block(wide.shape), wide, 0.0).astype(BF16)


def gather_rest(blocks):
    kept = jnp.where(own_block(blocks.shape), blocks, 0.0)
    kept = kept + pltpu.roll(kept, 64, 1)
    kept = kept + pltpu.roll(kept, 32, 1)
    return kept[:, :HEAD]


def stack_rest(values):
    tall = jnp.concatenate([values[MAIN:]] * 4, axis=0)
    return jnp.where(own_block(tall.shape), tall, jnp.zeros_like(tall))


def weave(grads, slots, cols):
    tiles = [grad.reshape(64, 8, grad.shape[-1]) for grad in grads]
    turned = [pltpu.roll(tile, 4, 1) for tile in tiles]
    upper = lax.broadcasted_iota(jnp.int32, tiles[0].shape, 1) < 4
    for half in range(2):
        one, two = half * 2, half * 2 + 1
        rows = slice(half * 8, half * 8 + 8)
        slots[0, :, rows, cols] = jnp.where(upper, tiles[one], turned[two]).astype(BF16)
        slots[1, :, rows, cols] = jnp.where(upper, turned[one], tiles[two]).astype(BF16)


def load(pairs, sems):
    copies = [pltpu.make_async_copy(*pair, sems.at[at]) for at, pair in enumerate(pairs)]
    for copy in copies:
        copy.start()
    return copies


def merge_norm(after_mlp):
    pieces = [after_mlp[p * MERGED : (p + 1) * MERGED] for p in range(4)]
    mean = sum(jnp.sum(v, axis=-1, keepdims=True) for v in pieces) / 2048.0
    pieces = [v - mean for v in pieces]
    inverse_out = lax.rsqrt(
        sum(jnp.sum(v * v, axis=-1, keepdims=True) for v in pieces) / 2048.0 + EPS
    )
    return [v * inverse_out for v in pieces], inverse_out


def near_order():
    source = lax.broadcasted_iota(jnp.int32, (512, 1), 0)
    target = lax.broadcasted_iota(jnp.int32, (1, 512), 1)
    place = ((source >> 2) & 3) * 128 + (source >> 4) * 4 + (source & 3)
    return jnp.where(target == place, 1.0, 0.0).astype(BF16)


def gelu_parts(values):
    density = jnp.exp2(values * values * (-0.5 * LOG2E))
    inverse = 1.0 / (1.0 + jnp.abs(values) * (0.3275911 * 0.7071067811865476))
    series = 0.5 * 1.061405429
    for term in (-1.453152027, 1.421413741, -0.284496736, 0.254829592):
        series = series * inverse + 0.5 * term
    tail = series * inverse * density
    return jnp.where(values < 0.0, tail, 1.0 - tail), density


def forward_kernel(
    where_ref, order_ref, cot_order_ref, ids_ref, places_ref, cols_t_ref,
    quad0_hbm, quad1_hbm, quad2_hbm, quad3_hbm, w_qkv_hbm, w_out_hbm, w_up_hbm, w_down_hbm,
    w_merge_hbm,
    level_two_ref, grad_after_ref, near0, near1, near2, near3, tokens_hbm, packed_hbm, keys_t_hbm,
    attended_hbm, first_t_hbm, middle_hbm, probs_hbm, rest_hbm, slope_hbm, keep_hbm, send_hbm,
    quads_ref, bias_ref, bias_rest, query_t, query_rest, values_t, slope_ref, hidden_ref,
    probs_ref, rest_ref, w_qkv, w_out, w_up, w_down, w_merge, slots, near_ref, tokens_ref,
    packed_ref, keys_t_ref, attended_ref, first_t_ref, middle_ref, mlp_ref, quad_sems, in_sems, out_sems,
):
    saves = []

    def save(*pairs):
        saves.extend(load(pairs, out_sems.at[pl.ds(len(saves), len(pairs))]))

    quads = (quad0_hbm, quad1_hbm, quad2_hbm, quad3_hbm)
    quads = load([(quads[q], quads_ref.at[q]) for q in range(4)], quad_sems)
    weights = load(
        [(w_qkv_hbm, w_qkv), (w_out_hbm, w_out), (w_down_hbm, w_down), (w_merge_hbm, w_merge)]
        + [(w_up_hbm.at[:, pl.ds(p * 512, 512)], w_up.at[p]) for p in range(4)],
        in_sems,
    )
    query_t[...] = jnp.zeros_like(query_t)
    ids = ids_ref[...].astype(F32).astype(BF16)
    by_row = dot(places_ref[0], ids) * places_ref[1].astype(F32)
    by_col = dot(ids, places_ref[0], 0, 1) * cols_t_ref[...]
    by_row = jnp.sum(by_row, axis=1, keepdims=True)
    by_col = jnp.sum(by_col, axis=0, keepdims=True)
    rest = jnp.concatenate([by_col[:, MAIN:]] * 4, axis=1)
    bias_ref[...] = jnp.where(by_row == by_col[:, :MAIN], 0.0, -1e30)
    bias_rest[...] = jnp.where(by_row == rest, 0.0, -1e30)
    for quad in quads:
        quad.wait()
    tokens = sum(dot(order_ref[q], quads_ref[q]) for q in range(4))
    tokens_ref[...] = tokens.astype(BF16)
    halves = sum(dot(cot_order_ref[q], quads_ref[q]) for q in range(4))
    cotangent = jnp.concatenate([halves[:MERGED], halves[MERGED:]], axis=1).astype(BF16)
    normed_in = normalize(tokens)[0]
    first_norm = normed_in.astype(BF16)
    first_t_ref[...] = turned(normed_in)
    save((tokens_ref, tokens_hbm), (first_t_ref, first_t_hbm))
    weights[0].wait()
    for part in range(3):
        wide = dot(first_norm, w_qkv[:, part * 512 : part * 512 + 512])
        wide = wide * QUERY_SCALE if part == 0 else wide
        for group in range(4):
            packed_ref[part * 4 + group] = wide[:, group * 128 : group * 128 + 128].astype(BF16)
        by_feature = jnp.swapaxes(wide, 0, 1)
        if part:
            (keys_t_ref, values_t)[part - 1][...] = by_feature.astype(BF16)
            continue
        for head in range(16):
            rows = slice(head % 4 * HEAD, head % 4 * HEAD + HEAD)
            own = by_feature[head * HEAD : head * HEAD + HEAD, :MAIN]
            query_t[head, rows, :] = own.astype(BF16)
        for group in range(4):
            rest = by_feature[group * 128 : group * 128 + 128, MAIN:]
            query_rest[group] = spread_rest(rest)
    save((packed_ref, packed_hbm), (keys_t_ref, keys_t_hbm))

    def attend(group, _):
        keys = packed_ref[4 + group]
        ahead = dot(keys, query_t[group * 4])
        for head in range(5):
            scores = ahead + (bias_rest if head == 4 else bias_ref)[...]
            if head < 4:
                turn = query_rest[group] if head == 3 else query_t[group * 4 + head + 1]
                ahead = dot(keys, turn)
            raised = jnp.exp2(scores - jnp.max(scores, axis=0, keepdims=True))
            inverse = 1.0 / jnp.sum(raised, axis=0, keepdims=True)
            probs = (raised * inverse).astype(BF16)
            if head == 4:
                rest_ref[group] = probs
                rows = block_of(group, 128)
                rest = gather_rest(dot(values_t[rows, :], probs))
                attended_ref[rows, MAIN:] = rest.astype(BF16)
            else:
                probs_ref[group * 4 + head] = probs
                rows = block_of(group * 4 + head, HEAD)
                attended_ref[rows, :MAIN] = dot(values_t[rows, :], probs).astype(BF16)
        return 0

    lax.fori_loop(0, 4, attend, 0)
    save((probs_ref, probs_hbm), (rest_ref, rest_hbm), (attended_ref, attended_hbm))

    attended = turned(attended_ref[...])
    weights[1].wait()
    attn_out = dot(attended, w_out[...]).astype(BF16)
    narrow_middle = (tokens + attn_out.astype(F32)).astype(BF16)
    middle_ref[...] = narrow_middle
    save((middle_ref, middle_hbm))
    middle = narrow_middle.astype(F32)
    second_norm = normalize(middle)[0].astype(BF16)
    mlp_ref[...] = middle
    for at in (2, 4, 5, 6, 7):
        weights[at].wait()

    def feed(part, _):
        before = dot(second_norm, w_up[part])
        cumulative, density = gelu_parts(before)
        hidden = (before * cumulative).astype(BF16)
        hidden_ref[part] = hidden
        slope_ref[part] = (cumulative + before * density * 0.3989422804014327).astype(BF16)
        mlp_ref[...] += dot(hidden, w_down[block_of(part, 512), :])
        return 0

    lax.fori_loop(0, 4, feed, 0)
    save((slope_ref, slope_hbm))
    after_mlp = mlp_ref[...].astype(BF16)
    pieces, inverse_out = merge_norm(after_mlp.astype(F32))
    merged_norm = [v.astype(BF16) for v in pieces]
    order = near_order()
    spread = [dot(v, order) for v in merged_norm]
    blocks = [
        jnp.concatenate([v[:, at * 128 : at * 128 + 128] for v in spread], axis=1).astype(BF16)
        for at in range(4)
    ]
    y = (where_ref[0] >> 1) & 3
    for step, near in enumerate((near0, near1, near2, near3)):
        block = blocks[step]
        for own in range(1, 4):
            block = jnp.where(y == own, blocks[(own + step) % 4], block)
        near_ref[step, :, :512] = block
        near_ref[step, :, 512:] = cotangent
        save((near_ref.at[step], near))

    weights[3].wait()
    level_two_ref[...] = sum(
        dot(merged_norm[p], w_merge[p * 512 : p * 512 + 512]) for p in range(4)
    ).astype(BF16)
    upstream = [dot(cotangent, w_merge[p * 512 : p * 512 + 512], 1, 1) for p in range(4)]
    mean_grad = sum(jnp.sum(v, axis=-1, keepdims=True) for v in upstream) / 2048.0
    mean_cross = (
        sum(jnp.sum(v * u, axis=-1, keepdims=True) for v, u in zip(upstream, pieces)) / 2048.0
    )
    grad_after = jnp.concatenate(
        [inverse_out * (v - mean_grad - u * mean_cross) for v, u in zip(upstream, pieces)], axis=0
    ).astype(BF16)
    grad_after_ref[...] = grad_after
    core = where_ref[0] & 1

    def down(part, _):
        grad = dot(hidden_ref[part], grad_after, 0, 0).astype(BF16).reshape(16, 2, 16, 512)
        chips = block_of(part, 16)
        for unit in range(4):
            for parity in range(2):
                slots[parity, unit, chips] = grad[:, parity, :, unit * 128 : unit * 128 + 128]
        return 0

    lax.fori_loop(0, 4, down, 0)
    save((slots.at[core], keep_hbm), (slots.at[1 - core], send_hbm))
    for copy in saves:
        copy.wait()


def middle_kernel(
    where_ref, grad_after_ref, middle_ref, attended_ref, w_down_hbm, slope_hbm, w_up_hbm,
    middle_grad_ref, keep_hbm, send_hbm,
    w_down, slope_ref, w_up, slots, grads_ref, back_ref, sems, out_sems,
):
    loads = []
    for part in range(4):
        cols = pl.ds(part * 512, 512)
        pairs = [(w_down_hbm.at[cols], w_down.at[cols])]
        pairs += [(slope_hbm.at[part], slope_ref.at[part])]
        pairs += [(w_up_hbm.at[:, cols], w_up.at[part])]
        loads.append(load(pairs, sems.at[pl.ds(part * 3, 3)]))
    core = where_ref[0] & 1
    grad_after = grad_after_ref[...]
    normed_mid, inverse_mid = normalize(middle_ref[...].astype(F32))
    second_t = turned(normed_mid)

    def save(units, at):
        return load(
            [(slots.at[core, units], keep_hbm.at[units]),
             (slots.at[1 - core, units], send_hbm.at[units])],
            out_sems.at[pl.ds(at, 2)],
        )

    back_ref[...] = jnp.zeros_like(back_ref)
    for copy in sum(loads, []):
        copy.wait()

    def back(part, _):
        grad_before = dot(grad_after, w_down[block_of(part, 512), :], 1, 1)
        grad_before = (grad_before * slope_ref[part].astype(F32)).astype(BF16)
        grads_ref[part] = dot(second_t, grad_before)
        back_ref[...] += dot(grad_before, w_up[part], 1, 1)
        return 0

    lax.fori_loop(0, 4, back, 0)

    def lay_out(unit, _):
        cols = block_of(unit, 128)
        weave([grads_ref[p, :, cols] for p in range(4)], slots.at[:, unit], slice(0, 128))
        return 0

    lax.fori_loop(0, 4, lay_out, 0)
    saves = save(pl.ds(0, 4), 0)
    middle_grad = (
        grad_after.astype(F32) + norm_back(normed_mid, inverse_mid, back_ref[...])
    ).astype(BF16)
    middle_grad_ref[...] = middle_grad
    grad = dot(attended_ref[...], middle_grad)
    columns = [grad[:, p * 128 : p * 128 + 128] for p in range(4)]
    weave(columns, slots.at[:, 4], slice(0, 128))
    saves += save(pl.ds(4, 1), 2)
    for copy in saves:
        copy.wait()


def backward_kernel(
    where_ref, middle_grad_ref, attended_ref, w_out,
    near0_hbm, near1_hbm, near2_hbm, near3_hbm, packed_hbm, keys_t_hbm, probs_hbm, rest_hbm,
    w_qkv_hbm, first_t_hbm, tokens_hbm, order_hbm, level_order_hbm, level_two_hbm,
    out0, out1, out2, out3, keep_hbm, send_hbm,
    grad_heads, grad_heads_t, grad_heads_rest, products, query_grad_t, packed_grad, probs_ref,
    near_ref, packed_ref, keys_t_ref, rest_ref, w_qkv, first_t_ref, tokens_ref, order_ref,
    level_order_ref, level_two_ref, slots, grads_ref, back_ref, near_sems, sems, out_sems,
):
    loads = load(
        [(packed_hbm, packed_ref), (keys_t_hbm, keys_t_ref), (rest_hbm, rest_ref)]
        + [(probs_hbm.at[pl.ds(g * 4, 4)], probs_ref.at[pl.ds(g * 4, 4)]) for g in range(4)]
        + [(w_qkv_hbm.at[:, pl.ds(p * 512, 512)], w_qkv.at[p]) for p in range(3)]
        + [(first_t_hbm, first_t_ref), (tokens_hbm, tokens_ref),
           (order_hbm, order_ref), (level_order_hbm, level_order_ref),
           (level_two_hbm, level_two_ref)],
        sems,
    )
    nears = (near0_hbm, near1_hbm, near2_hbm, near3_hbm)
    nears = load([(nears[step], near_ref.at[step]) for step in range(4)], near_sems)
    core = where_ref[0] & 1
    middle_grad = middle_grad_ref[...]
    wide = dot(middle_grad, w_out[...], 1, 1).astype(BF16)
    for group in range(4):
        grad_heads[group] = wide[:, group * 128 : group * 128 + 128]
    upstream_t = dot(w_out[...], middle_grad, 1, 1).astype(BF16)
    products[...] = upstream_t.astype(F32) * attended_ref[...].astype(F32)
    grad_heads_t[...] = jnp.zeros_like(grad_heads_t)
    for head in range(16):
        rows = slice(head % 4 * HEAD, head % 4 * HEAD + HEAD)
        grad_heads_t[head, rows, :] = upstream_t[head * HEAD : head * HEAD + HEAD, :MAIN]
    for group in range(4):
        rest = upstream_t[group * 128 : group * 128 + 128].astype(F32)
        grad_heads_rest[group] = spread_rest(rest[:, MAIN:])

    head_of_lane = lax.broadcasted_iota(jnp.int32, (TOKENS, 128), 1) >> 5
    for copy in loads[:7]:
        copy.wait()

    def attend_back(group, _):
        rows = block_of(group, 128)
        queries = packed_ref[group]
        values = packed_ref[8 + group]
        upstream = grad_heads[group]
        grad_keys = jnp.zeros((TOKENS, 128), F32)
        grad_values = jnp.zeros((TOKENS, 128), F32)
        totals = []
        for part in range(4):
            head = group * 4 + part
            at = block_of(head, HEAD)
            weights = probs_ref[head]
            total = jnp.sum(products[at, :], axis=0, keepdims=True)
            totals.append(total[:, MAIN:])
            grad_weights = dot(values, grad_heads_t[head])
            scores = (weights.astype(F32) * (grad_weights - total[:, :MAIN])).astype(BF16)
            in_head = head_of_lane == part
            grad_keys = jnp.where(in_head, dot(scores, queries[:MAIN]), grad_keys)
            grad_values = jnp.where(in_head, dot(weights, upstream[:MAIN]), grad_values)
            query_grad = dot(keys_t_ref[at, :], scores) * HEAD ** (-0.5)
            query_grad_t[at, :MAIN] = query_grad.astype(BF16)
        weights = rest_ref[group]
        total = jnp.concatenate(totals, axis=1)
        grad_weights = dot(values, grad_heads_rest[group])
        scores = (weights.astype(F32) * (grad_weights - total)).astype(BF16)
        grad_keys = grad_keys + dot(scores, stack_rest(queries))
        grad_values = grad_values + dot(weights, stack_rest(upstream))
        query_grad = gather_rest(dot(keys_t_ref[rows, :], scores)) * HEAD ** (-0.5)
        query_grad_t[rows, MAIN:] = query_grad.astype(BF16)
        packed_grad[4 + group] = (grad_keys * (1 / LOG2E)).astype(BF16)
        packed_grad[8 + group] = grad_values.astype(BF16)
        return 0

    lax.fori_loop(0, 4, attend_back, 0)

    for copy in nears:
        copy.wait()
    near = jnp.concatenate([near_ref[step].astype(F32) for step in range(4)], axis=0).astype(BF16)
    grad = dot(near[:, :512], near[:, 512:], 0, 0)
    weave([grad[:, q * 256 : q * 256 + 256] for q in range(4)], slots, slice(384, 640))

    for group in range(4):
        packed_grad[group] = turned(query_grad_t[group * 128 : group * 128 + 128, :])
    for copy in loads[7:]:
        copy.wait()
    first_t = first_t_ref[...]
    back_ref[...] = jnp.zeros_like(back_ref)

    def project_back(part, _):
        wide = jnp.concatenate([packed_grad[part * 4 + g] for g in range(4)], axis=1)
        grads_ref[part] = dot(first_t, wide)
        back_ref[...] += dot(wide, w_qkv[part], 1, 1)
        return 0

    lax.fori_loop(0, 3, project_back, 0)
    grads = [grads_ref[q // 4, :, q % 4 * 128 : q % 4 * 128 + 128] for q in range(12)]
    for part in range(3):
        weave([grads[q * 3 + part] for q in range(4)], slots, slice(part * 128, part * 128 + 128))
    saves = load([(slots.at[core], keep_hbm), (slots.at[1 - core], send_hbm)], out_sems)

    normed_in, inverse_in = normalize(tokens_ref[...].astype(F32))
    grad_first = back_ref[...].astype(BF16).astype(F32)
    grad_tokens = (
        middle_grad.astype(F32) + norm_back(normed_in, inverse_in, grad_first)
    ).astype(BF16)
    for quad, out in enumerate((out0, out1, out2, out3)):
        rows = dot(order_ref[quad], grad_tokens)
        for half in range(2):
            level_two = level_two_ref[:, half * 512 : half * 512 + 512]
            rows = rows + dot(level_order_ref[half * 4 + quad], level_two)
        out[...] = rows.astype(BF16)
    for copy in saves:
        copy.wait()


def pair_kernel(keep_hbm, arrived_hbm, *refs, place):
    blocks_hbm, keep_ref, arrived_ref, keep_sems, arrived_sems, out_sems = refs[-6:]
    cols = pl.ds(place, keep_hbm.shape[-1])
    parts = [pl.ds(p * 16, 16) for p in range(4)]
    keeps = load([(keep_hbm.at[p], keep_ref.at[p]) for p in parts], keep_sems)
    arrivals = load([(arrived_hbm.at[p], arrived_ref.at[p]) for p in parts], arrived_sems)
    saves = []
    for part, rows in enumerate(parts):
        keeps[part].wait()
        arrivals[part].wait()
        total = keep_ref[rows].astype(F32) + arrived_ref[rows].astype(F32)
        keep_ref[rows] = total.astype(BF16)
        saves += load(
            [(keep_ref.at[rows], blocks_hbm.at[rows, :, cols])], out_sems.at[pl.ds(part, 1)]
        )
    for save in saves:
        save.wait()


def pair_total(keep_hbm, arrived_hbm, units, keep_ref, arrived_ref, keep_sems, arrived_sems):
    keeps = [(keep_hbm.at[unit], keep_ref.at[at]) for at, unit in enumerate(units)]
    arrivals = [(arrived_hbm.at[unit], arrived_ref.at[at]) for at, unit in enumerate(units)]
    copies = list(zip(load(keeps, keep_sems), load(arrivals, arrived_sems)))
    for at in range(len(units)):
        for copy in copies[at]:
            copy.wait()
        yield at, (keep_ref[at].astype(F32) + arrived_ref[at].astype(F32)).astype(BF16)


def ring_kernel(where_ref, keep_hbm, arrived_hbm, own, send1, send2, send3, *scratch):
    z = where_ref[0] >> 3
    units = [(z + step) & 3 for step in range(4)]
    for at, total in pair_total(keep_hbm, arrived_hbm, units, *scratch):
        (own, send1, send2, send3)[at][...] = total


def halves_kernel(where_ref, keep_hbm, arrived_hbm, own, send, out, *scratch):
    half = (where_ref[0] >> 1) & 1
    units = [half * 2, half * 2 + 1, 2 - half * 2, 3 - half * 2, 4]
    for at, total in pair_total(keep_hbm, arrived_hbm, units, *scratch):
        if at == 4:
            out[...] = total
        else:
            (own, send)[at // 2][:, :, at % 2 * 128 : at % 2 * 128 + 128] = total


def assemble_kernel(*refs):
    downs, ups, out_hbm, blocks_hbm = refs[:4], refs[4:6], refs[6], refs[7]
    down_ref, up_ref, total_ref, sems, out_sem = refs[8:]
    copies = load(
        [(downs[at], down_ref.at[at]) for at in range(4)]
        + [(ups[at], up_ref.at[at]) for at in range(2)]
        + [(out_hbm, total_ref.at[:, :, pl.ds(384, 128)])],
        sems,
    )
    for copy in copies[:4]:
        copy.wait()
    total = sum(down_ref[step].astype(F32) for step in range(4))
    total_ref[:, :, :128] = total.astype(BF16)
    for copy in copies[4:]:
        copy.wait()
    total_ref[:, :, 128:384] = (up_ref[0].astype(F32) + up_ref[1].astype(F32)).astype(BF16)
    save, = load([(total_ref, blocks_hbm.at[:, :, pl.ds(0, 512)])], out_sem)
    save.wait()


def share_kernel(landed_hbm, qkv_ref, out_ref, up_ref, down_ref, merge_ref, landed_ref, sems):
    parts = [pl.ds(p * 16, 16) for p in range(4)]
    loads = load([(landed_hbm.at[p], landed_ref.at[p]) for p in parts], sems)
    down, up, merge = [0.0] * 4, [0.0] * 2, [0.0] * 4
    shared = 0.0
    for chip in range(64):
        z, y = chip // 16, chip // 2 % 4
        if chip % 16 == 0:
            loads[z].wait()
        block = landed_ref[chip].astype(F32)
        down[z] = down[z] + block[:, :128]
        up[y % 2] = up[y % 2] + block[:, 128:384]
        shared = shared + block[:, 384:896]
        merge[y] = merge[y] + block[:, 896:]
    for block in range(4):
        down_ref[:, block * 128 : block * 128 + 128] = down[block]
        rows = slice(block * 4, block * 4 + 4)
        out_ref[:, block * 128 : block * 128 + 128] = shared[rows, :128]
        qkv_ref[:, block * 384 : block * 384 + 384] = shared[rows, 128:]
        for half in range(2):
            at = block * 512 + half * 256
            up_ref[:, at : at + 256] = up[half][rows]
        for y in range(4):
            merge_ref[y * 4 : y * 4 + 4, block * 256 : block * 256 + 256] = merge[y][rows]


def call(kernel, inputs, held, outputs, saved, scratch, micros, kind=BF16, free=(), aliases=(),
         weight=1, loose=False):
    whole, there = pl.BlockSpec(memory_space=pltpu.VMEM), pl.BlockSpec(memory_space=pltpu.HBM)
    specs = [whole if at < held else there for at in range(len(inputs))]
    for at in free:
        specs[at] = pl.BlockSpec(memory_space=pl.ANY)
    if inputs[0].ndim == 1:
        specs[0] = pl.BlockSpec(memory_space=pltpu.SMEM)
    return pl.pallas_call(
        kernel,
        out_shape=[jax.ShapeDtypeStruct(shape, kind) for shape in outputs],
        in_specs=specs,
        out_specs=[
            pl.BlockSpec(memory_space=pl.ANY) if loose else whole if at < saved else there
            for at in range(len(outputs))
        ],
        scratch_shapes=scratch,
        input_output_aliases=dict(aliases),
        compiler_params=pltpu.CompilerParams(vmem_limit_bytes=(56 if micros > 5 else 14) * 2**20),
        cost_estimate=pl.CostEstimate(
            flops=weight * micros * 10**9, bytes_accessed=micros * 10**6, transcendentals=0
        ),
    )(*inputs)


def vmem(*shape):
    return pltpu.VMEM(shape, BF16)


def dmas(count):
    return pltpu.SemaphoreType.DMA((count,))


def exchanged(send):
    return lax.ppermute(send, "core", [(0, 1), (1, 0)])


def pair_scratch(count):
    return [vmem(count, 64, 16, 128), vmem(count, 64, 16, 128), dmas(count), dmas(count)]


def shifted_block(block, down, right):
    route = []
    for source in range(128):
        row, col = source // 16, source % 16
        route.append((source, (row + down) % 8 * 16 + (col + right) % 16))
    return lax.ppermute(block, GRID, route)


def quadrants(field):
    field = field.transpose(1, 2, 0, 3)
    rows, cols = field.shape[0] // 2, field.shape[1] // 2
    corners = field[:rows, :cols], field[:rows, cols:], field[rows:, :cols], field[rows:, cols:]
    return [corner.reshape(-1, field.shape[-1]) for corner in corners]


def roll_back(tokens, cotangent):
    corners = [
        jnp.concatenate([corner, cot[:, :512], cot[:, 512:]], axis=0)
        for corner, cot in zip(quadrants(tokens), quadrants(cotangent))
    ]
    upper_left, upper_right, lower_left, lower_right = corners
    return [
        lower_right,
        shifted_block(lower_left, 0, -1),
        shifted_block(upper_right, -1, 0),
        shifted_block(upper_left, -1, -1),
    ]


def send_forth(corners):
    upper_left, upper_right, lower_left, lower_right = corners
    return [
        shifted_block(lower_right, 1, 1),
        shifted_block(lower_left, 1, 0),
        shifted_block(upper_right, 0, 1),
        upper_left,
    ]


def from_corners(corners):
    upper = jnp.concatenate(corners[:2], axis=1)
    lower = jnp.concatenate(corners[2:], axis=1)
    return jnp.concatenate([upper, lower], axis=0).transpose(2, 0, 1, 3)


def body(tokens, window_ids, cotangent, w_qkv, w_out, w_up, w_down, w_merge):
    order, cot_order = token_order(), cotangent_order()
    level_order = np.concatenate([cot_order[:, :MERGED], cot_order[:, MERGED:]]).transpose(0, 2, 1)
    by_feature, field, hidden_shape = (512, TOKENS), (TOKENS, 512), (4, TOKENS, 512)
    near_shape, corner = (MERGED, 1536), (PACKED, 512)
    places = window_places()
    where = lax.axis_index(("z", "y", "core")).reshape(1)
    quads = roll_back(tokens, cotangent)

    probs_shape, rest_shape = (16, TOKENS, MAIN), (4, TOKENS, 128)
    packed_shape, down_shape = (12, TOKENS, 128), (4, 64, 16, 128)
    (level_two, grad_after, near0, near1, near2, near3, tokens_in, packed, keys_t, attended,
     first_t, middle, probs, rest, slope, down_keep, down_send) = call(
        forward_kernel,
        [where, jnp.asarray(order, BF16), jnp.asarray(cot_order, BF16), window_ids,
         jnp.asarray(places, BF16), jnp.asarray(places[1].T, F32), *quads, w_qkv,
         w_out, w_up, w_down, w_merge], 6,
        [(MERGED, 1024), field] + [near_shape] * 4 + [field, packed_shape, by_feature, by_feature,
         by_feature, field, probs_shape, rest_shape, hidden_shape, down_shape, down_shape], 2,
        [vmem(4, *corner), pltpu.VMEM((TOKENS, MAIN), F32), pltpu.VMEM((TOKENS, 128), F32),
         vmem(16, 128, MAIN), vmem(4, 128, 128), vmem(*by_feature), vmem(*hidden_shape),
         vmem(*hidden_shape), vmem(*probs_shape), vmem(*rest_shape), vmem(*w_qkv.shape),
         vmem(*w_out.shape), vmem(4, 512, 512), vmem(*w_down.shape), vmem(*w_merge.shape),
         vmem(2, *down_shape), vmem(4, *near_shape), vmem(*field), vmem(*packed_shape),
         vmem(*by_feature), vmem(*by_feature), vmem(*by_feature), vmem(*field),
         pltpu.VMEM(field, F32), dmas(4), dmas(8), dmas(15)],
        20, free=range(6, 10),
    )
    near = [near0]
    for step, block in ((1, near1), (2, near2), (3, near3)):
        near.append(lax.ppermute(block, "y", [(i, (i + step) % 4) for i in range(4)]))
    middle_grad, keep, send = call(
        middle_kernel,
        [where, grad_after, middle, attended, w_down, slope, w_up], 4,
        [field, (5, 64, 16, 128), (5, 64, 16, 128)], 1,
        [vmem(*w_down.shape), vmem(4, TOKENS, 512), vmem(4, 512, 512), vmem(2, 5, 64, 16, 128),
         pltpu.VMEM((4, 512, 512), F32), pltpu.VMEM(field, F32), dmas(12), dmas(4)],
        7,
    )
    down_keep, *near = lax.optimization_barrier((down_keep, *near))
    down_own, *down_sends = call(
        ring_kernel, [where, down_keep, exchanged(down_send)], 1, [(64, 16, 128)] * 4, 4,
        pair_scratch(4), 2, free=(2,), weight=60,
    )
    downs = [down_own]
    for step, block in enumerate(down_sends, 1):
        downs.append(lax.ppermute(block, "z", [(i, (i + step) % 4) for i in range(4)]))
    up_own, up_send, out_sum = call(
        halves_kernel, [where, keep, exchanged(send)], 1,
        [(64, 16, 256), (64, 16, 256), (64, 16, 128)], 3, pair_scratch(5), 2, free=(2,),
    )
    up_arrived = lax.ppermute(up_send, "y", [(i, i ^ 1) for i in range(4)])
    middle_grad, *_ = lax.optimization_barrier((middle_grad, down_own, up_own))
    *corners, late_keep, late_send = call(
        backward_kernel,
        [where, middle_grad, attended, w_out, *near, packed, keys_t, probs, rest, w_qkv, first_t,
         tokens_in, jnp.asarray(order.transpose(0, 2, 1), BF16), jnp.asarray(level_order, BF16),
         level_two], 4,
        [corner] * 4 + [(64, 16, 640)] * 2, 4,
        [vmem(4, TOKENS, 128), vmem(16, 128, MAIN), vmem(4, 128, 128),
         pltpu.VMEM(by_feature, F32), vmem(*by_feature), vmem(*packed_shape), vmem(*probs_shape),
         vmem(4, *near_shape), vmem(*packed_shape), vmem(*by_feature), vmem(*rest_shape),
         vmem(3, 512, 512), vmem(*by_feature), vmem(*field), vmem(4, PACKED, TOKENS),
         vmem(8, PACKED, MERGED), vmem(MERGED, 1024), vmem(2, 64, 16, 640),
         pltpu.VMEM((3, 512, 512), F32), pltpu.VMEM(field, F32), dmas(4), dmas(15), dmas(2)],
        12, free=range(5, 8),
    )
    blocks, = call(
        assemble_kernel, [*downs, up_own, up_arrived, out_sum], 0, [(64, 16, 1152)], 0,
        [vmem(4, 64, 16, 128), vmem(2, 64, 16, 256), vmem(64, 16, 512), dmas(7), dmas(1)], 2,
        free=range(7), weight=60,
        loose=True,
    )
    blocks, = call(
        functools.partial(pair_kernel, place=512),
        [late_keep, exchanged(late_send), blocks], 0, [blocks.shape], 0,
        [vmem(64, 16, 640), vmem(64, 16, 640), dmas(4), dmas(4), dmas(4)], 2, free=(1, 2),
        aliases={2: 0}, loose=True,
    )
    corners = send_forth(corners)
    blocks, *corners = lax.optimization_barrier((blocks, *corners))
    landed = lax.all_to_all(blocks, PAIRS, 0, 0, tiled=True)
    grad_qkv, grad_out, grad_up, grad_down, grad_merge = call(
        share_kernel, [landed], 0, [(4, 1536), (4, 512), (4, 2048), (16, 512), (16, 1024)], 5,
        [vmem(*blocks.shape), dmas(4)], 3, kind=F32,
    )
    grad_tokens = from_corners([c[:MERGED].reshape(6, 6, 2, 512) for c in corners])
    halves = [(c[MERGED : MERGED + 18], c[MERGED + 18 :]) for c in corners]
    level_two = from_corners(
        [jnp.concatenate(pair, axis=1).reshape(3, 3, 2, 1024) for pair in halves]
    )
    return (level_two, grad_tokens, grad_qkv, grad_out, grad_up, grad_down, grad_merge)


def solution(mesh):
    cube = jax.sharding.Mesh(mesh.devices.reshape(4, 2, 4, 2, 2), GRID)
    lat, lon = GRID[:2], GRID[2:]
    field = P(None, lat, lon, None)
    share = P(GRID, None)
    return jax.shard_map(
        body,
        mesh=cube,
        in_specs=(field, P(lat, lon), field, P(), P(), P(), P(), P()),
        out_specs=(field, field, share, share, share, share, share),
        check_vma=False,
    )
```

```python
import functools

import jax
import jax.numpy as jnp
import numpy as np
from jax import lax
from jax.experimental import pallas as pl
from jax.experimental.pallas import tpu as pltpu
from jax.sharding import PartitionSpec as P

HEAD = 32
WIN = 12
TOKENS = 2 * WIN * WIN
MERGED = TOKENS // 4
MAIN = 256
EPS = 1e-05
LOG2E = 1.4426950408889634
QUERY_SCALE = HEAD ** (-0.5) * LOG2E
GRID = ("z", "x_lo", "y", "x_hi", "core")
BF16 = jnp.bfloat16
F32 = jnp.float32

PAIRS = ("z", "x_lo", "y", "x_hi")


PACKED = MERGED + 36


def token_order():
    order = np.zeros((4, TOKENS, PACKED), np.float32)
    for quad in range(4):
        for row in range(6):
            for col in range(6):
                for level in range(2):
                    position = (col % 2) * 2 + row % 2
                    patch = quad * 18 + (row // 2 * 3 + col // 2) * 2 + level
                    order[quad, position * MERGED + patch, (row * 6 + col) * 2 + level] = 1.0
    return order


def window_places():
    places = np.zeros((2, TOKENS, WIN), np.float32)
    for row in range(WIN):
        for col in range(WIN):
            position = (col % 2) * 2 + row % 2
            quad = row // 6 * 2 + col // 6
            patch = quad * 18 + (row % 6 // 2 * 3 + col % 6 // 2) * 2
            for level in range(2):
                places[0, position * MERGED + patch + level, row] = 1.0
                places[1, position * MERGED + patch + level, col] = 1.0
    return places


def cotangent_order():
    order = np.zeros((4, 2 * MERGED, PACKED), np.float32)
    for quad in range(4):
        for half in range(2):
            for patch in range(18):
                order[quad, half * MERGED + quad * 18 + patch, MERGED + half * 18 + patch] = 1.0
    return order


def dot(left, right, left_dim=1, right_dim=0):
    return lax.dot_general(
        left, right, (((left_dim,), (right_dim,)), ((), ())), preferred_element_type=F32
    )


def normalize(wide):
    centered = wide - jnp.mean(wide, axis=-1, keepdims=True)
    inverse_std = lax.rsqrt(jnp.mean(centered * centered, axis=-1, keepdims=True) + EPS)
    return centered * inverse_std, inverse_std


def norm_back(normed, inverse_std, upstream):
    mean_grad = jnp.mean(upstream, axis=-1, keepdims=True)
    mean_cross = jnp.mean(upstream * normed, axis=-1, keepdims=True)
    return inverse_std * (upstream - mean_grad - normed * mean_cross)


def turned(values):
    return jnp.swapaxes(values.astype(F32), 0, 1).astype(BF16)


def own_block(shape):
    rows = lax.broadcasted_iota(jnp.int32, shape, 0) >> 5
    return rows == lax.broadcasted_iota(jnp.int32, shape, 1) >> 5


def spread_rest(values):
    wide = jnp.concatenate([values] * 4, axis=1)
    return jnp.where(own_block(wide.shape), wide, 0.0).astype(BF16)


def gather_rest(blocks):
    kept = jnp.where(own_block(blocks.shape), blocks, 0.0)
    kept = kept + pltpu.roll(kept, 64, 1)
    kept = kept + pltpu.roll(kept, 32, 1)
    return kept[:, :HEAD]


def stack_rest(values):
    tall = jnp.concatenate([values[MAIN:]] * 4, axis=0)
    return jnp.where(own_block(tall.shape), tall, jnp.zeros_like(tall))


def weave(grads, slots, cols):
    tiles = [grad.reshape(64, 8, grad.shape[-1]) for grad in grads]
    turned = [pltpu.roll(tile, 4, 1) for tile in tiles]
    upper = lax.broadcasted_iota(jnp.int32, tiles[0].shape, 1) < 4
    for half in range(2):
        one, two = half * 2, half * 2 + 1
        rows = slice(half * 8, half * 8 + 8)
        slots[0, :, rows, cols] = jnp.where(upper, tiles[one], turned[two]).astype(BF16)
        slots[1, :, rows, cols] = jnp.where(upper, turned[one], tiles[two]).astype(BF16)


def load(pairs, sems):
    copies = [pltpu.make_async_copy(*pair, sems.at[at]) for at, pair in enumerate(pairs)]
    for copy in copies:
        copy.start()
    return copies


def merge_norm(after_mlp):
    pieces = [after_mlp[p * MERGED : (p + 1) * MERGED] for p in range(4)]
    mean = sum(jnp.sum(v, axis=-1, keepdims=True) for v in pieces) / 2048.0
    pieces = [v - mean for v in pieces]
    inverse_out = lax.rsqrt(
        sum(jnp.sum(v * v, axis=-1, keepdims=True) for v in pieces) / 2048.0 + EPS
    )
    return [v * inverse_out for v in pieces], inverse_out


def near_order():
    source = lax.broadcasted_iota(jnp.int32, (512, 1), 0)
    target = lax.broadcasted_iota(jnp.int32, (1, 512), 1)
    place = ((source >> 2) & 3) * 128 + (source >> 4) * 4 + (source & 3)
    return jnp.where(target == place, 1.0, 0.0).astype(BF16)


def gelu_parts(values):
    density = jnp.exp2(values * values * (-0.5 * LOG2E))
    inverse = 1.0 / (1.0 + jnp.abs(values) * (0.3275911 * 0.7071067811865476))
    series = 0.5 * 1.061405429
    for term in (-1.453152027, 1.421413741, -0.284496736, 0.254829592):
        series = series * inverse + 0.5 * term
    tail = series * inverse * density
    return jnp.where(values < 0.0, tail, 1.0 - tail), density


def forward_kernel(
    where_ref, order_ref, cot_order_ref, ids_ref, places_ref, cols_t_ref,
    quad0_hbm, quad1_hbm, quad2_hbm, quad3_hbm, w_qkv_hbm, w_out_hbm, w_up_hbm, w_down_hbm,
    w_merge_hbm,
    level_two_ref, grad_after_ref, near0, near1, near2, near3, tokens_hbm, packed_hbm, keys_t_hbm,
    attended_hbm, first_t_hbm, middle_hbm, probs_hbm, rest_hbm, slope_hbm, keep_hbm, send_hbm,
    quads_ref, bias_ref, bias_rest, query_t, query_rest, values_t, slope_ref, hidden_ref,
    probs_ref, rest_ref, w_qkv, w_out, w_up, w_down, w_merge, slots, near_ref, tokens_ref,
    packed_ref, keys_t_ref, attended_ref, first_t_ref, middle_ref, quad_sems, in_sems, out_sems,
):
    saves = []

    def save(*pairs):
        saves.extend(load(pairs, out_sems.at[pl.ds(len(saves), len(pairs))]))

    quads = (quad0_hbm, quad1_hbm, quad2_hbm, quad3_hbm)
    quads = load([(quads[q], quads_ref.at[q]) for q in range(4)], quad_sems)
    weights = load(
        [(w_qkv_hbm, w_qkv), (w_out_hbm, w_out), (w_up_hbm, w_up), (w_down_hbm, w_down),
         (w_merge_hbm, w_merge)],
        in_sems,
    )
    query_t[...] = jnp.zeros_like(query_t)
    ids = ids_ref[...].astype(F32).astype(BF16)
    by_row = dot(places_ref[0], ids) * places_ref[1].astype(F32)
    by_col = dot(ids, places_ref[0], 0, 1) * cols_t_ref[...]
    by_row = jnp.sum(by_row, axis=1, keepdims=True)
    by_col = jnp.sum(by_col, axis=0, keepdims=True)
    rest = jnp.concatenate([by_col[:, MAIN:]] * 4, axis=1)
    bias_ref[...] = jnp.where(by_row == by_col[:, :MAIN], 0.0, -1e30)
    bias_rest[...] = jnp.where(by_row == rest, 0.0, -1e30)
    for quad in quads:
        quad.wait()
    tokens = sum(dot(order_ref[q], quads_ref[q]) for q in range(4))
    tokens_ref[...] = tokens.astype(BF16)
    halves = sum(dot(cot_order_ref[q], quads_ref[q]) for q in range(4))
    cotangent = jnp.concatenate([halves[:MERGED], halves[MERGED:]], axis=1).astype(BF16)
    normed_in = normalize(tokens)[0]
    first_norm = normed_in.astype(BF16)
    first_t_ref[...] = turned(normed_in)
    save((tokens_ref, tokens_hbm), (first_t_ref, first_t_hbm))
    weights[0].wait()
    for part in range(3):
        wide = dot(first_norm, w_qkv[:, part * 512 : part * 512 + 512])
        wide = wide * QUERY_SCALE if part == 0 else wide
        for group in range(4):
            packed_ref[part * 4 + group] = wide[:, group * 128 : group * 128 + 128].astype(BF16)
        by_feature = jnp.swapaxes(wide, 0, 1)
        if part:
            (keys_t_ref, values_t)[part - 1][...] = by_feature.astype(BF16)
            continue
        for head in range(16):
            rows = slice(head % 4 * HEAD, head % 4 * HEAD + HEAD)
            own = by_feature[head * HEAD : head * HEAD + HEAD, :MAIN]
            query_t[head, rows, :] = own.astype(BF16)
        for group in range(4):
            rest = by_feature[group * 128 : group * 128 + 128, MAIN:]
            query_rest[group] = spread_rest(rest)
    save((packed_ref, packed_hbm), (keys_t_ref, keys_t_hbm))

    def scores_of(at):
        group, head = at // 5, at % 5
        turn = query_rest[group] if head == 4 else query_t[group * 4 + head]
        return dot(packed_ref[4 + group], turn)

    ahead = scores_of(0)
    for at in range(20):
        group, head = at // 5, at % 5
        scores = ahead + (bias_rest if head == 4 else bias_ref)[...]
        if at < 19:
            ahead = scores_of(at + 1)
        raised = jnp.exp2(scores - jnp.max(scores, axis=0, keepdims=True))
        inverse = 1.0 / jnp.sum(raised, axis=0, keepdims=True)
        probs = (raised * inverse).astype(BF16)
        if head == 4:
            rest_ref[group] = probs
            rows = slice(group * 128, group * 128 + 128)
            rest = gather_rest(dot(values_t[rows, :], probs))
            attended_ref[rows, MAIN:] = rest.astype(BF16)
        else:
            probs_ref[group * 4 + head] = probs
            rows = slice(group * 128 + head * HEAD, group * 128 + head * HEAD + HEAD)
            attended_ref[rows, :MAIN] = dot(values_t[rows, :], probs).astype(BF16)
    save((probs_ref, probs_hbm), (rest_ref, rest_hbm), (attended_ref, attended_hbm))

    attended = turned(attended_ref[...])
    weights[1].wait()
    attn_out = dot(attended, w_out[...]).astype(BF16)
    narrow_middle = (tokens + attn_out.astype(F32)).astype(BF16)
    middle_ref[...] = narrow_middle
    save((middle_ref, middle_hbm))
    middle = narrow_middle.astype(F32)
    second_norm = normalize(middle)[0].astype(BF16)
    mlp = jnp.zeros((TOKENS, 512), F32)
    weights[2].wait()
    weights[3].wait()
    ahead = dot(second_norm, w_up[:, :512])
    for part in range(4):
        cols = slice(part * 512, part * 512 + 512)
        before = ahead
        if part < 3:
            ahead = dot(second_norm, w_up[:, part * 512 + 512 : part * 512 + 1024])
        cumulative, density = gelu_parts(before)
        hidden = (before * cumulative).astype(BF16)
        hidden_ref[:, cols] = hidden
        slope_ref[:, cols] = (cumulative + before * density * 0.3989422804014327).astype(BF16)
        mlp = mlp + dot(hidden, w_down[cols])
    save((slope_ref, slope_hbm))
    after_mlp = (middle + mlp).astype(BF16)
    pieces, inverse_out = merge_norm(after_mlp.astype(F32))
    merged_norm = [v.astype(BF16) for v in pieces]
    order = near_order()
    spread = [dot(v, order) for v in merged_norm]
    blocks = [
        jnp.concatenate([v[:, at * 128 : at * 128 + 128] for v in spread], axis=1).astype(BF16)
        for at in range(4)
    ]
    y = (where_ref[0] >> 1) & 3
    for step, near in enumerate((near0, near1, near2, near3)):
        block = blocks[step]
        for own in range(1, 4):
            block = jnp.where(y == own, blocks[(own + step) % 4], block)
        near_ref[step, :, :512] = block
        near_ref[step, :, 512:] = cotangent
        save((near_ref.at[step], near))

    weights[4].wait()
    level_two_ref[...] = sum(
        dot(merged_norm[p], w_merge[p * 512 : p * 512 + 512]) for p in range(4)
    ).astype(BF16)
    upstream = [dot(cotangent, w_merge[p * 512 : p * 512 + 512], 1, 1) for p in range(4)]
    mean_grad = sum(jnp.sum(v, axis=-1, keepdims=True) for v in upstream) / 2048.0
    mean_cross = (
        sum(jnp.sum(v * u, axis=-1, keepdims=True) for v, u in zip(upstream, pieces)) / 2048.0
    )
    grad_after = jnp.concatenate(
        [inverse_out * (v - mean_grad - u * mean_cross) for v, u in zip(upstream, pieces)], axis=0
    ).astype(BF16)
    grad_after_ref[...] = grad_after
    core = where_ref[0] & 1
    for part in range(4):
        grad = dot(hidden_ref[:, part * 512 : part * 512 + 512], grad_after, 0, 0).astype(BF16)
        grad = grad.reshape(16, 2, 16, 512)
        for unit in range(4):
            for parity in range(2):
                slots[parity, unit, part * 16 : part * 16 + 16] = grad[
                    :, parity, :, unit * 128 : unit * 128 + 128
                ]
    save((slots.at[core], keep_hbm), (slots.at[1 - core], send_hbm))
    for copy in saves:
        copy.wait()


def middle_kernel(
    where_ref, grad_after_ref, middle_ref, attended_ref, w_down_hbm, slope_hbm, w_up_hbm,
    middle_grad_ref, keep_hbm, send_hbm,
    w_down, slope_ref, w_up, slots, sems, out_sems,
):
    loads = []
    for part in range(4):
        cols = pl.ds(part * 512, 512)
        pairs = [(w_down_hbm.at[cols], w_down.at[cols])]
        pairs += [(slope_hbm.at[:, cols], slope_ref.at[part])]
        pairs += [(w_up_hbm.at[:, cols], w_up.at[part])]
        loads.append(load(pairs, sems.at[pl.ds(part * 3, 3)]))
    core = where_ref[0] & 1
    grad_after = grad_after_ref[...]
    normed_mid, inverse_mid = normalize(middle_ref[...].astype(F32))
    second_t = turned(normed_mid)

    def save(units, at):
        return load(
            [(slots.at[core, units], keep_hbm.at[units]),
             (slots.at[1 - core, units], send_hbm.at[units])],
            out_sems.at[pl.ds(at, 2)],
        )

    back_up = jnp.zeros((TOKENS, 512), F32)
    grads_up = []
    for part in range(4):
        cols = slice(part * 512, part * 512 + 512)
        for copy in loads[part]:
            copy.wait()
        grad_before = (
            dot(grad_after, w_down[cols], 1, 1) * slope_ref[part].astype(F32)
        ).astype(BF16)
        grads_up.append(dot(second_t, grad_before))
        back_up = back_up + dot(grad_before, w_up[part], 1, 1)
    for unit in range(4):
        cols = slice(unit * 128, unit * 128 + 128)
        weave([grad[:, cols] for grad in grads_up], slots.at[:, unit], slice(0, 128))
    saves = save(pl.ds(0, 4), 0)
    middle_grad = (
        grad_after.astype(F32) + norm_back(normed_mid, inverse_mid, back_up)
    ).astype(BF16)
    middle_grad_ref[...] = middle_grad
    grad = dot(attended_ref[...], middle_grad)
    columns = [grad[:, p * 128 : p * 128 + 128] for p in range(4)]
    weave(columns, slots.at[:, 4], slice(0, 128))
    saves += save(pl.ds(4, 1), 2)
    for copy in saves:
        copy.wait()


def backward_kernel(
    where_ref, middle_grad_ref, attended_ref, w_out,
    near0_hbm, near1_hbm, near2_hbm, near3_hbm, packed_hbm, keys_t_hbm, probs_hbm, rest_hbm,
    w_qkv_hbm, first_t_hbm, tokens_hbm, order_hbm, level_order_hbm, level_two_hbm,
    out0, out1, out2, out3, keep_hbm, send_hbm,
    grad_heads, grad_heads_t, grad_heads_rest, products, query_grad_t, packed_grad, probs_ref,
    near_ref, packed_ref, keys_t_ref, rest_ref, w_qkv, first_t_ref, tokens_ref, order_ref,
    level_order_ref, level_two_ref, slots, near_sems, sems, out_sems,
):
    loads = load(
        [(packed_hbm, packed_ref), (keys_t_hbm, keys_t_ref), (rest_hbm, rest_ref)]
        + [(probs_hbm.at[pl.ds(g * 4, 4)], probs_ref.at[pl.ds(g * 4, 4)]) for g in range(4)]
        + [(w_qkv_hbm, w_qkv), (first_t_hbm, first_t_ref), (tokens_hbm, tokens_ref),
           (order_hbm, order_ref), (level_order_hbm, level_order_ref),
           (level_two_hbm, level_two_ref)],
        sems,
    )
    nears = (near0_hbm, near1_hbm, near2_hbm, near3_hbm)
    nears = load([(nears[step], near_ref.at[step]) for step in range(4)], near_sems)
    core = where_ref[0] & 1
    middle_grad = middle_grad_ref[...]
    wide = dot(middle_grad, w_out[...], 1, 1).astype(BF16)
    for group in range(4):
        grad_heads[group] = wide[:, group * 128 : group * 128 + 128]
    upstream_t = dot(w_out[...], middle_grad, 1, 1).astype(BF16)
    products[...] = upstream_t.astype(F32) * attended_ref[...].astype(F32)
    grad_heads_t[...] = jnp.zeros_like(grad_heads_t)
    for head in range(16):
        rows = slice(head % 4 * HEAD, head % 4 * HEAD + HEAD)
        grad_heads_t[head, rows, :] = upstream_t[head * HEAD : head * HEAD + HEAD, :MAIN]
    for group in range(4):
        rest = upstream_t[group * 128 : group * 128 + 128].astype(F32)
        grad_heads_rest[group] = spread_rest(rest[:, MAIN:])

    head_of_lane = lax.broadcasted_iota(jnp.int32, (TOKENS, 128), 1) >> 5
    for copy in loads[:3]:
        copy.wait()
    for group in range(4):
        loads[3 + group].wait()
        rows = slice(group * 128, group * 128 + 128)
        queries = packed_ref[group]
        values = packed_ref[8 + group]
        upstream = grad_heads[group]
        grad_keys = jnp.zeros((TOKENS, 128), F32)
        grad_values = jnp.zeros((TOKENS, 128), F32)
        totals = []
        for part in range(4):
            head = group * 4 + part
            at = slice(head * HEAD, head * HEAD + HEAD)
            weights = probs_ref[head]
            total = jnp.sum(products[at, :], axis=0, keepdims=True)
            totals.append(total[:, MAIN:])
            grad_weights = dot(values, grad_heads_t[head])
            scores = (weights.astype(F32) * (grad_weights - total[:, :MAIN])).astype(BF16)
            in_head = head_of_lane == part
            grad_keys = jnp.where(in_head, dot(scores, queries[:MAIN]), grad_keys)
            grad_values = jnp.where(in_head, dot(weights, upstream[:MAIN]), grad_values)
            query_grad = dot(keys_t_ref[at, :], scores) * HEAD ** (-0.5)
            query_grad_t[at, :MAIN] = query_grad.astype(BF16)
        weights = rest_ref[group]
        total = jnp.concatenate(totals, axis=1)
        grad_weights = dot(values, grad_heads_rest[group])
        scores = (weights.astype(F32) * (grad_weights - total)).astype(BF16)
        grad_keys = grad_keys + dot(scores, stack_rest(queries))
        grad_values = grad_values + dot(weights, stack_rest(upstream))
        query_grad = gather_rest(dot(keys_t_ref[rows, :], scores)) * HEAD ** (-0.5)
        query_grad_t[rows, MAIN:] = query_grad.astype(BF16)
        packed_grad[4 + group] = (grad_keys * (1 / LOG2E)).astype(BF16)
        packed_grad[8 + group] = grad_values.astype(BF16)

    for copy in nears:
        copy.wait()
    near = jnp.concatenate([near_ref[step].astype(F32) for step in range(4)], axis=0).astype(BF16)
    grad = dot(near[:, :512], near[:, 512:], 0, 0)
    weave([grad[:, q * 256 : q * 256 + 256] for q in range(4)], slots, slice(384, 640))

    for group in range(4):
        packed_grad[group] = turned(query_grad_t[group * 128 : group * 128 + 128, :])
    for copy in loads[7:]:
        copy.wait()
    first_t = first_t_ref[...]
    back_qkv = jnp.zeros((TOKENS, 512), F32)
    grads = []
    for part in range(3):
        wide = jnp.concatenate([packed_grad[part * 4 + g] for g in range(4)], axis=1)
        grad = dot(first_t, wide)
        grads += [grad[:, q * 128 : q * 128 + 128] for q in range(4)]
        back_qkv = back_qkv + dot(wide, w_qkv[:, part * 512 : part * 512 + 512], 1, 1)
    for part in range(3):
        weave([grads[q * 3 + part] for q in range(4)], slots, slice(part * 128, part * 128 + 128))
    saves = load([(slots.at[core], keep_hbm), (slots.at[1 - core], send_hbm)], out_sems)

    normed_in, inverse_in = normalize(tokens_ref[...].astype(F32))
    grad_first = back_qkv.astype(BF16).astype(F32)
    grad_tokens = (
        middle_grad.astype(F32) + norm_back(normed_in, inverse_in, grad_first)
    ).astype(BF16)
    for quad, out in enumerate((out0, out1, out2, out3)):
        rows = dot(order_ref[quad], grad_tokens)
        for half in range(2):
            level_two = level_two_ref[:, half * 512 : half * 512 + 512]
            rows = rows + dot(level_order_ref[half * 4 + quad], level_two)
        out[...] = rows.astype(BF16)
    for copy in saves:
        copy.wait()


def pair_kernel(keep_hbm, arrived_hbm, *refs, place):
    blocks_hbm, keep_ref, arrived_ref, keep_sems, arrived_sems, out_sems = refs[-6:]
    cols = pl.ds(place, keep_hbm.shape[-1])
    parts = [pl.ds(p * 16, 16) for p in range(4)]
    keeps = load([(keep_hbm.at[p], keep_ref.at[p]) for p in parts], keep_sems)
    arrivals = load([(arrived_hbm.at[p], arrived_ref.at[p]) for p in parts], arrived_sems)
    saves = []
    for part, rows in enumerate(parts):
        keeps[part].wait()
        arrivals[part].wait()
        total = keep_ref[rows].astype(F32) + arrived_ref[rows].astype(F32)
        keep_ref[rows] = total.astype(BF16)
        saves += load(
            [(keep_ref.at[rows], blocks_hbm.at[rows, :, cols])], out_sems.at[pl.ds(part, 1)]
        )
    for save in saves:
        save.wait()


def pair_total(keep_hbm, arrived_hbm, units, keep_ref, arrived_ref, keep_sems, arrived_sems):
    keeps = [(keep_hbm.at[unit], keep_ref.at[at]) for at, unit in enumerate(units)]
    arrivals = [(arrived_hbm.at[unit], arrived_ref.at[at]) for at, unit in enumerate(units)]
    copies = list(zip(load(keeps, keep_sems), load(arrivals, arrived_sems)))
    for at in range(len(units)):
        for copy in copies[at]:
            copy.wait()
        yield at, (keep_ref[at].astype(F32) + arrived_ref[at].astype(F32)).astype(BF16)


def ring_kernel(where_ref, keep_hbm, arrived_hbm, own, send1, send2, send3, *scratch):
    z = where_ref[0] >> 3
    units = [(z + step) & 3 for step in range(4)]
    for at, total in pair_total(keep_hbm, arrived_hbm, units, *scratch):
        (own, send1, send2, send3)[at][...] = total


def halves_kernel(where_ref, keep_hbm, arrived_hbm, own, send, out, *scratch):
    half = (where_ref[0] >> 1) & 1
    units = [half * 2, half * 2 + 1, 2 - half * 2, 3 - half * 2, 4]
    for at, total in pair_total(keep_hbm, arrived_hbm, units, *scratch):
        if at == 4:
            out[...] = total
        else:
            (own, send)[at // 2][:, :, at % 2 * 128 : at % 2 * 128 + 128] = total


def assemble_kernel(*refs):
    downs, ups, out_hbm, blocks_hbm = refs[:4], refs[4:6], refs[6], refs[7]
    down_ref, up_ref, total_ref, sems, out_sem = refs[8:]
    copies = load(
        [(downs[at], down_ref.at[at]) for at in range(4)]
        + [(ups[at], up_ref.at[at]) for at in range(2)]
        + [(out_hbm, total_ref.at[:, :, pl.ds(384, 128)])],
        sems,
    )
    for copy in copies[:4]:
        copy.wait()
    total = sum(down_ref[step].astype(F32) for step in range(4))
    total_ref[:, :, :128] = total.astype(BF16)
    for copy in copies[4:]:
        copy.wait()
    total_ref[:, :, 128:384] = (up_ref[0].astype(F32) + up_ref[1].astype(F32)).astype(BF16)
    save, = load([(total_ref, blocks_hbm.at[:, :, pl.ds(0, 512)])], out_sem)
    save.wait()


def share_kernel(landed_hbm, qkv_ref, out_ref, up_ref, down_ref, merge_ref, landed_ref, sems):
    parts = [pl.ds(p * 16, 16) for p in range(4)]
    loads = load([(landed_hbm.at[p], landed_ref.at[p]) for p in parts], sems)
    down, up, merge = [0.0] * 4, [0.0] * 2, [0.0] * 4
    shared = 0.0
    for chip in range(64):
        z, y = chip // 16, chip // 2 % 4
        if chip % 16 == 0:
            loads[z].wait()
        block = landed_ref[chip].astype(F32)
        down[z] = down[z] + block[:, :128]
        up[y % 2] = up[y % 2] + block[:, 128:384]
        shared = shared + block[:, 384:896]
        merge[y] = merge[y] + block[:, 896:]
    for block in range(4):
        down_ref[:, block * 128 : block * 128 + 128] = down[block]
        rows = slice(block * 4, block * 4 + 4)
        out_ref[:, block * 128 : block * 128 + 128] = shared[rows, :128]
        qkv_ref[:, block * 384 : block * 384 + 384] = shared[rows, 128:]
        for half in range(2):
            at = block * 512 + half * 256
            up_ref[:, at : at + 256] = up[half][rows]
        for y in range(4):
            merge_ref[y * 4 : y * 4 + 4, block * 256 : block * 256 + 256] = merge[y][rows]


def call(kernel, inputs, held, outputs, saved, scratch, micros, kind=BF16, free=(), aliases=(),
         weight=1, loose=False):
    whole, there = pl.BlockSpec(memory_space=pltpu.VMEM), pl.BlockSpec(memory_space=pltpu.HBM)
    specs = [whole if at < held else there for at in range(len(inputs))]
    for at in free:
        specs[at] = pl.BlockSpec(memory_space=pl.ANY)
    if inputs[0].ndim == 1:
        specs[0] = pl.BlockSpec(memory_space=pltpu.SMEM)
    return pl.pallas_call(
        kernel,
        out_shape=[jax.ShapeDtypeStruct(shape, kind) for shape in outputs],
        in_specs=specs,
        out_specs=[
            pl.BlockSpec(memory_space=pl.ANY) if loose else whole if at < saved else there
            for at in range(len(outputs))
        ],
        scratch_shapes=scratch,
        input_output_aliases=dict(aliases),
        compiler_params=pltpu.CompilerParams(vmem_limit_bytes=(56 if micros > 5 else 14) * 2**20),
        cost_estimate=pl.CostEstimate(
            flops=weight * micros * 10**9, bytes_accessed=micros * 10**6, transcendentals=0
        ),
    )(*inputs)


def vmem(*shape):
    return pltpu.VMEM(shape, BF16)


def dmas(count):
    return pltpu.SemaphoreType.DMA((count,))


def exchanged(send):
    return lax.ppermute(send, "core", [(0, 1), (1, 0)])


def pair_scratch(count):
    return [vmem(count, 64, 16, 128), vmem(count, 64, 16, 128), dmas(count), dmas(count)]


def shifted_block(block, down, right):
    route = []
    for source in range(128):
        row, col = source // 16, source % 16
        route.append((source, (row + down) % 8 * 16 + (col + right) % 16))
    return lax.ppermute(block, GRID, route)


def quadrants(field):
    field = field.transpose(1, 2, 0, 3)
    rows, cols = field.shape[0] // 2, field.shape[1] // 2
    corners = field[:rows, :cols], field[:rows, cols:], field[rows:, :cols], field[rows:, cols:]
    return [corner.reshape(-1, field.shape[-1]) for corner in corners]


def roll_back(tokens, cotangent):
    corners = [
        jnp.concatenate([corner, cot[:, :512], cot[:, 512:]], axis=0)
        for corner, cot in zip(quadrants(tokens), quadrants(cotangent))
    ]
    upper_left, upper_right, lower_left, lower_right = corners
    return [
        lower_right,
        shifted_block(lower_left, 0, -1),
        shifted_block(upper_right, -1, 0),
        shifted_block(upper_left, -1, -1),
    ]


def send_forth(corners):
    upper_left, upper_right, lower_left, lower_right = corners
    return [
        shifted_block(lower_right, 1, 1),
        shifted_block(lower_left, 1, 0),
        shifted_block(upper_right, 0, 1),
        upper_left,
    ]


def from_corners(corners):
    upper = jnp.concatenate(corners[:2], axis=1)
    lower = jnp.concatenate(corners[2:], axis=1)
    return jnp.concatenate([upper, lower], axis=0).transpose(2, 0, 1, 3)


def body(tokens, window_ids, cotangent, w_qkv, w_out, w_up, w_down, w_merge):
    order, cot_order = token_order(), cotangent_order()
    level_order = np.concatenate([cot_order[:, :MERGED], cot_order[:, MERGED:]]).transpose(0, 2, 1)
    by_feature, field, hidden_shape = (512, TOKENS), (TOKENS, 512), (TOKENS, 2048)
    near_shape, corner = (MERGED, 1536), (PACKED, 512)
    places = window_places()
    where = lax.axis_index(("z", "y", "core")).reshape(1)
    quads = roll_back(tokens, cotangent)

    probs_shape, rest_shape = (16, TOKENS, MAIN), (4, TOKENS, 128)
    packed_shape, down_shape = (12, TOKENS, 128), (4, 64, 16, 128)
    (level_two, grad_after, near0, near1, near2, near3, tokens_in, packed, keys_t, attended,
     first_t, middle, probs, rest, slope, down_keep, down_send) = call(
        forward_kernel,
        [where, jnp.asarray(order, BF16), jnp.asarray(cot_order, BF16), window_ids,
         jnp.asarray(places, BF16), jnp.asarray(places[1].T, F32), *quads, w_qkv,
         w_out, w_up, w_down, w_merge], 6,
        [(MERGED, 1024), field] + [near_shape] * 4 + [field, packed_shape, by_feature, by_feature,
         by_feature, field, probs_shape, rest_shape, hidden_shape, down_shape, down_shape], 2,
        [vmem(4, *corner), pltpu.VMEM((TOKENS, MAIN), F32), pltpu.VMEM((TOKENS, 128), F32),
         vmem(16, 128, MAIN), vmem(4, 128, 128), vmem(*by_feature), vmem(*hidden_shape),
         vmem(*hidden_shape), vmem(*probs_shape), vmem(*rest_shape), vmem(*w_qkv.shape),
         vmem(*w_out.shape), vmem(*w_up.shape), vmem(*w_down.shape), vmem(*w_merge.shape),
         vmem(2, *down_shape), vmem(4, *near_shape), vmem(*field), vmem(*packed_shape),
         vmem(*by_feature), vmem(*by_feature), vmem(*by_feature), vmem(*field),
         dmas(4), dmas(5), dmas(15)],
        20, free=range(6, 10),
    )
    near = [near0]
    for step, block in ((1, near1), (2, near2), (3, near3)):
        near.append(lax.ppermute(block, "y", [(i, (i + step) % 4) for i in range(4)]))
    middle_grad, keep, send = call(
        middle_kernel,
        [where, grad_after, middle, attended, w_down, slope, w_up], 4,
        [field, (5, 64, 16, 128), (5, 64, 16, 128)], 1,
        [vmem(*w_down.shape), vmem(4, TOKENS, 512), vmem(4, 512, 512), vmem(2, 5, 64, 16, 128),
         dmas(12), dmas(4)],
        7,
    )
    down_keep, *near = lax.optimization_barrier((down_keep, *near))
    down_own, *down_sends = call(
        ring_kernel, [where, down_keep, exchanged(down_send)], 1, [(64, 16, 128)] * 4, 4,
        pair_scratch(4), 2, free=(2,), weight=60,
    )
    downs = [down_own]
    for step, block in enumerate(down_sends, 1):
        downs.append(lax.ppermute(block, "z", [(i, (i + step) % 4) for i in range(4)]))
    up_own, up_send, out_sum = call(
        halves_kernel, [where, keep, exchanged(send)], 1,
        [(64, 16, 256), (64, 16, 256), (64, 16, 128)], 3, pair_scratch(5), 2, free=(2,),
    )
    up_arrived = lax.ppermute(up_send, "y", [(i, i ^ 1) for i in range(4)])
    middle_grad, *_ = lax.optimization_barrier((middle_grad, down_own, up_own))
    *corners, late_keep, late_send = call(
        backward_kernel,
        [where, middle_grad, attended, w_out, *near, packed, keys_t, probs, rest, w_qkv, first_t,
         tokens_in, jnp.asarray(order.transpose(0, 2, 1), BF16), jnp.asarray(level_order, BF16),
         level_two], 4,
        [corner] * 4 + [(64, 16, 640)] * 2, 4,
        [vmem(4, TOKENS, 128), vmem(16, 128, MAIN), vmem(4, 128, 128),
         pltpu.VMEM(by_feature, F32), vmem(*by_feature), vmem(*packed_shape), vmem(*probs_shape),
         vmem(4, *near_shape), vmem(*packed_shape), vmem(*by_feature), vmem(*rest_shape),
         vmem(*w_qkv.shape), vmem(*by_feature), vmem(*field), vmem(4, PACKED, TOKENS),
         vmem(8, PACKED, MERGED), vmem(MERGED, 1024), vmem(2, 64, 16, 640),
         dmas(4), dmas(13), dmas(2)],
        12, free=range(5, 8),
    )
    blocks, = call(
        assemble_kernel, [*downs, up_own, up_arrived, out_sum], 0, [(64, 16, 1152)], 0,
        [vmem(4, 64, 16, 128), vmem(2, 64, 16, 256), vmem(64, 16, 512), dmas(7), dmas(1)], 2,
        free=range(7), weight=60,
        loose=True,
    )
    blocks, *corners = lax.optimization_barrier((blocks, *corners))
    blocks, = call(
        functools.partial(pair_kernel, place=512),
        [late_keep, exchanged(late_send), blocks], 0, [blocks.shape], 0,
        [vmem(64, 16, 640), vmem(64, 16, 640), dmas(4), dmas(4), dmas(4)], 2, free=(1, 2),
        aliases={2: 0}, loose=True,
    )
    corners = send_forth(corners)
    blocks, *corners = lax.optimization_barrier((blocks, *corners))
    landed = lax.all_to_all(blocks, PAIRS, 0, 0, tiled=True)
    grad_qkv, grad_out, grad_up, grad_down, grad_merge = call(
        share_kernel, [landed], 0, [(4, 1536), (4, 512), (4, 2048), (16, 512), (16, 1024)], 5,
        [vmem(*blocks.shape), dmas(4)], 3, kind=F32,
    )
    grad_tokens = from_corners([c[:MERGED].reshape(6, 6, 2, 512) for c in corners])
    halves = [(c[MERGED : MERGED + 18], c[MERGED + 18 :]) for c in corners]
    level_two = from_corners(
        [jnp.concatenate(pair, axis=1).reshape(3, 3, 2, 1024) for pair in halves]
    )
    return (level_two, grad_tokens, grad_qkv, grad_out, grad_up, grad_down, grad_merge)


def solution(mesh):
    cube = jax.sharding.Mesh(mesh.devices.reshape(4, 2, 4, 2, 2), GRID)
    lat, lon = GRID[:2], GRID[2:]
    field = P(None, lat, lon, None)
    share = P(GRID, None)
    return jax.shard_map(
        body,
        mesh=cube,
        in_specs=(field, P(lat, lon), field, P(), P(), P(), P(), P()),
        out_specs=(field, field, share, share, share, share, share),
        check_vma=False,
    )
```

```python
import functools

import jax
import jax.numpy as jnp
import numpy as np
from jax import lax
from jax.experimental import pallas as pl
from jax.experimental.pallas import tpu as pltpu
from jax.sharding import PartitionSpec as P

HEAD = 32
WIN = 12
TOKENS = 2 * WIN * WIN
MERGED = TOKENS // 4
MAIN = 256
EPS = 1e-05
LOG2E = 1.4426950408889634
QUERY_SCALE = HEAD ** (-0.5) * LOG2E
GRID = ("z", "x_lo", "y", "x_hi", "core")
BF16 = jnp.bfloat16
F32 = jnp.float32

PAIRS = ("z", "x_lo", "y", "x_hi")


PACKED = MERGED + 36


def token_order():
    order = np.zeros((4, TOKENS, PACKED), np.float32)
    for quad in range(4):
        for row in range(6):
            for col in range(6):
                for level in range(2):
                    position = (col % 2) * 2 + row % 2
                    patch = quad * 18 + (row // 2 * 3 + col // 2) * 2 + level
                    order[quad, position * MERGED + patch, (row * 6 + col) * 2 + level] = 1.0
    return order


def window_places():
    places = np.zeros((2, TOKENS, WIN), np.float32)
    for row in range(WIN):
        for col in range(WIN):
            position = (col % 2) * 2 + row % 2
            quad = row // 6 * 2 + col // 6
            patch = quad * 18 + (row % 6 // 2 * 3 + col % 6 // 2) * 2
            for level in range(2):
                places[0, position * MERGED + patch + level, row] = 1.0
                places[1, position * MERGED + patch + level, col] = 1.0
    return places


def cotangent_order():
    order = np.zeros((4, 2 * MERGED, PACKED), np.float32)
    for quad in range(4):
        for half in range(2):
            for patch in range(18):
                order[quad, half * MERGED + quad * 18 + patch, MERGED + half * 18 + patch] = 1.0
    return order


def dot(left, right, left_dim=1, right_dim=0):
    return lax.dot_general(
        left, right, (((left_dim,), (right_dim,)), ((), ())), preferred_element_type=F32
    )


def normalize(wide):
    centered = wide - jnp.mean(wide, axis=-1, keepdims=True)
    inverse_std = lax.rsqrt(jnp.mean(centered * centered, axis=-1, keepdims=True) + EPS)
    return centered * inverse_std, inverse_std


def norm_back(normed, inverse_std, upstream):
    mean_grad = jnp.mean(upstream, axis=-1, keepdims=True)
    mean_cross = jnp.mean(upstream * normed, axis=-1, keepdims=True)
    return inverse_std * (upstream - mean_grad - normed * mean_cross)


def turned(values):
    return jnp.swapaxes(values.astype(F32), 0, 1).astype(BF16)


def own_block(shape):
    rows = lax.broadcasted_iota(jnp.int32, shape, 0) >> 5
    return rows == lax.broadcasted_iota(jnp.int32, shape, 1) >> 5


def spread_rest(values):
    wide = jnp.concatenate([values] * 4, axis=1)
    return jnp.where(own_block(wide.shape), wide, 0.0).astype(BF16)


def gather_rest(blocks):
    kept = jnp.where(own_block(blocks.shape), blocks, 0.0)
    kept = kept + pltpu.roll(kept, 64, 1)
    kept = kept + pltpu.roll(kept, 32, 1)
    return kept[:, :HEAD]


def stack_rest(values):
    tall = jnp.concatenate([values[MAIN:]] * 4, axis=0)
    return jnp.where(own_block(tall.shape), tall, jnp.zeros_like(tall))


def weave(grads, slots, cols):
    tiles = [grad.reshape(64, 8, grad.shape[-1]) for grad in grads]
    turned = [pltpu.roll(tile, 4, 1) for tile in tiles]
    upper = lax.broadcasted_iota(jnp.int32, tiles[0].shape, 1) < 4
    for half in range(2):
        one, two = half * 2, half * 2 + 1
        rows = slice(half * 8, half * 8 + 8)
        slots[0, :, rows, cols] = jnp.where(upper, tiles[one], turned[two]).astype(BF16)
        slots[1, :, rows, cols] = jnp.where(upper, turned[one], tiles[two]).astype(BF16)


def load(pairs, sems):
    copies = [pltpu.make_async_copy(*pair, sems.at[at]) for at, pair in enumerate(pairs)]
    for copy in copies:
        copy.start()
    return copies


def merge_norm(after_mlp):
    pieces = [after_mlp[p * MERGED : (p + 1) * MERGED] for p in range(4)]
    mean = sum(jnp.sum(v, axis=-1, keepdims=True) for v in pieces) / 2048.0
    pieces = [v - mean for v in pieces]
    inverse_out = lax.rsqrt(
        sum(jnp.sum(v * v, axis=-1, keepdims=True) for v in pieces) / 2048.0 + EPS
    )
    return [v * inverse_out for v in pieces], inverse_out


def near_order():
    source = lax.broadcasted_iota(jnp.int32, (512, 1), 0)
    target = lax.broadcasted_iota(jnp.int32, (1, 512), 1)
    place = ((source >> 2) & 3) * 128 + (source >> 4) * 4 + (source & 3)
    return jnp.where(target == place, 1.0, 0.0).astype(BF16)


def gelu_parts(values):
    density = jnp.exp2(values * values * (-0.5 * LOG2E))
    inverse = 1.0 / (1.0 + jnp.abs(values) * (0.3275911 * 0.7071067811865476))
    series = 0.5 * 1.061405429
    for term in (-1.453152027, 1.421413741, -0.284496736, 0.254829592):
        series = series * inverse + 0.5 * term
    tail = series * inverse * density
    return jnp.where(values < 0.0, tail, 1.0 - tail), density


def forward_kernel(
    where_ref, order_ref, cot_order_ref, ids_ref, places_ref, cols_t_ref,
    quad0_hbm, quad1_hbm, quad2_hbm, quad3_hbm, w_qkv_hbm, w_out_hbm, w_up_hbm, w_down_hbm,
    w_merge_hbm,
    level_two_ref, grad_after_ref, near0, near1, near2, near3, tokens_hbm, packed_hbm, keys_t_hbm,
    attended_hbm, first_t_hbm, middle_hbm, probs_hbm, rest_hbm, slope_hbm, keep_hbm, send_hbm,
    quads_ref, bias_ref, bias_rest, query_t, query_rest, values_t, slope_ref, hidden_ref,
    probs_ref, rest_ref, w_qkv, w_out, w_up, w_down, w_merge, slots, near_ref, tokens_ref,
    packed_ref, keys_t_ref, attended_ref, first_t_ref, middle_ref, quad_sems, in_sems, out_sems,
):
    saves = []

    def save(*pairs):
        saves.extend(load(pairs, out_sems.at[pl.ds(len(saves), len(pairs))]))

    quads = (quad0_hbm, quad1_hbm, quad2_hbm, quad3_hbm)
    quads = load([(quads[q], quads_ref.at[q]) for q in range(4)], quad_sems)
    weights = load(
        [(w_qkv_hbm, w_qkv), (w_out_hbm, w_out), (w_up_hbm, w_up), (w_down_hbm, w_down),
         (w_merge_hbm, w_merge)],
        in_sems,
    )
    query_t[...] = jnp.zeros_like(query_t)
    ids = ids_ref[...].astype(F32).astype(BF16)
    by_row = dot(places_ref[0], ids) * places_ref[1].astype(F32)
    by_col = dot(ids, places_ref[0], 0, 1) * cols_t_ref[...]
    by_row = jnp.sum(by_row, axis=1, keepdims=True)
    by_col = jnp.sum(by_col, axis=0, keepdims=True)
    rest = jnp.concatenate([by_col[:, MAIN:]] * 4, axis=1)
    bias_ref[...] = jnp.where(by_row == by_col[:, :MAIN], 0.0, -1e30)
    bias_rest[...] = jnp.where(by_row == rest, 0.0, -1e30)
    for quad in quads:
        quad.wait()
    tokens = sum(dot(order_ref[q], quads_ref[q]) for q in range(4))
    tokens_ref[...] = tokens.astype(BF16)
    halves = sum(dot(cot_order_ref[q], quads_ref[q]) for q in range(4))
    cotangent = jnp.concatenate([halves[:MERGED], halves[MERGED:]], axis=1).astype(BF16)
    normed_in = normalize(tokens)[0]
    first_norm = normed_in.astype(BF16)
    first_t_ref[...] = turned(normed_in)
    save((tokens_ref, tokens_hbm), (first_t_ref, first_t_hbm))
    weights[0].wait()
    for part in range(3):
        wide = dot(first_norm, w_qkv[:, part * 512 : part * 512 + 512])
        wide = wide * QUERY_SCALE if part == 0 else wide
        for group in range(4):
            packed_ref[part * 4 + group] = wide[:, group * 128 : group * 128 + 128].astype(BF16)
        by_feature = jnp.swapaxes(wide, 0, 1)
        if part:
            (keys_t_ref, values_t)[part - 1][...] = by_feature.astype(BF16)
            continue
        for head in range(16):
            rows = slice(head % 4 * HEAD, head % 4 * HEAD + HEAD)
            own = by_feature[head * HEAD : head * HEAD + HEAD, :MAIN]
            query_t[head, rows, :] = own.astype(BF16)
        for group in range(4):
            rest = by_feature[group * 128 : group * 128 + 128, MAIN:]
            query_rest[group] = spread_rest(rest)
    save((packed_ref, packed_hbm), (keys_t_ref, keys_t_hbm))

    def scores_of(at):
        group, head = at // 5, at % 5
        turn = query_rest[group] if head == 4 else query_t[group * 4 + head]
        return dot(packed_ref[4 + group], turn)

    ahead = scores_of(0)
    for at in range(20):
        group, head = at // 5, at % 5
        scores = ahead + (bias_rest if head == 4 else bias_ref)[...]
        if at < 19:
            ahead = scores_of(at + 1)
        raised = jnp.exp2(scores - jnp.max(scores, axis=0, keepdims=True))
        inverse = 1.0 / jnp.sum(raised, axis=0, keepdims=True)
        probs = (raised * inverse).astype(BF16)
        if head == 4:
            rest_ref[group] = probs
            rows = slice(group * 128, group * 128 + 128)
            rest = gather_rest(dot(values_t[rows, :], probs))
            attended_ref[rows, MAIN:] = rest.astype(BF16)
        else:
            probs_ref[group * 4 + head] = probs
            rows = slice(group * 128 + head * HEAD, group * 128 + head * HEAD + HEAD)
            attended_ref[rows, :MAIN] = dot(values_t[rows, :], probs).astype(BF16)
    save((probs_ref, probs_hbm), (rest_ref, rest_hbm), (attended_ref, attended_hbm))

    attended = turned(attended_ref[...])
    weights[1].wait()
    attn_out = dot(attended, w_out[...]).astype(BF16)
    narrow_middle = (tokens + attn_out.astype(F32)).astype(BF16)
    middle_ref[...] = narrow_middle
    save((middle_ref, middle_hbm))
    middle = narrow_middle.astype(F32)
    second_norm = normalize(middle)[0].astype(BF16)
    mlp = jnp.zeros((TOKENS, 512), F32)
    weights[2].wait()
    weights[3].wait()
    ahead = dot(second_norm, w_up[:, :512])
    for part in range(4):
        cols = slice(part * 512, part * 512 + 512)
        before = ahead
        if part < 3:
            ahead = dot(second_norm, w_up[:, part * 512 + 512 : part * 512 + 1024])
        cumulative, density = gelu_parts(before)
        hidden = (before * cumulative).astype(BF16)
        hidden_ref[:, cols] = hidden
        slope_ref[:, cols] = (cumulative + before * density * 0.3989422804014327).astype(BF16)
        mlp = mlp + dot(hidden, w_down[cols])
    save((slope_ref, slope_hbm))
    after_mlp = (middle + mlp).astype(BF16)
    pieces, inverse_out = merge_norm(after_mlp.astype(F32))
    merged_norm = [v.astype(BF16) for v in pieces]
    order = near_order()
    spread = [dot(v, order) for v in merged_norm]
    blocks = [
        jnp.concatenate([v[:, at * 128 : at * 128 + 128] for v in spread], axis=1).astype(BF16)
        for at in range(4)
    ]
    y = (where_ref[0] >> 1) & 3
    for step, near in enumerate((near0, near1, near2, near3)):
        block = blocks[step]
        for own in range(1, 4):
            block = jnp.where(y == own, blocks[(own + step) % 4], block)
        near_ref[step, :, :512] = block
        near_ref[step, :, 512:] = cotangent
        save((near_ref.at[step], near))

    weights[4].wait()
    level_two_ref[...] = sum(
        dot(merged_norm[p], w_merge[p * 512 : p * 512 + 512]) for p in range(4)
    ).astype(BF16)
    upstream = [dot(cotangent, w_merge[p * 512 : p * 512 + 512], 1, 1) for p in range(4)]
    mean_grad = sum(jnp.sum(v, axis=-1, keepdims=True) for v in upstream) / 2048.0
    mean_cross = (
        sum(jnp.sum(v * u, axis=-1, keepdims=True) for v, u in zip(upstream, pieces)) / 2048.0
    )
    grad_after = jnp.concatenate(
        [inverse_out * (v - mean_grad - u * mean_cross) for v, u in zip(upstream, pieces)], axis=0
    ).astype(BF16)
    grad_after_ref[...] = grad_after
    core = where_ref[0] & 1
    for part in range(4):
        grad = dot(hidden_ref[:, part * 512 : part * 512 + 512], grad_after, 0, 0).astype(BF16)
        grad = grad.reshape(16, 2, 16, 512)
        for unit in range(4):
            for parity in range(2):
                slots[parity, unit, part * 16 : part * 16 + 16] = grad[
                    :, parity, :, unit * 128 : unit * 128 + 128
                ]
    save((slots.at[core], keep_hbm), (slots.at[1 - core], send_hbm))
    for copy in saves:
        copy.wait()


def middle_kernel(
    where_ref, grad_after_ref, middle_ref, attended_ref, w_down_hbm, slope_hbm, w_up_hbm,
    middle_grad_ref, keep_hbm, send_hbm,
    w_down, slope_ref, w_up, slots, sems, out_sems,
):
    loads = []
    for part in range(4):
        cols = pl.ds(part * 512, 512)
        pairs = [(w_down_hbm.at[cols], w_down.at[cols])]
        pairs += [(slope_hbm.at[:, cols], slope_ref.at[part])]
        pairs += [(w_up_hbm.at[:, cols], w_up.at[part])]
        loads.append(load(pairs, sems.at[pl.ds(part * 3, 3)]))
    core = where_ref[0] & 1
    grad_after = grad_after_ref[...]
    normed_mid, inverse_mid = normalize(middle_ref[...].astype(F32))
    second_t = turned(normed_mid)

    def save(units, at):
        return load(
            [(slots.at[core, units], keep_hbm.at[units]),
             (slots.at[1 - core, units], send_hbm.at[units])],
            out_sems.at[pl.ds(at, 2)],
        )

    back_up = jnp.zeros((TOKENS, 512), F32)
    grads_up = []
    for part in range(4):
        cols = slice(part * 512, part * 512 + 512)
        for copy in loads[part]:
            copy.wait()
        grad_before = (
            dot(grad_after, w_down[cols], 1, 1) * slope_ref[part].astype(F32)
        ).astype(BF16)
        grads_up.append(dot(second_t, grad_before))
        back_up = back_up + dot(grad_before, w_up[part], 1, 1)
    for unit in range(4):
        cols = slice(unit * 128, unit * 128 + 128)
        weave([grad[:, cols] for grad in grads_up], slots.at[:, unit], slice(0, 128))
    saves = save(pl.ds(0, 4), 0)
    middle_grad = (
        grad_after.astype(F32) + norm_back(normed_mid, inverse_mid, back_up)
    ).astype(BF16)
    middle_grad_ref[...] = middle_grad
    grad = dot(attended_ref[...], middle_grad)
    columns = [grad[:, p * 128 : p * 128 + 128] for p in range(4)]
    weave(columns, slots.at[:, 4], slice(0, 128))
    saves += save(pl.ds(4, 1), 2)
    for copy in saves:
        copy.wait()


def backward_kernel(
    where_ref, middle_grad_ref, attended_ref, w_out,
    near0_hbm, near1_hbm, near2_hbm, near3_hbm, packed_hbm, keys_t_hbm, probs_hbm, rest_hbm,
    w_qkv_hbm, first_t_hbm, tokens_hbm, order_hbm, level_order_hbm, level_two_hbm,
    out0, out1, out2, out3, keep_hbm, send_hbm,
    grad_heads, grad_heads_t, grad_heads_rest, products, query_grad_t, packed_grad, probs_ref,
    near_ref, packed_ref, keys_t_ref, rest_ref, w_qkv, first_t_ref, tokens_ref, order_ref,
    level_order_ref, level_two_ref, slots, near_sems, sems, out_sems,
):
    loads = load(
        [(packed_hbm, packed_ref), (keys_t_hbm, keys_t_ref), (rest_hbm, rest_ref)]
        + [(probs_hbm.at[pl.ds(g * 4, 4)], probs_ref.at[pl.ds(g * 4, 4)]) for g in range(4)]
        + [(w_qkv_hbm, w_qkv), (first_t_hbm, first_t_ref), (tokens_hbm, tokens_ref),
           (order_hbm, order_ref), (level_order_hbm, level_order_ref),
           (level_two_hbm, level_two_ref)],
        sems,
    )
    nears = (near0_hbm, near1_hbm, near2_hbm, near3_hbm)
    nears = load([(nears[step], near_ref.at[step]) for step in range(4)], near_sems)
    core = where_ref[0] & 1
    middle_grad = middle_grad_ref[...]
    wide = dot(middle_grad, w_out[...], 1, 1).astype(BF16)
    for group in range(4):
        grad_heads[group] = wide[:, group * 128 : group * 128 + 128]
    upstream_t = dot(w_out[...], middle_grad, 1, 1).astype(BF16)
    products[...] = upstream_t.astype(F32) * attended_ref[...].astype(F32)
    grad_heads_t[...] = jnp.zeros_like(grad_heads_t)
    for head in range(16):
        rows = slice(head % 4 * HEAD, head % 4 * HEAD + HEAD)
        grad_heads_t[head, rows, :] = upstream_t[head * HEAD : head * HEAD + HEAD, :MAIN]
    for group in range(4):
        rest = upstream_t[group * 128 : group * 128 + 128].astype(F32)
        grad_heads_rest[group] = spread_rest(rest[:, MAIN:])

    head_of_lane = lax.broadcasted_iota(jnp.int32, (TOKENS, 128), 1) >> 5
    for copy in loads[:3]:
        copy.wait()
    for group in range(4):
        loads[3 + group].wait()
        rows = slice(group * 128, group * 128 + 128)
        queries = packed_ref[group]
        values = packed_ref[8 + group]
        upstream = grad_heads[group]
        grad_keys = jnp.zeros((TOKENS, 128), F32)
        grad_values = jnp.zeros((TOKENS, 128), F32)
        totals = []
        for part in range(4):
            head = group * 4 + part
            at = slice(head * HEAD, head * HEAD + HEAD)
            weights = probs_ref[head]
            total = jnp.sum(products[at, :], axis=0, keepdims=True)
            totals.append(total[:, MAIN:])
            grad_weights = dot(values, grad_heads_t[head])
            scores = (weights.astype(F32) * (grad_weights - total[:, :MAIN])).astype(BF16)
            in_head = head_of_lane == part
            grad_keys = jnp.where(in_head, dot(scores, queries[:MAIN]), grad_keys)
            grad_values = jnp.where(in_head, dot(weights, upstream[:MAIN]), grad_values)
            query_grad = dot(keys_t_ref[at, :], scores) * HEAD ** (-0.5)
            query_grad_t[at, :MAIN] = query_grad.astype(BF16)
        weights = rest_ref[group]
        total = jnp.concatenate(totals, axis=1)
        grad_weights = dot(values, grad_heads_rest[group])
        scores = (weights.astype(F32) * (grad_weights - total)).astype(BF16)
        grad_keys = grad_keys + dot(scores, stack_rest(queries))
        grad_values = grad_values + dot(weights, stack_rest(upstream))
        query_grad = gather_rest(dot(keys_t_ref[rows, :], scores)) * HEAD ** (-0.5)
        query_grad_t[rows, MAIN:] = query_grad.astype(BF16)
        packed_grad[4 + group] = (grad_keys * (1 / LOG2E)).astype(BF16)
        packed_grad[8 + group] = grad_values.astype(BF16)

    for copy in nears:
        copy.wait()
    near = jnp.concatenate([near_ref[step].astype(F32) for step in range(4)], axis=0).astype(BF16)
    grad = dot(near[:, :512], near[:, 512:], 0, 0)
    weave([grad[:, q * 256 : q * 256 + 256] for q in range(4)], slots, slice(384, 640))

    for group in range(4):
        packed_grad[group] = turned(query_grad_t[group * 128 : group * 128 + 128, :])
    for copy in loads[7:]:
        copy.wait()
    first_t = first_t_ref[...]
    back_qkv = jnp.zeros((TOKENS, 512), F32)
    grads = []
    for part in range(3):
        wide = jnp.concatenate([packed_grad[part * 4 + g] for g in range(4)], axis=1)
        grad = dot(first_t, wide)
        grads += [grad[:, q * 128 : q * 128 + 128] for q in range(4)]
        back_qkv = back_qkv + dot(wide, w_qkv[:, part * 512 : part * 512 + 512], 1, 1)
    for part in range(3):
        weave([grads[q * 3 + part] for q in range(4)], slots, slice(part * 128, part * 128 + 128))
    saves = load([(slots.at[core], keep_hbm), (slots.at[1 - core], send_hbm)], out_sems)

    normed_in, inverse_in = normalize(tokens_ref[...].astype(F32))
    grad_first = back_qkv.astype(BF16).astype(F32)
    grad_tokens = (
        middle_grad.astype(F32) + norm_back(normed_in, inverse_in, grad_first)
    ).astype(BF16)
    for quad, out in enumerate((out0, out1, out2, out3)):
        rows = dot(order_ref[quad], grad_tokens)
        for half in range(2):
            level_two = level_two_ref[:, half * 512 : half * 512 + 512]
            rows = rows + dot(level_order_ref[half * 4 + quad], level_two)
        out[...] = rows.astype(BF16)
    for copy in saves:
        copy.wait()


def pair_kernel(keep_hbm, arrived_hbm, *refs, place):
    blocks_hbm, keep_ref, arrived_ref, keep_sems, arrived_sems, out_sems = refs[-6:]
    cols = pl.ds(place, keep_hbm.shape[-1])
    parts = [pl.ds(p * 16, 16) for p in range(4)]
    keeps = load([(keep_hbm.at[p], keep_ref.at[p]) for p in parts], keep_sems)
    arrivals = load([(arrived_hbm.at[p], arrived_ref.at[p]) for p in parts], arrived_sems)
    saves = []
    for part, rows in enumerate(parts):
        keeps[part].wait()
        arrivals[part].wait()
        total = keep_ref[rows].astype(F32) + arrived_ref[rows].astype(F32)
        keep_ref[rows] = total.astype(BF16)
        saves += load(
            [(keep_ref.at[rows], blocks_hbm.at[rows, :, cols])], out_sems.at[pl.ds(part, 1)]
        )
    for save in saves:
        save.wait()


def pair_total(keep_hbm, arrived_hbm, units, keep_ref, arrived_ref, keep_sems, arrived_sems):
    keeps = [(keep_hbm.at[unit], keep_ref.at[at]) for at, unit in enumerate(units)]
    arrivals = [(arrived_hbm.at[unit], arrived_ref.at[at]) for at, unit in enumerate(units)]
    copies = list(zip(load(keeps, keep_sems), load(arrivals, arrived_sems)))
    for at in range(len(units)):
        for copy in copies[at]:
            copy.wait()
        yield at, (keep_ref[at].astype(F32) + arrived_ref[at].astype(F32)).astype(BF16)


def ring_kernel(where_ref, keep_hbm, arrived_hbm, own, send1, send2, send3, *scratch):
    z = where_ref[0] >> 3
    units = [(z + step) & 3 for step in range(4)]
    for at, total in pair_total(keep_hbm, arrived_hbm, units, *scratch):
        (own, send1, send2, send3)[at][...] = total


def halves_kernel(where_ref, keep_hbm, arrived_hbm, own, send, out, *scratch):
    half = (where_ref[0] >> 1) & 1
    units = [half * 2, half * 2 + 1, 2 - half * 2, 3 - half * 2, 4]
    for at, total in pair_total(keep_hbm, arrived_hbm, units, *scratch):
        if at == 4:
            out[...] = total
        else:
            (own, send)[at // 2][:, :, at % 2 * 128 : at % 2 * 128 + 128] = total


def assemble_kernel(*refs):
    downs, ups, out_hbm, blocks_hbm = refs[:4], refs[4:6], refs[6], refs[7]
    down_ref, up_ref, total_ref, sems, out_sem = refs[8:]
    copies = load(
        [(downs[at], down_ref.at[at]) for at in range(4)]
        + [(ups[at], up_ref.at[at]) for at in range(2)]
        + [(out_hbm, total_ref.at[:, :, pl.ds(384, 128)])],
        sems,
    )
    for copy in copies[:4]:
        copy.wait()
    total = sum(down_ref[step].astype(F32) for step in range(4))
    total_ref[:, :, :128] = total.astype(BF16)
    for copy in copies[4:]:
        copy.wait()
    total_ref[:, :, 128:384] = (up_ref[0].astype(F32) + up_ref[1].astype(F32)).astype(BF16)
    save, = load([(total_ref, blocks_hbm.at[:, :, pl.ds(0, 512)])], out_sem)
    save.wait()


def share_kernel(landed_hbm, qkv_ref, out_ref, up_ref, down_ref, merge_ref, landed_ref, sems):
    parts = [pl.ds(p * 16, 16) for p in range(4)]
    loads = load([(landed_hbm.at[p], landed_ref.at[p]) for p in parts], sems)
    down, up, merge = [0.0] * 4, [0.0] * 2, [0.0] * 4
    shared = 0.0
    for chip in range(64):
        z, y = chip // 16, chip // 2 % 4
        if chip % 16 == 0:
            loads[z].wait()
        block = landed_ref[chip].astype(F32)
        down[z] = down[z] + block[:, :128]
        up[y % 2] = up[y % 2] + block[:, 128:384]
        shared = shared + block[:, 384:896]
        merge[y] = merge[y] + block[:, 896:]
    for block in range(4):
        down_ref[:, block * 128 : block * 128 + 128] = down[block]
        rows = slice(block * 4, block * 4 + 4)
        out_ref[:, block * 128 : block * 128 + 128] = shared[rows, :128]
        qkv_ref[:, block * 384 : block * 384 + 384] = shared[rows, 128:]
        for half in range(2):
            at = block * 512 + half * 256
            up_ref[:, at : at + 256] = up[half][rows]
        for y in range(4):
            merge_ref[y * 4 : y * 4 + 4, block * 256 : block * 256 + 256] = merge[y][rows]


def call(kernel, inputs, held, outputs, saved, scratch, micros, kind=BF16, free=(), aliases=(),
         weight=1, loose=False):
    whole, there = pl.BlockSpec(memory_space=pltpu.VMEM), pl.BlockSpec(memory_space=pltpu.HBM)
    specs = [whole if at < held else there for at in range(len(inputs))]
    for at in free:
        specs[at] = pl.BlockSpec(memory_space=pl.ANY)
    if inputs[0].ndim == 1:
        specs[0] = pl.BlockSpec(memory_space=pltpu.SMEM)
    return pl.pallas_call(
        kernel,
        out_shape=[jax.ShapeDtypeStruct(shape, kind) for shape in outputs],
        in_specs=specs,
        out_specs=[
            pl.BlockSpec(memory_space=pl.ANY) if loose else whole if at < saved else there
            for at in range(len(outputs))
        ],
        scratch_shapes=scratch,
        input_output_aliases=dict(aliases),
        compiler_params=pltpu.CompilerParams(vmem_limit_bytes=(56 if micros > 5 else 14) * 2**20),
        cost_estimate=pl.CostEstimate(
            flops=weight * micros * 10**9, bytes_accessed=micros * 10**6, transcendentals=0
        ),
    )(*inputs)


def vmem(*shape):
    return pltpu.VMEM(shape, BF16)


def dmas(count):
    return pltpu.SemaphoreType.DMA((count,))


def exchanged(send):
    return lax.ppermute(send, "core", [(0, 1), (1, 0)])


def pair_scratch(count):
    return [vmem(count, 64, 16, 128), vmem(count, 64, 16, 128), dmas(count), dmas(count)]


def shifted_block(block, down, right):
    route = []
    for source in range(128):
        row, col = source // 16, source % 16
        route.append((source, (row + down) % 8 * 16 + (col + right) % 16))
    return lax.ppermute(block, GRID, route)


def quadrants(field):
    field = field.transpose(1, 2, 0, 3)
    rows, cols = field.shape[0] // 2, field.shape[1] // 2
    corners = field[:rows, :cols], field[:rows, cols:], field[rows:, :cols], field[rows:, cols:]
    return [corner.reshape(-1, field.shape[-1]) for corner in corners]


def roll_back(tokens, cotangent):
    corners = [
        jnp.concatenate([corner, cot[:, :512], cot[:, 512:]], axis=0)
        for corner, cot in zip(quadrants(tokens), quadrants(cotangent))
    ]
    upper_left, upper_right, lower_left, lower_right = corners
    return [
        lower_right,
        shifted_block(lower_left, 0, -1),
        shifted_block(upper_right, -1, 0),
        shifted_block(upper_left, -1, -1),
    ]


def send_forth(corners):
    upper_left, upper_right, lower_left, lower_right = corners
    return [
        shifted_block(lower_right, 1, 1),
        shifted_block(lower_left, 1, 0),
        shifted_block(upper_right, 0, 1),
        upper_left,
    ]


def from_corners(corners):
    upper = jnp.concatenate(corners[:2], axis=1)
    lower = jnp.concatenate(corners[2:], axis=1)
    return jnp.concatenate([upper, lower], axis=0).transpose(2, 0, 1, 3)


def body(tokens, window_ids, cotangent, w_qkv, w_out, w_up, w_down, w_merge):
    order, cot_order = token_order(), cotangent_order()
    level_order = np.concatenate([cot_order[:, :MERGED], cot_order[:, MERGED:]]).transpose(0, 2, 1)
    by_feature, field, hidden_shape = (512, TOKENS), (TOKENS, 512), (TOKENS, 2048)
    near_shape, corner = (MERGED, 1536), (PACKED, 512)
    places = window_places()
    where = lax.axis_index(("z", "y", "core")).reshape(1)
    quads = roll_back(tokens, cotangent)

    probs_shape, rest_shape = (16, TOKENS, MAIN), (4, TOKENS, 128)
    packed_shape, down_shape = (12, TOKENS, 128), (4, 64, 16, 128)
    (level_two, grad_after, near0, near1, near2, near3, tokens_in, packed, keys_t, attended,
     first_t, middle, probs, rest, slope, down_keep, down_send) = call(
        forward_kernel,
        [where, jnp.asarray(order, BF16), jnp.asarray(cot_order, BF16), window_ids,
         jnp.asarray(places, BF16), jnp.asarray(places[1].T, F32), *quads, w_qkv,
         w_out, w_up, w_down, w_merge], 6,
        [(MERGED, 1024), field] + [near_shape] * 4 + [field, packed_shape, by_feature, by_feature,
         by_feature, field, probs_shape, rest_shape, hidden_shape, down_shape, down_shape], 2,
        [vmem(4, *corner), pltpu.VMEM((TOKENS, MAIN), F32), pltpu.VMEM((TOKENS, 128), F32),
         vmem(16, 128, MAIN), vmem(4, 128, 128), vmem(*by_feature), vmem(*hidden_shape),
         vmem(*hidden_shape), vmem(*probs_shape), vmem(*rest_shape), vmem(*w_qkv.shape),
         vmem(*w_out.shape), vmem(*w_up.shape), vmem(*w_down.shape), vmem(*w_merge.shape),
         vmem(2, *down_shape), vmem(4, *near_shape), vmem(*field), vmem(*packed_shape),
         vmem(*by_feature), vmem(*by_feature), vmem(*by_feature), vmem(*field),
         dmas(4), dmas(5), dmas(15)],
        20, free=range(6, 10),
    )
    near = [near0]
    for step, block in ((1, near1), (2, near2), (3, near3)):
        near.append(lax.ppermute(block, "y", [(i, (i + step) % 4) for i in range(4)]))
    middle_grad, keep, send = call(
        middle_kernel,
        [where, grad_after, middle, attended, w_down, slope, w_up], 4,
        [field, (5, 64, 16, 128), (5, 64, 16, 128)], 1,
        [vmem(*w_down.shape), vmem(4, TOKENS, 512), vmem(4, 512, 512), vmem(2, 5, 64, 16, 128),
         dmas(12), dmas(4)],
        7,
    )
    down_keep, *near = lax.optimization_barrier((down_keep, *near))
    down_own, *down_sends = call(
        ring_kernel, [where, down_keep, exchanged(down_send)], 1, [(64, 16, 128)] * 4, 4,
        pair_scratch(4), 2, free=(2,), weight=60,
    )
    downs = [down_own]
    for step, block in enumerate(down_sends, 1):
        downs.append(lax.ppermute(block, "z", [(i, (i + step) % 4) for i in range(4)]))
    up_own, up_send, out_sum = call(
        halves_kernel, [where, keep, exchanged(send)], 1,
        [(64, 16, 256), (64, 16, 256), (64, 16, 128)], 3, pair_scratch(5), 2, free=(2,),
    )
    up_arrived = lax.ppermute(up_send, "y", [(i, i ^ 1) for i in range(4)])
    middle_grad, *_ = lax.optimization_barrier((middle_grad, down_own, up_own))
    *corners, late_keep, late_send = call(
        backward_kernel,
        [where, middle_grad, attended, w_out, *near, packed, keys_t, probs, rest, w_qkv, first_t,
         tokens_in, jnp.asarray(order.transpose(0, 2, 1), BF16), jnp.asarray(level_order, BF16),
         level_two], 4,
        [corner] * 4 + [(64, 16, 640)] * 2, 4,
        [vmem(4, TOKENS, 128), vmem(16, 128, MAIN), vmem(4, 128, 128),
         pltpu.VMEM(by_feature, F32), vmem(*by_feature), vmem(*packed_shape), vmem(*probs_shape),
         vmem(4, *near_shape), vmem(*packed_shape), vmem(*by_feature), vmem(*rest_shape),
         vmem(*w_qkv.shape), vmem(*by_feature), vmem(*field), vmem(4, PACKED, TOKENS),
         vmem(8, PACKED, MERGED), vmem(MERGED, 1024), vmem(2, 64, 16, 640),
         dmas(4), dmas(13), dmas(2)],
        12, free=range(5, 8),
    )
    blocks, = call(
        assemble_kernel, [*downs, up_own, up_arrived, out_sum], 0, [(64, 16, 1152)], 0,
        [vmem(4, 64, 16, 128), vmem(2, 64, 16, 256), vmem(64, 16, 512), dmas(7), dmas(1)], 2,
        free=range(7), weight=60,
        loose=True,
    )
    blocks, *corners = lax.optimization_barrier((blocks, *corners))
    blocks, = call(
        functools.partial(pair_kernel, place=512),
        [late_keep, exchanged(late_send), blocks], 0, [blocks.shape], 0,
        [vmem(64, 16, 640), vmem(64, 16, 640), dmas(4), dmas(4), dmas(4)], 2, free=(1, 2),
        aliases={2: 0}, loose=True,
    )
    corners = send_forth(corners)
    landed = lax.all_to_all(blocks, PAIRS, 0, 0, tiled=True)
    grad_qkv, grad_out, grad_up, grad_down, grad_merge = call(
        share_kernel, [landed], 0, [(4, 1536), (4, 512), (4, 2048), (16, 512), (16, 1024)], 5,
        [vmem(*blocks.shape), dmas(4)], 3, kind=F32,
    )
    grad_tokens = from_corners([c[:MERGED].reshape(6, 6, 2, 512) for c in corners])
    halves = [(c[MERGED : MERGED + 18], c[MERGED + 18 :]) for c in corners]
    level_two = from_corners(
        [jnp.concatenate(pair, axis=1).reshape(3, 3, 2, 1024) for pair in halves]
    )
    return (level_two, grad_tokens, grad_qkv, grad_out, grad_up, grad_down, grad_merge)


def solution(mesh):
    cube = jax.sharding.Mesh(mesh.devices.reshape(4, 2, 4, 2, 2), GRID)
    lat, lon = GRID[:2], GRID[2:]
    field = P(None, lat, lon, None)
    share = P(GRID, None)
    return jax.shard_map(
        body,
        mesh=cube,
        in_specs=(field, P(lat, lon), field, P(), P(), P(), P(), P()),
        out_specs=(field, field, share, share, share, share, share),
        check_vma=False,
    )
```

```python
import functools

import jax
import jax.numpy as jnp
import numpy as np
from jax import lax
from jax.experimental import pallas as pl
from jax.experimental.pallas import tpu as pltpu
from jax.sharding import PartitionSpec as P

HEAD = 32
WIN = 12
TOKENS = 2 * WIN * WIN
MERGED = TOKENS // 4
MAIN = 256
EPS = 1e-05
LOG2E = 1.4426950408889634
QUERY_SCALE = HEAD ** (-0.5) * LOG2E
GRID = ("z", "x_lo", "y", "x_hi", "core")
BF16 = jnp.bfloat16
F32 = jnp.float32

PAIRS = ("z", "x_lo", "y", "x_hi")


PACKED = MERGED + 36


def token_order():
    order = np.zeros((4, TOKENS, PACKED), np.float32)
    for quad in range(4):
        for row in range(6):
            for col in range(6):
                for level in range(2):
                    position = (col % 2) * 2 + row % 2
                    patch = quad * 18 + (row // 2 * 3 + col // 2) * 2 + level
                    order[quad, position * MERGED + patch, (row * 6 + col) * 2 + level] = 1.0
    return order


def window_places():
    places = np.zeros((2, TOKENS, WIN), np.float32)
    for row in range(WIN):
        for col in range(WIN):
            position = (col % 2) * 2 + row % 2
            quad = row // 6 * 2 + col // 6
            patch = quad * 18 + (row % 6 // 2 * 3 + col % 6 // 2) * 2
            for level in range(2):
                places[0, position * MERGED + patch + level, row] = 1.0
                places[1, position * MERGED + patch + level, col] = 1.0
    return places


def cotangent_order():
    order = np.zeros((4, 2 * MERGED, PACKED), np.float32)
    for quad in range(4):
        for half in range(2):
            for patch in range(18):
                order[quad, half * MERGED + quad * 18 + patch, MERGED + half * 18 + patch] = 1.0
    return order


def dot(left, right, left_dim=1, right_dim=0):
    return lax.dot_general(
        left, right, (((left_dim,), (right_dim,)), ((), ())), preferred_element_type=F32
    )


def normalize(wide):
    centered = wide - jnp.mean(wide, axis=-1, keepdims=True)
    inverse_std = lax.rsqrt(jnp.mean(centered * centered, axis=-1, keepdims=True) + EPS)
    return centered * inverse_std, inverse_std


def norm_back(normed, inverse_std, upstream):
    mean_grad = jnp.mean(upstream, axis=-1, keepdims=True)
    mean_cross = jnp.mean(upstream * normed, axis=-1, keepdims=True)
    return inverse_std * (upstream - mean_grad - normed * mean_cross)


def turned(values):
    return jnp.swapaxes(values.astype(F32), 0, 1).astype(BF16)


def own_block(shape):
    rows = lax.broadcasted_iota(jnp.int32, shape, 0) >> 5
    return rows == lax.broadcasted_iota(jnp.int32, shape, 1) >> 5


def spread_rest(values):
    wide = jnp.concatenate([values] * 4, axis=1)
    return jnp.where(own_block(wide.shape), wide, 0.0).astype(BF16)


def gather_rest(blocks):
    kept = jnp.where(own_block(blocks.shape), blocks, 0.0)
    kept = kept + pltpu.roll(kept, 64, 1)
    kept = kept + pltpu.roll(kept, 32, 1)
    return kept[:, :HEAD]


def stack_rest(values):
    tall = jnp.concatenate([values[MAIN:]] * 4, axis=0)
    return jnp.where(own_block(tall.shape), tall, jnp.zeros_like(tall))


def weave(grads, slots, cols):
    tiles = [grad.reshape(64, 8, grad.shape[-1]) for grad in grads]
    turned = [pltpu.roll(tile, 4, 1) for tile in tiles]
    upper = lax.broadcasted_iota(jnp.int32, tiles[0].shape, 1) < 4
    for half in range(2):
        one, two = half * 2, half * 2 + 1
        rows = slice(half * 8, half * 8 + 8)
        slots[0, :, rows, cols] = jnp.where(upper, tiles[one], turned[two]).astype(BF16)
        slots[1, :, rows, cols] = jnp.where(upper, turned[one], tiles[two]).astype(BF16)


def load(pairs, sems):
    copies = [pltpu.make_async_copy(*pair, sems.at[at]) for at, pair in enumerate(pairs)]
    for copy in copies:
        copy.start()
    return copies


def merge_norm(after_mlp):
    pieces = [after_mlp[p * MERGED : (p + 1) * MERGED] for p in range(4)]
    mean = sum(jnp.sum(v, axis=-1, keepdims=True) for v in pieces) / 2048.0
    pieces = [v - mean for v in pieces]
    inverse_out = lax.rsqrt(
        sum(jnp.sum(v * v, axis=-1, keepdims=True) for v in pieces) / 2048.0 + EPS
    )
    return [v * inverse_out for v in pieces], inverse_out


def near_order():
    source = lax.broadcasted_iota(jnp.int32, (512, 1), 0)
    target = lax.broadcasted_iota(jnp.int32, (1, 512), 1)
    place = ((source >> 2) & 3) * 128 + (source >> 4) * 4 + (source & 3)
    return jnp.where(target == place, 1.0, 0.0).astype(BF16)


def gelu_parts(values):
    density = jnp.exp2(values * values * (-0.5 * LOG2E))
    inverse = 1.0 / (1.0 + jnp.abs(values) * (0.3275911 * 0.7071067811865476))
    series = 0.5 * 1.061405429
    for term in (-1.453152027, 1.421413741, -0.284496736, 0.254829592):
        series = series * inverse + 0.5 * term
    tail = series * inverse * density
    return jnp.where(values < 0.0, tail, 1.0 - tail), density


def forward_kernel(
    where_ref, order_ref, cot_order_ref, ids_ref, places_ref, cols_t_ref,
    quad0_hbm, quad1_hbm, quad2_hbm, quad3_hbm, w_qkv_hbm, w_out_hbm, w_up_hbm, w_down_hbm,
    w_merge_hbm,
    level_two_ref, grad_after_ref, near0, near1, near2, near3, tokens_hbm, packed_hbm, keys_t_hbm,
    attended_hbm, first_t_hbm, middle_hbm, probs_hbm, rest_hbm, slope_hbm, keep_hbm, send_hbm,
    quads_ref, bias_ref, bias_rest, query_t, query_rest, values_t, slope_ref, hidden_ref,
    probs_ref, rest_ref, w_qkv, w_out, w_up, w_down, w_merge, slots, near_ref, tokens_ref,
    packed_ref, keys_t_ref, attended_ref, first_t_ref, middle_ref, quad_sems, in_sems, out_sems,
):
    saves = []

    def save(*pairs):
        saves.extend(load(pairs, out_sems.at[pl.ds(len(saves), len(pairs))]))

    quads = (quad0_hbm, quad1_hbm, quad2_hbm, quad3_hbm)
    quads = load([(quads[q], quads_ref.at[q]) for q in range(4)], quad_sems)
    weights = load(
        [(w_qkv_hbm, w_qkv), (w_out_hbm, w_out), (w_up_hbm, w_up), (w_down_hbm, w_down),
         (w_merge_hbm, w_merge)],
        in_sems,
    )
    query_t[...] = jnp.zeros_like(query_t)
    ids = ids_ref[...].astype(F32).astype(BF16)
    by_row = dot(places_ref[0], ids) * places_ref[1].astype(F32)
    by_col = dot(ids, places_ref[0], 0, 1) * cols_t_ref[...]
    by_row = jnp.sum(by_row, axis=1, keepdims=True)
    by_col = jnp.sum(by_col, axis=0, keepdims=True)
    rest = jnp.concatenate([by_col[:, MAIN:]] * 4, axis=1)
    bias_ref[...] = jnp.where(by_row == by_col[:, :MAIN], 0.0, -1e30)
    bias_rest[...] = jnp.where(by_row == rest, 0.0, -1e30)
    for quad in quads:
        quad.wait()
    tokens = sum(dot(order_ref[q], quads_ref[q]) for q in range(4))
    tokens_ref[...] = tokens.astype(BF16)
    halves = sum(dot(cot_order_ref[q], quads_ref[q]) for q in range(4))
    cotangent = jnp.concatenate([halves[:MERGED], halves[MERGED:]], axis=1).astype(BF16)
    normed_in = normalize(tokens)[0]
    first_norm = normed_in.astype(BF16)
    first_t_ref[...] = turned(normed_in)
    save((tokens_ref, tokens_hbm), (first_t_ref, first_t_hbm))
    weights[0].wait()
    for part in range(3):
        wide = dot(first_norm, w_qkv[:, part * 512 : part * 512 + 512])
        wide = wide * QUERY_SCALE if part == 0 else wide
        for group in range(4):
            packed_ref[part * 4 + group] = wide[:, group * 128 : group * 128 + 128].astype(BF16)
        by_feature = jnp.swapaxes(wide, 0, 1)
        if part:
            (keys_t_ref, values_t)[part - 1][...] = by_feature.astype(BF16)
            continue
        for head in range(16):
            rows = slice(head % 4 * HEAD, head % 4 * HEAD + HEAD)
            own = by_feature[head * HEAD : head * HEAD + HEAD, :MAIN]
            query_t[head, rows, :] = own.astype(BF16)
        for group in range(4):
            rest = by_feature[group * 128 : group * 128 + 128, MAIN:]
            query_rest[group] = spread_rest(rest)
    save((packed_ref, packed_hbm), (keys_t_ref, keys_t_hbm))

    def scores_of(at):
        group, head = at // 5, at % 5
        turn = query_rest[group] if head == 4 else query_t[group * 4 + head]
        return dot(packed_ref[4 + group], turn)

    ahead = scores_of(0)
    for at in range(20):
        group, head = at // 5, at % 5
        scores = ahead + (bias_rest if head == 4 else bias_ref)[...]
        if at < 19:
            ahead = scores_of(at + 1)
        raised = jnp.exp2(scores - jnp.max(scores, axis=0, keepdims=True))
        inverse = 1.0 / jnp.sum(raised, axis=0, keepdims=True)
        probs = (raised * inverse).astype(BF16)
        if head == 4:
            rest_ref[group] = probs
            rows = slice(group * 128, group * 128 + 128)
            rest = gather_rest(dot(values_t[rows, :], probs))
            attended_ref[rows, MAIN:] = rest.astype(BF16)
        else:
            probs_ref[group * 4 + head] = probs
            rows = slice(group * 128 + head * HEAD, group * 128 + head * HEAD + HEAD)
            attended_ref[rows, :MAIN] = dot(values_t[rows, :], probs).astype(BF16)
    save((probs_ref, probs_hbm), (rest_ref, rest_hbm), (attended_ref, attended_hbm))

    attended = turned(attended_ref[...])
    weights[1].wait()
    attn_out = dot(attended, w_out[...]).astype(BF16)
    narrow_middle = (tokens + attn_out.astype(F32)).astype(BF16)
    middle_ref[...] = narrow_middle
    save((middle_ref, middle_hbm))
    middle = narrow_middle.astype(F32)
    second_norm = normalize(middle)[0].astype(BF16)
    mlp = jnp.zeros((TOKENS, 512), F32)
    weights[2].wait()
    weights[3].wait()
    ahead = dot(second_norm, w_up[:, :512])
    for part in range(4):
        cols = slice(part * 512, part * 512 + 512)
        before = ahead
        if part < 3:
            ahead = dot(second_norm, w_up[:, part * 512 + 512 : part * 512 + 1024])
        cumulative, density = gelu_parts(before)
        hidden = (before * cumulative).astype(BF16)
        hidden_ref[:, cols] = hidden
        slope_ref[:, cols] = (cumulative + before * density * 0.3989422804014327).astype(BF16)
        mlp = mlp + dot(hidden, w_down[cols])
    save((slope_ref, slope_hbm))
    after_mlp = (middle + mlp).astype(BF16)
    pieces, inverse_out = merge_norm(after_mlp.astype(F32))
    merged_norm = [v.astype(BF16) for v in pieces]
    order = near_order()
    spread = [dot(v, order) for v in merged_norm]
    blocks = [
        jnp.concatenate([v[:, at * 128 : at * 128 + 128] for v in spread], axis=1).astype(BF16)
        for at in range(4)
    ]
    y = (where_ref[0] >> 1) & 3
    for step, near in enumerate((near0, near1, near2, near3)):
        block = blocks[step]
        for own in range(1, 4):
            block = jnp.where(y == own, blocks[(own + step) % 4], block)
        near_ref[step, :, :512] = block
        near_ref[step, :, 512:] = cotangent
        save((near_ref.at[step], near))

    weights[4].wait()
    level_two_ref[...] = sum(
        dot(merged_norm[p], w_merge[p * 512 : p * 512 + 512]) for p in range(4)
    ).astype(BF16)
    upstream = [dot(cotangent, w_merge[p * 512 : p * 512 + 512], 1, 1) for p in range(4)]
    mean_grad = sum(jnp.sum(v, axis=-1, keepdims=True) for v in upstream) / 2048.0
    mean_cross = (
        sum(jnp.sum(v * u, axis=-1, keepdims=True) for v, u in zip(upstream, pieces)) / 2048.0
    )
    grad_after = jnp.concatenate(
        [inverse_out * (v - mean_grad - u * mean_cross) for v, u in zip(upstream, pieces)], axis=0
    ).astype(BF16)
    grad_after_ref[...] = grad_after
    core = where_ref[0] & 1
    for part in range(4):
        grad = dot(hidden_ref[:, part * 512 : part * 512 + 512], grad_after, 0, 0).astype(BF16)
        grad = grad.reshape(16, 2, 16, 512)
        for unit in range(4):
            for parity in range(2):
                slots[parity, unit, part * 16 : part * 16 + 16] = grad[
                    :, parity, :, unit * 128 : unit * 128 + 128
                ]
    save((slots.at[core], keep_hbm), (slots.at[1 - core], send_hbm))
    for copy in saves:
        copy.wait()


def middle_kernel(
    where_ref, grad_after_ref, middle_ref, attended_ref, w_down_hbm, slope_hbm, w_up_hbm,
    middle_grad_ref, keep_hbm, send_hbm,
    w_down, slope_ref, w_up, slots, sems, out_sems,
):
    loads = []
    for part in range(4):
        cols = pl.ds(part * 512, 512)
        pairs = [(w_down_hbm.at[cols], w_down.at[cols])]
        pairs += [(slope_hbm.at[:, cols], slope_ref.at[part])]
        pairs += [(w_up_hbm.at[:, cols], w_up.at[part])]
        loads.append(load(pairs, sems.at[pl.ds(part * 3, 3)]))
    core = where_ref[0] & 1
    grad_after = grad_after_ref[...]
    normed_mid, inverse_mid = normalize(middle_ref[...].astype(F32))
    second_t = turned(normed_mid)

    def save(units, at):
        return load(
            [(slots.at[core, units], keep_hbm.at[units]),
             (slots.at[1 - core, units], send_hbm.at[units])],
            out_sems.at[pl.ds(at, 2)],
        )

    back_up = jnp.zeros((TOKENS, 512), F32)
    grads_up = []
    for part in range(4):
        cols = slice(part * 512, part * 512 + 512)
        for copy in loads[part]:
            copy.wait()
        grad_before = (
            dot(grad_after, w_down[cols], 1, 1) * slope_ref[part].astype(F32)
        ).astype(BF16)
        grads_up.append(dot(second_t, grad_before))
        back_up = back_up + dot(grad_before, w_up[part], 1, 1)
    for unit in range(4):
        cols = slice(unit * 128, unit * 128 + 128)
        weave([grad[:, cols] for grad in grads_up], slots.at[:, unit], slice(0, 128))
    saves = save(pl.ds(0, 4), 0)
    middle_grad = (
        grad_after.astype(F32) + norm_back(normed_mid, inverse_mid, back_up)
    ).astype(BF16)
    middle_grad_ref[...] = middle_grad
    grad = dot(attended_ref[...], middle_grad)
    columns = [grad[:, p * 128 : p * 128 + 128] for p in range(4)]
    weave(columns, slots.at[:, 4], slice(0, 128))
    saves += save(pl.ds(4, 1), 2)
    for copy in saves:
        copy.wait()


def backward_kernel(
    where_ref, middle_grad_ref, attended_ref, w_out,
    near0_hbm, near1_hbm, near2_hbm, near3_hbm, packed_hbm, keys_t_hbm, probs_hbm, rest_hbm,
    w_qkv_hbm, first_t_hbm, tokens_hbm, order_hbm, level_order_hbm, level_two_hbm,
    out0, out1, out2, out3, keep_hbm, send_hbm,
    grad_heads, grad_heads_t, grad_heads_rest, products, query_grad_t, packed_grad, probs_ref,
    near_ref, packed_ref, keys_t_ref, rest_ref, w_qkv, first_t_ref, tokens_ref, order_ref,
    level_order_ref, level_two_ref, slots, near_sems, sems, out_sems,
):
    loads = load(
        [(packed_hbm, packed_ref), (keys_t_hbm, keys_t_ref), (rest_hbm, rest_ref)]
        + [(probs_hbm.at[pl.ds(g * 4, 4)], probs_ref.at[pl.ds(g * 4, 4)]) for g in range(4)]
        + [(w_qkv_hbm, w_qkv), (first_t_hbm, first_t_ref), (tokens_hbm, tokens_ref),
           (order_hbm, order_ref), (level_order_hbm, level_order_ref),
           (level_two_hbm, level_two_ref)],
        sems,
    )
    nears = (near0_hbm, near1_hbm, near2_hbm, near3_hbm)
    nears = load([(nears[step], near_ref.at[step]) for step in range(4)], near_sems)
    core = where_ref[0] & 1
    middle_grad = middle_grad_ref[...]
    wide = dot(middle_grad, w_out[...], 1, 1).astype(BF16)
    for group in range(4):
        grad_heads[group] = wide[:, group * 128 : group * 128 + 128]
    upstream_t = dot(w_out[...], middle_grad, 1, 1).astype(BF16)
    products[...] = upstream_t.astype(F32) * attended_ref[...].astype(F32)
    grad_heads_t[...] = jnp.zeros_like(grad_heads_t)
    for head in range(16):
        rows = slice(head % 4 * HEAD, head % 4 * HEAD + HEAD)
        grad_heads_t[head, rows, :] = upstream_t[head * HEAD : head * HEAD + HEAD, :MAIN]
    for group in range(4):
        rest = upstream_t[group * 128 : group * 128 + 128].astype(F32)
        grad_heads_rest[group] = spread_rest(rest[:, MAIN:])

    head_of_lane = lax.broadcasted_iota(jnp.int32, (TOKENS, 128), 1) >> 5
    for copy in loads[:3]:
        copy.wait()
    for group in range(4):
        loads[3 + group].wait()
        rows = slice(group * 128, group * 128 + 128)
        queries = packed_ref[group]
        values = packed_ref[8 + group]
        upstream = grad_heads[group]
        grad_keys = jnp.zeros((TOKENS, 128), F32)
        grad_values = jnp.zeros((TOKENS, 128), F32)
        totals = []
        for part in range(4):
            head = group * 4 + part
            at = slice(head * HEAD, head * HEAD + HEAD)
            weights = probs_ref[head]
            total = jnp.sum(products[at, :], axis=0, keepdims=True)
            totals.append(total[:, MAIN:])
            grad_weights = dot(values, grad_heads_t[head])
            scores = (weights.astype(F32) * (grad_weights - total[:, :MAIN])).astype(BF16)
            in_head = head_of_lane == part
            grad_keys = jnp.where(in_head, dot(scores, queries[:MAIN]), grad_keys)
            grad_values = jnp.where(in_head, dot(weights, upstream[:MAIN]), grad_values)
            query_grad = dot(keys_t_ref[at, :], scores) * HEAD ** (-0.5)
            query_grad_t[at, :MAIN] = query_grad.astype(BF16)
        weights = rest_ref[group]
        total = jnp.concatenate(totals, axis=1)
        grad_weights = dot(values, grad_heads_rest[group])
        scores = (weights.astype(F32) * (grad_weights - total)).astype(BF16)
        grad_keys = grad_keys + dot(scores, stack_rest(queries))
        grad_values = grad_values + dot(weights, stack_rest(upstream))
        query_grad = gather_rest(dot(keys_t_ref[rows, :], scores)) * HEAD ** (-0.5)
        query_grad_t[rows, MAIN:] = query_grad.astype(BF16)
        packed_grad[4 + group] = (grad_keys * (1 / LOG2E)).astype(BF16)
        packed_grad[8 + group] = grad_values.astype(BF16)

    for copy in nears:
        copy.wait()
    near = jnp.concatenate([near_ref[step].astype(F32) for step in range(4)], axis=0).astype(BF16)
    grad = dot(near[:, :512], near[:, 512:], 0, 0)
    weave([grad[:, q * 256 : q * 256 + 256] for q in range(4)], slots, slice(384, 640))

    for group in range(4):
        packed_grad[group] = turned(query_grad_t[group * 128 : group * 128 + 128, :])
    for copy in loads[7:]:
        copy.wait()
    first_t = first_t_ref[...]
    back_qkv = jnp.zeros((TOKENS, 512), F32)
    grads = []
    for part in range(3):
        wide = jnp.concatenate([packed_grad[part * 4 + g] for g in range(4)], axis=1)
        grad = dot(first_t, wide)
        grads += [grad[:, q * 128 : q * 128 + 128] for q in range(4)]
        back_qkv = back_qkv + dot(wide, w_qkv[:, part * 512 : part * 512 + 512], 1, 1)
    for part in range(3):
        weave([grads[q * 3 + part] for q in range(4)], slots, slice(part * 128, part * 128 + 128))
    saves = load([(slots.at[core], keep_hbm), (slots.at[1 - core], send_hbm)], out_sems)

    normed_in, inverse_in = normalize(tokens_ref[...].astype(F32))
    grad_first = back_qkv.astype(BF16).astype(F32)
    grad_tokens = (
        middle_grad.astype(F32) + norm_back(normed_in, inverse_in, grad_first)
    ).astype(BF16)
    for quad, out in enumerate((out0, out1, out2, out3)):
        rows = dot(order_ref[quad], grad_tokens)
        for half in range(2):
            level_two = level_two_ref[:, half * 512 : half * 512 + 512]
            rows = rows + dot(level_order_ref[half * 4 + quad], level_two)
        out[...] = rows.astype(BF16)
    for copy in saves:
        copy.wait()


def pair_kernel(keep_hbm, arrived_hbm, *refs, place):
    blocks_hbm, keep_ref, arrived_ref, keep_sems, arrived_sems, out_sems = refs[-6:]
    cols = pl.ds(place, keep_hbm.shape[-1])
    parts = [pl.ds(p * 16, 16) for p in range(4)]
    keeps = load([(keep_hbm.at[p], keep_ref.at[p]) for p in parts], keep_sems)
    arrivals = load([(arrived_hbm.at[p], arrived_ref.at[p]) for p in parts], arrived_sems)
    saves = []
    for part, rows in enumerate(parts):
        keeps[part].wait()
        arrivals[part].wait()
        total = keep_ref[rows].astype(F32) + arrived_ref[rows].astype(F32)
        keep_ref[rows] = total.astype(BF16)
        saves += load(
            [(keep_ref.at[rows], blocks_hbm.at[rows, :, cols])], out_sems.at[pl.ds(part, 1)]
        )
    for save in saves:
        save.wait()


def pair_total(keep_hbm, arrived_hbm, units, keep_ref, arrived_ref, keep_sems, arrived_sems):
    keeps = [(keep_hbm.at[unit], keep_ref.at[at]) for at, unit in enumerate(units)]
    arrivals = [(arrived_hbm.at[unit], arrived_ref.at[at]) for at, unit in enumerate(units)]
    copies = list(zip(load(keeps, keep_sems), load(arrivals, arrived_sems)))
    for at in range(len(units)):
        for copy in copies[at]:
            copy.wait()
        yield at, (keep_ref[at].astype(F32) + arrived_ref[at].astype(F32)).astype(BF16)


def ring_kernel(where_ref, keep_hbm, arrived_hbm, own, send1, send2, send3, *scratch):
    z = where_ref[0] >> 3
    units = [(z + step) & 3 for step in range(4)]
    for at, total in pair_total(keep_hbm, arrived_hbm, units, *scratch):
        (own, send1, send2, send3)[at][...] = total


def halves_kernel(where_ref, keep_hbm, arrived_hbm, own, send, out, *scratch):
    half = (where_ref[0] >> 1) & 1
    units = [half * 2, half * 2 + 1, 2 - half * 2, 3 - half * 2, 4]
    for at, total in pair_total(keep_hbm, arrived_hbm, units, *scratch):
        if at == 4:
            out[...] = total
        else:
            (own, send)[at // 2][:, :, at % 2 * 128 : at % 2 * 128 + 128] = total


def assemble_kernel(*refs):
    downs, ups, out_hbm, blocks_hbm = refs[:4], refs[4:6], refs[6], refs[7]
    down_ref, up_ref, total_ref, sems, out_sem = refs[8:]
    copies = load(
        [(downs[at], down_ref.at[at]) for at in range(4)]
        + [(ups[at], up_ref.at[at]) for at in range(2)]
        + [(out_hbm, total_ref.at[:, :, pl.ds(384, 128)])],
        sems,
    )
    for copy in copies[:4]:
        copy.wait()
    total = sum(down_ref[step].astype(F32) for step in range(4))
    total_ref[:, :, :128] = total.astype(BF16)
    for copy in copies[4:]:
        copy.wait()
    total_ref[:, :, 128:384] = (up_ref[0].astype(F32) + up_ref[1].astype(F32)).astype(BF16)
    save, = load([(total_ref, blocks_hbm.at[:, :, pl.ds(0, 512)])], out_sem)
    save.wait()


def share_kernel(landed_hbm, qkv_ref, out_ref, up_ref, down_ref, merge_ref, landed_ref, sems):
    parts = [pl.ds(p * 16, 16) for p in range(4)]
    loads = load([(landed_hbm.at[p], landed_ref.at[p]) for p in parts], sems)
    down, up, merge = [0.0] * 4, [0.0] * 2, [0.0] * 4
    shared = 0.0
    for chip in range(64):
        z, y = chip // 16, chip // 2 % 4
        if chip % 16 == 0:
            loads[z].wait()
        block = landed_ref[chip].astype(F32)
        down[z] = down[z] + block[:, :128]
        up[y % 2] = up[y % 2] + block[:, 128:384]
        shared = shared + block[:, 384:896]
        merge[y] = merge[y] + block[:, 896:]
    for block in range(4):
        down_ref[:, block * 128 : block * 128 + 128] = down[block]
        rows = slice(block * 4, block * 4 + 4)
        out_ref[:, block * 128 : block * 128 + 128] = shared[rows, :128]
        qkv_ref[:, block * 384 : block * 384 + 384] = shared[rows, 128:]
        for half in range(2):
            at = block * 512 + half * 256
            up_ref[:, at : at + 256] = up[half][rows]
        for y in range(4):
            merge_ref[y * 4 : y * 4 + 4, block * 256 : block * 256 + 256] = merge[y][rows]


def call(kernel, inputs, held, outputs, saved, scratch, micros, kind=BF16, free=(), aliases=(),
         weight=1, loose=False):
    whole, there = pl.BlockSpec(memory_space=pltpu.VMEM), pl.BlockSpec(memory_space=pltpu.HBM)
    specs = [whole if at < held else there for at in range(len(inputs))]
    for at in free:
        specs[at] = pl.BlockSpec(memory_space=pl.ANY)
    if inputs[0].ndim == 1:
        specs[0] = pl.BlockSpec(memory_space=pltpu.SMEM)
    return pl.pallas_call(
        kernel,
        out_shape=[jax.ShapeDtypeStruct(shape, kind) for shape in outputs],
        in_specs=specs,
        out_specs=[
            pl.BlockSpec(memory_space=pl.ANY) if loose else whole if at < saved else there
            for at in range(len(outputs))
        ],
        scratch_shapes=scratch,
        input_output_aliases=dict(aliases),
        compiler_params=pltpu.CompilerParams(vmem_limit_bytes=(56 if micros > 5 else 14) * 2**20),
        cost_estimate=pl.CostEstimate(
            flops=weight * micros * 10**9, bytes_accessed=micros * 10**6, transcendentals=0
        ),
    )(*inputs)


def vmem(*shape):
    return pltpu.VMEM(shape, BF16)


def dmas(count):
    return pltpu.SemaphoreType.DMA((count,))


def exchanged(send):
    return lax.ppermute(send, "core", [(0, 1), (1, 0)])


def pair_scratch(count):
    return [vmem(count, 64, 16, 128), vmem(count, 64, 16, 128), dmas(count), dmas(count)]


def shifted_block(block, down, right):
    route = []
    for source in range(128):
        row, col = source // 16, source % 16
        route.append((source, (row + down) % 8 * 16 + (col + right) % 16))
    return lax.ppermute(block, GRID, route)


def quadrants(field):
    field = field.transpose(1, 2, 0, 3)
    rows, cols = field.shape[0] // 2, field.shape[1] // 2
    corners = field[:rows, :cols], field[:rows, cols:], field[rows:, :cols], field[rows:, cols:]
    return [corner.reshape(-1, field.shape[-1]) for corner in corners]


def roll_back(tokens, cotangent):
    corners = [
        jnp.concatenate([corner, cot[:, :512], cot[:, 512:]], axis=0)
        for corner, cot in zip(quadrants(tokens), quadrants(cotangent))
    ]
    upper_left, upper_right, lower_left, lower_right = corners
    from_both = shifted_block(upper_left, -1, -1)
    from_below = shifted_block(upper_right, -1, 0)
    from_right = shifted_block(lower_left, 0, -1)
    return [lower_right, from_right, from_below, from_both]


def send_forth(corners):
    upper_left, upper_right, lower_left, lower_right = corners
    return [
        shifted_block(lower_right, 1, 1),
        shifted_block(lower_left, 1, 0),
        shifted_block(upper_right, 0, 1),
        upper_left,
    ]


def from_corners(corners):
    upper = jnp.concatenate(corners[:2], axis=1)
    lower = jnp.concatenate(corners[2:], axis=1)
    return jnp.concatenate([upper, lower], axis=0).transpose(2, 0, 1, 3)


def body(tokens, window_ids, cotangent, w_qkv, w_out, w_up, w_down, w_merge):
    order, cot_order = token_order(), cotangent_order()
    level_order = np.concatenate([cot_order[:, :MERGED], cot_order[:, MERGED:]]).transpose(0, 2, 1)
    by_feature, field, hidden_shape = (512, TOKENS), (TOKENS, 512), (TOKENS, 2048)
    near_shape, corner = (MERGED, 1536), (PACKED, 512)
    places = window_places()
    where = lax.axis_index(("z", "y", "core")).reshape(1)
    quads = roll_back(tokens, cotangent)

    probs_shape, rest_shape = (16, TOKENS, MAIN), (4, TOKENS, 128)
    packed_shape, down_shape = (12, TOKENS, 128), (4, 64, 16, 128)
    (level_two, grad_after, near0, near1, near2, near3, tokens_in, packed, keys_t, attended,
     first_t, middle, probs, rest, slope, down_keep, down_send) = call(
        forward_kernel,
        [where, jnp.asarray(order, BF16), jnp.asarray(cot_order, BF16), window_ids,
         jnp.asarray(places, BF16), jnp.asarray(places[1].T, F32), *quads, w_qkv,
         w_out, w_up, w_down, w_merge], 6,
        [(MERGED, 1024), field] + [near_shape] * 4 + [field, packed_shape, by_feature, by_feature,
         by_feature, field, probs_shape, rest_shape, hidden_shape, down_shape, down_shape], 2,
        [vmem(4, *corner), pltpu.VMEM((TOKENS, MAIN), F32), pltpu.VMEM((TOKENS, 128), F32),
         vmem(16, 128, MAIN), vmem(4, 128, 128), vmem(*by_feature), vmem(*hidden_shape),
         vmem(*hidden_shape), vmem(*probs_shape), vmem(*rest_shape), vmem(*w_qkv.shape),
         vmem(*w_out.shape), vmem(*w_up.shape), vmem(*w_down.shape), vmem(*w_merge.shape),
         vmem(2, *down_shape), vmem(4, *near_shape), vmem(*field), vmem(*packed_shape),
         vmem(*by_feature), vmem(*by_feature), vmem(*by_feature), vmem(*field),
         dmas(4), dmas(5), dmas(15)],
        20, free=range(6, 10),
    )
    near = [near0]
    for step, block in ((1, near1), (2, near2), (3, near3)):
        near.append(lax.ppermute(block, "y", [(i, (i + step) % 4) for i in range(4)]))
    middle_grad, keep, send = call(
        middle_kernel,
        [where, grad_after, middle, attended, w_down, slope, w_up], 4,
        [field, (5, 64, 16, 128), (5, 64, 16, 128)], 1,
        [vmem(*w_down.shape), vmem(4, TOKENS, 512), vmem(4, 512, 512), vmem(2, 5, 64, 16, 128),
         dmas(12), dmas(4)],
        7,
    )
    down_keep, *near = lax.optimization_barrier((down_keep, *near))
    down_own, *down_sends = call(
        ring_kernel, [where, down_keep, exchanged(down_send)], 1, [(64, 16, 128)] * 4, 4,
        pair_scratch(4), 2, free=(2,), weight=60,
    )
    downs = [down_own]
    for step, block in enumerate(down_sends, 1):
        downs.append(lax.ppermute(block, "z", [(i, (i + step) % 4) for i in range(4)]))
    up_own, up_send, out_sum = call(
        halves_kernel, [where, keep, exchanged(send)], 1,
        [(64, 16, 256), (64, 16, 256), (64, 16, 128)], 3, pair_scratch(5), 2, free=(2,),
    )
    up_arrived = lax.ppermute(up_send, "y", [(i, i ^ 1) for i in range(4)])
    middle_grad, *_ = lax.optimization_barrier((middle_grad, down_own, up_own))
    *corners, late_keep, late_send = call(
        backward_kernel,
        [where, middle_grad, attended, w_out, *near, packed, keys_t, probs, rest, w_qkv, first_t,
         tokens_in, jnp.asarray(order.transpose(0, 2, 1), BF16), jnp.asarray(level_order, BF16),
         level_two], 4,
        [corner] * 4 + [(64, 16, 640)] * 2, 4,
        [vmem(4, TOKENS, 128), vmem(16, 128, MAIN), vmem(4, 128, 128),
         pltpu.VMEM(by_feature, F32), vmem(*by_feature), vmem(*packed_shape), vmem(*probs_shape),
         vmem(4, *near_shape), vmem(*packed_shape), vmem(*by_feature), vmem(*rest_shape),
         vmem(*w_qkv.shape), vmem(*by_feature), vmem(*field), vmem(4, PACKED, TOKENS),
         vmem(8, PACKED, MERGED), vmem(MERGED, 1024), vmem(2, 64, 16, 640),
         dmas(4), dmas(13), dmas(2)],
        12, free=range(5, 8),
    )
    blocks, = call(
        assemble_kernel, [*downs, up_own, up_arrived, out_sum], 0, [(64, 16, 1152)], 0,
        [vmem(4, 64, 16, 128), vmem(2, 64, 16, 256), vmem(64, 16, 512), dmas(7), dmas(1)], 2,
        free=range(7), weight=60,
        loose=True,
    )
    blocks, *corners = lax.optimization_barrier((blocks, *corners))
    blocks, = call(
        functools.partial(pair_kernel, place=512),
        [late_keep, exchanged(late_send), blocks], 0, [blocks.shape], 0,
        [vmem(64, 16, 640), vmem(64, 16, 640), dmas(4), dmas(4), dmas(4)], 2, free=(1, 2),
        aliases={2: 0}, loose=True,
    )
    corners = send_forth(corners)
    blocks, *corners = lax.optimization_barrier((blocks, *corners))
    landed = lax.all_to_all(blocks, PAIRS, 0, 0, tiled=True)
    grad_qkv, grad_out, grad_up, grad_down, grad_merge = call(
        share_kernel, [landed], 0, [(4, 1536), (4, 512), (4, 2048), (16, 512), (16, 1024)], 5,
        [vmem(*blocks.shape), dmas(4)], 3, kind=F32,
    )
    grad_tokens = from_corners([c[:MERGED].reshape(6, 6, 2, 512) for c in corners])
    halves = [(c[MERGED : MERGED + 18], c[MERGED + 18 :]) for c in corners]
    level_two = from_corners(
        [jnp.concatenate(pair, axis=1).reshape(3, 3, 2, 1024) for pair in halves]
    )
    return (level_two, grad_tokens, grad_qkv, grad_out, grad_up, grad_down, grad_merge)


def solution(mesh):
    cube = jax.sharding.Mesh(mesh.devices.reshape(4, 2, 4, 2, 2), GRID)
    lat, lon = GRID[:2], GRID[2:]
    field = P(None, lat, lon, None)
    share = P(GRID, None)
    return jax.shard_map(
        body,
        mesh=cube,
        in_specs=(field, P(lat, lon), field, P(), P(), P(), P(), P()),
        out_specs=(field, field, share, share, share, share, share),
        check_vma=False,
    )
```
